256 devices in a mesh: gx: 16 (over y, x), gy: 8 (over z_hi, core), gz: 2 (over z_lo).
Axes of the slice: x: 4, y: 4, z: 8 (z_hi: 4, z_lo: 2; z = z_hi * 2 + z_lo), core: 2. Of those that a mesh axis runs over, the one named last changes fastest.
Arguments:
- checkpoint: float32 [5, 32, 128, 1024], P(None, 'gz', 'gx', 'gy'), may hold values from -0.6 to 0.6
- gruneisen: float32 [32, 128, 1024], P('gz', 'gx', 'gy'), may hold values from 1 to 3
- switch: int32 [2, 32, 128, 1024], P(None, 'gz', 'gx', 'gy'), may hold values 0 or 1
- probes: int32 [65536], P(('gx', 'gy', 'gz')), may hold values from 0 to 16383
- observed: float32 [65536], P(('gx', 'gy', 'gz')), may hold values from -1 to 1
Outputs:
- direction: float32 [32, 128, 1024], P('gz', 'gx', 'gy')
- misfit: float32 [], replicated
The draws below stay inside these ranges and needn't reach their ends.
Inputs may be any that keep to these rules, and one draw needn't show every extreme that they name: `probes`: entry k names a cell of the block of the device that holds entry k, as the flat index (z * 8 + x) * 128 + y within that block; cells may repeat.
All inputs are finite; a program needn't handle non-finite values. No bound on the sum of `switch` on one device may be relied on, other than what follows from the above.
Results may differ from the reference program's by a relative error of at most 0.0001.
Values sent between devices are 32-bit elements; how exact they have to be, the bound alone decides.
No kernel may reach another device: no remote copies, remote signals or barrier semaphores. Data moves between devices by JAX's collectives and lax.ppermute only.
A program may use at most 64 MiB of HBM per device.

```python
import math
import jax
import jax.numpy as jnp
from jax import lax

CX = 8
CY = 128
CZ = 16
PROBE_DEV = 256
STEPS = 2
NX = 128
NY = 1024
NZ = 32
PROBES = 65536
N_GY = 8
N_GZ = 2


def plant(values, own_key, least, top_value):
    longest = values.shape.index(max(values.shape))
    spots = []
    for shift in (0, 1):
        where = [jax.random.randint(jax.random.fold_in(own_key, axis), (), 0, length) for axis, length in enumerate(values.shape)]
        where[longest] = (where[longest] + shift) % values.shape[longest]
        spots.append(tuple(where))
    return values.at[spots[0]].set(least).at[spots[1]].set(top_value)


def steps_of(key, extent, split, least, largest):
    def one(axis_at, parts):
        heights = jax.random.uniform(jax.random.fold_in(jax.random.fold_in(key, 6), axis_at), (parts,), jnp.float32, least / len(split), largest / len(split))
        return jnp.repeat(jnp.exp(heights), extent[axis_at] // parts).reshape((-1,) + (1,) * (len(extent) - axis_at - 1))

    factor_of = one(*split[0])
    for cut in split[1:]:
        factor_of = factor_of * one(*cut)
    return factor_of


def normal_values(rng, shape, spread, most, split=(), held_as=jnp.bfloat16):
    factor_of = steps_of(rng, shape, split, -0.22, 0.18) if split else 1.0
    values = jax.random.normal(rng, shape, jnp.float32) * spread * factor_of
    return jnp.minimum(jnp.maximum(values, -most), most).astype(held_as)


def setup_inputs(seed: int = 0) -> dict:
    streams_of = jax.random.split(jax.random.key(seed), 6)
    checkpoint = normal_values(streams_of[0], (5, NZ, NX, NY), 0.15, 0.6, ((1, 2), (2, 16), (3, 8)), jnp.float32)
    gruneisen = jnp.clip(jnp.exp(math.log(3.0) - 1.0986123 * jax.random.uniform(streams_of[1], (NZ, NX, NY), jnp.float32) ** steps_of(streams_of[1], (NZ, NX, NY), ((0, 2), (1, 16), (2, 8)), -0.2, 0.2)), 1.0, 3.0)
    switch = plant((jax.random.randint(streams_of[2], (STEPS, NZ, NX, NY), 0, 2) < 1).astype(jnp.int32), jax.random.fold_in(streams_of[2], 1), 0, 1)
    probes = plant(jax.random.randint(streams_of[3], (PROBES,), 0, CX * CY * CZ), jax.random.fold_in(streams_of[3], 1), 0, (CX * CY * CZ) - 1).astype(jnp.int32)
    observed = normal_values(streams_of[4], (PROBES,), 0.2, 1.0, ((0, 256),), jnp.float32)
    return {"checkpoint": checkpoint, "gruneisen": gruneisen, "switch": switch, "probes": probes, "observed": observed}


bulk_modulus = 2.0
slope_coeff = 1.5
signal_speed = 2.5
time_ratio = 0.1
quad_viscosity = 4.0
small_eps = 1e-12

def trim_others(values, keep_dim, first_dim):
    for spatial in range(3):
        if spatial != keep_dim:
            where_dim = first_dim + spatial
            values = lax.slice_in_dim(values, 2, values.shape[where_dim] - 2, axis=where_dim)
    return values

def inner_cells(values, where_dim):
    return lax.slice_in_dim(values, 1, values.shape[where_dim] - 1, axis=where_dim)

def pair_slices(values, where_dim):
    length = values.shape[where_dim]
    return (lax.slice_in_dim(values, 1, length, axis=where_dim), lax.slice_in_dim(values, 0, length - 1, axis=where_dim))

def advance(pad_state, pad_gamma, pad_switch):
    density = 1.0 + pad_state[0]
    velocity = pad_state[1:4] / density
    internal = pad_state[4] / density - 0.5 * lax.optimization_barrier(jnp.sum(velocity * velocity, axis=0))
    pressure = bulk_modulus * (pad_state[0] + slope_coeff * pad_state[0] * pad_state[0]) + pad_gamma * density * internal
    change = jnp.zeros_like(pad_state[:, 2:-2, 2:-2, 2:-2])
    for component, spatial in ((0, 1), (1, 2), (2, 0)):
        state_line = trim_others(pad_state, spatial, 1)
        speed_line = trim_others(velocity[component], spatial, 0)
        length = speed_line.shape[spatial]
        slope_cells = 0.5 * (lax.slice_in_dim(speed_line, 2, length, axis=spatial) - lax.slice_in_dim(speed_line, 0, length - 2, axis=spatial))
        squeeze = jnp.minimum(slope_cells, 0.0)
        dens_mid = inner_cells(trim_others(density, spatial, 0), spatial)
        press_mid = inner_cells(trim_others(pressure, spatial, 0), spatial)
        switch_mid = inner_cells(trim_others(pad_switch, spatial, 0), spatial)
        total_press = press_mid + switch_mid * quad_viscosity * dens_mid * squeeze * squeeze
        speed_mid = inner_cells(speed_line, spatial)
        state_mid = inner_cells(state_line, spatial + 1)
        momentum_rows = [state_mid[1 + member] * speed_mid for member in range(3)]
        momentum_rows[component] = momentum_rows[component] + total_press
        flux_rows = jnp.stack([state_mid[1 + component]] + momentum_rows + [(state_mid[4] + total_press) * speed_mid])
        flux_upper, flux_lower = pair_slices(flux_rows, spatial + 1)
        state_upper, state_lower = pair_slices(state_mid, spatial + 1)
        face_flux = 0.5 * (flux_lower + flux_upper) - 0.5 * signal_speed * (state_upper - state_lower)
        face_upper, face_lower = pair_slices(face_flux, spatial + 1)
        change = change + face_upper - face_lower
    return pad_state[:, 2:-2, 2:-2, 2:-2] - time_ratio * change

def reference(checkpoint, gruneisen, switch, probes, observed):
    switch_f = switch.astype(jnp.float32)
    pad_w = ((2, 2), (2, 2), (2, 2))

    def forward(gamma_field):
        current = checkpoint
        for step_index in range(STEPS):
            current = advance(jnp.pad(current, ((0, 0),) + pad_w), jnp.pad(gamma_field, pad_w), jnp.pad(switch_f[step_index], pad_w))
        return current
    owner_rank = jnp.arange(probes.shape[0], dtype=jnp.int32) // PROBE_DEV
    block_z = owner_rank % N_GZ
    block_y = owner_rank // N_GZ % N_GY
    block_x = owner_rank // (N_GZ * N_GY)
    local_z = probes // (CX * CY)
    local_x = probes // CY % CX
    local_y = probes % CY
    flat_index = ((block_z * CZ + local_z) * NX + block_x * CX + local_x) * NY + block_y * CY + local_y

    def total_of(gamma_field):
        final_state = forward(gamma_field)
        density = 1.0 + final_state[0].reshape(-1)[flat_index]
        probe_speed = final_state[1].reshape(-1)[flat_index] / density
        residual = probe_speed - observed
        return jnp.sum(residual * residual)
    total_misfit, pullback = jax.vjp(total_of, gruneisen)
    gradient_field, = pullback(jnp.ones((), gruneisen.dtype))
    misfit = total_misfit / probes.shape[0]
    direction = gradient_field / jnp.sqrt(jnp.mean(gradient_field * gradient_field) + small_eps)
    return (direction, misfit)
```

```python
import functools
import jax
import jax.numpy as jnp
from jax import lax
from jax.experimental import pallas as pl
from jax.experimental.pallas import tpu as pltpu
from jax.sharding import PartitionSpec as P

NZ, NX, NY = 16, 8, 128
CELLS = NZ * NX
bulk_modulus = 2.0
slope_coeff = 1.5
signal_speed = 2.5
time_ratio = 0.1
quad_viscosity = 4.0
small_eps = 1e-12
HALF_C = 0.5 * signal_speed
HALF_T = 0.5 * time_ratio
F32 = jnp.float32


def primitives(r, mx, my, mz, en, gamma):
    inv = 1.0 / (1.0 + r)
    ux, uy, uz = mx * inv, my * inv, mz * inv
    heat = en - 0.5 * (mx * ux + my * uy + mz * uz)
    press = bulk_modulus * (r + slope_coeff * r * r) + gamma * heat
    return ux, uy, uz, heat, press


def total_pressure(press, sw, r, slope):
    squeeze = jnp.minimum(slope, 0.0)
    return press + sw * quad_viscosity * (1.0 + r) * squeeze * squeeze


def flux(state, axis, speed, total):
    rows = [state[1 + axis]] + [state[1 + k] * speed for k in range(3)]
    rows[1 + axis] = rows[1 + axis] + total
    return rows + [(state[4] + total) * speed]


def upper_part(f, u):
    return 0.5 * f - HALF_C * u


def lower_part(f, u):
    return 0.5 * f + HALF_C * u


def layer(z):
    return pl.ds(NX * z, NX)


def x_row(x):
    return pl.ds(x, NZ, stride=NX)


def lanes():
    return lax.broadcasted_iota(jnp.int32, (NX, NY), 1)


def y_next(value, column, lane):
    return jnp.where(lane == NY - 1, column, pltpu.roll(value, NY - 1, 1))


def y_prev(value, column, lane):
    return jnp.where(lane == 0, column, pltpu.roll(value, 1, 1))


def inside(flag):
    return jnp.where(flag, 1.0, 0.0).astype(F32)


def masks(mesh):
    ix, iy, iz = lax.axis_index("gx"), lax.axis_index("gy"), lax.axis_index("gz")
    return (
        (inside(ix > 0), inside(ix < mesh["gx"] - 1)),
        (inside(iy > 0), inside(iy < mesh["gy"] - 1)),
        (inside(iz > 0), inside(iz < mesh["gz"] - 1)),
        iz == 0,
    )


def face_layer(is_first, depth):
    return jnp.where(is_first, NZ - 1 - depth, depth)


def dyn_layer(z):
    return pl.ds(pl.multiple_of(NX * z, NX), NX)


def pack_columns(values, lane):
    out = pltpu.roll(values[0], 1, 1)
    for i in range(1, len(values)):
        out = jnp.where(lane < 2 * i, out, pltpu.roll(values[i], 2 * i + 1, 1))
    return out


def prep_kernel(mesh, u_ref, g_ref, s_ref, xlo, xhi, ylo, yhi, zs, yown, yp):
    _, _, _, first = masks(mesh)
    for out, edge, second in ((xlo, 0, 1), (xhi, NX - 1, NX - 2)):
        st = [u_ref[k, x_row(edge), :] for k in range(5)]
        press = primitives(*st, g_ref[x_row(edge), :])[4]
        for k in range(5):
            out[k] = st[k]
        out[5] = press
        out[6] = s_ref[0, x_row(edge), :].astype(F32)
        out[7] = u_ref[1, x_row(second), :] / (1.0 + u_ref[0, x_row(second), :])
    za, zb = face_layer(first, 0), face_layer(first, 1)
    st = [u_ref[k, dyn_layer(za), :] for k in range(5)]
    for k in range(5):
        zs[k] = st[k]
    zs[5] = primitives(*st, g_ref[dyn_layer(za), :])[4]
    zs[6] = s_ref[0, dyn_layer(za), :].astype(F32)
    zs[7] = u_ref[3, dyn_layer(zb), :] / (1.0 + u_ref[0, dyn_layer(zb), :])
    lane = lanes()
    for z in range(NZ):
        vals = [u_ref[k, layer(z), :] for k in range(5)]
        vals += [g_ref[layer(z), :], s_ref[0, layer(z), :].astype(F32)]
        out = pltpu.roll(vals[0], 2, 1)
        for i in range(1, 7):
            out = jnp.where(lane < 4 * i, out, pltpu.roll(vals[i], 4 * i + 2, 1))
        yp[layer(z), :] = out
    rows = yp[...].T
    for out, edge, second, own in ((yhi, 1, 0, 1), (ylo, 2, 3, 0)):
        st = [rows[4 * k + edge : 4 * k + edge + 1] for k in range(7)]
        prim = primitives(*st[:6])
        for k in range(5):
            out[k : k + 1] = st[k]
        out[5:6] = prim[4]
        out[6:7] = st[6]
        out[7:8] = rows[8 + second : 9 + second] / (1.0 + rows[second : second + 1])
        yown[own : own + 1] = prim[1]


def step_kernel(
    mesh, u_ref, g_ref, s_ref, xl, xh, yl, yh, zr, yown,
    o_ref, xlo, xhi, ylo, yhi, zs,
    vx, vy, vz, pr, ax, bx, az, bz, ch, yr, yc, yp,
):
    (mxl, mxh), (myl, myh), (mzl, mzh), first = masks(mesh)
    lane = lanes()
    for z in range(NZ):
        ux, uy, uz, _, press = primitives(*[u_ref[k, layer(z), :] for k in range(5)], g_ref[layer(z), :])
        vx[pl.ds(24 * z + 8, 8), :] = ux
        vy[layer(z), :] = uy
        vz[layer(z + 1), :] = uz
        pr[layer(z), :] = press
    low = [xl[k] * mxl for k in range(8)]
    high = [xh[k] * mxh for k in range(8)]
    speed = low[1] / (1.0 + low[0])
    vx[pl.ds(7, NZ, stride=24), :] = speed
    slope = 0.5 * (vx[pl.ds(8, NZ, stride=24), :] - low[7])
    fl = flux(low[:5], 0, speed, total_pressure(low[5], low[6], low[0], slope))
    for k in range(5):
        bx[k, pl.ds(7, NZ, stride=16), :] = lower_part(fl[k], low[k])
    speed = high[1] / (1.0 + high[0])
    vx[pl.ds(16, NZ, stride=24), :] = speed
    slope = 0.5 * (high[7] - vx[pl.ds(15, NZ, stride=24), :])
    fl = flux(high[:5], 0, speed, total_pressure(high[5], high[6], high[0], slope))
    for k in range(5):
        ax[k, pl.ds(8, NZ, stride=16), :] = upper_part(fl[k], high[k])
    far = [zr[k] for k in range(8)]
    speed = far[3] / (1.0 + far[0])
    own = vz[dyn_layer(face_layer(first, 0) + 1), :]
    slope = (far[7] - own) * jnp.where(first, 0.5, -0.5)
    fl = flux(far[:5], 2, speed, total_pressure(far[5], far[6], far[0], slope))
    for k in range(5):
        bz[k, layer(0), :] = lower_part(fl[k], far[k]) * mzl
        az[k, layer(NZ), :] = upper_part(fl[k], far[k]) * mzh
    vz[layer(0), :] = speed * mzl
    vz[layer(NZ + 1), :] = speed * mzh
    low = [yl[k : k + 1] * myl for k in range(8)]
    high = [yh[k : k + 1] * myh for k in range(8)]
    speed = low[2] / (1.0 + low[0])
    yr[10:11, :] = speed
    slope = 0.5 * (yown[0:1] - low[7])
    fl = flux(low[:5], 1, speed, total_pressure(low[5], low[6], low[0], slope))
    for k in range(5):
        yr[k : k + 1, :] = lower_part(fl[k], low[k])
    speed = high[2] / (1.0 + high[0])
    yr[11:12, :] = speed
    slope = 0.5 * (high[7] - yown[1:2])
    fl = flux(high[:5], 1, speed, total_pressure(high[5], high[6], high[0], slope))
    for k in range(5):
        yr[5 + k : 6 + k, :] = upper_part(fl[k], high[k])
    yr[12:16, :] = jnp.zeros((4, NY), F32)
    yc[...] = yr[...].T
    for z in range(NZ):
        st = [u_ref[k, layer(z), :] for k in range(5)]
        sw = s_ref[0, layer(z), :].astype(F32)
        press = pr[layer(z), :]
        visc = sw * quad_viscosity * (1.0 + st[0])
        uy = vy[layer(z), :]
        ux = vx[pl.ds(24 * z + 8, 8), :]
        uz = vz[layer(z + 1), :]

        def col(i):
            return yc[layer(z), i : i + 1]

        def total(up, down):
            squeeze = jnp.minimum(0.5 * (up - down), 0.0)
            return press + visc * squeeze * squeeze

        fx = flux(st, 0, ux, total(vx[pl.ds(24 * z + 9, 8), :], vx[pl.ds(24 * z + 7, 8), :]))
        fy = flux(st, 1, uy, total(y_next(uy, col(11), lane), y_prev(uy, col(10), lane)))
        fz = flux(st, 2, uz, total(vz[layer(z + 2), :], vz[layer(z), :]))
        for k in range(5):
            ax[k, pl.ds(16 * z, 8), :] = upper_part(fx[k], st[k])
            bx[k, pl.ds(16 * z + 8, 8), :] = lower_part(fx[k], st[k])
            az[k, layer(z), :] = upper_part(fz[k], st[k])
            bz[k, layer(z + 1), :] = lower_part(fz[k], st[k])
            ch[k, layer(z), :] = (
                3.0 * signal_speed * st[k]
                + y_next(upper_part(fy[k], st[k]), col(5 + k), lane)
                - y_prev(lower_part(fy[k], st[k]), col(k), lane)
            )
    for z in range(NZ):
        new = []
        for k in range(5):
            change = (
                ch[k, layer(z), :]
                + (ax[k, pl.ds(16 * z + 1, 8), :] - bx[k, pl.ds(16 * z + 7, 8), :])
                + (az[k, layer(z + 1), :] - bz[k, layer(z), :])
            )
            new.append(u_ref[k, layer(z), :] - time_ratio * change)
            o_ref[k, layer(z), :] = new[k]
        yp[layer(z), :] = pack_columns(new[:3], lane)
    for out, edge, second in ((xlo, 0, 1), (xhi, NX - 1, NX - 2)):
        st = [o_ref[k, x_row(edge), :] for k in range(5)]
        out[0] = st[0]
        out[1] = st[1]
        out[2] = primitives(*st, g_ref[x_row(edge), :])[4]
        out[3] = s_ref[1, x_row(edge), :].astype(F32)
        out[4] = o_ref[1, x_row(second), :] / (1.0 + o_ref[0, x_row(second), :])
    za = face_layer(first, 0)
    r, mx, mz = [o_ref[k, dyn_layer(za), :] for k in (0, 1, 3)]
    sign = jnp.where(first, HALF_C, -HALF_C)
    zs[0] = 0.5 * mz + sign * r
    zs[1] = 0.5 * mx * (mz / (1.0 + r)) + sign * mx
    rows = yp[...].T
    r, mx, my = rows[0:1], rows[2:3], rows[4:5]
    yhi[...] = jnp.zeros((8, NY), F32)
    yhi[0:1] = lower_part(my, r)
    yhi[1:2] = lower_part(mx * (my / (1.0 + r)), mx)
    r, mx, my = rows[1:2], rows[3:4], rows[5:6]
    ylo[...] = jnp.zeros((8, NY), F32)
    ylo[0:1] = upper_part(my, r)
    ylo[1:2] = upper_part(mx * (my / (1.0 + r)), mx)


def columns_of(low, high, count, low_mask, high_mask):
    rows = [low[k : k + 1] * low_mask for k in range(count)]
    rows += [high[k : k + 1] * high_mask for k in range(count)]
    rows.append(jnp.zeros((8 - 2 * count, NY), F32))
    return jnp.concatenate(rows, axis=0).T


def speed_kernel(
    mesh, u_ref, g_ref, s_ref, xl, xh, yl, yh, zr, n_ref, m_ref,
    lam_ref, cf_ref, cfh_ref, mis_ref, xlo, xhi, ylo, yhi, zs,
    vx, ax, bx, az, bz, ch, yc, yp,
):
    (mxl, mxh), (myl, myh), (mzl, mzh), first = masks(mesh)
    lane = lanes()
    for z in range(NZ):
        vx[pl.ds(24 * z + 8, 8), :] = u_ref[1, layer(z), :] / (1.0 + u_ref[0, layer(z), :])
    for side, ref, mask in ((0, xl, mxl), (1, xh, mxh)):
        r, mx, press, sw, second = [ref[k] * mask for k in range(5)]
        speed = mx / (1.0 + r)
        vx[pl.ds(16 if side else 7, NZ, stride=24), :] = speed
        own = vx[pl.ds(15 if side else 8, NZ, stride=24), :]
        slope = 0.5 * (second - own if side else own - second)
        squeeze = jnp.minimum(slope, 0.0)
        visc = sw * quad_viscosity * (1.0 + r) * squeeze
        cfh_ref[side] = 2.0 * visc
        f1 = mx * speed + press + visc * squeeze
        if side:
            ax[0, pl.ds(8, NZ, stride=16), :] = upper_part(mx, r)
            ax[1, pl.ds(8, NZ, stride=16), :] = upper_part(f1, mx)
        else:
            bx[0, pl.ds(7, NZ, stride=16), :] = lower_part(mx, r)
            bx[1, pl.ds(7, NZ, stride=16), :] = lower_part(f1, mx)
    for k in range(2):
        bz[k, layer(0), :] = zr[k] * mzl
        az[k, layer(NZ), :] = zr[k] * mzh
    yc[...] = columns_of(yl, yh, 2, myl, myh)
    for z in range(NZ):
        r, mx, my, mz, en = [u_ref[k, layer(z), :] for k in range(5)]
        ux, uy, uz, _, press = primitives(r, mx, my, mz, en, g_ref[layer(z), :])
        squeeze = jnp.minimum(0.5 * (vx[pl.ds(24 * z + 9, 8), :] - vx[pl.ds(24 * z + 7, 8), :]), 0.0)
        visc = s_ref[1, layer(z), :].astype(F32) * quad_viscosity * (1.0 + r) * squeeze
        cf_ref[layer(z), :] = 2.0 * visc
        f1 = mx * ux + press + visc * squeeze
        for k, st, fx, fy, fz in ((0, r, mx, my, mz), (1, mx, f1, mx * uy, mx * uz)):
            ax[k, pl.ds(16 * z, 8), :] = upper_part(fx, st)
            bx[k, pl.ds(16 * z + 8, 8), :] = lower_part(fx, st)
            az[k, layer(z), :] = upper_part(fz, st)
            bz[k, layer(z + 1), :] = lower_part(fz, st)
            ch[k, layer(z), :] = (
                3.0 * signal_speed * st
                + y_next(upper_part(fy, st), yc[layer(z), 2 + k : 3 + k], lane)
                - y_prev(lower_part(fy, st), yc[layer(z), k : k + 1], lane)
            )
    mis = jnp.zeros((NX, NY), F32)
    for z in range(NZ):
        new = []
        for k in range(2):
            change = (
                ch[k, layer(z), :]
                + (ax[k, pl.ds(16 * z + 1, 8), :] - bx[k, pl.ds(16 * z + 7, 8), :])
                + (az[k, layer(z + 1), :] - bz[k, layer(z), :])
            )
            new.append(u_ref[k, layer(z), :] - time_ratio * change)
        inv = 1.0 / (1.0 + new[0])
        speed = new[1] * inv
        off = speed - m_ref[layer(z), :]
        weight = n_ref[layer(z), :] * off
        mis = mis + weight * off
        lam_m = 2.0 * weight * inv
        lam_r = -lam_m * speed
        lam_ref[0, layer(z), :] = lam_r
        lam_ref[1, layer(z), :] = lam_m
        yp[layer(z), :] = pack_columns([lam_r, lam_m], lane)
    mis_ref[...] = mis
    for out, edge, second in ((xlo, 0, 1), (xhi, NX - 1, NX - 2)):
        out[0] = lam_ref[0, x_row(edge), :]
        out[1] = lam_ref[1, x_row(edge), :]
        out[2] = lam_ref[1, x_row(second), :]
    za = face_layer(first, 0)
    for k in range(2):
        zs[k] = lam_ref[k, dyn_layer(za), :]
    rows = yp[...].T
    for k in range(2):
        yhi[k : k + 1] = rows[2 * k : 2 * k + 1]
        ylo[k : k + 1] = rows[2 * k + 1 : 2 * k + 2]
    yhi[2:8] = jnp.zeros((6, NY), F32)
    ylo[2:8] = jnp.zeros((6, NY), F32)


def adjoint_kernel(
    mesh, u_ref, g_ref, lam_ref, cf_ref, cfh_ref, xl, xh, yl, yh, zr,
    out_ref, dg_ref, xlo, xhi, ylo, yhi, zs,
    lx, lz, px, dx, yc, yp,
):
    (mxl, mxh), (myl, myh), (mzl, mzh), first = masks(mesh)
    lane = lanes()
    for k in range(2):
        for z in range(NZ):
            lx[k, pl.ds(24 * z + 8, 8), :] = lam_ref[k, layer(z), :]
            lz[k, layer(z + 1), :] = lam_ref[k, layer(z), :]
        lx[k, pl.ds(7, NZ, stride=24), :] = xl[k] * mxl
        lx[k, pl.ds(16, NZ, stride=24), :] = xh[k] * mxh
        lz[k, layer(0), :] = zr[k] * mzl
        lz[k, layer(NZ + 1), :] = zr[k] * mzh
    dx[pl.ds(7, NZ, stride=24), :] = HALF_T * (lam_ref[1, x_row(0), :] - xl[2] * mxl) * cfh_ref[0]
    dx[pl.ds(16, NZ, stride=24), :] = HALF_T * (xh[2] * mxh - lam_ref[1, x_row(NX - 1), :]) * cfh_ref[1]
    for z in range(NZ):
        phi = HALF_T * (lx[1, pl.ds(24 * z + 9, 8), :] - lx[1, pl.ds(24 * z + 7, 8), :])
        px[layer(z), :] = phi
        dx[pl.ds(24 * z + 8, 8), :] = phi * cf_ref[layer(z), :]
    yc[...] = columns_of(yl, yh, 2, myl, myh)
    for z in range(NZ):
        r, mx, my, mz, en = [u_ref[k, layer(z), :] for k in range(5)]
        gamma = g_ref[layer(z), :]
        inv = 1.0 / (1.0 + r)
        ux, uy, uz = mx * inv, my * inv, mz * inv
        heat = en - 0.5 * (mx * ux + my * uy + mz * uz)
        lr, lm = lam_ref[0, layer(z), :], lam_ref[1, layer(z), :]
        lr_x = [lx[0, pl.ds(24 * z + s, 8), :] for s in (7, 9)]
        lm_x = [lx[1, pl.ds(24 * z + s, 8), :] for s in (7, 9)]
        lr_z = [lz[0, layer(z + s), :] for s in (0, 2)]
        lm_z = [lz[1, layer(z + s), :] for s in (0, 2)]
        lr_y = [y_prev(lr, yc[layer(z), 0:1], lane), y_next(lr, yc[layer(z), 2:3], lane)]
        lm_y = [y_prev(lm, yc[layer(z), 1:2], lane), y_next(lm, yc[layer(z), 3:4], lane)]
        phi_x0 = HALF_T * (lr_x[1] - lr_x[0])
        phi_y0 = HALF_T * (lr_y[1] - lr_y[0])
        phi_z0 = HALF_T * (lr_z[1] - lr_z[0])
        phi_x1 = px[layer(z), :]
        phi_y1 = HALF_T * (lm_y[1] - lm_y[0])
        phi_z1 = HALF_T * (lm_z[1] - lm_z[0])
        near = (lm_x[0] + lm_x[1]) + (lm_y[0] + lm_y[1]) + (lm_z[0] + lm_z[1])
        d_speed = phi_x1 * mx + 0.5 * (dx[pl.ds(24 * z + 7, 8), :] - dx[pl.ds(24 * z + 9, 8), :])
        d_en = phi_x1 * gamma
        out_mx = (
            lm * (1.0 - 3.0 * time_ratio * signal_speed)
            + (time_ratio * HALF_C) * near
            + phi_x0
            + (phi_x1 - d_en) * ux
            + phi_y1 * uy
            + phi_z1 * uz
            + d_speed * inv
        )
        out_my = phi_y0 - d_en * uy + phi_y1 * ux
        out_mz = phi_z0 - d_en * uz + phi_z1 * ux
        out_ref[0, layer(z), :] = out_mx
        out_ref[1, layer(z), :] = out_my
        out_ref[2, layer(z), :] = out_mz
        out_ref[3, layer(z), :] = d_en
        dg_ref[layer(z), :] = phi_x1 * heat
        yp[layer(z), :] = pack_columns([out_my, d_en], lane)
    for out, edge in ((xlo, 0), (xhi, NX - 1)):
        out[0] = out_ref[0, x_row(edge), :]
        out[1] = out_ref[3, x_row(edge), :]
    za = face_layer(first, 0)
    zs[0] = out_ref[2, dyn_layer(za), :]
    zs[1] = out_ref[3, dyn_layer(za), :]
    rows = yp[...].T
    for k in range(2):
        yhi[k : k + 1] = rows[2 * k : 2 * k + 1]
        ylo[k : k + 1] = rows[2 * k + 1 : 2 * k + 2]
    yhi[2:8] = jnp.zeros((6, NY), F32)
    ylo[2:8] = jnp.zeros((6, NY), F32)


def gradient_kernel(
    mesh, u_ref, lam_ref, dg_ref, mis_ref, v_ref, xl, xh, yl, yh, zr,
    grad_ref, row_ref,
    lx, lz, yc,
):
    (mxl, mxh), (myl, myh), (mzl, mzh), first = masks(mesh)
    lane = lanes()
    for k in range(2):
        for z in range(NZ):
            lx[k, pl.ds(24 * z + 8, 8), :] = lam_ref[3 * k, layer(z), :]
            lz[k, layer(z + 1), :] = lam_ref[2 + k, layer(z), :]
        lx[k, pl.ds(7, NZ, stride=24), :] = xl[k] * mxl
        lx[k, pl.ds(16, NZ, stride=24), :] = xh[k] * mxh
        lz[k, layer(0), :] = zr[k] * mzl
        lz[k, layer(NZ + 1), :] = zr[k] * mzh
    yc[...] = columns_of(yl, yh, 2, myl, myh)
    acc = jnp.zeros((NX, NY), F32)
    for z in range(NZ):
        r, mx, my, mz, en = [u_ref[k, layer(z), :] for k in range(5)]
        inv = 1.0 / (1.0 + r)
        ux, uy, uz = mx * inv, my * inv, mz * inv
        heat = en - 0.5 * (mx * ux + my * uy + mz * uz)
        dif_x = [lx[k, pl.ds(24 * z + 9, 8), :] - lx[k, pl.ds(24 * z + 7, 8), :] for k in range(2)]
        dif_z = [lz[k, layer(z + 2), :] - lz[k, layer(z), :] for k in range(2)]
        dif_y = []
        for k in range(2):
            own = lam_ref[1 + 2 * k, layer(z), :]
            dif_y.append(
                y_next(own, yc[layer(z), 2 + k : 3 + k], lane) - y_prev(own, yc[layer(z), k : k + 1], lane)
            )
        d_press = HALF_T * (
            (dif_x[0] + ux * dif_x[1]) + (dif_y[0] + uy * dif_y[1]) + (dif_z[0] + uz * dif_z[1])
        )
        grad = dg_ref[layer(z), :] + d_press * heat
        grad_ref[layer(z), :] = grad
        acc = acc + grad * grad
    total = jnp.sum(jnp.sum(acc, axis=0, keepdims=True), axis=1, keepdims=True)
    miss = jnp.sum(jnp.sum(mis_ref[...], axis=0, keepdims=True), axis=1, keepdims=True)
    miss = miss + jnp.sum(v_ref[...], axis=1, keepdims=True)
    row_ref[...] = jnp.where(lane == 0, total, jnp.where(lane == 1, miss, 0.0))


def split3(value):
    hi = value.astype(jnp.bfloat16)
    rest = value - hi.astype(F32)
    mid = rest.astype(jnp.bfloat16)
    low = (rest - mid.astype(F32)).astype(jnp.bfloat16)
    return hi, mid, low


def probe_kernel(p_ref, o_ref, n_ref, m_ref, v_ref):
    count = p_ref.shape[1]
    probes, obs = p_ref[...], o_ref[...]
    row = lax.broadcasted_iota(jnp.int32, (CELLS, count), 0)
    on_a = row == lax.shift_right_logical(probes, 7)
    on_b = row == lax.bitwise_and(probes, NY - 1)
    one_a = jnp.where(on_a, 1.0, 0.0).astype(jnp.bfloat16)
    one_b = jnp.where(on_b, 1.0, 0.0).astype(jnp.bfloat16)

    def nt(a, b):
        return lax.dot_general(a, b, (((1,), (1,)), ((), ())), preferred_element_type=F32)

    parts = [jnp.where(on_a, part.astype(F32), 0.0).astype(jnp.bfloat16) for part in split3(obs)]
    hits = nt(one_a, one_b)
    sums = nt(parts[0], one_b) + (nt(parts[1], one_b) + nt(parts[2], one_b))
    n_ref[...] = hits
    mean = sums / jnp.maximum(hits, 1.0)
    m_ref[...] = mean
    mean_t = split3(mean.T)
    picked = sum(jnp.dot(part, one_a, preferred_element_type=F32) for part in reversed(mean_t))
    at_probe = jnp.sum(jnp.where(on_b, picked, 0.0), axis=0, keepdims=True)
    off = obs - at_probe
    v_ref[...] = off * off


def rows_of(*shape):
    return jax.ShapeDtypeStruct(shape, F32)


def vmem(*shape):
    return pltpu.VMEM(shape, F32)


def call(kernel, outs, scratch, flops=100000):
    return pl.pallas_call(
        kernel,
        out_shape=outs,
        scratch_shapes=scratch,
        cost_estimate=pl.CostEstimate(flops=flops, bytes_accessed=100000, transcendentals=0),
    )


def exchange(sizes, xlo, xhi, ylo, yhi, zs):
    def ring(axis, step):
        n = sizes[axis]
        return [(i, (i + step) % n) for i in range(n)]

    zr = lax.ppermute(zs, "gz", ring("gz", 1))
    xl = lax.ppermute(xhi, "gx", ring("gx", 1))
    xh = lax.ppermute(xlo, "gx", ring("gx", -1))
    yl = lax.ppermute(yhi, "gy", ring("gy", 1))
    yh = lax.ppermute(ylo, "gy", ring("gy", -1))
    return xl, xh, yl, yh, zr


def local(sizes, checkpoint, gruneisen, switch, probes, observed):
    bind = functools.partial
    state = checkpoint.reshape(5, CELLS, NY)
    gamma = gruneisen.reshape(CELLS, NY)
    sw = switch.reshape(2, CELLS, NY)
    plane = rows_of(8, NY)

    def slabs(x_items, z_items):
        x = rows_of(x_items, NZ, NY)
        return [x, x, plane, plane, rows_of(z_items, NX, NY)]

    *sent, yown = call(bind(prep_kernel, sizes), slabs(8, 8) + [plane], [vmem(CELLS, NY)])(state, gamma, sw)
    got = exchange(sizes, *sent)
    hits, mean, spread = call(
        probe_kernel,
        [rows_of(CELLS, NY), rows_of(CELLS, NY), rows_of(1, probes.shape[0])],
        [],
    )(probes.reshape(1, -1), observed.reshape(1, -1))
    tall = (NZ + 2) * NX
    state_1, *sent = call(
        bind(step_kernel, sizes),
        [rows_of(5, CELLS, NY)] + slabs(5, 2),
        [
            vmem(NZ * 24, NY), vmem(CELLS, NY), vmem(tall, NY), vmem(CELLS, NY),
            vmem(5, NZ * 16, NY), vmem(5, NZ * 16, NY), vmem(5, tall, NY), vmem(5, tall, NY),
            vmem(5, CELLS, NY), vmem(16, NY), vmem(CELLS, 16), vmem(CELLS, NY),
        ],
    )(state, gamma, sw, *got, yown)
    got = exchange(sizes, *sent)
    lam_2, coef, coef_halo, mis, *sent = call(
        bind(speed_kernel, sizes),
        [rows_of(2, CELLS, NY), rows_of(CELLS, NY), rows_of(2, NZ, NY), plane] + slabs(3, 2),
        [
            vmem(NZ * 24, NY), vmem(2, NZ * 16, NY), vmem(2, NZ * 16, NY), vmem(2, tall, NY), vmem(2, tall, NY),
            vmem(2, CELLS, NY), vmem(CELLS, 8), vmem(CELLS, NY),
        ],
    )(state_1, gamma, sw, *got, hits, mean)
    got = exchange(sizes, *sent)
    lam_1, d_gamma, *sent = call(
        bind(adjoint_kernel, sizes),
        [rows_of(4, CELLS, NY), rows_of(CELLS, NY)] + slabs(2, 2),
        [
            vmem(2, NZ * 24, NY), vmem(2, tall, NY), vmem(CELLS, NY), vmem(NZ * 24, NY),
            vmem(CELLS, 8), vmem(CELLS, NY),
        ],
    )(state_1, gamma, lam_2, coef, coef_halo, *got)
    got = exchange(sizes, *sent)
    gradient, row = call(
        bind(gradient_kernel, sizes),
        [rows_of(CELLS, NY), plane],
        [vmem(2, NZ * 24, NY), vmem(2, tall, NY), vmem(CELLS, 8)],
    )(state, lam_1, d_gamma, mis, spread, *got)
    for axes in (("gy",), ("gx", "gz")):
        group = 1
        for axis in axes:
            group *= sizes[axis]
        row = jnp.broadcast_to(row[:1], (group, NY))
        row = jnp.sum(lax.all_to_all(row, axes, 0, 0, tiled=True), axis=0, keepdims=True)
    devices = sizes["gx"] * sizes["gy"] * sizes["gz"]
    direction = gradient / jnp.sqrt(row[0, 0] / (devices * CELLS * NY) + small_eps)
    misfit = row[0, 1] / (devices * probes.shape[0])
    return direction.reshape(NZ, NX, NY), misfit


def solution(mesh):
    block = P("gz", "gx", "gy")
    parted = P(None, "gz", "gx", "gy")
    listed = P(("gx", "gy", "gz"))
    return jax.shard_map(
        functools.partial(local, dict(mesh.shape)),
        mesh=mesh,
        in_specs=(parted, block, parted, listed, listed),
        out_specs=(block, P()),
        check_vma=False,
    )
```

```python
import functools
import jax
import jax.numpy as jnp
from jax import lax
from jax.experimental import pallas as pl
from jax.experimental.pallas import tpu as pltpu
from jax.sharding import PartitionSpec as P

NZ, NX, NY = 16, 8, 128
CELLS = NZ * NX
bulk_modulus = 2.0
slope_coeff = 1.5
signal_speed = 2.5
time_ratio = 0.1
quad_viscosity = 4.0
small_eps = 1e-12
HALF_C = 0.5 * signal_speed
HALF_T = 0.5 * time_ratio
F32 = jnp.float32


def primitives(r, mx, my, mz, en, gamma):
    inv = 1.0 / (1.0 + r)
    ux, uy, uz = mx * inv, my * inv, mz * inv
    heat = en - 0.5 * (mx * ux + my * uy + mz * uz)
    press = bulk_modulus * (r + slope_coeff * r * r) + gamma * heat
    return ux, uy, uz, heat, press


def total_pressure(press, sw, r, slope):
    squeeze = jnp.minimum(slope, 0.0)
    return press + sw * quad_viscosity * (1.0 + r) * squeeze * squeeze


def flux(state, axis, speed, total):
    rows = [state[1 + axis]] + [state[1 + k] * speed for k in range(3)]
    rows[1 + axis] = rows[1 + axis] + total
    return rows + [(state[4] + total) * speed]


def upper_part(f, u):
    return 0.5 * f - HALF_C * u


def lower_part(f, u):
    return 0.5 * f + HALF_C * u


def layer(z):
    return pl.ds(NX * z, NX)


def x_row(x):
    return pl.ds(x, NZ, stride=NX)


def lanes():
    return lax.broadcasted_iota(jnp.int32, (NX, NY), 1)


def y_next(value, column, lane):
    return jnp.where(lane == NY - 1, column, pltpu.roll(value, NY - 1, 1))


def y_prev(value, column, lane):
    return jnp.where(lane == 0, column, pltpu.roll(value, 1, 1))


def inside(flag):
    return jnp.where(flag, 1.0, 0.0).astype(F32)


def masks(mesh):
    ix, iy, iz = lax.axis_index("gx"), lax.axis_index("gy"), lax.axis_index("gz")
    return (
        (inside(ix > 0), inside(ix < mesh["gx"] - 1)),
        (inside(iy > 0), inside(iy < mesh["gy"] - 1)),
        (inside(iz > 0), inside(iz < mesh["gz"] - 1)),
        iz == 0,
    )


def face_layer(is_first, depth):
    return jnp.where(is_first, NZ - 1 - depth, depth)


def dyn_layer(z):
    return pl.ds(pl.multiple_of(NX * z, NX), NX)


def pack_columns(values, lane):
    out = pltpu.roll(values[0], 1, 1)
    for i in range(1, len(values)):
        out = jnp.where(lane < 2 * i, out, pltpu.roll(values[i], 2 * i + 1, 1))
    return out


def prep_kernel(mesh, u_ref, g_ref, s_ref, xlo, xhi, ylo, yhi, zs, yown, yp):
    _, _, _, first = masks(mesh)
    for out, edge, second in ((xlo, 0, 1), (xhi, NX - 1, NX - 2)):
        st = [u_ref[k, x_row(edge), :] for k in range(5)]
        press = primitives(*st, g_ref[x_row(edge), :])[4]
        for k in range(5):
            out[k] = st[k]
        out[5] = press
        out[6] = s_ref[0, x_row(edge), :].astype(F32)
        out[7] = u_ref[1, x_row(second), :] / (1.0 + u_ref[0, x_row(second), :])
    za, zb = face_layer(first, 0), face_layer(first, 1)
    st = [u_ref[k, dyn_layer(za), :] for k in range(5)]
    for k in range(5):
        zs[k] = st[k]
    zs[5] = primitives(*st, g_ref[dyn_layer(za), :])[4]
    zs[6] = s_ref[0, dyn_layer(za), :].astype(F32)
    zs[7] = u_ref[3, dyn_layer(zb), :] / (1.0 + u_ref[0, dyn_layer(zb), :])
    lane = lanes()
    for z in range(NZ):
        vals = [u_ref[k, layer(z), :] for k in range(5)]
        vals += [g_ref[layer(z), :], s_ref[0, layer(z), :].astype(F32)]
        out = pltpu.roll(vals[0], 2, 1)
        for i in range(1, 7):
            out = jnp.where(lane < 4 * i, out, pltpu.roll(vals[i], 4 * i + 2, 1))
        yp[layer(z), :] = out
    rows = yp[...].T
    for out, edge, second, own in ((yhi, 1, 0, 1), (ylo, 2, 3, 0)):
        st = [rows[4 * k + edge : 4 * k + edge + 1] for k in range(7)]
        prim = primitives(*st[:6])
        for k in range(5):
            out[k : k + 1] = st[k]
        out[5:6] = prim[4]
        out[6:7] = st[6]
        out[7:8] = rows[8 + second : 9 + second] / (1.0 + rows[second : second + 1])
        yown[own : own + 1] = prim[1]


def step_kernel(
    mesh, u_ref, g_ref, s_ref, xl, xh, yl, yh, zr, yown,
    o_ref, xlo, xhi, ylo, yhi, zs,
    vx, vy, vz, pr, ax, bx, az, bz, ch, yr, yc, yp,
):
    (mxl, mxh), (myl, myh), (mzl, mzh), first = masks(mesh)
    lane = lanes()
    for z in range(NZ):
        ux, uy, uz, _, press = primitives(*[u_ref[k, layer(z), :] for k in range(5)], g_ref[layer(z), :])
        vx[pl.ds(24 * z + 8, 8), :] = ux
        vy[layer(z), :] = uy
        vz[layer(z + 1), :] = uz
        pr[layer(z), :] = press
    low = [xl[k] * mxl for k in range(8)]
    high = [xh[k] * mxh for k in range(8)]
    speed = low[1] / (1.0 + low[0])
    vx[pl.ds(7, NZ, stride=24), :] = speed
    slope = 0.5 * (vx[pl.ds(8, NZ, stride=24), :] - low[7])
    fl = flux(low[:5], 0, speed, total_pressure(low[5], low[6], low[0], slope))
    for k in range(5):
        bx[k, pl.ds(7, NZ, stride=16), :] = lower_part(fl[k], low[k])
    speed = high[1] / (1.0 + high[0])
    vx[pl.ds(16, NZ, stride=24), :] = speed
    slope = 0.5 * (high[7] - vx[pl.ds(15, NZ, stride=24), :])
    fl = flux(high[:5], 0, speed, total_pressure(high[5], high[6], high[0], slope))
    for k in range(5):
        ax[k, pl.ds(8, NZ, stride=16), :] = upper_part(fl[k], high[k])
    far = [zr[k] for k in range(8)]
    speed = far[3] / (1.0 + far[0])
    own = vz[dyn_layer(face_layer(first, 0) + 1), :]
    slope = (far[7] - own) * jnp.where(first, 0.5, -0.5)
    fl = flux(far[:5], 2, speed, total_pressure(far[5], far[6], far[0], slope))
    for k in range(5):
        bz[k, layer(0), :] = lower_part(fl[k], far[k]) * mzl
        az[k, layer(NZ), :] = upper_part(fl[k], far[k]) * mzh
    vz[layer(0), :] = speed * mzl
    vz[layer(NZ + 1), :] = speed * mzh
    low = [yl[k : k + 1] * myl for k in range(8)]
    high = [yh[k : k + 1] * myh for k in range(8)]
    speed = low[2] / (1.0 + low[0])
    yr[10:11, :] = speed
    slope = 0.5 * (yown[0:1] - low[7])
    fl = flux(low[:5], 1, speed, total_pressure(low[5], low[6], low[0], slope))
    for k in range(5):
        yr[k : k + 1, :] = lower_part(fl[k], low[k])
    speed = high[2] / (1.0 + high[0])
    yr[11:12, :] = speed
    slope = 0.5 * (high[7] - yown[1:2])
    fl = flux(high[:5], 1, speed, total_pressure(high[5], high[6], high[0], slope))
    for k in range(5):
        yr[5 + k : 6 + k, :] = upper_part(fl[k], high[k])
    yr[12:16, :] = jnp.zeros((4, NY), F32)
    yc[...] = yr[...].T
    for z in range(NZ):
        st = [u_ref[k, layer(z), :] for k in range(5)]
        sw = s_ref[0, layer(z), :].astype(F32)
        press = pr[layer(z), :]
        visc = sw * quad_viscosity * (1.0 + st[0])
        uy = vy[layer(z), :]
        ux = vx[pl.ds(24 * z + 8, 8), :]
        uz = vz[layer(z + 1), :]

        def col(i):
            return yc[layer(z), i : i + 1]

        def total(up, down):
            squeeze = jnp.minimum(0.5 * (up - down), 0.0)
            return press + visc * squeeze * squeeze

        fx = flux(st, 0, ux, total(vx[pl.ds(24 * z + 9, 8), :], vx[pl.ds(24 * z + 7, 8), :]))
        fy = flux(st, 1, uy, total(y_next(uy, col(11), lane), y_prev(uy, col(10), lane)))
        fz = flux(st, 2, uz, total(vz[layer(z + 2), :], vz[layer(z), :]))
        for k in range(5):
            ax[k, pl.ds(16 * z, 8), :] = upper_part(fx[k], st[k])
            bx[k, pl.ds(16 * z + 8, 8), :] = lower_part(fx[k], st[k])
            az[k, layer(z), :] = upper_part(fz[k], st[k])
            bz[k, layer(z + 1), :] = lower_part(fz[k], st[k])
            ch[k, layer(z), :] = (
                3.0 * signal_speed * st[k]
                + y_next(upper_part(fy[k], st[k]), col(5 + k), lane)
                - y_prev(lower_part(fy[k], st[k]), col(k), lane)
            )
    for z in range(NZ):
        new = []
        for k in range(5):
            change = (
                ch[k, layer(z), :]
                + (ax[k, pl.ds(16 * z + 1, 8), :] - bx[k, pl.ds(16 * z + 7, 8), :])
                + (az[k, layer(z + 1), :] - bz[k, layer(z), :])
            )
            new.append(u_ref[k, layer(z), :] - time_ratio * change)
            o_ref[k, layer(z), :] = new[k]
        yp[layer(z), :] = pack_columns(new[:3], lane)
    for out, edge, second in ((xlo, 0, 1), (xhi, NX - 1, NX - 2)):
        st = [o_ref[k, x_row(edge), :] for k in range(5)]
        out[0] = st[0]
        out[1] = st[1]
        out[2] = primitives(*st, g_ref[x_row(edge), :])[4]
        out[3] = s_ref[1, x_row(edge), :].astype(F32)
        out[4] = o_ref[1, x_row(second), :] / (1.0 + o_ref[0, x_row(second), :])
    za = face_layer(first, 0)
    r, mx, mz = [o_ref[k, dyn_layer(za), :] for k in (0, 1, 3)]
    sign = jnp.where(first, HALF_C, -HALF_C)
    zs[0] = 0.5 * mz + sign * r
    zs[1] = 0.5 * mx * (mz / (1.0 + r)) + sign * mx
    rows = yp[...].T
    r, mx, my = rows[0:1], rows[2:3], rows[4:5]
    yhi[...] = jnp.zeros((8, NY), F32)
    yhi[0:1] = lower_part(my, r)
    yhi[1:2] = lower_part(mx * (my / (1.0 + r)), mx)
    r, mx, my = rows[1:2], rows[3:4], rows[5:6]
    ylo[...] = jnp.zeros((8, NY), F32)
    ylo[0:1] = upper_part(my, r)
    ylo[1:2] = upper_part(mx * (my / (1.0 + r)), mx)


def columns_of(low, high, count, low_mask, high_mask):
    rows = [low[k : k + 1] * low_mask for k in range(count)]
    rows += [high[k : k + 1] * high_mask for k in range(count)]
    rows.append(jnp.zeros((8 - 2 * count, NY), F32))
    return jnp.concatenate(rows, axis=0).T


def speed_kernel(
    mesh, u_ref, g_ref, s_ref, xl, xh, yl, yh, zr, n_ref, m_ref,
    lam_ref, cf_ref, cfh_ref, mis_ref, xlo, xhi, ylo, yhi, zs,
    vx, ax, bx, az, bz, ch, yc, yp,
):
    (mxl, mxh), (myl, myh), (mzl, mzh), first = masks(mesh)
    lane = lanes()
    for z in range(NZ):
        vx[pl.ds(24 * z + 8, 8), :] = u_ref[1, layer(z), :] / (1.0 + u_ref[0, layer(z), :])
    for side, ref, mask in ((0, xl, mxl), (1, xh, mxh)):
        r, mx, press, sw, second = [ref[k] * mask for k in range(5)]
        speed = mx / (1.0 + r)
        vx[pl.ds(16 if side else 7, NZ, stride=24), :] = speed
        own = vx[pl.ds(15 if side else 8, NZ, stride=24), :]
        slope = 0.5 * (second - own if side else own - second)
        squeeze = jnp.minimum(slope, 0.0)
        visc = sw * quad_viscosity * (1.0 + r) * squeeze
        cfh_ref[side] = 2.0 * visc
        f1 = mx * speed + press + visc * squeeze
        if side:
            ax[0, pl.ds(8, NZ, stride=16), :] = upper_part(mx, r)
            ax[1, pl.ds(8, NZ, stride=16), :] = upper_part(f1, mx)
        else:
            bx[0, pl.ds(7, NZ, stride=16), :] = lower_part(mx, r)
            bx[1, pl.ds(7, NZ, stride=16), :] = lower_part(f1, mx)
    for k in range(2):
        bz[k, layer(0), :] = zr[k] * mzl
        az[k, layer(NZ), :] = zr[k] * mzh
    yc[...] = columns_of(yl, yh, 2, myl, myh)
    for z in range(NZ):
        r, mx, my, mz, en = [u_ref[k, layer(z), :] for k in range(5)]
        ux, uy, uz, _, press = primitives(r, mx, my, mz, en, g_ref[layer(z), :])
        squeeze = jnp.minimum(0.5 * (vx[pl.ds(24 * z + 9, 8), :] - vx[pl.ds(24 * z + 7, 8), :]), 0.0)
        visc = s_ref[1, layer(z), :].astype(F32) * quad_viscosity * (1.0 + r) * squeeze
        cf_ref[layer(z), :] = 2.0 * visc
        f1 = mx * ux + press + visc * squeeze
        for k, st, fx, fy, fz in ((0, r, mx, my, mz), (1, mx, f1, mx * uy, mx * uz)):
            ax[k, pl.ds(16 * z, 8), :] = upper_part(fx, st)
            bx[k, pl.ds(16 * z + 8, 8), :] = lower_part(fx, st)
            az[k, layer(z), :] = upper_part(fz, st)
            bz[k, layer(z + 1), :] = lower_part(fz, st)
            ch[k, layer(z), :] = (
                3.0 * signal_speed * st
                + y_next(upper_part(fy, st), yc[layer(z), 2 + k : 3 + k], lane)
                - y_prev(lower_part(fy, st), yc[layer(z), k : k + 1], lane)
            )
    mis = jnp.zeros((NX, NY), F32)
    for z in range(NZ):
        new = []
        for k in range(2):
            change = (
                ch[k, layer(z), :]
                + (ax[k, pl.ds(16 * z + 1, 8), :] - bx[k, pl.ds(16 * z + 7, 8), :])
                + (az[k, layer(z + 1), :] - bz[k, layer(z), :])
            )
            new.append(u_ref[k, layer(z), :] - time_ratio * change)
        inv = 1.0 / (1.0 + new[0])
        speed = new[1] * inv
        off = speed - m_ref[layer(z), :]
        weight = n_ref[layer(z), :] * off
        mis = mis + weight * off
        lam_m = 2.0 * weight * inv
        lam_r = -lam_m * speed
        lam_ref[0, layer(z), :] = lam_r
        lam_ref[1, layer(z), :] = lam_m
        yp[layer(z), :] = pack_columns([lam_r, lam_m], lane)
    mis_ref[...] = mis
    for out, edge, second in ((xlo, 0, 1), (xhi, NX - 1, NX - 2)):
        out[0] = lam_ref[0, x_row(edge), :]
        out[1] = lam_ref[1, x_row(edge), :]
        out[2] = lam_ref[1, x_row(second), :]
    za = face_layer(first, 0)
    for k in range(2):
        zs[k] = lam_ref[k, dyn_layer(za), :]
    rows = yp[...].T
    for k in range(2):
        yhi[k : k + 1] = rows[2 * k : 2 * k + 1]
        ylo[k : k + 1] = rows[2 * k + 1 : 2 * k + 2]
    yhi[2:8] = jnp.zeros((6, NY), F32)
    ylo[2:8] = jnp.zeros((6, NY), F32)


def adjoint_kernel(
    mesh, u_ref, g_ref, lam_ref, cf_ref, cfh_ref, xl, xh, yl, yh, zr,
    out_ref, dg_ref, xlo, xhi, ylo, yhi, zs,
    lx, lz, px, dx, yc, yp,
):
    (mxl, mxh), (myl, myh), (mzl, mzh), first = masks(mesh)
    lane = lanes()
    for k in range(2):
        for z in range(NZ):
            lx[k, pl.ds(24 * z + 8, 8), :] = lam_ref[k, layer(z), :]
            lz[k, layer(z + 1), :] = lam_ref[k, layer(z), :]
        lx[k, pl.ds(7, NZ, stride=24), :] = xl[k] * mxl
        lx[k, pl.ds(16, NZ, stride=24), :] = xh[k] * mxh
        lz[k, layer(0), :] = zr[k] * mzl
        lz[k, layer(NZ + 1), :] = zr[k] * mzh
    dx[pl.ds(7, NZ, stride=24), :] = HALF_T * (lam_ref[1, x_row(0), :] - xl[2] * mxl) * cfh_ref[0]
    dx[pl.ds(16, NZ, stride=24), :] = HALF_T * (xh[2] * mxh - lam_ref[1, x_row(NX - 1), :]) * cfh_ref[1]
    for z in range(NZ):
        phi = HALF_T * (lx[1, pl.ds(24 * z + 9, 8), :] - lx[1, pl.ds(24 * z + 7, 8), :])
        px[layer(z), :] = phi
        dx[pl.ds(24 * z + 8, 8), :] = phi * cf_ref[layer(z), :]
    yc[...] = columns_of(yl, yh, 2, myl, myh)
    for z in range(NZ):
        r, mx, my, mz, en = [u_ref[k, layer(z), :] for k in range(5)]
        gamma = g_ref[layer(z), :]
        inv = 1.0 / (1.0 + r)
        ux, uy, uz = mx * inv, my * inv, mz * inv
        heat = en - 0.5 * (mx * ux + my * uy + mz * uz)
        lr, lm = lam_ref[0, layer(z), :], lam_ref[1, layer(z), :]
        lr_x = [lx[0, pl.ds(24 * z + s, 8), :] for s in (7, 9)]
        lm_x = [lx[1, pl.ds(24 * z + s, 8), :] for s in (7, 9)]
        lr_z = [lz[0, layer(z + s), :] for s in (0, 2)]
        lm_z = [lz[1, layer(z + s), :] for s in (0, 2)]
        lr_y = [y_prev(lr, yc[layer(z), 0:1], lane), y_next(lr, yc[layer(z), 2:3], lane)]
        lm_y = [y_prev(lm, yc[layer(z), 1:2], lane), y_next(lm, yc[layer(z), 3:4], lane)]
        phi_x0 = HALF_T * (lr_x[1] - lr_x[0])
        phi_y0 = HALF_T * (lr_y[1] - lr_y[0])
        phi_z0 = HALF_T * (lr_z[1] - lr_z[0])
        phi_x1 = px[layer(z), :]
        phi_y1 = HALF_T * (lm_y[1] - lm_y[0])
        phi_z1 = HALF_T * (lm_z[1] - lm_z[0])
        near = (lm_x[0] + lm_x[1]) + (lm_y[0] + lm_y[1]) + (lm_z[0] + lm_z[1])
        d_speed = phi_x1 * mx + 0.5 * (dx[pl.ds(24 * z + 7, 8), :] - dx[pl.ds(24 * z + 9, 8), :])
        d_en = phi_x1 * gamma
        out_mx = (
            lm * (1.0 - 3.0 * time_ratio * signal_speed)
            + (time_ratio * HALF_C) * near
            + phi_x0
            + (phi_x1 - d_en) * ux
            + phi_y1 * uy
            + phi_z1 * uz
            + d_speed * inv
        )
        out_my = phi_y0 - d_en * uy + phi_y1 * ux
        out_mz = phi_z0 - d_en * uz + phi_z1 * ux
        out_ref[0, layer(z), :] = out_mx
        out_ref[1, layer(z), :] = out_my
        out_ref[2, layer(z), :] = out_mz
        out_ref[3, layer(z), :] = d_en
        dg_ref[layer(z), :] = phi_x1 * heat
        yp[layer(z), :] = pack_columns([out_my, d_en], lane)
    for out, edge in ((xlo, 0), (xhi, NX - 1)):
        out[0] = out_ref[0, x_row(edge), :]
        out[1] = out_ref[3, x_row(edge), :]
    za = face_layer(first, 0)
    zs[0] = out_ref[2, dyn_layer(za), :]
    zs[1] = out_ref[3, dyn_layer(za), :]
    rows = yp[...].T
    for k in range(2):
        yhi[k : k + 1] = rows[2 * k : 2 * k + 1]
        ylo[k : k + 1] = rows[2 * k + 1 : 2 * k + 2]
    yhi[2:8] = jnp.zeros((6, NY), F32)
    ylo[2:8] = jnp.zeros((6, NY), F32)


def gradient_kernel(
    mesh, u_ref, lam_ref, dg_ref, mis_ref, v_ref, xl, xh, yl, yh, zr,
    grad_ref, row_ref,
    lx, lz, yc,
):
    (mxl, mxh), (myl, myh), (mzl, mzh), first = masks(mesh)
    lane = lanes()
    for k in range(2):
        for z in range(NZ):
            lx[k, pl.ds(24 * z + 8, 8), :] = lam_ref[3 * k, layer(z), :]
            lz[k, layer(z + 1), :] = lam_ref[2 + k, layer(z), :]
        lx[k, pl.ds(7, NZ, stride=24), :] = xl[k] * mxl
        lx[k, pl.ds(16, NZ, stride=24), :] = xh[k] * mxh
        lz[k, layer(0), :] = zr[k] * mzl
        lz[k, layer(NZ + 1), :] = zr[k] * mzh
    yc[...] = columns_of(yl, yh, 2, myl, myh)
    acc = jnp.zeros((NX, NY), F32)
    for z in range(NZ):
        r, mx, my, mz, en = [u_ref[k, layer(z), :] for k in range(5)]
        inv = 1.0 / (1.0 + r)
        ux, uy, uz = mx * inv, my * inv, mz * inv
        heat = en - 0.5 * (mx * ux + my * uy + mz * uz)
        dif_x = [lx[k, pl.ds(24 * z + 9, 8), :] - lx[k, pl.ds(24 * z + 7, 8), :] for k in range(2)]
        dif_z = [lz[k, layer(z + 2), :] - lz[k, layer(z), :] for k in range(2)]
        dif_y = []
        for k in range(2):
            own = lam_ref[1 + 2 * k, layer(z), :]
            dif_y.append(
                y_next(own, yc[layer(z), 2 + k : 3 + k], lane) - y_prev(own, yc[layer(z), k : k + 1], lane)
            )
        d_press = HALF_T * (
            (dif_x[0] + ux * dif_x[1]) + (dif_y[0] + uy * dif_y[1]) + (dif_z[0] + uz * dif_z[1])
        )
        grad = dg_ref[layer(z), :] + d_press * heat
        grad_ref[layer(z), :] = grad
        acc = acc + grad * grad
    total = jnp.sum(jnp.sum(acc, axis=0, keepdims=True), axis=1, keepdims=True)
    miss = jnp.sum(jnp.sum(mis_ref[...], axis=0, keepdims=True), axis=1, keepdims=True)
    miss = miss + jnp.sum(v_ref[...], axis=1, keepdims=True)
    row = jnp.where(lane == 0, total, jnp.where(lane == 1, miss, 0.0))
    for i in range(row_ref.shape[0] // NX):
        row_ref[layer(i), :] = row


def scale_kernel(devices, count, grad_ref, rows_ref, out_ref, misfit_ref):
    acc = rows_ref[layer(0), :]
    for i in range(1, devices // NX):
        acc = acc + rows_ref[layer(i), :]
    row = jnp.sum(acc, axis=0, keepdims=True)
    misfit_ref[0, 0] = row[0, 1] / (devices * count)
    scale = 1.0 / jnp.sqrt(row[0:1, 0:1] / (devices * CELLS * NY) + small_eps)
    out_ref[...] = grad_ref[...] * scale


def split3(value):
    hi = value.astype(jnp.bfloat16)
    rest = value - hi.astype(F32)
    mid = rest.astype(jnp.bfloat16)
    low = (rest - mid.astype(F32)).astype(jnp.bfloat16)
    return hi, mid, low


def probe_kernel(p_ref, o_ref, n_ref, m_ref, v_ref):
    count = p_ref.shape[1]
    probes, obs = p_ref[...], o_ref[...]
    row = lax.broadcasted_iota(jnp.int32, (CELLS, count), 0)
    on_a = row == lax.shift_right_logical(probes, 7)
    on_b = row == lax.bitwise_and(probes, NY - 1)
    one_a = jnp.where(on_a, 1.0, 0.0).astype(jnp.bfloat16)
    one_b = jnp.where(on_b, 1.0, 0.0).astype(jnp.bfloat16)

    def nt(a, b):
        return lax.dot_general(a, b, (((1,), (1,)), ((), ())), preferred_element_type=F32)

    parts = [jnp.where(on_a, part.astype(F32), 0.0).astype(jnp.bfloat16) for part in split3(obs)]
    hits = nt(one_a, one_b)
    sums = nt(parts[0], one_b) + (nt(parts[1], one_b) + nt(parts[2], one_b))
    n_ref[...] = hits
    mean = sums / jnp.maximum(hits, 1.0)
    m_ref[...] = mean
    mean_t = split3(mean.T)
    picked = sum(jnp.dot(part, one_a, preferred_element_type=F32) for part in reversed(mean_t))
    at_probe = jnp.sum(jnp.where(on_b, picked, 0.0), axis=0, keepdims=True)
    off = obs - at_probe
    v_ref[...] = off * off


SMALL = pltpu.CompilerParams(vmem_limit_bytes=12 * 1024 * 1024)


def rows_of(*shape):
    return jax.ShapeDtypeStruct(shape, F32)


def vmem(*shape):
    return pltpu.VMEM(shape, F32)


def call(kernel, outs, scratch, flops=100000):
    return pl.pallas_call(
        kernel,
        out_shape=outs,
        scratch_shapes=scratch,
        cost_estimate=pl.CostEstimate(flops=flops, bytes_accessed=100000, transcendentals=0),
        compiler_params=SMALL,
    )


def exchange(sizes, xlo, xhi, ylo, yhi, zs):
    def ring(axis, step):
        n = sizes[axis]
        return [(i, (i + step) % n) for i in range(n)]

    zr = lax.ppermute(zs, "gz", ring("gz", 1))
    xl = lax.ppermute(xhi, "gx", ring("gx", 1))
    xh = lax.ppermute(xlo, "gx", ring("gx", -1))
    yl = lax.ppermute(yhi, "gy", ring("gy", 1))
    yh = lax.ppermute(ylo, "gy", ring("gy", -1))
    return xl, xh, yl, yh, zr


def local(sizes, checkpoint, gruneisen, switch, probes, observed):
    bind = functools.partial
    state = checkpoint.reshape(5, CELLS, NY)
    gamma = gruneisen.reshape(CELLS, NY)
    sw = switch.reshape(2, CELLS, NY)
    plane = rows_of(8, NY)

    def slabs(x_items, z_items):
        x = rows_of(x_items, NZ, NY)
        return [x, x, plane, plane, rows_of(z_items, NX, NY)]

    *sent, yown = call(bind(prep_kernel, sizes), slabs(8, 8) + [plane], [vmem(CELLS, NY)])(state, gamma, sw)
    got = exchange(sizes, *sent)
    hits, mean, spread = call(
        probe_kernel,
        [rows_of(CELLS, NY), rows_of(CELLS, NY), rows_of(1, probes.shape[0])],
        [],
    )(probes.reshape(1, -1), observed.reshape(1, -1))
    tall = (NZ + 2) * NX
    state_1, *sent = call(
        bind(step_kernel, sizes),
        [rows_of(5, CELLS, NY)] + slabs(5, 2),
        [
            vmem(NZ * 24, NY), vmem(CELLS, NY), vmem(tall, NY), vmem(CELLS, NY),
            vmem(5, NZ * 16, NY), vmem(5, NZ * 16, NY), vmem(5, tall, NY), vmem(5, tall, NY),
            vmem(5, CELLS, NY), vmem(16, NY), vmem(CELLS, 16), vmem(CELLS, NY),
        ],
    )(state, gamma, sw, *got, yown)
    got = exchange(sizes, *sent)
    lam_2, coef, coef_halo, mis, *sent = call(
        bind(speed_kernel, sizes),
        [rows_of(2, CELLS, NY), rows_of(CELLS, NY), rows_of(2, NZ, NY), plane] + slabs(3, 2),
        [
            vmem(NZ * 24, NY), vmem(2, NZ * 16, NY), vmem(2, NZ * 16, NY), vmem(2, tall, NY), vmem(2, tall, NY),
            vmem(2, CELLS, NY), vmem(CELLS, 8), vmem(CELLS, NY),
        ],
    )(state_1, gamma, sw, *got, hits, mean)
    got = exchange(sizes, *sent)
    lam_1, d_gamma, *sent = call(
        bind(adjoint_kernel, sizes),
        [rows_of(4, CELLS, NY), rows_of(CELLS, NY)] + slabs(2, 2),
        [
            vmem(2, NZ * 24, NY), vmem(2, tall, NY), vmem(CELLS, NY), vmem(NZ * 24, NY),
            vmem(CELLS, 8), vmem(CELLS, NY),
        ],
    )(state_1, gamma, lam_2, coef, coef_halo, *got)
    got = exchange(sizes, *sent)
    devices = sizes["gx"] * sizes["gy"] * sizes["gz"]
    gradient, rows = call(
        bind(gradient_kernel, sizes),
        [rows_of(CELLS, NY), rows_of(devices, NY)],
        [vmem(2, NZ * 24, NY), vmem(2, tall, NY), vmem(CELLS, 8)],
    )(state, lam_1, d_gamma, mis, spread, *got)
    rows = lax.all_to_all(rows, ("gx", "gy", "gz"), 0, 0, tiled=True)
    direction, misfit = pl.pallas_call(
        bind(scale_kernel, devices, probes.shape[0]),
        out_shape=[rows_of(CELLS, NY), rows_of(1, 1)],
        out_specs=[pl.BlockSpec(memory_space=pltpu.VMEM), pl.BlockSpec(memory_space=pltpu.SMEM)],
        compiler_params=SMALL,
    )(gradient, rows)
    return direction.reshape(NZ, NX, NY), misfit.reshape(())


def solution(mesh):
    block = P("gz", "gx", "gy")
    parted = P(None, "gz", "gx", "gy")
    listed = P(("gx", "gy", "gz"))
    return jax.shard_map(
        functools.partial(local, dict(mesh.shape)),
        mesh=mesh,
        in_specs=(parted, block, parted, listed, listed),
        out_specs=(block, P()),
        check_vma=False,
    )
```

```python
import functools
import jax
import jax.numpy as jnp
from jax import lax
from jax.experimental import pallas as pl
from jax.experimental.pallas import tpu as pltpu
from jax.sharding import PartitionSpec as P

NZ, NX, NY = 16, 8, 128
CELLS = NZ * NX
bulk_modulus = 2.0
slope_coeff = 1.5
signal_speed = 2.5
time_ratio = 0.1
quad_viscosity = 4.0
small_eps = 1e-12
HALF_C = 0.5 * signal_speed
HALF_T = 0.5 * time_ratio
F32 = jnp.float32


def primitives(r, mx, my, mz, en, gamma):
    inv = 1.0 / (1.0 + r)
    ux, uy, uz = mx * inv, my * inv, mz * inv
    heat = en - 0.5 * (mx * ux + my * uy + mz * uz)
    press = bulk_modulus * (r + slope_coeff * r * r) + gamma * heat
    return ux, uy, uz, heat, press


def total_pressure(press, sw, r, slope):
    squeeze = jnp.minimum(slope, 0.0)
    return press + sw * quad_viscosity * (1.0 + r) * squeeze * squeeze


def flux(state, axis, speed, total):
    rows = [state[1 + axis]] + [state[1 + k] * speed for k in range(3)]
    rows[1 + axis] = rows[1 + axis] + total
    return rows + [(state[4] + total) * speed]


def upper_part(f, u):
    return 0.5 * f - HALF_C * u


def lower_part(f, u):
    return 0.5 * f + HALF_C * u


def layer(z):
    return pl.ds(NX * z, NX)


def x_row(x):
    return pl.ds(x, NZ, stride=NX)


def lanes():
    return lax.broadcasted_iota(jnp.int32, (NX, NY), 1)


def y_next(value, column, lane):
    return jnp.where(lane == NY - 1, column, pltpu.roll(value, NY - 1, 1))


def y_prev(value, column, lane):
    return jnp.where(lane == 0, column, pltpu.roll(value, 1, 1))


def inside(flag):
    return jnp.where(flag, 1.0, 0.0).astype(F32)


def masks(mesh):
    ix, iy, iz = lax.axis_index("gx"), lax.axis_index("gy"), lax.axis_index("gz")
    return (
        (inside(ix > 0), inside(ix < mesh["gx"] - 1)),
        (inside(iy > 0), inside(iy < mesh["gy"] - 1)),
        (inside(iz > 0), inside(iz < mesh["gz"] - 1)),
        iz == 0,
    )


def face_layer(is_first, depth):
    return jnp.where(is_first, NZ - 1 - depth, depth)


def dyn_layer(z):
    return pl.ds(pl.multiple_of(NX * z, NX), NX)


def pack_columns(values, lane):
    out = pltpu.roll(values[0], 1, 1)
    for i in range(1, len(values)):
        out = jnp.where(lane < 2 * i, out, pltpu.roll(values[i], 2 * i + 1, 1))
    return out


def pack_edges(values, lane):
    out = pltpu.roll(values[0], 2, 1)
    for i in range(1, len(values)):
        out = jnp.where(lane < 4 * i, out, pltpu.roll(values[i], 4 * i + 2, 1))
    return out


def prep_kernel(mesh, u_ref, g_ref, s_ref, xlo, xhi, ylo, yhi, zs, yown, yp):
    _, _, _, first = masks(mesh)
    for out, edge, second in ((xlo, 0, 1), (xhi, NX - 1, NX - 2)):
        st = [u_ref[k, x_row(edge), :] for k in range(5)]
        press = primitives(*st, g_ref[x_row(edge), :])[4]
        for k in range(5):
            out[k] = st[k]
        out[5] = press
        out[6] = s_ref[0, x_row(edge), :].astype(F32)
        out[7] = u_ref[1, x_row(second), :] / (1.0 + u_ref[0, x_row(second), :])
    za, zb = face_layer(first, 0), face_layer(first, 1)
    st = [u_ref[k, dyn_layer(za), :] for k in range(5)]
    for k in range(5):
        zs[k] = st[k]
    zs[5] = primitives(*st, g_ref[dyn_layer(za), :])[4]
    zs[6] = s_ref[0, dyn_layer(za), :].astype(F32)
    zs[7] = u_ref[3, dyn_layer(zb), :] / (1.0 + u_ref[0, dyn_layer(zb), :])
    lane = lanes()
    for z in range(NZ):
        vals = [u_ref[k, layer(z), :] for k in range(5)]
        vals += [g_ref[layer(z), :], s_ref[0, layer(z), :].astype(F32)]
        yp[layer(z), :] = pack_edges(vals, lane)
    rows = yp[...].T
    for out, edge, second, own in ((yhi, 1, 0, 1), (ylo, 2, 3, 0)):
        st = [rows[4 * k + edge : 4 * k + edge + 1] for k in range(7)]
        prim = primitives(*st[:6])
        for k in range(5):
            out[k : k + 1] = st[k]
        out[5:6] = prim[4]
        out[6:7] = st[6]
        out[7:8] = rows[8 + second : 9 + second] / (1.0 + rows[second : second + 1])
        yown[own : own + 1] = prim[1]


def step_kernel(
    mesh, u_ref, g_ref, s_ref, xl, xh, yl, yh, zr, yown,
    o_ref, xlo, xhi, ylo, yhi, zs,
    vx, vy, vz, pr, ax, bx, az, bz, ch, yr, yc, yp,
):
    (mxl, mxh), (myl, myh), (mzl, mzh), first = masks(mesh)
    lane = lanes()
    for z in range(NZ):
        ux, uy, uz, _, press = primitives(*[u_ref[k, layer(z), :] for k in range(5)], g_ref[layer(z), :])
        vx[pl.ds(24 * z + 8, 8), :] = ux
        vy[layer(z), :] = uy
        vz[layer(z + 1), :] = uz
        pr[layer(z), :] = press
    low = [xl[k] * mxl for k in range(8)]
    high = [xh[k] * mxh for k in range(8)]
    speed = low[1] / (1.0 + low[0])
    vx[pl.ds(7, NZ, stride=24), :] = speed
    slope = 0.5 * (vx[pl.ds(8, NZ, stride=24), :] - low[7])
    fl = flux(low[:5], 0, speed, total_pressure(low[5], low[6], low[0], slope))
    for k in range(5):
        bx[k, pl.ds(7, NZ, stride=16), :] = lower_part(fl[k], low[k])
    speed = high[1] / (1.0 + high[0])
    vx[pl.ds(16, NZ, stride=24), :] = speed
    slope = 0.5 * (high[7] - vx[pl.ds(15, NZ, stride=24), :])
    fl = flux(high[:5], 0, speed, total_pressure(high[5], high[6], high[0], slope))
    for k in range(5):
        ax[k, pl.ds(8, NZ, stride=16), :] = upper_part(fl[k], high[k])
    far = [zr[k] for k in range(8)]
    speed = far[3] / (1.0 + far[0])
    own = vz[dyn_layer(face_layer(first, 0) + 1), :]
    slope = (far[7] - own) * jnp.where(first, 0.5, -0.5)
    fl = flux(far[:5], 2, speed, total_pressure(far[5], far[6], far[0], slope))
    for k in range(5):
        bz[k, layer(0), :] = lower_part(fl[k], far[k]) * mzl
        az[k, layer(NZ), :] = upper_part(fl[k], far[k]) * mzh
    vz[layer(0), :] = speed * mzl
    vz[layer(NZ + 1), :] = speed * mzh
    low = [yl[k : k + 1] * myl for k in range(8)]
    high = [yh[k : k + 1] * myh for k in range(8)]
    speed = low[2] / (1.0 + low[0])
    yr[10:11, :] = speed
    slope = 0.5 * (yown[0:1] - low[7])
    fl = flux(low[:5], 1, speed, total_pressure(low[5], low[6], low[0], slope))
    for k in range(5):
        yr[k : k + 1, :] = lower_part(fl[k], low[k])
    speed = high[2] / (1.0 + high[0])
    yr[11:12, :] = speed
    slope = 0.5 * (high[7] - yown[1:2])
    fl = flux(high[:5], 1, speed, total_pressure(high[5], high[6], high[0], slope))
    for k in range(5):
        yr[5 + k : 6 + k, :] = upper_part(fl[k], high[k])
    yr[12:16, :] = jnp.zeros((4, NY), F32)
    yc[...] = yr[...].T
    for z in range(NZ):
        st = [u_ref[k, layer(z), :] for k in range(5)]
        sw = s_ref[0, layer(z), :].astype(F32)
        press = pr[layer(z), :]
        visc = sw * quad_viscosity * (1.0 + st[0])
        uy = vy[layer(z), :]
        ux = vx[pl.ds(24 * z + 8, 8), :]
        uz = vz[layer(z + 1), :]

        def col(i):
            return yc[layer(z), i : i + 1]

        def total(up, down):
            squeeze = jnp.minimum(0.5 * (up - down), 0.0)
            return press + visc * squeeze * squeeze

        fx = flux(st, 0, ux, total(vx[pl.ds(24 * z + 9, 8), :], vx[pl.ds(24 * z + 7, 8), :]))
        fy = flux(st, 1, uy, total(y_next(uy, col(11), lane), y_prev(uy, col(10), lane)))
        fz = flux(st, 2, uz, total(vz[layer(z + 2), :], vz[layer(z), :]))
        for k in range(5):
            ax[k, pl.ds(16 * z, 8), :] = upper_part(fx[k], st[k])
            bx[k, pl.ds(16 * z + 8, 8), :] = lower_part(fx[k], st[k])
            az[k, layer(z), :] = upper_part(fz[k], st[k])
            bz[k, layer(z + 1), :] = lower_part(fz[k], st[k])
            ch[k, layer(z), :] = (
                3.0 * signal_speed * st[k]
                + y_next(upper_part(fy[k], st[k]), col(5 + k), lane)
                - y_prev(lower_part(fy[k], st[k]), col(k), lane)
            )
    for z in range(NZ):
        new = []
        for k in range(5):
            change = (
                ch[k, layer(z), :]
                + (ax[k, pl.ds(16 * z + 1, 8), :] - bx[k, pl.ds(16 * z + 7, 8), :])
                + (az[k, layer(z + 1), :] - bz[k, layer(z), :])
            )
            new.append(u_ref[k, layer(z), :] - time_ratio * change)
            o_ref[k, layer(z), :] = new[k]
        yp[layer(z), :] = pack_columns(new[:3], lane)
    for out, edge, second in ((xlo, 0, 1), (xhi, NX - 1, NX - 2)):
        st = [o_ref[k, x_row(edge), :] for k in range(5)]
        out[0] = st[0]
        out[1] = st[1]
        out[2] = primitives(*st, g_ref[x_row(edge), :])[4]
        out[3] = s_ref[1, x_row(edge), :].astype(F32)
        out[4] = o_ref[1, x_row(second), :] / (1.0 + o_ref[0, x_row(second), :])
    za = face_layer(first, 0)
    r, mx, mz = [o_ref[k, dyn_layer(za), :] for k in (0, 1, 3)]
    sign = jnp.where(first, HALF_C, -HALF_C)
    zs[0] = 0.5 * mz + sign * r
    zs[1] = 0.5 * mx * (mz / (1.0 + r)) + sign * mx
    rows = yp[...].T
    r, mx, my = rows[0:1], rows[2:3], rows[4:5]
    yhi[...] = jnp.zeros((8, NY), F32)
    yhi[0:1] = lower_part(my, r)
    yhi[1:2] = lower_part(mx * (my / (1.0 + r)), mx)
    r, mx, my = rows[1:2], rows[3:4], rows[5:6]
    ylo[...] = jnp.zeros((8, NY), F32)
    ylo[0:1] = upper_part(my, r)
    ylo[1:2] = upper_part(mx * (my / (1.0 + r)), mx)


def columns_of(low, high, count, low_mask, high_mask):
    rows = [low[k : k + 1] * low_mask for k in range(count)]
    rows += [high[k : k + 1] * high_mask for k in range(count)]
    rows.append(jnp.zeros((8 - 2 * count, NY), F32))
    return jnp.concatenate(rows, axis=0).T


def speed_kernel(
    mesh, u_ref, g_ref, s_ref, xl, xh, yl, yh, zr, n_ref, m_ref,
    lam_ref, cf_ref, cfh_ref, mis_ref, ylo, yhi, zs, yown,
    vx, ax, bx, az, bz, ch, yc, yp,
):
    (mxl, mxh), (myl, myh), (mzl, mzh), first = masks(mesh)
    lane = lanes()
    for z in range(NZ):
        vx[pl.ds(24 * z + 8, 8), :] = u_ref[1, layer(z), :] / (1.0 + u_ref[0, layer(z), :])
    for side, ref, mask in ((0, xl, mxl), (1, xh, mxh)):
        r, mx, press, sw, second = [ref[k] * mask for k in range(5)]
        speed = mx / (1.0 + r)
        vx[pl.ds(16 if side else 7, NZ, stride=24), :] = speed
        own = vx[pl.ds(15 if side else 8, NZ, stride=24), :]
        slope = 0.5 * (second - own if side else own - second)
        squeeze = jnp.minimum(slope, 0.0)
        visc = sw * quad_viscosity * (1.0 + r) * squeeze
        cfh_ref[side] = 2.0 * visc
        f1 = mx * speed + press + visc * squeeze
        if side:
            ax[0, pl.ds(8, NZ, stride=16), :] = upper_part(mx, r)
            ax[1, pl.ds(8, NZ, stride=16), :] = upper_part(f1, mx)
        else:
            bx[0, pl.ds(7, NZ, stride=16), :] = lower_part(mx, r)
            bx[1, pl.ds(7, NZ, stride=16), :] = lower_part(f1, mx)
    for k in range(2):
        bz[k, layer(0), :] = zr[k] * mzl
        az[k, layer(NZ), :] = zr[k] * mzh
    yc[...] = columns_of(yl, yh, 2, myl, myh)
    for z in range(NZ):
        r, mx, my, mz, en = [u_ref[k, layer(z), :] for k in range(5)]
        ux, uy, uz, _, press = primitives(r, mx, my, mz, en, g_ref[layer(z), :])
        squeeze = jnp.minimum(0.5 * (vx[pl.ds(24 * z + 9, 8), :] - vx[pl.ds(24 * z + 7, 8), :]), 0.0)
        visc = s_ref[1, layer(z), :].astype(F32) * quad_viscosity * (1.0 + r) * squeeze
        cf_ref[layer(z), :] = 2.0 * visc
        f1 = mx * ux + press + visc * squeeze
        for k, st, fx, fy, fz in ((0, r, mx, my, mz), (1, mx, f1, mx * uy, mx * uz)):
            ax[k, pl.ds(16 * z, 8), :] = upper_part(fx, st)
            bx[k, pl.ds(16 * z + 8, 8), :] = lower_part(fx, st)
            az[k, layer(z), :] = upper_part(fz, st)
            bz[k, layer(z + 1), :] = lower_part(fz, st)
            ch[k, layer(z), :] = (
                3.0 * signal_speed * st
                + y_next(upper_part(fy, st), yc[layer(z), 2 + k : 3 + k], lane)
                - y_prev(lower_part(fy, st), yc[layer(z), k : k + 1], lane)
            )
    mis = jnp.zeros((NX, NY), F32)
    for z in range(NZ):
        new = []
        for k in range(2):
            change = (
                ch[k, layer(z), :]
                + (ax[k, pl.ds(16 * z + 1, 8), :] - bx[k, pl.ds(16 * z + 7, 8), :])
                + (az[k, layer(z + 1), :] - bz[k, layer(z), :])
            )
            new.append(u_ref[k, layer(z), :] - time_ratio * change)
        inv = 1.0 / (1.0 + new[0])
        speed = new[1] * inv
        off = speed - m_ref[layer(z), :]
        weight = n_ref[layer(z), :] * off
        mis = mis + weight * off
        lam_m = 2.0 * weight * inv
        lam_r = -lam_m * speed
        lam_ref[0, layer(z), :] = lam_r
        lam_ref[1, layer(z), :] = lam_m
        inv = 1.0 / (1.0 + u_ref[0, layer(z), :])
        extra = [u_ref[1, layer(z), :] * inv, u_ref[2, layer(z), :] * inv, g_ref[layer(z), :]]
        yp[layer(z), :] = pack_edges([lam_r, lam_m] + extra, lane)
    mis_ref[...] = mis
    za, zb = dyn_layer(face_layer(first, 0)), dyn_layer(face_layer(first, 1))
    inv = 1.0 / (1.0 + u_ref[0, za, :])
    ux = u_ref[1, za, :] * inv
    zs[0] = lam_ref[0, za, :]
    zs[1] = lam_ref[1, za, :]
    zs[2] = jnp.where(first, -HALF_T, HALF_T) * (lam_ref[0, zb, :] + lam_ref[1, zb, :] * ux)
    zs[3] = ux
    zs[4] = u_ref[3, za, :] * inv
    zs[5] = g_ref[za, :]
    rows = yp[...].T
    for out, edge, second, own, sign in ((yhi, 1, 0, 2, -HALF_T), (ylo, 2, 3, 0, HALF_T)):
        lam_r, lam_m, ux, uy, gamma = [rows[4 * i + edge : 4 * i + edge + 1] for i in range(5)]
        out[0:1] = lam_r
        out[1:2] = lam_m
        out[2:3] = sign * (rows[second : second + 1] + rows[4 + second : 5 + second] * ux)
        out[3:4] = ux
        out[4:5] = uy
        out[5:6] = gamma
        out[6:8] = jnp.zeros((2, NY), F32)
        yown[own : own + 1] = lam_r
        yown[own + 1 : own + 2] = lam_m
    yown[4:8] = jnp.zeros((4, NY), F32)


NEAR = time_ratio * HALF_C
STAY = 1.0 - 3.0 * time_ratio * signal_speed


def edge_kernel(mesh, u_ref, g_ref, lam_ref, cf_ref, yl, yh, zr, xlo, xhi, yc):
    _, (myl, myh), (mzl, mzh), _ = masks(mesh)
    low_y, high_y = yl[1:2] * myl, yh[1:2] * myh
    yc[:, 0:8] = jnp.concatenate([low_y, high_y, jnp.zeros((6, NY), F32)], axis=0).T
    lane = lax.broadcasted_iota(jnp.int32, (NZ, NY), 1)
    deep = lax.broadcasted_iota(jnp.int32, (NZ, NY), 0)
    for out, e, i, i2, sign in ((xhi, NX - 1, NX - 2, NX - 3, 1.0), (xlo, 0, 1, 2, -1.0)):
        r, mx, my, mz = [u_ref[k, x_row(e), :] for k in range(4)]
        inv = 1.0 / (1.0 + r)
        lm, lm_i = lam_ref[1, x_row(e), :], lam_ref[1, x_row(i), :]
        col = yc[x_row(e), :]
        side = zr[1, e : e + 1, :]
        up_y = jnp.where(lane == NY - 1, col[:, 1:2], pltpu.roll(lm, NY - 1, 1))
        down_y = jnp.where(lane == 0, col[:, 0:1], pltpu.roll(lm, 1, 1))
        up_z = jnp.where(deep == NZ - 1, side * mzh, pltpu.roll(lm, NZ - 1, 0))
        down_z = jnp.where(deep == 0, side * mzl, pltpu.roll(lm, 1, 0))
        slope = (sign * HALF_T) * (lm - lam_ref[1, x_row(i2), :]) * cf_ref[x_row(i), :]
        out[0] = lam_ref[0, x_row(e), :]
        out[1] = lm
        out[2] = lm_i
        out[3] = (
            STAY * lm
            + NEAR * (lm_i + (up_y + down_y) + (up_z + down_z))
            - (sign * HALF_T) * lam_ref[0, x_row(i), :]
            + HALF_T * ((up_y - down_y) * (my * inv) + (up_z - down_z) * (mz * inv))
            + (sign * 0.5) * slope * inv
        )
        gamma = g_ref[x_row(e), :]
        out[4] = (2.0 - gamma) * (mx * inv)
        out[5] = inv
        out[6] = gamma
        out[7] = jnp.where(deep == 0, low_y, jnp.where(deep == 1, high_y, jnp.where(deep == 2, side, 0.0)))


def gradient_kernel(
    mesh, u0_ref, u_ref, g_ref, lam_ref, cf_ref, cfh_ref, yown, yl, yh, zr, xl, xh, mis_ref, v_ref,
    grad_ref, row_ref,
    lx, lz, px, dx, dg, yc, gx, gy, gz,
):
    (mxl, mxh), (myl, myh), (mzl, mzh), first = masks(mesh)
    lane = lanes()
    for k in range(2):
        for z in range(NZ):
            lx[k, pl.ds(24 * z + 8, 8), :] = lam_ref[k, layer(z), :]
            lz[k, layer(z + 1), :] = lam_ref[k, layer(z), :]
        lx[k, pl.ds(7, NZ, stride=24), :] = xl[k] * mxl
        lx[k, pl.ds(16, NZ, stride=24), :] = xh[k] * mxh
        lz[k, layer(0), :] = zr[k] * mzl
        lz[k, layer(NZ + 1), :] = zr[k] * mzh
    phi_low = HALF_T * (lam_ref[1, x_row(0), :] - xl[2] * mxl)
    phi_high = HALF_T * (xh[2] * mxh - lam_ref[1, x_row(NX - 1), :])
    dx[pl.ds(7, NZ, stride=24), :] = phi_low * cfh_ref[0]
    dx[pl.ds(16, NZ, stride=24), :] = phi_high * cfh_ref[1]
    for z in range(NZ):
        phi = HALF_T * (lx[1, pl.ds(24 * z + 9, 8), :] - lx[1, pl.ds(24 * z + 7, 8), :])
        px[layer(z), :] = phi
        dx[pl.ds(24 * z + 8, 8), :] = phi * cf_ref[layer(z), :]
    gx[1, pl.ds(7, NZ, stride=24), :] = mxl * phi_low * xl[6]
    gx[1, pl.ds(16, NZ, stride=24), :] = mxh * phi_high * xh[6]
    gx[0, pl.ds(7, NZ, stride=24), :] = mxl * (
        xl[3]
        + HALF_T * lam_ref[0, x_row(0), :]
        + NEAR * lam_ref[1, x_row(0), :]
        + phi_low * xl[4]
        - 0.5 * dx[pl.ds(8, NZ, stride=24), :] * xl[5]
    )
    gx[0, pl.ds(16, NZ, stride=24), :] = mxh * (
        xh[3]
        - HALF_T * lam_ref[0, x_row(NX - 1), :]
        + NEAR * lam_ref[1, x_row(NX - 1), :]
        + phi_high * xh[4]
        + 0.5 * dx[pl.ds(15, NZ, stride=24), :] * xh[5]
    )
    at_x = lax.bitwise_and(lax.broadcasted_iota(jnp.int32, (1, NY), 1), NX - 1)
    from_high, from_low = pltpu.roll(xh[7], NX - 1, 1) * mxh, pltpu.roll(xl[7], NY - NX + 1, 1) * mxl
    halo = []
    for side, ref, mask, sign in ((0, yl, myl, HALF_T), (1, yh, myh, -HALF_T)):
        items = ref[...]
        up = jnp.where(at_x == NX - 1, from_high[side : side + 1], pltpu.roll(items, NY - 1, 1)[1:2])
        down = jnp.where(at_x == 0, from_low[side : side + 1], pltpu.roll(items, 1, 1)[1:2])
        d_en = HALF_T * (up - down) * items[5:6]
        own_r, own_m = yown[2 * side : 2 * side + 1], yown[2 * side + 1 : 2 * side + 2]
        d_my = items[2:3] + sign * (own_r + own_m * items[3:4]) - d_en * items[4:5]
        halo += [items[0:1] * mask, items[1:2] * mask, d_my * mask, d_en * mask]
    yc[...] = jnp.concatenate(halo, axis=0).T
    deep = lax.broadcasted_iota(jnp.int32, (NX, NY), 0)
    up = jnp.where(deep == NX - 1, xh[7, 2:3, :] * mxh, pltpu.roll(zr[1], NX - 1, 0))
    down = jnp.where(deep == 0, xl[7, 2:3, :] * mxl, pltpu.roll(zr[1], 1, 0))
    d_en = HALF_T * (up - down) * zr[5]
    za = dyn_layer(face_layer(first, 0))
    d_mz = (
        zr[2]
        + jnp.where(first, -HALF_T, HALF_T) * (lam_ref[0, za, :] + lam_ref[1, za, :] * zr[3])
        - d_en * zr[4]
    )
    for k, value in ((0, d_mz), (1, d_en)):
        gz[k, layer(0), :] = value * mzl
        gz[k, layer(NZ + 1), :] = value * mzh
    for z in range(NZ):
        r, mx, my, mz, en = [u_ref[k, layer(z), :] for k in range(5)]
        gamma = g_ref[layer(z), :]
        inv = 1.0 / (1.0 + r)
        ux, uy, uz = mx * inv, my * inv, mz * inv
        heat = en - 0.5 * (mx * ux + my * uy + mz * uz)
        lr, lm = lam_ref[0, layer(z), :], lam_ref[1, layer(z), :]
        lr_x = [lx[0, pl.ds(24 * z + s, 8), :] for s in (7, 9)]
        lm_x = [lx[1, pl.ds(24 * z + s, 8), :] for s in (7, 9)]
        lr_z = [lz[0, layer(z + s), :] for s in (0, 2)]
        lm_z = [lz[1, layer(z + s), :] for s in (0, 2)]
        lr_y = [y_prev(lr, yc[layer(z), 0:1], lane), y_next(lr, yc[layer(z), 4:5], lane)]
        lm_y = [y_prev(lm, yc[layer(z), 1:2], lane), y_next(lm, yc[layer(z), 5:6], lane)]
        phi_x0 = HALF_T * (lr_x[1] - lr_x[0])
        phi_y0 = HALF_T * (lr_y[1] - lr_y[0])
        phi_z0 = HALF_T * (lr_z[1] - lr_z[0])
        phi_x1 = px[layer(z), :]
        phi_y1 = HALF_T * (lm_y[1] - lm_y[0])
        phi_z1 = HALF_T * (lm_z[1] - lm_z[0])
        near = (lm_x[0] + lm_x[1]) + (lm_y[0] + lm_y[1]) + (lm_z[0] + lm_z[1])
        d_speed = phi_x1 * mx + 0.5 * (dx[pl.ds(24 * z + 7, 8), :] - dx[pl.ds(24 * z + 9, 8), :])
        d_en = phi_x1 * gamma
        gx[0, pl.ds(24 * z + 8, 8), :] = (
            STAY * lm
            + NEAR * near
            + phi_x0
            + (phi_x1 - d_en) * ux
            + phi_y1 * uy
            + phi_z1 * uz
            + d_speed * inv
        )
        gx[1, pl.ds(24 * z + 8, 8), :] = d_en
        gy[layer(z), :] = phi_y0 - d_en * uy + phi_y1 * ux
        gz[0, layer(z + 1), :] = phi_z0 - d_en * uz + phi_z1 * ux
        gz[1, layer(z + 1), :] = d_en
        dg[layer(z), :] = phi_x1 * heat
    acc = jnp.zeros((NX, NY), F32)
    for z in range(NZ):
        r, mx, my, mz, en = [u0_ref[k, layer(z), :] for k in range(5)]
        inv = 1.0 / (1.0 + r)
        ux, uy, uz = mx * inv, my * inv, mz * inv
        heat = en - 0.5 * (mx * ux + my * uy + mz * uz)
        dif_x = [gx[k, pl.ds(24 * z + 9, 8), :] - gx[k, pl.ds(24 * z + 7, 8), :] for k in range(2)]
        dif_z = [gz[k, layer(z + 2), :] - gz[k, layer(z), :] for k in range(2)]
        dif_y = []
        for k, own in ((0, gy[layer(z), :]), (1, gz[1, layer(z + 1), :])):
            dif_y.append(
                y_next(own, yc[layer(z), 6 + k : 7 + k], lane) - y_prev(own, yc[layer(z), 2 + k : 3 + k], lane)
            )
        d_press = HALF_T * (
            (dif_x[0] + ux * dif_x[1]) + (dif_y[0] + uy * dif_y[1]) + (dif_z[0] + uz * dif_z[1])
        )
        grad = dg[layer(z), :] + d_press * heat
        grad_ref[layer(z), :] = grad
        acc = acc + grad * grad
    total = jnp.sum(jnp.sum(acc, axis=0, keepdims=True), axis=1, keepdims=True)
    miss = jnp.sum(jnp.sum(mis_ref[...], axis=0, keepdims=True), axis=1, keepdims=True)
    miss = miss + jnp.sum(v_ref[...], axis=1, keepdims=True)
    row = jnp.where(lane == 0, total, jnp.where(lane == 1, miss, 0.0))
    for i in range(row_ref.shape[0] // NX):
        row_ref[layer(i), :] = row


def scale_kernel(devices, count, grad_ref, rows_ref, out_ref, misfit_ref):
    acc = rows_ref[layer(0), :]
    for i in range(1, devices // NX):
        acc = acc + rows_ref[layer(i), :]
    row = jnp.sum(acc, axis=0, keepdims=True)
    misfit_ref[0, 0] = row[0, 1] / (devices * count)
    scale = 1.0 / jnp.sqrt(row[0:1, 0:1] / (devices * CELLS * NY) + small_eps)
    out_ref[...] = grad_ref[...] * scale


def split3(value):
    hi = value.astype(jnp.bfloat16)
    rest = value - hi.astype(F32)
    mid = rest.astype(jnp.bfloat16)
    low = (rest - mid.astype(F32)).astype(jnp.bfloat16)
    return hi, mid, low


def probe_kernel(p_ref, o_ref, n_ref, m_ref, v_ref):
    count = p_ref.shape[1]
    probes, obs = p_ref[...], o_ref[...]
    row = lax.broadcasted_iota(jnp.int32, (CELLS, count), 0)
    on_a = row == lax.shift_right_logical(probes, 7)
    on_b = row == lax.bitwise_and(probes, NY - 1)
    one_a = jnp.where(on_a, 1.0, 0.0).astype(jnp.bfloat16)
    one_b = jnp.where(on_b, 1.0, 0.0).astype(jnp.bfloat16)

    def nt(a, b):
        return lax.dot_general(a, b, (((1,), (1,)), ((), ())), preferred_element_type=F32)

    parts = [jnp.where(on_a, part.astype(F32), 0.0).astype(jnp.bfloat16) for part in split3(obs)]
    hits = nt(one_a, one_b)
    sums = nt(parts[0], one_b) + (nt(parts[1], one_b) + nt(parts[2], one_b))
    n_ref[...] = hits
    mean = sums / jnp.maximum(hits, 1.0)
    m_ref[...] = mean
    mean_t = split3(mean.T)
    picked = sum(jnp.dot(part, one_a, preferred_element_type=F32) for part in reversed(mean_t))
    at_probe = jnp.sum(jnp.where(on_b, picked, 0.0), axis=0, keepdims=True)
    off = obs - at_probe
    v_ref[...] = off * off


SMALL = pltpu.CompilerParams(vmem_limit_bytes=12 * 1024 * 1024)


def rows_of(*shape):
    return jax.ShapeDtypeStruct(shape, F32)


def vmem(*shape):
    return pltpu.VMEM(shape, F32)


def call(kernel, outs, scratch, params=SMALL):
    return pl.pallas_call(
        kernel,
        out_shape=outs,
        scratch_shapes=scratch,
        cost_estimate=pl.CostEstimate(flops=100000, bytes_accessed=100000, transcendentals=0),
        compiler_params=params,
    )


def ring(sizes, axis, step):
    n = sizes[axis]
    return [(i, (i + step) % n) for i in range(n)]


def exchange_x(sizes, xlo, xhi):
    return (
        lax.ppermute(xhi, "gx", ring(sizes, "gx", 1)),
        lax.ppermute(xlo, "gx", ring(sizes, "gx", -1)),
    )


def exchange_yz(sizes, ylo, yhi, zs):
    zr = lax.ppermute(zs, "gz", ring(sizes, "gz", 1))
    yl = lax.ppermute(yhi, "gy", ring(sizes, "gy", 1))
    yh = lax.ppermute(ylo, "gy", ring(sizes, "gy", -1))
    return yl, yh, zr


def exchange(sizes, xlo, xhi, ylo, yhi, zs):
    xl, xh = exchange_x(sizes, xlo, xhi)
    return xl, xh, *exchange_yz(sizes, ylo, yhi, zs)


def local(sizes, checkpoint, gruneisen, switch, probes, observed):
    bind = functools.partial
    state = checkpoint.reshape(5, CELLS, NY)
    gamma = gruneisen.reshape(CELLS, NY)
    sw = switch.reshape(2, CELLS, NY)
    plane = rows_of(8, NY)

    def slabs(x_items, z_items):
        x = rows_of(x_items, NZ, NY)
        return [x, x, plane, plane, rows_of(z_items, NX, NY)]

    *sent, yown = call(bind(prep_kernel, sizes), slabs(8, 8) + [plane], [vmem(CELLS, NY)], None)(state, gamma, sw)
    got = exchange(sizes, *sent)
    hits, mean, spread = call(
        probe_kernel,
        [rows_of(CELLS, NY), rows_of(CELLS, NY), rows_of(1, probes.shape[0])],
        [],
    )(probes.reshape(1, -1), observed.reshape(1, -1))
    tall = (NZ + 2) * NX
    state_1, *sent = call(
        bind(step_kernel, sizes),
        [rows_of(5, CELLS, NY)] + slabs(5, 2),
        [
            vmem(NZ * 24, NY), vmem(CELLS, NY), vmem(tall, NY), vmem(CELLS, NY),
            vmem(5, NZ * 16, NY), vmem(5, NZ * 16, NY), vmem(5, tall, NY), vmem(5, tall, NY),
            vmem(5, CELLS, NY), vmem(16, NY), vmem(CELLS, 16), vmem(CELLS, NY),
        ],
    )(state, gamma, sw, *got, yown)
    got = exchange(sizes, *sent)
    lam_2, coef, coef_halo, mis, *sent, yown = call(
        bind(speed_kernel, sizes),
        [rows_of(2, CELLS, NY), rows_of(CELLS, NY), rows_of(2, NZ, NY), plane]
        + [plane, plane, rows_of(6, NX, NY), plane],
        [
            vmem(NZ * 24, NY), vmem(2, NZ * 16, NY), vmem(2, NZ * 16, NY), vmem(2, tall, NY), vmem(2, tall, NY),
            vmem(2, CELLS, NY), vmem(CELLS, 8), vmem(CELLS, NY),
        ],
    )(state_1, gamma, sw, *got, hits, mean)
    got_yz = exchange_yz(sizes, *sent)
    sent = call(bind(edge_kernel, sizes), slabs(8, 1)[:2], [vmem(CELLS, NY)])(state_1, gamma, lam_2, coef, *got_yz)
    got_x = exchange_x(sizes, *sent)
    devices = sizes["gx"] * sizes["gy"] * sizes["gz"]
    gradient, rows = call(
        bind(gradient_kernel, sizes),
        [rows_of(CELLS, NY), rows_of(devices, NY)],
        [
            vmem(2, NZ * 24, NY), vmem(2, tall, NY), vmem(CELLS, NY), vmem(NZ * 24, NY), vmem(CELLS, NY),
            vmem(CELLS, 8), vmem(2, NZ * 24, NY), vmem(CELLS, NY), vmem(2, tall, NY),
        ],
    )(state, state_1, gamma, lam_2, coef, coef_halo, yown, *got_yz, *got_x, mis, spread)
    rows = lax.all_to_all(rows, ("gx", "gy", "gz"), 0, 0, tiled=True)
    direction, misfit = pl.pallas_call(
        bind(scale_kernel, devices, probes.shape[0]),
        out_shape=[rows_of(CELLS, NY), rows_of(1, 1)],
        out_specs=[pl.BlockSpec(memory_space=pltpu.VMEM), pl.BlockSpec(memory_space=pltpu.SMEM)],
        compiler_params=SMALL,
    )(gradient, rows)
    return direction.reshape(NZ, NX, NY), misfit.reshape(())


def solution(mesh):
    block = P("gz", "gx", "gy")
    parted = P(None, "gz", "gx", "gy")
    listed = P(("gx", "gy", "gz"))
    return jax.shard_map(
        functools.partial(local, dict(mesh.shape)),
        mesh=mesh,
        in_specs=(parted, block, parted, listed, listed),
        out_specs=(block, P()),
        check_vma=False,
    )
```

```python
import functools
import jax
import jax.numpy as jnp
from jax import lax
from jax.experimental import pallas as pl
from jax.experimental.pallas import tpu as pltpu
from jax.sharding import PartitionSpec as P

NZ, NX, NY = 16, 8, 128
CELLS = NZ * NX
bulk_modulus = 2.0
slope_coeff = 1.5
signal_speed = 2.5
time_ratio = 0.1
quad_viscosity = 4.0
small_eps = 1e-12
HALF_C = 0.5 * signal_speed
HALF_T = 0.5 * time_ratio
NEAR = time_ratio * HALF_C
STAY = 1.0 - 3.0 * time_ratio * signal_speed
F32 = jnp.float32


def primitives(r, mx, my, mz, en, gamma):
    inv = 1.0 / (1.0 + r)
    ux, uy, uz = mx * inv, my * inv, mz * inv
    heat = en - 0.5 * (mx * ux + my * uy + mz * uz)
    press = bulk_modulus * (r + slope_coeff * r * r) + gamma * heat
    return ux, uy, uz, heat, press


def total_pressure(press, sw, r, slope):
    squeeze = jnp.minimum(slope, 0.0)
    return press + sw * quad_viscosity * (1.0 + r) * squeeze * squeeze


def flux(state, axis, speed, total):
    rows = [state[1 + axis]] + [state[1 + k] * speed for k in range(3)]
    rows[1 + axis] = rows[1 + axis] + total
    return rows + [(state[4] + total) * speed]


def upper_part(f, u):
    return 0.5 * f - HALF_C * u


def lower_part(f, u):
    return 0.5 * f + HALF_C * u


def layer(z):
    return pl.ds(NX * z, NX)


def x_row(x):
    return pl.ds(x, NZ, stride=NX)


def lanes():
    return lax.broadcasted_iota(jnp.int32, (NX, NY), 1)


def y_next(value, column, lane):
    return jnp.where(lane == NY - 1, column, pltpu.roll(value, NY - 1, 1))


def y_prev(value, column, lane):
    return jnp.where(lane == 0, column, pltpu.roll(value, 1, 1))


def inside(flag):
    return jnp.where(flag, 1.0, 0.0).astype(F32)


def masks(mesh):
    ix, iy, iz = lax.axis_index("gx"), lax.axis_index("gy"), lax.axis_index("gz")
    return (
        (inside(ix > 0), inside(ix < mesh["gx"] - 1)),
        (inside(iy > 0), inside(iy < mesh["gy"] - 1)),
        (inside(iz > 0), inside(iz < mesh["gz"] - 1)),
        iz == 0,
    )


def face_layer(is_first, depth):
    return jnp.where(is_first, NZ - 1 - depth, depth)


def dyn_layer(z):
    return pl.ds(pl.multiple_of(NX * z, NX), NX)


def pack_edges(values, lane, depth=2):
    out = pltpu.roll(values[0], depth, 1)
    for i in range(1, len(values)):
        out = jnp.where(lane < 2 * depth * i, out, pltpu.roll(values[i], depth * (2 * i + 1), 1))
    return out


def begun(u, f, far, sign):
    return STAY * u + time_ratio * (sign * 0.5 * f + HALF_C * far)


def prep_kernel(mesh, u_ref, g_ref, s_ref, ylo, yhi, zs, yp):
    _, _, _, first = masks(mesh)
    lane = lanes()
    for z in range(NZ):
        vals = [u_ref[k, layer(z), :] for k in range(5)]
        vals += [g_ref[layer(z), :], s_ref[0, layer(z), :].astype(F32)]
        yp[layer(z), :] = pack_edges(vals, lane, 3)
    rows = yp[...].T
    for out, c1, c2, c3, sign in ((yhi, 2, 1, 0, 1.0), (ylo, 3, 4, 5, -1.0)):
        st, st2, st3 = [[rows[6 * k + c : 6 * k + c + 1] for k in range(7)] for c in (c1, c2, c3)]
        prim, prim2 = primitives(*st[:6]), primitives(*st2[:6])
        slope = (sign * 0.5) * (prim[1] - st3[2] / (1.0 + st3[0]))
        fl = flux(st2[:5], 1, prim2[1], total_pressure(prim2[4], st2[6], st2[0], slope))
        items = st[:5] + [prim[4], st[6], prim2[1]] + [begun(st[k], fl[k], st2[k], sign) for k in range(3)]
        for k in range(11):
            out[k : k + 1] = items[k]
        out[11:16] = jnp.zeros((5, NY), F32)
    za, zb, zc = [dyn_layer(face_layer(first, d)) for d in range(3)]
    sign = jnp.where(first, 1.0, -1.0)
    st, st2 = [[u_ref[k, at, :] for k in range(5)] for at in (za, zb)]
    prim, prim2 = primitives(*st, g_ref[za, :]), primitives(*st2, g_ref[zb, :])
    slope = (sign * 0.5) * (prim[2] - u_ref[3, zc, :] / (1.0 + u_ref[0, zc, :]))
    fl = flux(st2, 2, prim2[2], total_pressure(prim2[4], s_ref[0, zb, :].astype(F32), st2[0], slope))
    items = st + [prim[4], s_ref[0, za, :].astype(F32), prim2[2]]
    items += [begun(st[k], fl[k], st2[k], sign) for k in (0, 1, 3)]
    for k in range(11):
        zs[k] = items[k]


def side_kernel(
    mesh, u_ref, g_ref, s_ref, ylo, yhi, yl, yh, zr,
    part, xlo, xhi, zz,
    vy, vz, pr, az, bz, yr, yc,
):
    _, (myl, myh), (mzl, mzh), first = masks(mesh)
    lane = lanes()
    for z in range(NZ):
        _, uy, uz, _, press = primitives(*[u_ref[k, layer(z), :] for k in range(5)], g_ref[layer(z), :])
        vy[layer(z), :] = uy
        vz[layer(z + 1), :] = uz
        pr[layer(z), :] = press
    far = [zr[k] for k in range(8)]
    speed = far[3] / (1.0 + far[0])
    own = vz[dyn_layer(face_layer(first, 0) + 1), :]
    slope = (far[7] - own) * jnp.where(first, 0.5, -0.5)
    fl = flux(far[:5], 2, speed, total_pressure(far[5], far[6], far[0], slope))
    for k in range(5):
        bz[k, layer(0), :] = lower_part(fl[k], far[k]) * mzl
        az[k, layer(NZ), :] = upper_part(fl[k], far[k]) * mzh
    vz[layer(0), :] = speed * mzl
    vz[layer(NZ + 1), :] = speed * mzh
    low = [yl[k : k + 1] * myl for k in range(8)]
    high = [yh[k : k + 1] * myh for k in range(8)]
    speed = low[2] / (1.0 + low[0])
    yr[10:11, :] = speed
    slope = 0.5 * (ylo[2:3] / (1.0 + ylo[0:1]) - low[7])
    fl = flux(low[:5], 1, speed, total_pressure(low[5], low[6], low[0], slope))
    for k in range(5):
        yr[k : k + 1, :] = lower_part(fl[k], low[k])
    speed = high[2] / (1.0 + high[0])
    yr[11:12, :] = speed
    slope = 0.5 * (high[7] - yhi[2:3] / (1.0 + yhi[0:1]))
    fl = flux(high[:5], 1, speed, total_pressure(high[5], high[6], high[0], slope))
    for k in range(5):
        yr[5 + k : 6 + k, :] = upper_part(fl[k], high[k])
    yr[12:16, :] = jnp.zeros((4, NY), F32)
    yc[...] = yr[...].T
    for z in range(NZ):
        st = [u_ref[k, layer(z), :] for k in range(5)]
        press = pr[layer(z), :]
        visc = s_ref[0, layer(z), :].astype(F32) * quad_viscosity * (1.0 + st[0])
        uy, uz = vy[layer(z), :], vz[layer(z + 1), :]

        def col(i):
            return yc[layer(z), i : i + 1]

        def total(up, down):
            squeeze = jnp.minimum(0.5 * (up - down), 0.0)
            return press + visc * squeeze * squeeze

        fy = flux(st, 1, uy, total(y_next(uy, col(11), lane), y_prev(uy, col(10), lane)))
        fz = flux(st, 2, uz, total(vz[layer(z + 2), :], vz[layer(z), :]))
        for k in range(5):
            az[k, layer(z), :] = upper_part(fz[k], st[k])
            bz[k, layer(z + 1), :] = lower_part(fz[k], st[k])
            part[k, layer(z), :] = STAY * st[k] - time_ratio * (
                y_next(upper_part(fy[k], st[k]), col(5 + k), lane)
                - y_prev(lower_part(fy[k], st[k]), col(k), lane)
            )
    for z in range(NZ):
        for k in range(5):
            part[k, layer(z), :] = part[k, layer(z), :] - time_ratio * (
                az[k, layer(z + 1), :] - bz[k, layer(z), :]
            )
    for k in range(8):
        zz[k : k + 1, :] = low[k]
        zz[8 + k : 9 + k, :] = high[k]
    for out, e, i, j, sign in ((xhi, NX - 1, NX - 2, NX - 3, 1.0), (xlo, 0, 1, 2, -1.0)):
        st, st1, st2 = [[u_ref[k, x_row(at), :] for k in range(5)] for at in (e, i, j)]
        ux = st[1] / (1.0 + st[0])
        prim1, prim2 = primitives(*st1, g_ref[x_row(i), :]), primitives(*st2, g_ref[x_row(j), :])
        last = j - 1 if sign > 0 else j + 1
        ux3 = u_ref[1, x_row(last), :] / (1.0 + u_ref[0, x_row(last), :])
        slope1, slope2 = (sign * 0.5) * (ux - prim2[0]), (sign * 0.5) * (prim1[0] - ux3)
        f1 = flux(st1, 0, prim1[0], total_pressure(prim1[4], s_ref[0, x_row(i), :].astype(F32), st1[0], slope1))
        f2 = flux(st2, 0, prim2[0], total_pressure(prim2[4], s_ref[0, x_row(j), :].astype(F32), st2[0], slope2))
        for k in range(5):
            out[k] = st[k]
        out[5] = g_ref[x_row(e), :]
        out[6] = s_ref[0, x_row(e), :].astype(F32)
        out[7] = prim1[0]
        out[8] = s_ref[1, x_row(e), :].astype(F32)
        for k in range(5):
            out[9 + k] = part[k, x_row(e), :] + time_ratio * (sign * 0.5 * f1[k] + HALF_C * st1[k])
        for k in range(2):
            out[14 + k] = part[k, x_row(i), :] + time_ratio * (sign * 0.5 * f2[k] + HALF_C * st2[k])
        out[16] = zz[...]
        for k in range(8):
            out[17, k : k + 1, :] = zr[k, e : e + 1, :]
        out[17, 8:9, :] = zr[1, i : i + 1, :] / (1.0 + zr[0, i : i + 1, :])
        out[17, 9:16, :] = jnp.zeros((7, NY), F32)


def shifted_x(own, low, high, at_x):
    up = jnp.where(at_x == NX - 1, pltpu.roll(high, NX - 1, 1), pltpu.roll(own, NY - 1, 1))
    down = jnp.where(at_x == 0, pltpu.roll(low, NY - NX + 1, 1), pltpu.roll(own, 1, 1))
    return up, down


def halo_step(
    mesh, u_ref, g_ref, s_ref, part, ylo, yhi, yl, yh, zr, xl, xh, zz,
    o_ref, hxl, hxh, hyl, hyh, hz, vx, ax, bx, zc,
):
    (mxl, mxh), (myl, myh), (mzl, mzh), first = masks(mesh)
    for z in range(NZ):
        vx[pl.ds(24 * z + 8, 8), :] = u_ref[1, layer(z), :] / (1.0 + u_ref[0, layer(z), :])
    low = [xl[k] * mxl for k in range(8)]
    high = [xh[k] * mxh for k in range(8)]
    prim = primitives(*low[:6])
    vx[pl.ds(7, NZ, stride=24), :] = prim[0]
    slope = 0.5 * (vx[pl.ds(8, NZ, stride=24), :] - low[7])
    f_low = flux(low[:5], 0, prim[0], total_pressure(prim[4], low[6], low[0], slope))
    prim = primitives(*high[:6])
    vx[pl.ds(16, NZ, stride=24), :] = prim[0]
    slope = 0.5 * (high[7] - vx[pl.ds(15, NZ, stride=24), :])
    f_high = flux(high[:5], 0, prim[0], total_pressure(prim[4], high[6], high[0], slope))
    for k in range(5):
        bx[k, pl.ds(7, NZ, stride=16), :] = lower_part(f_low[k], low[k])
        ax[k, pl.ds(8, NZ, stride=16), :] = upper_part(f_high[k], high[k])
    for z in range(NZ):
        st = [u_ref[k, layer(z), :] for k in range(5)]
        ux, _, _, _, press = primitives(*st, g_ref[layer(z), :])
        slope = 0.5 * (vx[pl.ds(24 * z + 9, 8), :] - vx[pl.ds(24 * z + 7, 8), :])
        fx = flux(st, 0, ux, total_pressure(press, s_ref[0, layer(z), :].astype(F32), st[0], slope))
        for k in range(5):
            ax[k, pl.ds(16 * z, 8), :] = upper_part(fx[k], st[k])
            bx[k, pl.ds(16 * z + 8, 8), :] = lower_part(fx[k], st[k])
    for z in range(NZ):
        for k in range(5):
            o_ref[k, layer(z), :] = part[k, layer(z), :] - time_ratio * (
                ax[k, pl.ds(16 * z + 1, 8), :] - bx[k, pl.ds(16 * z + 7, 8), :]
            )
    for out, ref, mask in ((hxl, xl, mxl), (hxh, xh, mxh)):
        if ref is xl:
            near = [-ax[k, pl.ds(0, NZ, stride=16), :] for k in range(5)]
            next_ = [-upper_part(f_low[k], low[k]) for k in range(2)]
        else:
            near = [bx[k, pl.ds(15, NZ, stride=16), :] for k in range(5)]
            next_ = [lower_part(f_high[k], high[k]) for k in range(2)]
        st = [(ref[9 + k] + time_ratio * near[k]) * mask for k in range(5)]
        st2 = [(ref[14 + k] + time_ratio * next_[k]) * mask for k in range(2)]
        out[0] = st[0]
        out[1] = st[1]
        out[2] = primitives(*st, ref[5] * mask)[4]
        out[3] = ref[8] * mask
        out[4] = st2[1] / (1.0 + st2[0])
    lane = lax.broadcasted_iota(jnp.int32, (1, NY), 1)
    at_x = lax.bitwise_and(lane, NX - 1)
    for side, ref, mask, own, out, sign in ((0, yl, myl, ylo, hyl, -1.0), (1, yh, myh, yhi, hyh, 1.0)):

        def items(values, m):
            return [values[k : k + 1] * m for k in range(8)]

        here = items(ref, mask)
        near_l, near_h = items(xl[16, 8 * side : 8 * side + 8, :], mxl), items(xh[16, 8 * side : 8 * side + 8, :], mxh)
        ux, ux_l, ux_h = [v[1] / (1.0 + v[0]) for v in (here, near_l, near_h)]
        up, down = shifted_x(ux, ux_l, ux_h, at_x)
        slope = 0.5 * (up - down)
        slope_h = 0.5 * (pltpu.roll(ux_h, NY - 1, 1) - pltpu.roll(ux, NY - NX + 1, 1))
        slope_l = 0.5 * (pltpu.roll(ux, NX - 1, 1) - pltpu.roll(ux_l, 1, 1))

        def fx_of(v, speed, slope):
            return [v[1], v[1] * speed + total_pressure(v[5], v[6], v[0], slope), v[2] * speed]

        f_here, f_l, f_h = fx_of(here, ux, slope), fx_of(near_l, ux_l, slope_l), fx_of(near_h, ux_h, slope_h)
        uz = here[3] / (1.0 + here[0])
        near_z = items(zz[8 * side : 8 * side + 8, :], 1.0)
        uz_z = near_z[3] / (1.0 + near_z[0])
        fz, fz_z = [[v[3], v[1] * w, v[2] * w] for v, w in ((here, uz), (near_z, uz_z))]
        self_ = items(own, 1.0)
        uy = self_[2] / (1.0 + self_[0])
        uy_here = here[2] / (1.0 + here[0])
        slope = 0.5 * (self_[7] - uy_here if side == 0 else uy_here - self_[7])
        fy = [self_[2], self_[1] * uy, self_[2] * uy + total_pressure(self_[5], self_[6], self_[0], slope)]
        new = []
        for k in range(3):
            a_x, _ = shifted_x(upper_part(f_here[k], here[k]), ux_l, upper_part(f_h[k], near_h[k]), at_x)
            _, b_x = shifted_x(lower_part(f_here[k], here[k]), lower_part(f_l[k], near_l[k]), ux_h, at_x)
            a_z = jnp.where(
                lane >= NY - NX,
                pltpu.roll(upper_part(fz_z[k], near_z[k]), NY - NX, 1) * mzh,
                pltpu.roll(upper_part(fz[k], here[k]), NY - NX, 1),
            )
            b_z = jnp.where(
                lane < NX,
                pltpu.roll(lower_part(fz_z[k], near_z[k]), NX, 1) * mzl,
                pltpu.roll(lower_part(fz[k], here[k]), NX, 1),
            )
            facing = sign * 0.5 * fy[k] + HALF_C * self_[k]
            new.append(mask * (ref[8 + k : 9 + k] + time_ratio * (facing - (a_x - b_x) - (a_z - b_z))))
        r, mx, my = new
        combine = lower_part if side == 0 else upper_part
        out[0:1, :] = combine(my, r)
        out[1:2, :] = combine(mx * (my / (1.0 + r)), mx)
        out[2:8, :] = jnp.zeros((6, NY), F32)
    rows = []
    for side in range(2):
        v = [zz[8 * side + k : 8 * side + k + 1, :] for k in range(8)]
        speed = v[2] / (1.0 + v[0])
        fy = [v[2], v[1] * speed, v[3] * speed]
        combine = upper_part if side else lower_part
        rows += [combine(f, v[k]) for f, k in zip(fy, (0, 1, 3))]
    zc[...] = jnp.concatenate(rows + [jnp.zeros((2, NY), F32)], axis=0).T
    cols = zc[dyn_layer(jnp.where(first, 0, NZ - 1)), :]
    full = lanes()
    deep = lax.broadcasted_iota(jnp.int32, (NX, NY), 0)
    here = [zr[k] for k in range(8)]
    near_l = [xl[17, k : k + 1, :] * mxl for k in range(9)]
    near_h = [xh[17, k : k + 1, :] * mxh for k in range(9)]
    ux, ux_l, ux_h = [v[1] / (1.0 + v[0]) for v in (here, near_l, near_h)]

    def next_x(value, row):
        return jnp.where(deep == NX - 1, row, pltpu.roll(value, NX - 1, 0))

    def prev_x(value, row):
        return jnp.where(deep == 0, row, pltpu.roll(value, 1, 0))

    slope = 0.5 * (next_x(ux, ux_h) - prev_x(ux, ux_l))
    slope_h = 0.5 * (near_h[8] - ux[NX - 1 : NX])
    slope_l = 0.5 * (ux[0:1] - near_l[8])

    def fx_layer(v, speed, slope):
        return [v[1], v[1] * speed + total_pressure(v[5], v[6], v[0], slope), v[3] * speed]

    f_here, f_l, f_h = fx_layer(here, ux, slope), fx_layer(near_l, ux_l, slope_l), fx_layer(near_h, ux_h, slope_h)
    uy = here[2] / (1.0 + here[0])
    fy = [here[2], here[1] * uy, here[3] * uy]
    za, zb = dyn_layer(face_layer(first, 0)), dyn_layer(face_layer(first, 1))
    sign = jnp.where(first, 1.0, -1.0)
    st = [u_ref[k, za, :] for k in range(5)]
    prim = primitives(*st, g_ref[za, :])
    uz_b = u_ref[3, zb, :] / (1.0 + u_ref[0, zb, :])
    slope = (sign * 0.5) * (here[3] / (1.0 + here[0]) - uz_b)
    fz = flux(st, 2, prim[2], total_pressure(prim[4], s_ref[0, za, :].astype(F32), st[0], slope))
    new = []
    for n, k in enumerate((0, 1, 3)):
        a_x = next_x(upper_part(f_here[n], here[k]), upper_part(f_h[n], near_h[k]))
        b_x = prev_x(lower_part(f_here[n], here[k]), lower_part(f_l[n], near_l[k]))
        a_y = y_next(upper_part(fy[n], here[k]), cols[:, 3 + n : 4 + n], full)
        b_y = y_prev(lower_part(fy[n], here[k]), cols[:, n : n + 1], full)
        facing = sign * 0.5 * fz[k] + HALF_C * st[k]
        new.append(zr[8 + n] + time_ratio * (facing - (a_x - b_x) - (a_y - b_y)))
    r, mx, mz = new
    hz[0] = 0.5 * mz - (sign * HALF_C) * r
    hz[1] = 0.5 * mx * (mz / (1.0 + r)) - (sign * HALF_C) * mx


def forward_kernel(
    mesh, u0_ref, g_ref, s_ref, part, ylo_in, yhi_in, yl, yh, zr, xl, xh, zz, n_ref, m_ref,
    u_ref, lam_ref, cf_ref, cfh_ref, mis_ref, ylo, yhi, zs, yown,
    hxl, hxh, hyl, hyh, hz, vx, ax, bx, az, bz, ch, yc, yp, zc,
):
    halo_step(
        mesh, u0_ref, g_ref, s_ref, part, ylo_in, yhi_in, yl, yh, zr, xl, xh, zz,
        u_ref, hxl, hxh, hyl, hyh, hz, vx, ax, bx, zc,
    )
    speed_kernel(
        mesh, u_ref, g_ref, s_ref, hxl, hxh, hyl, hyh, hz, n_ref, m_ref,
        lam_ref, cf_ref, cfh_ref, mis_ref, ylo, yhi, zs, yown,
        vx, ax, bx, az, bz, ch, yc, yp,
    )


def columns_of(low, high, count, low_mask, high_mask):
    rows = [low[k : k + 1] * low_mask for k in range(count)]
    rows += [high[k : k + 1] * high_mask for k in range(count)]
    rows.append(jnp.zeros((8 - 2 * count, NY), F32))
    return jnp.concatenate(rows, axis=0).T


def speed_kernel(
    mesh, u_ref, g_ref, s_ref, xl, xh, yl, yh, zr, n_ref, m_ref,
    lam_ref, cf_ref, cfh_ref, mis_ref, ylo, yhi, zs, yown,
    vx, ax, bx, az, bz, ch, yc, yp,
):
    (mxl, mxh), (myl, myh), (mzl, mzh), first = masks(mesh)
    lane = lanes()
    for z in range(NZ):
        vx[pl.ds(24 * z + 8, 8), :] = u_ref[1, layer(z), :] / (1.0 + u_ref[0, layer(z), :])
    for side, ref, mask in ((0, xl, mxl), (1, xh, mxh)):
        r, mx, press, sw, second = [ref[k] * mask for k in range(5)]
        speed = mx / (1.0 + r)
        vx[pl.ds(16 if side else 7, NZ, stride=24), :] = speed
        own = vx[pl.ds(15 if side else 8, NZ, stride=24), :]
        slope = 0.5 * (second - own if side else own - second)
        squeeze = jnp.minimum(slope, 0.0)
        visc = sw * quad_viscosity * (1.0 + r) * squeeze
        cfh_ref[side] = 2.0 * visc
        f1 = mx * speed + press + visc * squeeze
        if side:
            ax[0, pl.ds(8, NZ, stride=16), :] = upper_part(mx, r)
            ax[1, pl.ds(8, NZ, stride=16), :] = upper_part(f1, mx)
        else:
            bx[0, pl.ds(7, NZ, stride=16), :] = lower_part(mx, r)
            bx[1, pl.ds(7, NZ, stride=16), :] = lower_part(f1, mx)
    for k in range(2):
        bz[k, layer(0), :] = zr[k] * mzl
        az[k, layer(NZ), :] = zr[k] * mzh
    yc[...] = columns_of(yl, yh, 2, myl, myh)
    for z in range(NZ):
        r, mx, my, mz, en = [u_ref[k, layer(z), :] for k in range(5)]
        ux, uy, uz, _, press = primitives(r, mx, my, mz, en, g_ref[layer(z), :])
        squeeze = jnp.minimum(0.5 * (vx[pl.ds(24 * z + 9, 8), :] - vx[pl.ds(24 * z + 7, 8), :]), 0.0)
        visc = s_ref[1, layer(z), :].astype(F32) * quad_viscosity * (1.0 + r) * squeeze
        cf_ref[layer(z), :] = 2.0 * visc
        f1 = mx * ux + press + visc * squeeze
        for k, st, fx, fy, fz in ((0, r, mx, my, mz), (1, mx, f1, mx * uy, mx * uz)):
            ax[k, pl.ds(16 * z, 8), :] = upper_part(fx, st)
            bx[k, pl.ds(16 * z + 8, 8), :] = lower_part(fx, st)
            az[k, layer(z), :] = upper_part(fz, st)
            bz[k, layer(z + 1), :] = lower_part(fz, st)
            ch[k, layer(z), :] = (
                3.0 * signal_speed * st
                + y_next(upper_part(fy, st), yc[layer(z), 2 + k : 3 + k], lane)
                - y_prev(lower_part(fy, st), yc[layer(z), k : k + 1], lane)
            )
    mis = jnp.zeros((NX, NY), F32)
    for z in range(NZ):
        new = []
        for k in range(2):
            change = (
                ch[k, layer(z), :]
                + (ax[k, pl.ds(16 * z + 1, 8), :] - bx[k, pl.ds(16 * z + 7, 8), :])
                + (az[k, layer(z + 1), :] - bz[k, layer(z), :])
            )
            new.append(u_ref[k, layer(z), :] - time_ratio * change)
        inv = 1.0 / (1.0 + new[0])
        speed = new[1] * inv
        off = speed - m_ref[layer(z), :]
        weight = n_ref[layer(z), :] * off
        mis = mis + weight * off
        lam_m = 2.0 * weight * inv
        lam_r = -lam_m * speed
        lam_ref[0, layer(z), :] = lam_r
        lam_ref[1, layer(z), :] = lam_m
        inv = 1.0 / (1.0 + u_ref[0, layer(z), :])
        extra = [u_ref[1, layer(z), :] * inv, u_ref[2, layer(z), :] * inv, g_ref[layer(z), :]]
        yp[layer(z), :] = pack_edges([lam_r, lam_m] + extra, lane)
    mis_ref[...] = mis
    za, zb = dyn_layer(face_layer(first, 0)), dyn_layer(face_layer(first, 1))
    inv = 1.0 / (1.0 + u_ref[0, za, :])
    ux = u_ref[1, za, :] * inv
    zs[0] = lam_ref[0, za, :]
    zs[1] = lam_ref[1, za, :]
    zs[2] = jnp.where(first, -HALF_T, HALF_T) * (lam_ref[0, zb, :] + lam_ref[1, zb, :] * ux)
    zs[3] = ux
    zs[4] = u_ref[3, za, :] * inv
    zs[5] = g_ref[za, :]
    rows = yp[...].T
    for out, edge, second, own, sign in ((yhi, 1, 0, 2, -HALF_T), (ylo, 2, 3, 0, HALF_T)):
        lam_r, lam_m, ux, uy, gamma = [rows[4 * i + edge : 4 * i + edge + 1] for i in range(5)]
        out[0:1] = lam_r
        out[1:2] = lam_m
        out[2:3] = sign * (rows[second : second + 1] + rows[4 + second : 5 + second] * ux)
        out[3:4] = ux
        out[4:5] = uy
        out[5:6] = gamma
        out[6:8] = jnp.zeros((2, NY), F32)
        yown[own : own + 1] = lam_r
        yown[own + 1 : own + 2] = lam_m
    yown[4:8] = jnp.zeros((4, NY), F32)


def edge_kernel(mesh, u_ref, g_ref, lam_ref, cf_ref, yl, yh, zr, xlo, xhi, yc):
    _, (myl, myh), (mzl, mzh), _ = masks(mesh)
    low_y, high_y = yl[1:2] * myl, yh[1:2] * myh
    yc[:, 0:8] = jnp.concatenate([low_y, high_y, jnp.zeros((6, NY), F32)], axis=0).T
    lane = lax.broadcasted_iota(jnp.int32, (NZ, NY), 1)
    deep = lax.broadcasted_iota(jnp.int32, (NZ, NY), 0)
    for out, e, i, i2, sign in ((xhi, NX - 1, NX - 2, NX - 3, 1.0), (xlo, 0, 1, 2, -1.0)):
        r, mx, my, mz = [u_ref[k, x_row(e), :] for k in range(4)]
        inv = 1.0 / (1.0 + r)
        lm, lm_i = lam_ref[1, x_row(e), :], lam_ref[1, x_row(i), :]
        col = yc[x_row(e), :]
        side = zr[1, e : e + 1, :]
        up_y = jnp.where(lane == NY - 1, col[:, 1:2], pltpu.roll(lm, NY - 1, 1))
        down_y = jnp.where(lane == 0, col[:, 0:1], pltpu.roll(lm, 1, 1))
        up_z = jnp.where(deep == NZ - 1, side * mzh, pltpu.roll(lm, NZ - 1, 0))
        down_z = jnp.where(deep == 0, side * mzl, pltpu.roll(lm, 1, 0))
        slope = (sign * HALF_T) * (lm - lam_ref[1, x_row(i2), :]) * cf_ref[x_row(i), :]
        out[0] = lam_ref[0, x_row(e), :]
        out[1] = lm
        out[2] = lm_i
        out[3] = (
            STAY * lm
            + NEAR * (lm_i + (up_y + down_y) + (up_z + down_z))
            - (sign * HALF_T) * lam_ref[0, x_row(i), :]
            + HALF_T * ((up_y - down_y) * (my * inv) + (up_z - down_z) * (mz * inv))
            + (sign * 0.5) * slope * inv
        )
        gamma = g_ref[x_row(e), :]
        out[4] = (2.0 - gamma) * (mx * inv)
        out[5] = inv
        out[6] = gamma
        out[7] = jnp.where(deep == 0, low_y, jnp.where(deep == 1, high_y, jnp.where(deep == 2, side, 0.0)))


def gradient_kernel(
    mesh, u0_ref, u_ref, g_ref, lam_ref, cf_ref, cfh_ref, yown, yl, yh, zr, xl, xh, mis_ref, v_ref,
    grad_ref, row_ref,
    lx, lz, px, dx, dg, yc, gx, gy, gz,
):
    (mxl, mxh), (myl, myh), (mzl, mzh), first = masks(mesh)
    lane = lanes()
    for k in range(2):
        for z in range(NZ):
            lx[k, pl.ds(24 * z + 8, 8), :] = lam_ref[k, layer(z), :]
            lz[k, layer(z + 1), :] = lam_ref[k, layer(z), :]
        lx[k, pl.ds(7, NZ, stride=24), :] = xl[k] * mxl
        lx[k, pl.ds(16, NZ, stride=24), :] = xh[k] * mxh
        lz[k, layer(0), :] = zr[k] * mzl
        lz[k, layer(NZ + 1), :] = zr[k] * mzh
    phi_low = HALF_T * (lam_ref[1, x_row(0), :] - xl[2] * mxl)
    phi_high = HALF_T * (xh[2] * mxh - lam_ref[1, x_row(NX - 1), :])
    dx[pl.ds(7, NZ, stride=24), :] = phi_low * cfh_ref[0]
    dx[pl.ds(16, NZ, stride=24), :] = phi_high * cfh_ref[1]
    for z in range(NZ):
        phi = HALF_T * (lx[1, pl.ds(24 * z + 9, 8), :] - lx[1, pl.ds(24 * z + 7, 8), :])
        px[layer(z), :] = phi
        dx[pl.ds(24 * z + 8, 8), :] = phi * cf_ref[layer(z), :]
    gx[1, pl.ds(7, NZ, stride=24), :] = mxl * phi_low * xl[6]
    gx[1, pl.ds(16, NZ, stride=24), :] = mxh * phi_high * xh[6]
    gx[0, pl.ds(7, NZ, stride=24), :] = mxl * (
        xl[3]
        + HALF_T * lam_ref[0, x_row(0), :]
        + NEAR * lam_ref[1, x_row(0), :]
        + phi_low * xl[4]
        - 0.5 * dx[pl.ds(8, NZ, stride=24), :] * xl[5]
    )
    gx[0, pl.ds(16, NZ, stride=24), :] = mxh * (
        xh[3]
        - HALF_T * lam_ref[0, x_row(NX - 1), :]
        + NEAR * lam_ref[1, x_row(NX - 1), :]
        + phi_high * xh[4]
        + 0.5 * dx[pl.ds(15, NZ, stride=24), :] * xh[5]
    )
    at_x = lax.bitwise_and(lax.broadcasted_iota(jnp.int32, (1, NY), 1), NX - 1)
    from_high, from_low = pltpu.roll(xh[7], NX - 1, 1) * mxh, pltpu.roll(xl[7], NY - NX + 1, 1) * mxl
    halo = []
    for side, ref, mask, sign in ((0, yl, myl, HALF_T), (1, yh, myh, -HALF_T)):
        items = ref[...]
        up = jnp.where(at_x == NX - 1, from_high[side : side + 1], pltpu.roll(items, NY - 1, 1)[1:2])
        down = jnp.where(at_x == 0, from_low[side : side + 1], pltpu.roll(items, 1, 1)[1:2])
        d_en = HALF_T * (up - down) * items[5:6]
        own_r, own_m = yown[2 * side : 2 * side + 1], yown[2 * side + 1 : 2 * side + 2]
        d_my = items[2:3] + sign * (own_r + own_m * items[3:4]) - d_en * items[4:5]
        halo += [items[0:1] * mask, items[1:2] * mask, d_my * mask, d_en * mask]
    yc[...] = jnp.concatenate(halo, axis=0).T
    deep = lax.broadcasted_iota(jnp.int32, (NX, NY), 0)
    up = jnp.where(deep == NX - 1, xh[7, 2:3, :] * mxh, pltpu.roll(zr[1], NX - 1, 0))
    down = jnp.where(deep == 0, xl[7, 2:3, :] * mxl, pltpu.roll(zr[1], 1, 0))
    d_en = HALF_T * (up - down) * zr[5]
    za = dyn_layer(face_layer(first, 0))
    d_mz = (
        zr[2]
        + jnp.where(first, -HALF_T, HALF_T) * (lam_ref[0, za, :] + lam_ref[1, za, :] * zr[3])
        - d_en * zr[4]
    )
    for k, value in ((0, d_mz), (1, d_en)):
        gz[k, layer(0), :] = value * mzl
        gz[k, layer(NZ + 1), :] = value * mzh
    for z in range(NZ):
        r, mx, my, mz, en = [u_ref[k, layer(z), :] for k in range(5)]
        gamma = g_ref[layer(z), :]
        inv = 1.0 / (1.0 + r)
        ux, uy, uz = mx * inv, my * inv, mz * inv
        heat = en - 0.5 * (mx * ux + my * uy + mz * uz)
        lr, lm = lam_ref[0, layer(z), :], lam_ref[1, layer(z), :]
        lr_x = [lx[0, pl.ds(24 * z + s, 8), :] for s in (7, 9)]
        lm_x = [lx[1, pl.ds(24 * z + s, 8), :] for s in (7, 9)]
        lr_z = [lz[0, layer(z + s), :] for s in (0, 2)]
        lm_z = [lz[1, layer(z + s), :] for s in (0, 2)]
        lr_y = [y_prev(lr, yc[layer(z), 0:1], lane), y_next(lr, yc[layer(z), 4:5], lane)]
        lm_y = [y_prev(lm, yc[layer(z), 1:2], lane), y_next(lm, yc[layer(z), 5:6], lane)]
        phi_x0 = HALF_T * (lr_x[1] - lr_x[0])
        phi_y0 = HALF_T * (lr_y[1] - lr_y[0])
        phi_z0 = HALF_T * (lr_z[1] - lr_z[0])
        phi_x1 = px[layer(z), :]
        phi_y1 = HALF_T * (lm_y[1] - lm_y[0])
        phi_z1 = HALF_T * (lm_z[1] - lm_z[0])
        near = (lm_x[0] + lm_x[1]) + (lm_y[0] + lm_y[1]) + (lm_z[0] + lm_z[1])
        d_speed = phi_x1 * mx + 0.5 * (dx[pl.ds(24 * z + 7, 8), :] - dx[pl.ds(24 * z + 9, 8), :])
        d_en = phi_x1 * gamma
        gx[0, pl.ds(24 * z + 8, 8), :] = (
            STAY * lm
            + NEAR * near
            + phi_x0
            + (phi_x1 - d_en) * ux
            + phi_y1 * uy
            + phi_z1 * uz
            + d_speed * inv
        )
        gx[1, pl.ds(24 * z + 8, 8), :] = d_en
        gy[layer(z), :] = phi_y0 - d_en * uy + phi_y1 * ux
        gz[0, layer(z + 1), :] = phi_z0 - d_en * uz + phi_z1 * ux
        gz[1, layer(z + 1), :] = d_en
        dg[layer(z), :] = phi_x1 * heat
    acc = jnp.zeros((NX, NY), F32)
    for z in range(NZ):
        r, mx, my, mz, en = [u0_ref[k, layer(z), :] for k in range(5)]
        inv = 1.0 / (1.0 + r)
        ux, uy, uz = mx * inv, my * inv, mz * inv
        heat = en - 0.5 * (mx * ux + my * uy + mz * uz)
        dif_x = [gx[k, pl.ds(24 * z + 9, 8), :] - gx[k, pl.ds(24 * z + 7, 8), :] for k in range(2)]
        dif_z = [gz[k, layer(z + 2), :] - gz[k, layer(z), :] for k in range(2)]
        dif_y = []
        for k, own in ((0, gy[layer(z), :]), (1, gz[1, layer(z + 1), :])):
            dif_y.append(
                y_next(own, yc[layer(z), 6 + k : 7 + k], lane) - y_prev(own, yc[layer(z), 2 + k : 3 + k], lane)
            )
        d_press = HALF_T * (
            (dif_x[0] + ux * dif_x[1]) + (dif_y[0] + uy * dif_y[1]) + (dif_z[0] + uz * dif_z[1])
        )
        grad = dg[layer(z), :] + d_press * heat
        grad_ref[layer(z), :] = grad
        acc = acc + grad * grad
    total = jnp.sum(jnp.sum(acc, axis=0, keepdims=True), axis=1, keepdims=True)
    miss = jnp.sum(jnp.sum(mis_ref[...], axis=0, keepdims=True), axis=1, keepdims=True)
    miss = miss + jnp.sum(v_ref[...], axis=1, keepdims=True)
    row = jnp.where(lane == 0, total, jnp.where(lane == 1, miss, 0.0))
    for i in range(row_ref.shape[0] // NX):
        row_ref[layer(i), :] = row


def scale_kernel(devices, count, grad_ref, rows_ref, out_ref, misfit_ref):
    acc = rows_ref[layer(0), :]
    for i in range(1, devices // NX):
        acc = acc + rows_ref[layer(i), :]
    row = jnp.sum(acc, axis=0, keepdims=True)
    misfit_ref[0, 0] = row[0, 1] / (devices * count)
    scale = 1.0 / jnp.sqrt(row[0:1, 0:1] / (devices * CELLS * NY) + small_eps)
    out_ref[...] = grad_ref[...] * scale


def split3(value):
    hi = value.astype(jnp.bfloat16)
    rest = value - hi.astype(F32)
    mid = rest.astype(jnp.bfloat16)
    low = (rest - mid.astype(F32)).astype(jnp.bfloat16)
    return hi, mid, low


def probe_kernel(p_ref, o_ref, n_ref, m_ref, v_ref):
    count = p_ref.shape[1]
    probes, obs = p_ref[...], o_ref[...]
    row = lax.broadcasted_iota(jnp.int32, (CELLS, count), 0)
    on_a = row == lax.shift_right_logical(probes, 7)
    on_b = row == lax.bitwise_and(probes, NY - 1)
    one_a = jnp.where(on_a, 1.0, 0.0).astype(jnp.bfloat16)
    one_b = jnp.where(on_b, 1.0, 0.0).astype(jnp.bfloat16)

    def nt(a, b):
        return lax.dot_general(a, b, (((1,), (1,)), ((), ())), preferred_element_type=F32)

    parts = [jnp.where(on_a, part.astype(F32), 0.0).astype(jnp.bfloat16) for part in split3(obs)]
    hits = nt(one_a, one_b)
    sums = nt(parts[0], one_b) + (nt(parts[1], one_b) + nt(parts[2], one_b))
    n_ref[...] = hits
    mean = sums / jnp.maximum(hits, 1.0)
    m_ref[...] = mean
    mean_t = split3(mean.T)
    picked = sum(jnp.dot(part, one_a, preferred_element_type=F32) for part in reversed(mean_t))
    at_probe = jnp.sum(jnp.where(on_b, picked, 0.0), axis=0, keepdims=True)
    off = obs - at_probe
    v_ref[...] = off * off


SMALL = pltpu.CompilerParams(vmem_limit_bytes=12 * 1024 * 1024)


def rows_of(*shape):
    return jax.ShapeDtypeStruct(shape, F32)


def vmem(*shape):
    return pltpu.VMEM(shape, F32)


def call(kernel, outs, scratch, params=SMALL):
    return pl.pallas_call(
        kernel,
        out_shape=outs,
        scratch_shapes=scratch,
        cost_estimate=pl.CostEstimate(flops=100000, bytes_accessed=100000, transcendentals=0),
        compiler_params=params,
    )


def ring(sizes, axis, step):
    n = sizes[axis]
    return [(i, (i + step) % n) for i in range(n)]


def exchange_x(sizes, xlo, xhi):
    return (
        lax.ppermute(xhi, "gx", ring(sizes, "gx", 1)),
        lax.ppermute(xlo, "gx", ring(sizes, "gx", -1)),
    )


def exchange_yz(sizes, ylo, yhi, zs):
    zr = lax.ppermute(zs, "gz", ring(sizes, "gz", 1))
    yl = lax.ppermute(yhi, "gy", ring(sizes, "gy", 1))
    yh = lax.ppermute(ylo, "gy", ring(sizes, "gy", -1))
    return yl, yh, zr


def local(sizes, checkpoint, gruneisen, switch, probes, observed):
    bind = functools.partial
    state = checkpoint.reshape(5, CELLS, NY)
    gamma = gruneisen.reshape(CELLS, NY)
    sw = switch.reshape(2, CELLS, NY)
    plane = rows_of(8, NY)

    def x_slabs(items):
        return [rows_of(items, NZ, NY)] * 2

    pair = rows_of(16, NY)
    tall = (NZ + 2) * NX
    sent = call(bind(prep_kernel, sizes), [pair, pair, rows_of(11, NX, NY)], [vmem(CELLS, NY)], None)(state, gamma, sw)
    got_yz = exchange_yz(sizes, *sent)
    hits, mean, spread = call(
        probe_kernel,
        [rows_of(CELLS, NY), rows_of(CELLS, NY), rows_of(1, probes.shape[0])],
        [],
    )(probes.reshape(1, -1), observed.reshape(1, -1))
    part, xlo, xhi, zz = call(
        bind(side_kernel, sizes),
        [rows_of(5, CELLS, NY)] + x_slabs(18) + [pair],
        [
            vmem(CELLS, NY), vmem(tall, NY), vmem(CELLS, NY),
            vmem(5, tall, NY), vmem(5, tall, NY), vmem(16, NY), vmem(CELLS, 16),
        ],
    )(state, gamma, sw, *sent[:2], *got_yz)
    got_x = exchange_x(sizes, xlo, xhi)
    zz = lax.ppermute(zz, "gz", ring(sizes, "gz", 1))
    state_1, lam_2, coef, coef_halo, mis, *sent, yown = call(
        bind(forward_kernel, sizes),
        [rows_of(5, CELLS, NY), rows_of(2, CELLS, NY), rows_of(CELLS, NY), rows_of(2, NZ, NY), plane]
        + [plane, plane, rows_of(6, NX, NY), plane],
        [
            vmem(5, NZ, NY), vmem(5, NZ, NY), vmem(8, NY), vmem(8, NY), vmem(2, NX, NY),
            vmem(NZ * 24, NY), vmem(5, NZ * 16, NY), vmem(5, NZ * 16, NY), vmem(2, tall, NY), vmem(2, tall, NY),
            vmem(2, CELLS, NY), vmem(CELLS, 8), vmem(CELLS, NY), vmem(CELLS, 8),
        ],
    )(state, gamma, sw, part, *sent[:2], *got_yz, *got_x, zz, hits, mean)
    got_yz = exchange_yz(sizes, *sent)
    sent = call(bind(edge_kernel, sizes), x_slabs(8), [vmem(CELLS, NY)])(state_1, gamma, lam_2, coef, *got_yz)
    got_x = exchange_x(sizes, *sent)
    devices = sizes["gx"] * sizes["gy"] * sizes["gz"]
    gradient, rows = call(
        bind(gradient_kernel, sizes),
        [rows_of(CELLS, NY), rows_of(devices, NY)],
        [
            vmem(2, NZ * 24, NY), vmem(2, tall, NY), vmem(CELLS, NY), vmem(NZ * 24, NY), vmem(CELLS, NY),
            vmem(CELLS, 8), vmem(2, NZ * 24, NY), vmem(CELLS, NY), vmem(2, tall, NY),
        ],
    )(state, state_1, gamma, lam_2, coef, coef_halo, yown, *got_yz, *got_x, mis, spread)
    rows = lax.all_to_all(rows, ("gx", "gy", "gz"), 0, 0, tiled=True)
    direction, misfit = pl.pallas_call(
        bind(scale_kernel, devices, probes.shape[0]),
        out_shape=[rows_of(CELLS, NY), rows_of(1, 1)],
        out_specs=[pl.BlockSpec(memory_space=pltpu.VMEM), pl.BlockSpec(memory_space=pltpu.SMEM)],
        compiler_params=SMALL,
    )(gradient, rows)
    return direction.reshape(NZ, NX, NY), misfit.reshape(())


def solution(mesh):
    block = P("gz", "gx", "gy")
    parted = P(None, "gz", "gx", "gy")
    listed = P(("gx", "gy", "gz"))
    return jax.shard_map(
        functools.partial(local, dict(mesh.shape)),
        mesh=mesh,
        in_specs=(parted, block, parted, listed, listed),
        out_specs=(block, P()),
        check_vma=False,
    )
```

```python
import functools
import jax
import jax.numpy as jnp
from jax import lax
from jax.experimental import pallas as pl
from jax.experimental.pallas import tpu as pltpu
from jax.sharding import PartitionSpec as P

NZ, NX, NY = 16, 8, 128
CELLS = NZ * NX
bulk_modulus = 2.0
slope_coeff = 1.5
signal_speed = 2.5
time_ratio = 0.1
quad_viscosity = 4.0
small_eps = 1e-12
HALF_C = 0.5 * signal_speed
HALF_T = 0.5 * time_ratio
NEAR = time_ratio * HALF_C
STAY = 1.0 - 3.0 * time_ratio * signal_speed
F32 = jnp.float32


def primitives(r, mx, my, mz, en, gamma):
    inv = 1.0 / (1.0 + r)
    ux, uy, uz = mx * inv, my * inv, mz * inv
    heat = en - 0.5 * (mx * ux + my * uy + mz * uz)
    press = bulk_modulus * (r + slope_coeff * r * r) + gamma * heat
    return ux, uy, uz, heat, press


def total_pressure(press, sw, r, slope):
    squeeze = jnp.minimum(slope, 0.0)
    return press + sw * quad_viscosity * (1.0 + r) * squeeze * squeeze


def flux(state, axis, speed, total):
    rows = [state[1 + axis]] + [state[1 + k] * speed for k in range(3)]
    rows[1 + axis] = rows[1 + axis] + total
    return rows + [(state[4] + total) * speed]


def upper_part(f, u):
    return 0.5 * f - HALF_C * u


def lower_part(f, u):
    return 0.5 * f + HALF_C * u


def layer(z):
    return pl.ds(NX * z, NX)


def x_row(x):
    return pl.ds(x, NZ, stride=NX)


def lanes():
    return lax.broadcasted_iota(jnp.int32, (NX, NY), 1)


def y_next(value, column, lane):
    return jnp.where(lane == NY - 1, column, pltpu.roll(value, NY - 1, 1))


def y_prev(value, column, lane):
    return jnp.where(lane == 0, column, pltpu.roll(value, 1, 1))


def inside(flag):
    return jnp.where(flag, 1.0, 0.0).astype(F32)


def masks(mesh):
    ix, iy, iz = lax.axis_index("gx"), lax.axis_index("gy"), lax.axis_index("gz")
    return (
        (inside(ix > 0), inside(ix < mesh["gx"] - 1)),
        (inside(iy > 0), inside(iy < mesh["gy"] - 1)),
        (inside(iz > 0), inside(iz < mesh["gz"] - 1)),
        iz == 0,
    )


def face_layer(is_first, depth):
    return jnp.where(is_first, NZ - 1 - depth, depth)


def dyn_layer(z):
    return pl.ds(pl.multiple_of(NX * z, NX), NX)


def pack_edges(values, lane, depth=2):
    out = pltpu.roll(values[0], depth, 1)
    for i in range(1, len(values)):
        out = jnp.where(lane < 2 * depth * i, out, pltpu.roll(values[i], depth * (2 * i + 1), 1))
    return out


def begun(u, f, far, sign):
    return STAY * u + time_ratio * (sign * 0.5 * f + HALF_C * far)


def prep_kernel(mesh, u_ref, g_ref, s_ref, ylo, yhi, zs, yp):
    _, _, _, first = masks(mesh)
    lane = lanes()
    for z in range(NZ):
        vals = [u_ref[k, layer(z), :] for k in range(5)]
        vals += [g_ref[layer(z), :], s_ref[0, layer(z), :].astype(F32)]
        yp[layer(z), :] = pack_edges(vals, lane, 3)
    rows = yp[...].T
    for out, c1, c2, c3, sign in ((yhi, 2, 1, 0, 1.0), (ylo, 3, 4, 5, -1.0)):
        st, st2, st3 = [[rows[6 * k + c : 6 * k + c + 1] for k in range(7)] for c in (c1, c2, c3)]
        prim, prim2 = primitives(*st[:6]), primitives(*st2[:6])
        slope = (sign * 0.5) * (prim[1] - st3[2] / (1.0 + st3[0]))
        fl = flux(st2[:5], 1, prim2[1], total_pressure(prim2[4], st2[6], st2[0], slope))
        items = st[:5] + [prim[4], st[6], prim2[1]] + [begun(st[k], fl[k], st2[k], sign) for k in range(3)]
        for k in range(11):
            out[k : k + 1] = items[k]
        out[11:16] = jnp.zeros((5, NY), F32)
    za, zb, zc = [dyn_layer(face_layer(first, d)) for d in range(3)]
    sign = jnp.where(first, 1.0, -1.0)
    st, st2 = [[u_ref[k, at, :] for k in range(5)] for at in (za, zb)]
    prim, prim2 = primitives(*st, g_ref[za, :]), primitives(*st2, g_ref[zb, :])
    slope = (sign * 0.5) * (prim[2] - u_ref[3, zc, :] / (1.0 + u_ref[0, zc, :]))
    fl = flux(st2, 2, prim2[2], total_pressure(prim2[4], s_ref[0, zb, :].astype(F32), st2[0], slope))
    items = st + [prim[4], s_ref[0, za, :].astype(F32), prim2[2]]
    items += [begun(st[k], fl[k], st2[k], sign) for k in (0, 1, 3)]
    for k in range(11):
        zs[k] = items[k]


def side_kernel(
    mesh, u_ref, g_ref, s_ref, ylo, yhi, yl, yh, zr,
    part, xlo, xhi, zz,
    vy, vz, pr, az, bz, yr, yc,
):
    _, (myl, myh), (mzl, mzh), first = masks(mesh)
    lane = lanes()
    for z in range(NZ):
        _, uy, uz, _, press = primitives(*[u_ref[k, layer(z), :] for k in range(5)], g_ref[layer(z), :])
        vy[layer(z), :] = uy
        vz[layer(z + 1), :] = uz
        pr[layer(z), :] = press
    far = [zr[k] for k in range(8)]
    speed = far[3] / (1.0 + far[0])
    own = vz[dyn_layer(face_layer(first, 0) + 1), :]
    slope = (far[7] - own) * jnp.where(first, 0.5, -0.5)
    fl = flux(far[:5], 2, speed, total_pressure(far[5], far[6], far[0], slope))
    for k in range(5):
        bz[k, layer(0), :] = lower_part(fl[k], far[k]) * mzl
        az[k, layer(NZ), :] = upper_part(fl[k], far[k]) * mzh
    vz[layer(0), :] = speed * mzl
    vz[layer(NZ + 1), :] = speed * mzh
    low = [yl[k : k + 1] * myl for k in range(8)]
    high = [yh[k : k + 1] * myh for k in range(8)]
    speed = low[2] / (1.0 + low[0])
    yr[10:11, :] = speed
    slope = 0.5 * (ylo[2:3] / (1.0 + ylo[0:1]) - low[7])
    fl = flux(low[:5], 1, speed, total_pressure(low[5], low[6], low[0], slope))
    for k in range(5):
        yr[k : k + 1, :] = lower_part(fl[k], low[k])
    speed = high[2] / (1.0 + high[0])
    yr[11:12, :] = speed
    slope = 0.5 * (high[7] - yhi[2:3] / (1.0 + yhi[0:1]))
    fl = flux(high[:5], 1, speed, total_pressure(high[5], high[6], high[0], slope))
    for k in range(5):
        yr[5 + k : 6 + k, :] = upper_part(fl[k], high[k])
    yr[12:16, :] = jnp.zeros((4, NY), F32)
    yc[...] = yr[...].T
    for z in range(NZ):
        st = [u_ref[k, layer(z), :] for k in range(5)]
        press = pr[layer(z), :]
        visc = s_ref[0, layer(z), :].astype(F32) * quad_viscosity * (1.0 + st[0])
        uy, uz = vy[layer(z), :], vz[layer(z + 1), :]

        def col(i):
            return yc[layer(z), i : i + 1]

        def total(up, down):
            squeeze = jnp.minimum(0.5 * (up - down), 0.0)
            return press + visc * squeeze * squeeze

        fy = flux(st, 1, uy, total(y_next(uy, col(11), lane), y_prev(uy, col(10), lane)))
        fz = flux(st, 2, uz, total(vz[layer(z + 2), :], vz[layer(z), :]))
        for k in range(5):
            az[k, layer(z), :] = upper_part(fz[k], st[k])
            bz[k, layer(z + 1), :] = lower_part(fz[k], st[k])
            part[k, layer(z), :] = STAY * st[k] - time_ratio * (
                y_next(upper_part(fy[k], st[k]), col(5 + k), lane)
                - y_prev(lower_part(fy[k], st[k]), col(k), lane)
            )
    for z in range(NZ):
        for k in range(5):
            part[k, layer(z), :] = part[k, layer(z), :] - time_ratio * (
                az[k, layer(z + 1), :] - bz[k, layer(z), :]
            )
    for k in range(8):
        zz[k : k + 1, :] = low[k]
        zz[8 + k : 9 + k, :] = high[k]
    for out, e, i, j, sign in ((xhi, NX - 1, NX - 2, NX - 3, 1.0), (xlo, 0, 1, 2, -1.0)):
        st, st1, st2 = [[u_ref[k, x_row(at), :] for k in range(5)] for at in (e, i, j)]
        ux = st[1] / (1.0 + st[0])
        prim1, prim2 = primitives(*st1, g_ref[x_row(i), :]), primitives(*st2, g_ref[x_row(j), :])
        last = j - 1 if sign > 0 else j + 1
        ux3 = u_ref[1, x_row(last), :] / (1.0 + u_ref[0, x_row(last), :])
        slope1, slope2 = (sign * 0.5) * (ux - prim2[0]), (sign * 0.5) * (prim1[0] - ux3)
        f1 = flux(st1, 0, prim1[0], total_pressure(prim1[4], s_ref[0, x_row(i), :].astype(F32), st1[0], slope1))
        f2 = flux(st2, 0, prim2[0], total_pressure(prim2[4], s_ref[0, x_row(j), :].astype(F32), st2[0], slope2))
        for k in range(5):
            out[k] = st[k]
        out[5] = g_ref[x_row(e), :]
        out[6] = s_ref[0, x_row(e), :].astype(F32)
        out[7] = prim1[0]
        out[8] = s_ref[1, x_row(e), :].astype(F32)
        for k in range(5):
            out[9 + k] = part[k, x_row(e), :] + time_ratio * (sign * 0.5 * f1[k] + HALF_C * st1[k])
        for k in range(2):
            out[14 + k] = part[k, x_row(i), :] + time_ratio * (sign * 0.5 * f2[k] + HALF_C * st2[k])
        out[16] = zz[...]
        for k in range(8):
            out[17, k : k + 1, :] = zr[k, e : e + 1, :]
        out[17, 8:9, :] = zr[1, i : i + 1, :] / (1.0 + zr[0, i : i + 1, :])
        out[17, 9:16, :] = jnp.zeros((7, NY), F32)


def shifted_x(own, low, high, at_x):
    up = jnp.where(at_x == NX - 1, pltpu.roll(high, NX - 1, 1), pltpu.roll(own, NY - 1, 1))
    down = jnp.where(at_x == 0, pltpu.roll(low, NY - NX + 1, 1), pltpu.roll(own, 1, 1))
    return up, down


def halo_step(
    mesh, u_ref, g_ref, s_ref, part, ylo, yhi, yl, yh, zr, xl, xh, zz,
    o_ref, xc, hxl, hxh, hyl, hyh, hz, vx, ax, bx, zc,
):
    (mxl, mxh), (myl, myh), (mzl, mzh), first = masks(mesh)
    for z in range(NZ):
        vx[pl.ds(24 * z + 8, 8), :] = u_ref[1, layer(z), :] / (1.0 + u_ref[0, layer(z), :])
    low = [xl[k] * mxl for k in range(8)]
    high = [xh[k] * mxh for k in range(8)]
    prim = primitives(*low[:6])
    vx[pl.ds(7, NZ, stride=24), :] = prim[0]
    slope = 0.5 * (vx[pl.ds(8, NZ, stride=24), :] - low[7])
    f_low = flux(low[:5], 0, prim[0], total_pressure(prim[4], low[6], low[0], slope))
    prim = primitives(*high[:6])
    vx[pl.ds(16, NZ, stride=24), :] = prim[0]
    slope = 0.5 * (high[7] - vx[pl.ds(15, NZ, stride=24), :])
    f_high = flux(high[:5], 0, prim[0], total_pressure(prim[4], high[6], high[0], slope))
    for k in range(5):
        bx[k, pl.ds(7, NZ, stride=16), :] = lower_part(f_low[k], low[k])
        ax[k, pl.ds(8, NZ, stride=16), :] = upper_part(f_high[k], high[k])
    for z in range(NZ):
        st = [u_ref[k, layer(z), :] for k in range(5)]
        ux, _, _, _, press = primitives(*st, g_ref[layer(z), :])
        slope = 0.5 * (vx[pl.ds(24 * z + 9, 8), :] - vx[pl.ds(24 * z + 7, 8), :])
        fx = flux(st, 0, ux, total_pressure(press, s_ref[0, layer(z), :].astype(F32), st[0], slope))
        for k in range(5):
            ax[k, pl.ds(16 * z, 8), :] = upper_part(fx[k], st[k])
            bx[k, pl.ds(16 * z + 8, 8), :] = lower_part(fx[k], st[k])
    for z in range(NZ):
        for k in range(5):
            o_ref[k, layer(z), :] = part[k, layer(z), :] - time_ratio * (
                ax[k, pl.ds(16 * z + 1, 8), :] - bx[k, pl.ds(16 * z + 7, 8), :]
            )
    for out, ref, mask in ((hxl, xl, mxl), (hxh, xh, mxh)):
        if ref is xl:
            near = [-ax[k, pl.ds(0, NZ, stride=16), :] for k in range(5)]
            next_ = [-upper_part(f_low[k], low[k]) for k in range(2)]
        else:
            near = [bx[k, pl.ds(15, NZ, stride=16), :] for k in range(5)]
            next_ = [lower_part(f_high[k], high[k]) for k in range(2)]
        st = [(ref[9 + k] + time_ratio * near[k]) * mask for k in range(5)]
        st2 = [(ref[14 + k] + time_ratio * next_[k]) * mask for k in range(2)]
        out[0] = st[0]
        out[1] = st[1]
        out[2] = primitives(*st, ref[5] * mask)[4]
        out[3] = ref[8] * mask
        out[4] = st2[1] / (1.0 + st2[0])
        base = 0 if ref is xl else 3
        inv, gamma = 1.0 / (1.0 + st[0]), ref[5] * mask
        xc[base] = (2.0 - gamma) * (st[1] * inv)
        xc[base + 1] = inv
        xc[base + 2] = gamma
    lane = lax.broadcasted_iota(jnp.int32, (1, NY), 1)
    at_x = lax.bitwise_and(lane, NX - 1)
    for side, ref, mask, own, out, sign in ((0, yl, myl, ylo, hyl, -1.0), (1, yh, myh, yhi, hyh, 1.0)):

        def items(values, m):
            return [values[k : k + 1] * m for k in range(8)]

        here = items(ref, mask)
        near_l, near_h = items(xl[16, 8 * side : 8 * side + 8, :], mxl), items(xh[16, 8 * side : 8 * side + 8, :], mxh)
        ux, ux_l, ux_h = [v[1] / (1.0 + v[0]) for v in (here, near_l, near_h)]
        up, down = shifted_x(ux, ux_l, ux_h, at_x)
        slope = 0.5 * (up - down)
        slope_h = 0.5 * (pltpu.roll(ux_h, NY - 1, 1) - pltpu.roll(ux, NY - NX + 1, 1))
        slope_l = 0.5 * (pltpu.roll(ux, NX - 1, 1) - pltpu.roll(ux_l, 1, 1))

        def fx_of(v, speed, slope):
            return [v[1], v[1] * speed + total_pressure(v[5], v[6], v[0], slope), v[2] * speed]

        f_here, f_l, f_h = fx_of(here, ux, slope), fx_of(near_l, ux_l, slope_l), fx_of(near_h, ux_h, slope_h)
        uz = here[3] / (1.0 + here[0])
        near_z = items(zz[8 * side : 8 * side + 8, :], 1.0)
        uz_z = near_z[3] / (1.0 + near_z[0])
        fz, fz_z = [[v[3], v[1] * w, v[2] * w] for v, w in ((here, uz), (near_z, uz_z))]
        self_ = items(own, 1.0)
        uy = self_[2] / (1.0 + self_[0])
        uy_here = here[2] / (1.0 + here[0])
        slope = 0.5 * (self_[7] - uy_here if side == 0 else uy_here - self_[7])
        fy = [self_[2], self_[1] * uy, self_[2] * uy + total_pressure(self_[5], self_[6], self_[0], slope)]
        new = []
        for k in range(3):
            a_x, _ = shifted_x(upper_part(f_here[k], here[k]), ux_l, upper_part(f_h[k], near_h[k]), at_x)
            _, b_x = shifted_x(lower_part(f_here[k], here[k]), lower_part(f_l[k], near_l[k]), ux_h, at_x)
            a_z = jnp.where(
                lane >= NY - NX,
                pltpu.roll(upper_part(fz_z[k], near_z[k]), NY - NX, 1) * mzh,
                pltpu.roll(upper_part(fz[k], here[k]), NY - NX, 1),
            )
            b_z = jnp.where(
                lane < NX,
                pltpu.roll(lower_part(fz_z[k], near_z[k]), NX, 1) * mzl,
                pltpu.roll(lower_part(fz[k], here[k]), NX, 1),
            )
            facing = sign * 0.5 * fy[k] + HALF_C * self_[k]
            new.append(mask * (ref[8 + k : 9 + k] + time_ratio * (facing - (a_x - b_x) - (a_z - b_z))))
        r, mx, my = new
        combine = lower_part if side == 0 else upper_part
        out[0:1, :] = combine(my, r)
        out[1:2, :] = combine(mx * (my / (1.0 + r)), mx)
        out[2:8, :] = jnp.zeros((6, NY), F32)
    rows = []
    for side in range(2):
        v = [zz[8 * side + k : 8 * side + k + 1, :] for k in range(8)]
        speed = v[2] / (1.0 + v[0])
        fy = [v[2], v[1] * speed, v[3] * speed]
        combine = upper_part if side else lower_part
        rows += [combine(f, v[k]) for f, k in zip(fy, (0, 1, 3))]
    zc[...] = jnp.concatenate(rows + [jnp.zeros((2, NY), F32)], axis=0).T
    cols = zc[dyn_layer(jnp.where(first, 0, NZ - 1)), :]
    full = lanes()
    deep = lax.broadcasted_iota(jnp.int32, (NX, NY), 0)
    here = [zr[k] for k in range(8)]
    near_l = [xl[17, k : k + 1, :] * mxl for k in range(9)]
    near_h = [xh[17, k : k + 1, :] * mxh for k in range(9)]
    ux, ux_l, ux_h = [v[1] / (1.0 + v[0]) for v in (here, near_l, near_h)]

    def next_x(value, row):
        return jnp.where(deep == NX - 1, row, pltpu.roll(value, NX - 1, 0))

    def prev_x(value, row):
        return jnp.where(deep == 0, row, pltpu.roll(value, 1, 0))

    slope = 0.5 * (next_x(ux, ux_h) - prev_x(ux, ux_l))
    slope_h = 0.5 * (near_h[8] - ux[NX - 1 : NX])
    slope_l = 0.5 * (ux[0:1] - near_l[8])

    def fx_layer(v, speed, slope):
        return [v[1], v[1] * speed + total_pressure(v[5], v[6], v[0], slope), v[3] * speed]

    f_here, f_l, f_h = fx_layer(here, ux, slope), fx_layer(near_l, ux_l, slope_l), fx_layer(near_h, ux_h, slope_h)
    uy = here[2] / (1.0 + here[0])
    fy = [here[2], here[1] * uy, here[3] * uy]
    za, zb = dyn_layer(face_layer(first, 0)), dyn_layer(face_layer(first, 1))
    sign = jnp.where(first, 1.0, -1.0)
    st = [u_ref[k, za, :] for k in range(5)]
    prim = primitives(*st, g_ref[za, :])
    uz_b = u_ref[3, zb, :] / (1.0 + u_ref[0, zb, :])
    slope = (sign * 0.5) * (here[3] / (1.0 + here[0]) - uz_b)
    fz = flux(st, 2, prim[2], total_pressure(prim[4], s_ref[0, za, :].astype(F32), st[0], slope))
    new = []
    for n, k in enumerate((0, 1, 3)):
        a_x = next_x(upper_part(f_here[n], here[k]), upper_part(f_h[n], near_h[k]))
        b_x = prev_x(lower_part(f_here[n], here[k]), lower_part(f_l[n], near_l[k]))
        a_y = y_next(upper_part(fy[n], here[k]), cols[:, 3 + n : 4 + n], full)
        b_y = y_prev(lower_part(fy[n], here[k]), cols[:, n : n + 1], full)
        facing = sign * 0.5 * fz[k] + HALF_C * st[k]
        new.append(zr[8 + n] + time_ratio * (facing - (a_x - b_x) - (a_y - b_y)))
    r, mx, mz = new
    hz[0] = 0.5 * mz - (sign * HALF_C) * r
    hz[1] = 0.5 * mx * (mz / (1.0 + r)) - (sign * HALF_C) * mx


def forward_kernel(
    mesh, u0_ref, g_ref, s_ref, part, ylo_in, yhi_in, yl, yh, zr, xl, xh, zz, n_ref, m_ref,
    u_ref, lam_ref, cf_ref, cfh_ref, mis_ref, xc, ylo, yhi, zs, yown,
    hxl, hxh, hyl, hyh, hz, vx, ax, bx, az, bz, ch, yc, yp, zc,
):
    halo_step(
        mesh, u0_ref, g_ref, s_ref, part, ylo_in, yhi_in, yl, yh, zr, xl, xh, zz,
        u_ref, xc, hxl, hxh, hyl, hyh, hz, vx, ax, bx, zc,
    )
    speed_kernel(
        mesh, u_ref, g_ref, s_ref, hxl, hxh, hyl, hyh, hz, n_ref, m_ref,
        lam_ref, cf_ref, cfh_ref, mis_ref, ylo, yhi, zs, yown,
        vx, ax, bx, az, bz, ch, yc, yp,
    )


def columns_of(low, high, count, low_mask, high_mask):
    rows = [low[k : k + 1] * low_mask for k in range(count)]
    rows += [high[k : k + 1] * high_mask for k in range(count)]
    rows.append(jnp.zeros((8 - 2 * count, NY), F32))
    return jnp.concatenate(rows, axis=0).T


def speed_kernel(
    mesh, u_ref, g_ref, s_ref, xl, xh, yl, yh, zr, n_ref, m_ref,
    lam_ref, cf_ref, cfh_ref, mis_ref, ylo, yhi, zs, yown,
    vx, ax, bx, az, bz, ch, yc, yp,
):
    (mxl, mxh), (myl, myh), (mzl, mzh), first = masks(mesh)
    lane = lanes()
    for z in range(NZ):
        vx[pl.ds(24 * z + 8, 8), :] = u_ref[1, layer(z), :] / (1.0 + u_ref[0, layer(z), :])
    for side, ref, mask in ((0, xl, mxl), (1, xh, mxh)):
        r, mx, press, sw, second = [ref[k] * mask for k in range(5)]
        speed = mx / (1.0 + r)
        vx[pl.ds(16 if side else 7, NZ, stride=24), :] = speed
        own = vx[pl.ds(15 if side else 8, NZ, stride=24), :]
        slope = 0.5 * (second - own if side else own - second)
        squeeze = jnp.minimum(slope, 0.0)
        visc = sw * quad_viscosity * (1.0 + r) * squeeze
        cfh_ref[side] = 2.0 * visc
        f1 = mx * speed + press + visc * squeeze
        if side:
            ax[0, pl.ds(8, NZ, stride=16), :] = upper_part(mx, r)
            ax[1, pl.ds(8, NZ, stride=16), :] = upper_part(f1, mx)
        else:
            bx[0, pl.ds(7, NZ, stride=16), :] = lower_part(mx, r)
            bx[1, pl.ds(7, NZ, stride=16), :] = lower_part(f1, mx)
    for k in range(2):
        bz[k, layer(0), :] = zr[k] * mzl
        az[k, layer(NZ), :] = zr[k] * mzh
    yc[...] = columns_of(yl, yh, 2, myl, myh)
    for z in range(NZ):
        r, mx, my, mz, en = [u_ref[k, layer(z), :] for k in range(5)]
        ux, uy, uz, _, press = primitives(r, mx, my, mz, en, g_ref[layer(z), :])
        squeeze = jnp.minimum(0.5 * (vx[pl.ds(24 * z + 9, 8), :] - vx[pl.ds(24 * z + 7, 8), :]), 0.0)
        visc = s_ref[1, layer(z), :].astype(F32) * quad_viscosity * (1.0 + r) * squeeze
        cf_ref[layer(z), :] = 2.0 * visc
        f1 = mx * ux + press + visc * squeeze
        for k, st, fx, fy, fz in ((0, r, mx, my, mz), (1, mx, f1, mx * uy, mx * uz)):
            ax[k, pl.ds(16 * z, 8), :] = upper_part(fx, st)
            bx[k, pl.ds(16 * z + 8, 8), :] = lower_part(fx, st)
            az[k, layer(z), :] = upper_part(fz, st)
            bz[k, layer(z + 1), :] = lower_part(fz, st)
            ch[k, layer(z), :] = (
                3.0 * signal_speed * st
                + y_next(upper_part(fy, st), yc[layer(z), 2 + k : 3 + k], lane)
                - y_prev(lower_part(fy, st), yc[layer(z), k : k + 1], lane)
            )
    mis = jnp.zeros((NX, NY), F32)
    for z in range(NZ):
        new = []
        for k in range(2):
            change = (
                ch[k, layer(z), :]
                + (ax[k, pl.ds(16 * z + 1, 8), :] - bx[k, pl.ds(16 * z + 7, 8), :])
                + (az[k, layer(z + 1), :] - bz[k, layer(z), :])
            )
            new.append(u_ref[k, layer(z), :] - time_ratio * change)
        inv = 1.0 / (1.0 + new[0])
        speed = new[1] * inv
        off = speed - m_ref[layer(z), :]
        weight = n_ref[layer(z), :] * off
        mis = mis + weight * off
        lam_m = 2.0 * weight * inv
        lam_r = -lam_m * speed
        lam_ref[0, layer(z), :] = lam_r
        lam_ref[1, layer(z), :] = lam_m
        inv = 1.0 / (1.0 + u_ref[0, layer(z), :])
        extra = [u_ref[1, layer(z), :] * inv, u_ref[2, layer(z), :] * inv, g_ref[layer(z), :]]
        yp[layer(z), :] = pack_edges([lam_r, lam_m] + extra, lane)
    mis_ref[...] = mis
    za, zb = dyn_layer(face_layer(first, 0)), dyn_layer(face_layer(first, 1))
    inv = 1.0 / (1.0 + u_ref[0, za, :])
    ux = u_ref[1, za, :] * inv
    zs[0] = lam_ref[0, za, :]
    zs[1] = lam_ref[1, za, :]
    zs[2] = jnp.where(first, -HALF_T, HALF_T) * (lam_ref[0, zb, :] + lam_ref[1, zb, :] * ux)
    zs[3] = ux
    zs[4] = u_ref[3, za, :] * inv
    zs[5] = g_ref[za, :]
    rows = yp[...].T
    for out, edge, second, own, sign in ((yhi, 1, 0, 2, -HALF_T), (ylo, 2, 3, 0, HALF_T)):
        lam_r, lam_m, ux, uy, gamma = [rows[4 * i + edge : 4 * i + edge + 1] for i in range(5)]
        out[0:1] = lam_r
        out[1:2] = lam_m
        out[2:3] = sign * (rows[second : second + 1] + rows[4 + second : 5 + second] * ux)
        out[3:4] = ux
        out[4:5] = uy
        out[5:6] = gamma
        out[6:8] = jnp.zeros((2, NY), F32)
        yown[own : own + 1] = lam_r
        yown[own + 1 : own + 2] = lam_m
    yown[4:8] = jnp.zeros((4, NY), F32)


def edge_kernel(mesh, u_ref, lam_ref, cf_ref, yl, yh, zr, xlo, xhi, yc):
    _, (myl, myh), (mzl, mzh), _ = masks(mesh)
    low_y, high_y = yl[1:2] * myl, yh[1:2] * myh
    yc[:, 0:8] = jnp.concatenate([low_y, high_y, jnp.zeros((6, NY), F32)], axis=0).T
    lane = lax.broadcasted_iota(jnp.int32, (NZ, NY), 1)
    deep = lax.broadcasted_iota(jnp.int32, (NZ, NY), 0)
    for out, e, i, i2, sign in ((xhi, NX - 1, NX - 2, NX - 3, 1.0), (xlo, 0, 1, 2, -1.0)):
        r, my, mz = [u_ref[k, x_row(e), :] for k in (0, 2, 3)]
        inv = 1.0 / (1.0 + r)
        lm, lm_i = lam_ref[1, x_row(e), :], lam_ref[1, x_row(i), :]
        col = yc[x_row(e), :]
        side = zr[1, e : e + 1, :]
        up_y = jnp.where(lane == NY - 1, col[:, 1:2], pltpu.roll(lm, NY - 1, 1))
        down_y = jnp.where(lane == 0, col[:, 0:1], pltpu.roll(lm, 1, 1))
        up_z = jnp.where(deep == NZ - 1, side * mzh, pltpu.roll(lm, NZ - 1, 0))
        down_z = jnp.where(deep == 0, side * mzl, pltpu.roll(lm, 1, 0))
        slope = (sign * HALF_T) * (lm - lam_ref[1, x_row(i2), :]) * cf_ref[x_row(i), :]
        out[0] = lam_ref[0, x_row(e), :]
        out[1] = lm
        out[2] = lm_i
        out[3] = (
            STAY * lm
            + NEAR * (lm_i + (up_y + down_y) + (up_z + down_z))
            - (sign * HALF_T) * lam_ref[0, x_row(i), :]
            + HALF_T * ((up_y - down_y) * (my * inv) + (up_z - down_z) * (mz * inv))
            + (sign * 0.5) * slope * inv
        )
        out[4] = jnp.where(deep == 0, low_y, jnp.where(deep == 1, high_y, jnp.where(deep == 2, side, 0.0)))


def gradient_kernel(
    mesh, u0_ref, u_ref, g_ref, lam_ref, cf_ref, cfh_ref, xc, yown, yl, yh, zr, xl, xh, mis_ref, v_ref,
    grad_ref, row_ref,
    lx, lz, px, dx, dg, yc, gx, gy, gz,
):
    (mxl, mxh), (myl, myh), (mzl, mzh), first = masks(mesh)
    lane = lanes()
    for k in range(2):
        for z in range(NZ):
            lx[k, pl.ds(24 * z + 8, 8), :] = lam_ref[k, layer(z), :]
            lz[k, layer(z + 1), :] = lam_ref[k, layer(z), :]
        lx[k, pl.ds(7, NZ, stride=24), :] = xl[k] * mxl
        lx[k, pl.ds(16, NZ, stride=24), :] = xh[k] * mxh
        lz[k, layer(0), :] = zr[k] * mzl
        lz[k, layer(NZ + 1), :] = zr[k] * mzh
    phi_low = HALF_T * (lam_ref[1, x_row(0), :] - xl[2] * mxl)
    phi_high = HALF_T * (xh[2] * mxh - lam_ref[1, x_row(NX - 1), :])
    dx[pl.ds(7, NZ, stride=24), :] = phi_low * cfh_ref[0]
    dx[pl.ds(16, NZ, stride=24), :] = phi_high * cfh_ref[1]
    for z in range(NZ):
        phi = HALF_T * (lx[1, pl.ds(24 * z + 9, 8), :] - lx[1, pl.ds(24 * z + 7, 8), :])
        px[layer(z), :] = phi
        dx[pl.ds(24 * z + 8, 8), :] = phi * cf_ref[layer(z), :]
    gx[1, pl.ds(7, NZ, stride=24), :] = mxl * phi_low * xc[2]
    gx[1, pl.ds(16, NZ, stride=24), :] = mxh * phi_high * xc[5]
    gx[0, pl.ds(7, NZ, stride=24), :] = mxl * (
        xl[3]
        + HALF_T * lam_ref[0, x_row(0), :]
        + NEAR * lam_ref[1, x_row(0), :]
        + phi_low * xc[0]
        - 0.5 * dx[pl.ds(8, NZ, stride=24), :] * xc[1]
    )
    gx[0, pl.ds(16, NZ, stride=24), :] = mxh * (
        xh[3]
        - HALF_T * lam_ref[0, x_row(NX - 1), :]
        + NEAR * lam_ref[1, x_row(NX - 1), :]
        + phi_high * xc[3]
        + 0.5 * dx[pl.ds(15, NZ, stride=24), :] * xc[4]
    )
    at_x = lax.bitwise_and(lax.broadcasted_iota(jnp.int32, (1, NY), 1), NX - 1)
    from_high, from_low = pltpu.roll(xh[4], NX - 1, 1) * mxh, pltpu.roll(xl[4], NY - NX + 1, 1) * mxl
    halo = []
    for side, ref, mask, sign in ((0, yl, myl, HALF_T), (1, yh, myh, -HALF_T)):
        items = ref[...]
        up = jnp.where(at_x == NX - 1, from_high[side : side + 1], pltpu.roll(items, NY - 1, 1)[1:2])
        down = jnp.where(at_x == 0, from_low[side : side + 1], pltpu.roll(items, 1, 1)[1:2])
        d_en = HALF_T * (up - down) * items[5:6]
        own_r, own_m = yown[2 * side : 2 * side + 1], yown[2 * side + 1 : 2 * side + 2]
        d_my = items[2:3] + sign * (own_r + own_m * items[3:4]) - d_en * items[4:5]
        halo += [items[0:1] * mask, items[1:2] * mask, d_my * mask, d_en * mask]
    yc[...] = jnp.concatenate(halo, axis=0).T
    deep = lax.broadcasted_iota(jnp.int32, (NX, NY), 0)
    up = jnp.where(deep == NX - 1, xh[4, 2:3, :] * mxh, pltpu.roll(zr[1], NX - 1, 0))
    down = jnp.where(deep == 0, xl[4, 2:3, :] * mxl, pltpu.roll(zr[1], 1, 0))
    d_en = HALF_T * (up - down) * zr[5]
    za = dyn_layer(face_layer(first, 0))
    d_mz = (
        zr[2]
        + jnp.where(first, -HALF_T, HALF_T) * (lam_ref[0, za, :] + lam_ref[1, za, :] * zr[3])
        - d_en * zr[4]
    )
    for k, value in ((0, d_mz), (1, d_en)):
        gz[k, layer(0), :] = value * mzl
        gz[k, layer(NZ + 1), :] = value * mzh
    for z in range(NZ):
        r, mx, my, mz, en = [u_ref[k, layer(z), :] for k in range(5)]
        gamma = g_ref[layer(z), :]
        inv = 1.0 / (1.0 + r)
        ux, uy, uz = mx * inv, my * inv, mz * inv
        heat = en - 0.5 * (mx * ux + my * uy + mz * uz)
        lr, lm = lam_ref[0, layer(z), :], lam_ref[1, layer(z), :]
        lr_x = [lx[0, pl.ds(24 * z + s, 8), :] for s in (7, 9)]
        lm_x = [lx[1, pl.ds(24 * z + s, 8), :] for s in (7, 9)]
        lr_z = [lz[0, layer(z + s), :] for s in (0, 2)]
        lm_z = [lz[1, layer(z + s), :] for s in (0, 2)]
        lr_y = [y_prev(lr, yc[layer(z), 0:1], lane), y_next(lr, yc[layer(z), 4:5], lane)]
        lm_y = [y_prev(lm, yc[layer(z), 1:2], lane), y_next(lm, yc[layer(z), 5:6], lane)]
        phi_x0 = HALF_T * (lr_x[1] - lr_x[0])
        phi_y0 = HALF_T * (lr_y[1] - lr_y[0])
        phi_z0 = HALF_T * (lr_z[1] - lr_z[0])
        phi_x1 = px[layer(z), :]
        phi_y1 = HALF_T * (lm_y[1] - lm_y[0])
        phi_z1 = HALF_T * (lm_z[1] - lm_z[0])
        near = (lm_x[0] + lm_x[1]) + (lm_y[0] + lm_y[1]) + (lm_z[0] + lm_z[1])
        d_speed = phi_x1 * mx + 0.5 * (dx[pl.ds(24 * z + 7, 8), :] - dx[pl.ds(24 * z + 9, 8), :])
        d_en = phi_x1 * gamma
        gx[0, pl.ds(24 * z + 8, 8), :] = (
            STAY * lm
            + NEAR * near
            + phi_x0
            + (phi_x1 - d_en) * ux
            + phi_y1 * uy
            + phi_z1 * uz
            + d_speed * inv
        )
        gx[1, pl.ds(24 * z + 8, 8), :] = d_en
        gy[layer(z), :] = phi_y0 - d_en * uy + phi_y1 * ux
        gz[0, layer(z + 1), :] = phi_z0 - d_en * uz + phi_z1 * ux
        gz[1, layer(z + 1), :] = d_en
        dg[layer(z), :] = phi_x1 * heat
    acc = jnp.zeros((NX, NY), F32)
    for z in range(NZ):
        r, mx, my, mz, en = [u0_ref[k, layer(z), :] for k in range(5)]
        inv = 1.0 / (1.0 + r)
        ux, uy, uz = mx * inv, my * inv, mz * inv
        heat = en - 0.5 * (mx * ux + my * uy + mz * uz)
        dif_x = [gx[k, pl.ds(24 * z + 9, 8), :] - gx[k, pl.ds(24 * z + 7, 8), :] for k in range(2)]
        dif_z = [gz[k, layer(z + 2), :] - gz[k, layer(z), :] for k in range(2)]
        dif_y = []
        for k, own in ((0, gy[layer(z), :]), (1, gz[1, layer(z + 1), :])):
            dif_y.append(
                y_next(own, yc[layer(z), 6 + k : 7 + k], lane) - y_prev(own, yc[layer(z), 2 + k : 3 + k], lane)
            )
        d_press = HALF_T * (
            (dif_x[0] + ux * dif_x[1]) + (dif_y[0] + uy * dif_y[1]) + (dif_z[0] + uz * dif_z[1])
        )
        grad = dg[layer(z), :] + d_press * heat
        grad_ref[layer(z), :] = grad
        acc = acc + grad * grad
    total = jnp.sum(jnp.sum(acc, axis=0, keepdims=True), axis=1, keepdims=True)
    miss = jnp.sum(jnp.sum(mis_ref[...], axis=0, keepdims=True), axis=1, keepdims=True)
    miss = miss + jnp.sum(v_ref[...], axis=1, keepdims=True)
    row = jnp.where(lane == 0, total, jnp.where(lane == 1, miss, 0.0))
    for i in range(row_ref.shape[0] // NX):
        row_ref[layer(i), :] = row


def scale_kernel(devices, count, grad_ref, rows_ref, out_ref, misfit_ref):
    acc = rows_ref[layer(0), :]
    for i in range(1, devices // NX):
        acc = acc + rows_ref[layer(i), :]
    row = jnp.sum(acc, axis=0, keepdims=True)
    misfit_ref[0, 0] = row[0, 1] / (devices * count)
    scale = 1.0 / jnp.sqrt(row[0:1, 0:1] / (devices * CELLS * NY) + small_eps)
    out_ref[...] = grad_ref[...] * scale


def split3(value):
    hi = value.astype(jnp.bfloat16)
    rest = value - hi.astype(F32)
    mid = rest.astype(jnp.bfloat16)
    low = (rest - mid.astype(F32)).astype(jnp.bfloat16)
    return hi, mid, low


def probe_kernel(p_ref, o_ref, n_ref, m_ref, v_ref):
    count = p_ref.shape[1]
    probes, obs = p_ref[...], o_ref[...]
    row = lax.broadcasted_iota(jnp.int32, (CELLS, count), 0)
    on_a = row == lax.shift_right_logical(probes, 7)
    on_b = row == lax.bitwise_and(probes, NY - 1)
    one_a = jnp.where(on_a, 1.0, 0.0).astype(jnp.bfloat16)
    one_b = jnp.where(on_b, 1.0, 0.0).astype(jnp.bfloat16)

    def nt(a, b):
        return lax.dot_general(a, b, (((1,), (1,)), ((), ())), preferred_element_type=F32)

    parts = [jnp.where(on_a, part.astype(F32), 0.0).astype(jnp.bfloat16) for part in split3(obs)]
    hits = nt(one_a, one_b)
    sums = nt(parts[0], one_b) + (nt(parts[1], one_b) + nt(parts[2], one_b))
    n_ref[...] = hits
    mean = sums / jnp.maximum(hits, 1.0)
    m_ref[...] = mean
    mean_t = split3(mean.T)
    picked = sum(jnp.dot(part, one_a, preferred_element_type=F32) for part in reversed(mean_t))
    at_probe = jnp.sum(jnp.where(on_b, picked, 0.0), axis=0, keepdims=True)
    off = obs - at_probe
    v_ref[...] = off * off


SMALL = pltpu.CompilerParams(vmem_limit_bytes=12 * 1024 * 1024)

LARGE = pltpu.CompilerParams(vmem_limit_bytes=55168 * 1024)


def rows_of(*shape):
    return jax.ShapeDtypeStruct(shape, F32)


def vmem(*shape):
    return pltpu.VMEM(shape, F32)


def call(kernel, outs, scratch, params=SMALL):
    return pl.pallas_call(
        kernel,
        out_shape=outs,
        scratch_shapes=scratch,
        cost_estimate=pl.CostEstimate(flops=100000, bytes_accessed=100000, transcendentals=0),
        compiler_params=params,
    )


def ring(sizes, axis, step):
    n = sizes[axis]
    return [(i, (i + step) % n) for i in range(n)]


def exchange_x(sizes, xlo, xhi):
    return (
        lax.ppermute(xhi, "gx", ring(sizes, "gx", 1)),
        lax.ppermute(xlo, "gx", ring(sizes, "gx", -1)),
    )


def exchange_z(sizes, zs):
    return lax.ppermute(zs, "gz", ring(sizes, "gz", 1))


def exchange_yz(sizes, ylo, yhi, zs):
    zr = exchange_z(sizes, zs)
    yl = lax.ppermute(yhi, "gy", ring(sizes, "gy", 1))
    yh = lax.ppermute(ylo, "gy", ring(sizes, "gy", -1))
    return yl, yh, zr


def local(sizes, checkpoint, gruneisen, switch, probes, observed):
    bind = functools.partial
    state = checkpoint.reshape(5, CELLS, NY)
    gamma = gruneisen.reshape(CELLS, NY)
    sw = switch.reshape(2, CELLS, NY)
    plane = rows_of(8, NY)

    def x_slabs(items):
        return [rows_of(items, NZ, NY)] * 2

    pair = rows_of(16, NY)
    tall = (NZ + 2) * NX
    *sent_y, sent_z = call(
        bind(prep_kernel, sizes), [pair, pair, rows_of(11, NX, NY)], [vmem(CELLS, NY)], LARGE
    )(state, gamma, sw)
    got_yz = exchange_yz(sizes, *sent_y, sent_z)
    hits, mean, spread = call(
        probe_kernel,
        [rows_of(CELLS, NY), rows_of(CELLS, NY), rows_of(1, probes.shape[0])],
        [],
    )(probes.reshape(1, -1), observed.reshape(1, -1))
    part, xlo, xhi, zz = call(
        bind(side_kernel, sizes),
        [rows_of(5, CELLS, NY)] + x_slabs(18) + [pair],
        [
            vmem(CELLS, NY), vmem(tall, NY), vmem(CELLS, NY),
            vmem(5, tall, NY), vmem(5, tall, NY), vmem(16, NY), vmem(CELLS, 16),
        ],
    )(state, gamma, sw, *sent_y, *got_yz)
    got_x = exchange_x(sizes, xlo, xhi)
    zz = exchange_z(sizes, zz)
    state_1, lam_2, coef, coef_halo, mis, beside, *sent, yown = call(
        bind(forward_kernel, sizes),
        [rows_of(5, CELLS, NY), rows_of(2, CELLS, NY), rows_of(CELLS, NY), rows_of(2, NZ, NY), plane]
        + [rows_of(6, NZ, NY), plane, plane, rows_of(6, NX, NY), plane],
        [
            vmem(5, NZ, NY), vmem(5, NZ, NY), vmem(8, NY), vmem(8, NY), vmem(2, NX, NY),
            vmem(NZ * 24, NY), vmem(5, NZ * 16, NY), vmem(5, NZ * 16, NY), vmem(2, tall, NY), vmem(2, tall, NY),
            vmem(2, CELLS, NY), vmem(CELLS, 8), vmem(CELLS, NY), vmem(CELLS, 8),
        ],
    )(state, gamma, sw, part, *sent_y, *got_yz, *got_x, zz, hits, mean)
    got_yz = exchange_yz(sizes, *sent)
    sent = call(bind(edge_kernel, sizes), x_slabs(5), [vmem(CELLS, NY)])(state_1, lam_2, coef, *got_yz)
    got_x = exchange_x(sizes, *sent)
    devices = sizes["gx"] * sizes["gy"] * sizes["gz"]
    gradient, rows = call(
        bind(gradient_kernel, sizes),
        [rows_of(CELLS, NY), rows_of(devices, NY)],
        [
            vmem(2, NZ * 24, NY), vmem(2, tall, NY), vmem(CELLS, NY), vmem(NZ * 24, NY), vmem(CELLS, NY),
            vmem(CELLS, 8), vmem(2, NZ * 24, NY), vmem(CELLS, NY), vmem(2, tall, NY),
        ],
    )(state, state_1, gamma, lam_2, coef, coef_halo, beside, yown, *got_yz, *got_x, mis, spread)
    rows = lax.all_to_all(rows, ("gx", "gy", "gz"), 0, 0, tiled=True)
    direction, misfit = pl.pallas_call(
        bind(scale_kernel, devices, probes.shape[0]),
        out_shape=[rows_of(CELLS, NY), rows_of(1, 1)],
        out_specs=[pl.BlockSpec(memory_space=pltpu.VMEM), pl.BlockSpec(memory_space=pltpu.SMEM)],
        compiler_params=SMALL,
    )(gradient, rows)
    return direction.reshape(NZ, NX, NY), misfit.reshape(())


def solution(mesh):
    block = P("gz", "gx", "gy")
    parted = P(None, "gz", "gx", "gy")
    listed = P(("gx", "gy", "gz"))
    return jax.shard_map(
        functools.partial(local, dict(mesh.shape)),
        mesh=mesh,
        in_specs=(parted, block, parted, listed, listed),
        out_specs=(block, P()),
        check_vma=False,
    )
```

```python
import functools
import jax
import jax.numpy as jnp
from jax import lax
from jax.experimental import pallas as pl
from jax.experimental.pallas import tpu as pltpu
from jax.sharding import PartitionSpec as P

NZ, NX, NY = 16, 8, 128
CELLS = NZ * NX
bulk_modulus = 2.0
slope_coeff = 1.5
signal_speed = 2.5
time_ratio = 0.1
quad_viscosity = 4.0
small_eps = 1e-12
HALF_C = 0.5 * signal_speed
HALF_T = 0.5 * time_ratio
NEAR = time_ratio * HALF_C
STAY = 1.0 - 3.0 * time_ratio * signal_speed
F32 = jnp.float32


def primitives(r, mx, my, mz, en, gamma):
    inv = 1.0 / (1.0 + r)
    ux, uy, uz = mx * inv, my * inv, mz * inv
    heat = en - 0.5 * (mx * ux + my * uy + mz * uz)
    press = bulk_modulus * (r + slope_coeff * r * r) + gamma * heat
    return ux, uy, uz, heat, press


def total_pressure(press, sw, r, slope):
    squeeze = jnp.minimum(slope, 0.0)
    return press + sw * quad_viscosity * (1.0 + r) * squeeze * squeeze


def flux(state, axis, speed, total):
    rows = [state[1 + axis]] + [state[1 + k] * speed for k in range(3)]
    rows[1 + axis] = rows[1 + axis] + total
    return rows + [(state[4] + total) * speed]


def upper_part(f, u):
    return 0.5 * f - HALF_C * u


def lower_part(f, u):
    return 0.5 * f + HALF_C * u


def layer(z):
    return pl.ds(NX * z, NX)


def x_row(x):
    return pl.ds(x, NZ, stride=NX)


def lanes():
    return lax.broadcasted_iota(jnp.int32, (NX, NY), 1)


def y_next(value, column, lane):
    return jnp.where(lane == NY - 1, column, pltpu.roll(value, NY - 1, 1))


def y_prev(value, column, lane):
    return jnp.where(lane == 0, column, pltpu.roll(value, 1, 1))


def inside(flag):
    return jnp.where(flag, 1.0, 0.0).astype(F32)


def masks(mesh):
    ix, iy, iz = lax.axis_index("gx"), lax.axis_index("gy"), lax.axis_index("gz")
    return (
        (inside(ix > 0), inside(ix < mesh["gx"] - 1)),
        (inside(iy > 0), inside(iy < mesh["gy"] - 1)),
        (inside(iz > 0), inside(iz < mesh["gz"] - 1)),
        iz == 0,
    )


def face_layer(is_first, depth):
    return jnp.where(is_first, NZ - 1 - depth, depth)


def dyn_layer(z):
    return pl.ds(pl.multiple_of(NX * z, NX), NX)


def pack_edges(values, lane, depth=2):
    out = pltpu.roll(values[0], depth, 1)
    for i in range(1, len(values)):
        out = jnp.where(lane < 2 * depth * i, out, pltpu.roll(values[i], depth * (2 * i + 1), 1))
    return out


def begun(u, f, far, sign):
    return STAY * u + time_ratio * (sign * 0.5 * f + HALF_C * far)


def prep_kernel(mesh, u_ref, g_ref, s_ref, ylo, yhi, zs, yp):
    _, _, _, first = masks(mesh)
    lane = lanes()
    for z in range(NZ):
        vals = [u_ref[k, layer(z), :] for k in range(5)]
        vals += [g_ref[layer(z), :], s_ref[0, layer(z), :].astype(F32)]
        yp[layer(z), :] = pack_edges(vals, lane, 3)
    rows = yp[...].T
    for out, c1, c2, c3, sign in ((yhi, 2, 1, 0, 1.0), (ylo, 3, 4, 5, -1.0)):
        st, st2, st3 = [[rows[6 * k + c : 6 * k + c + 1] for k in range(7)] for c in (c1, c2, c3)]
        prim, prim2 = primitives(*st[:6]), primitives(*st2[:6])
        slope = (sign * 0.5) * (prim[1] - st3[2] / (1.0 + st3[0]))
        fl = flux(st2[:5], 1, prim2[1], total_pressure(prim2[4], st2[6], st2[0], slope))
        items = st[:5] + [prim[4], st[6], prim2[1]] + [begun(st[k], fl[k], st2[k], sign) for k in range(3)]
        for k in range(11):
            out[k : k + 1] = items[k]
        out[11:16] = jnp.zeros((5, NY), F32)
    za, zb, zc = [dyn_layer(face_layer(first, d)) for d in range(3)]
    sign = jnp.where(first, 1.0, -1.0)
    st, st2 = [[u_ref[k, at, :] for k in range(5)] for at in (za, zb)]
    prim, prim2 = primitives(*st, g_ref[za, :]), primitives(*st2, g_ref[zb, :])
    slope = (sign * 0.5) * (prim[2] - u_ref[3, zc, :] / (1.0 + u_ref[0, zc, :]))
    fl = flux(st2, 2, prim2[2], total_pressure(prim2[4], s_ref[0, zb, :].astype(F32), st2[0], slope))
    items = st + [prim[4], s_ref[0, za, :].astype(F32), prim2[2]]
    items += [begun(st[k], fl[k], st2[k], sign) for k in (0, 1, 3)]
    for k in range(11):
        zs[k] = items[k]


def still_kernel(u_ref, g_ref, s_ref, vel, heat, press, slo, shi):
    for z in range(NZ):
        prim = primitives(*[u_ref[k, layer(z), :] for k in range(5)], g_ref[layer(z), :])
        for k in range(3):
            vel[k, layer(z), :] = prim[k]
        heat[layer(z), :] = prim[3]
        press[layer(z), :] = prim[4]
    for out, e, i, j, last, sign in ((shi, NX - 1, NX - 2, NX - 3, NX - 4, 1.0), (slo, 0, 1, 2, 3, -1.0)):
        for k in range(5):
            out[k] = u_ref[k, x_row(e), :]
        out[5] = g_ref[x_row(e), :]
        out[6] = s_ref[0, x_row(e), :].astype(F32)
        out[7] = vel[0, x_row(i), :]
        out[8] = s_ref[1, x_row(e), :].astype(F32)
        for at, before, after, base, count in ((i, e, j, 9, 5), (j, i, last, 14, 2)):
            st = [u_ref[k, x_row(at), :] for k in range(5)]
            slope = (sign * 0.5) * (vel[0, x_row(before), :] - vel[0, x_row(after), :])
            total = total_pressure(press[x_row(at), :], s_ref[0, x_row(at), :].astype(F32), st[0], slope)
            fl = flux(st, 0, vel[0, x_row(at), :], total)
            for k in range(count):
                out[base + k] = time_ratio * (sign * 0.5 * fl[k] + HALF_C * st[k])


def side_kernel(
    mesh, u_ref, s_ref, vel, pr, slo, shi, ylo, yhi, yl, yh, zr,
    part, xlo, xhi, zz,
    vz, az, bz, yr, yc,
):
    _, (myl, myh), (mzl, mzh), first = masks(mesh)
    lane = lanes()
    for z in range(NZ):
        vz[layer(z + 1), :] = vel[2, layer(z), :]
    far = [zr[k] for k in range(8)]
    speed = far[3] / (1.0 + far[0])
    own = vel[2, dyn_layer(face_layer(first, 0)), :]
    slope = (far[7] - own) * jnp.where(first, 0.5, -0.5)
    fl = flux(far[:5], 2, speed, total_pressure(far[5], far[6], far[0], slope))
    for k in range(5):
        bz[k, layer(0), :] = lower_part(fl[k], far[k]) * mzl
        az[k, layer(NZ), :] = upper_part(fl[k], far[k]) * mzh
    vz[layer(0), :] = speed * mzl
    vz[layer(NZ + 1), :] = speed * mzh
    low = [yl[k : k + 1] * myl for k in range(8)]
    high = [yh[k : k + 1] * myh for k in range(8)]
    speed = low[2] / (1.0 + low[0])
    yr[10:11, :] = speed
    slope = 0.5 * (ylo[2:3] / (1.0 + ylo[0:1]) - low[7])
    fl = flux(low[:5], 1, speed, total_pressure(low[5], low[6], low[0], slope))
    for k in range(5):
        yr[k : k + 1, :] = lower_part(fl[k], low[k])
    speed = high[2] / (1.0 + high[0])
    yr[11:12, :] = speed
    slope = 0.5 * (high[7] - yhi[2:3] / (1.0 + yhi[0:1]))
    fl = flux(high[:5], 1, speed, total_pressure(high[5], high[6], high[0], slope))
    for k in range(5):
        yr[5 + k : 6 + k, :] = upper_part(fl[k], high[k])
    yr[12:16, :] = jnp.zeros((4, NY), F32)
    yc[...] = yr[...].T
    for z in range(NZ):
        st = [u_ref[k, layer(z), :] for k in range(5)]
        press = pr[layer(z), :]
        visc = s_ref[0, layer(z), :].astype(F32) * quad_viscosity * (1.0 + st[0])
        uy, uz = vel[1, layer(z), :], vel[2, layer(z), :]

        def col(i):
            return yc[layer(z), i : i + 1]

        def total(up, down):
            squeeze = jnp.minimum(0.5 * (up - down), 0.0)
            return press + visc * squeeze * squeeze

        fy = flux(st, 1, uy, total(y_next(uy, col(11), lane), y_prev(uy, col(10), lane)))
        fz = flux(st, 2, uz, total(vz[layer(z + 2), :], vz[layer(z), :]))
        for k in range(5):
            az[k, layer(z), :] = upper_part(fz[k], st[k])
            bz[k, layer(z + 1), :] = lower_part(fz[k], st[k])
            part[k, layer(z), :] = STAY * st[k] - time_ratio * (
                y_next(upper_part(fy[k], st[k]), col(5 + k), lane)
                - y_prev(lower_part(fy[k], st[k]), col(k), lane)
            )
    for z in range(NZ):
        for k in range(5):
            part[k, layer(z), :] = part[k, layer(z), :] - time_ratio * (
                az[k, layer(z + 1), :] - bz[k, layer(z), :]
            )
    for k in range(8):
        zz[k : k + 1, :] = low[k]
        zz[8 + k : 9 + k, :] = high[k]
    for out, still, e, i in ((xhi, shi, NX - 1, NX - 2), (xlo, slo, 0, 1)):
        for k in range(9):
            out[k] = still[k]
        for k in range(5):
            out[9 + k] = part[k, x_row(e), :] + still[9 + k]
        for k in range(2):
            out[14 + k] = part[k, x_row(i), :] + still[14 + k]
        out[16] = zz[...]
        for k in range(8):
            out[17, k : k + 1, :] = zr[k, e : e + 1, :]
        out[17, 8:9, :] = zr[1, i : i + 1, :] / (1.0 + zr[0, i : i + 1, :])
        out[17, 9:16, :] = jnp.zeros((7, NY), F32)


def shifted_x(own, low, high, at_x):
    up = jnp.where(at_x == NX - 1, pltpu.roll(high, NX - 1, 1), pltpu.roll(own, NY - 1, 1))
    down = jnp.where(at_x == 0, pltpu.roll(low, NY - NX + 1, 1), pltpu.roll(own, 1, 1))
    return up, down


def halo_step(
    mesh, u_ref, g_ref, s_ref, vel, pr, part, ylo, yhi, yl, yh, zr, xl, xh, zz,
    o_ref, xc, hxl, hxh, hyl, hyh, hz, vx, ax, bx, zc,
):
    (mxl, mxh), (myl, myh), (mzl, mzh), first = masks(mesh)
    for z in range(NZ):
        vx[pl.ds(24 * z + 8, 8), :] = vel[0, layer(z), :]
    low = [xl[k] * mxl for k in range(8)]
    high = [xh[k] * mxh for k in range(8)]
    prim = primitives(*low[:6])
    vx[pl.ds(7, NZ, stride=24), :] = prim[0]
    slope = 0.5 * (vx[pl.ds(8, NZ, stride=24), :] - low[7])
    f_low = flux(low[:5], 0, prim[0], total_pressure(prim[4], low[6], low[0], slope))
    prim = primitives(*high[:6])
    vx[pl.ds(16, NZ, stride=24), :] = prim[0]
    slope = 0.5 * (high[7] - vx[pl.ds(15, NZ, stride=24), :])
    f_high = flux(high[:5], 0, prim[0], total_pressure(prim[4], high[6], high[0], slope))
    for k in range(5):
        bx[k, pl.ds(7, NZ, stride=16), :] = lower_part(f_low[k], low[k])
        ax[k, pl.ds(8, NZ, stride=16), :] = upper_part(f_high[k], high[k])
    for z in range(NZ):
        st = [u_ref[k, layer(z), :] for k in range(5)]
        ux, press = vel[0, layer(z), :], pr[layer(z), :]
        slope = 0.5 * (vx[pl.ds(24 * z + 9, 8), :] - vx[pl.ds(24 * z + 7, 8), :])
        fx = flux(st, 0, ux, total_pressure(press, s_ref[0, layer(z), :].astype(F32), st[0], slope))
        for k in range(5):
            ax[k, pl.ds(16 * z, 8), :] = upper_part(fx[k], st[k])
            bx[k, pl.ds(16 * z + 8, 8), :] = lower_part(fx[k], st[k])
    for z in range(NZ):
        for k in range(5):
            o_ref[k, layer(z), :] = part[k, layer(z), :] - time_ratio * (
                ax[k, pl.ds(16 * z + 1, 8), :] - bx[k, pl.ds(16 * z + 7, 8), :]
            )
    for out, ref, mask in ((hxl, xl, mxl), (hxh, xh, mxh)):
        if ref is xl:
            near = [-ax[k, pl.ds(0, NZ, stride=16), :] for k in range(5)]
            next_ = [-upper_part(f_low[k], low[k]) for k in range(2)]
        else:
            near = [bx[k, pl.ds(15, NZ, stride=16), :] for k in range(5)]
            next_ = [lower_part(f_high[k], high[k]) for k in range(2)]
        st = [(ref[9 + k] + time_ratio * near[k]) * mask for k in range(5)]
        st2 = [(ref[14 + k] + time_ratio * next_[k]) * mask for k in range(2)]
        out[0] = st[0]
        out[1] = st[1]
        out[2] = primitives(*st, ref[5] * mask)[4]
        out[3] = ref[8] * mask
        out[4] = st2[1] / (1.0 + st2[0])
        base = 0 if ref is xl else 3
        inv, gamma = 1.0 / (1.0 + st[0]), ref[5] * mask
        xc[base] = (2.0 - gamma) * (st[1] * inv)
        xc[base + 1] = inv
        xc[base + 2] = gamma
    lane = lax.broadcasted_iota(jnp.int32, (1, NY), 1)
    at_x = lax.bitwise_and(lane, NX - 1)
    for side, ref, mask, own, out, sign in ((0, yl, myl, ylo, hyl, -1.0), (1, yh, myh, yhi, hyh, 1.0)):

        def items(values, m):
            return [values[k : k + 1] * m for k in range(8)]

        here = items(ref, mask)
        near_l, near_h = items(xl[16, 8 * side : 8 * side + 8, :], mxl), items(xh[16, 8 * side : 8 * side + 8, :], mxh)
        ux, ux_l, ux_h = [v[1] / (1.0 + v[0]) for v in (here, near_l, near_h)]
        up, down = shifted_x(ux, ux_l, ux_h, at_x)
        slope = 0.5 * (up - down)
        slope_h = 0.5 * (pltpu.roll(ux_h, NY - 1, 1) - pltpu.roll(ux, NY - NX + 1, 1))
        slope_l = 0.5 * (pltpu.roll(ux, NX - 1, 1) - pltpu.roll(ux_l, 1, 1))

        def fx_of(v, speed, slope):
            return [v[1], v[1] * speed + total_pressure(v[5], v[6], v[0], slope), v[2] * speed]

        f_here, f_l, f_h = fx_of(here, ux, slope), fx_of(near_l, ux_l, slope_l), fx_of(near_h, ux_h, slope_h)
        uz = here[3] / (1.0 + here[0])
        near_z = items(zz[8 * side : 8 * side + 8, :], 1.0)
        uz_z = near_z[3] / (1.0 + near_z[0])
        fz, fz_z = [[v[3], v[1] * w, v[2] * w] for v, w in ((here, uz), (near_z, uz_z))]
        self_ = items(own, 1.0)
        uy = self_[2] / (1.0 + self_[0])
        uy_here = here[2] / (1.0 + here[0])
        slope = 0.5 * (self_[7] - uy_here if side == 0 else uy_here - self_[7])
        fy = [self_[2], self_[1] * uy, self_[2] * uy + total_pressure(self_[5], self_[6], self_[0], slope)]
        new = []
        for k in range(3):
            a_x, _ = shifted_x(upper_part(f_here[k], here[k]), ux_l, upper_part(f_h[k], near_h[k]), at_x)
            _, b_x = shifted_x(lower_part(f_here[k], here[k]), lower_part(f_l[k], near_l[k]), ux_h, at_x)
            a_z = jnp.where(
                lane >= NY - NX,
                pltpu.roll(upper_part(fz_z[k], near_z[k]), NY - NX, 1) * mzh,
                pltpu.roll(upper_part(fz[k], here[k]), NY - NX, 1),
            )
            b_z = jnp.where(
                lane < NX,
                pltpu.roll(lower_part(fz_z[k], near_z[k]), NX, 1) * mzl,
                pltpu.roll(lower_part(fz[k], here[k]), NX, 1),
            )
            facing = sign * 0.5 * fy[k] + HALF_C * self_[k]
            new.append(mask * (ref[8 + k : 9 + k] + time_ratio * (facing - (a_x - b_x) - (a_z - b_z))))
        r, mx, my = new
        combine = lower_part if side == 0 else upper_part
        out[0:1, :] = combine(my, r)
        out[1:2, :] = combine(mx * (my / (1.0 + r)), mx)
        out[2:8, :] = jnp.zeros((6, NY), F32)
    rows = []
    for side in range(2):
        v = [zz[8 * side + k : 8 * side + k + 1, :] for k in range(8)]
        speed = v[2] / (1.0 + v[0])
        fy = [v[2], v[1] * speed, v[3] * speed]
        combine = upper_part if side else lower_part
        rows += [combine(f, v[k]) for f, k in zip(fy, (0, 1, 3))]
    zc[...] = jnp.concatenate(rows + [jnp.zeros((2, NY), F32)], axis=0).T
    cols = zc[dyn_layer(jnp.where(first, 0, NZ - 1)), :]
    full = lanes()
    deep = lax.broadcasted_iota(jnp.int32, (NX, NY), 0)
    here = [zr[k] for k in range(8)]
    near_l = [xl[17, k : k + 1, :] * mxl for k in range(9)]
    near_h = [xh[17, k : k + 1, :] * mxh for k in range(9)]
    ux, ux_l, ux_h = [v[1] / (1.0 + v[0]) for v in (here, near_l, near_h)]

    def next_x(value, row):
        return jnp.where(deep == NX - 1, row, pltpu.roll(value, NX - 1, 0))

    def prev_x(value, row):
        return jnp.where(deep == 0, row, pltpu.roll(value, 1, 0))

    slope = 0.5 * (next_x(ux, ux_h) - prev_x(ux, ux_l))
    slope_h = 0.5 * (near_h[8] - ux[NX - 1 : NX])
    slope_l = 0.5 * (ux[0:1] - near_l[8])

    def fx_layer(v, speed, slope):
        return [v[1], v[1] * speed + total_pressure(v[5], v[6], v[0], slope), v[3] * speed]

    f_here, f_l, f_h = fx_layer(here, ux, slope), fx_layer(near_l, ux_l, slope_l), fx_layer(near_h, ux_h, slope_h)
    uy = here[2] / (1.0 + here[0])
    fy = [here[2], here[1] * uy, here[3] * uy]
    za, zb = dyn_layer(face_layer(first, 0)), dyn_layer(face_layer(first, 1))
    sign = jnp.where(first, 1.0, -1.0)
    st = [u_ref[k, za, :] for k in range(5)]
    slope = (sign * 0.5) * (here[3] / (1.0 + here[0]) - vel[2, zb, :])
    fz = flux(st, 2, vel[2, za, :], total_pressure(pr[za, :], s_ref[0, za, :].astype(F32), st[0], slope))
    new = []
    for n, k in enumerate((0, 1, 3)):
        a_x = next_x(upper_part(f_here[n], here[k]), upper_part(f_h[n], near_h[k]))
        b_x = prev_x(lower_part(f_here[n], here[k]), lower_part(f_l[n], near_l[k]))
        a_y = y_next(upper_part(fy[n], here[k]), cols[:, 3 + n : 4 + n], full)
        b_y = y_prev(lower_part(fy[n], here[k]), cols[:, n : n + 1], full)
        facing = sign * 0.5 * fz[k] + HALF_C * st[k]
        new.append(zr[8 + n] + time_ratio * (facing - (a_x - b_x) - (a_y - b_y)))
    r, mx, mz = new
    hz[0] = 0.5 * mz - (sign * HALF_C) * r
    hz[1] = 0.5 * mx * (mz / (1.0 + r)) - (sign * HALF_C) * mx


def forward_kernel(
    mesh, u0_ref, g_ref, s_ref, vel, pr, part, ylo_in, yhi_in, yl, yh, zr, xl, xh, zz, n_ref, m_ref,
    u_ref, lam_ref, cf_ref, cfh_ref, mis_ref, xc, ylo, yhi, zs, yown,
    hxl, hxh, hyl, hyh, hz, vx, ax, bx, az, bz, ch, yc, yp, zc,
):
    halo_step(
        mesh, u0_ref, g_ref, s_ref, vel, pr, part, ylo_in, yhi_in, yl, yh, zr, xl, xh, zz,
        u_ref, xc, hxl, hxh, hyl, hyh, hz, vx, ax, bx, zc,
    )
    speed_kernel(
        mesh, u_ref, g_ref, s_ref, hxl, hxh, hyl, hyh, hz, n_ref, m_ref,
        lam_ref, cf_ref, cfh_ref, mis_ref, ylo, yhi, zs, yown,
        vx, ax, bx, az, bz, ch, yc, yp,
    )


def columns_of(low, high, count, low_mask, high_mask):
    rows = [low[k : k + 1] * low_mask for k in range(count)]
    rows += [high[k : k + 1] * high_mask for k in range(count)]
    rows.append(jnp.zeros((8 - 2 * count, NY), F32))
    return jnp.concatenate(rows, axis=0).T


def speed_kernel(
    mesh, u_ref, g_ref, s_ref, xl, xh, yl, yh, zr, n_ref, m_ref,
    lam_ref, cf_ref, cfh_ref, mis_ref, ylo, yhi, zs, yown,
    vx, ax, bx, az, bz, ch, yc, yp,
):
    (mxl, mxh), (myl, myh), (mzl, mzh), first = masks(mesh)
    lane = lanes()
    for z in range(NZ):
        vx[pl.ds(24 * z + 8, 8), :] = u_ref[1, layer(z), :] / (1.0 + u_ref[0, layer(z), :])
    for side, ref, mask in ((0, xl, mxl), (1, xh, mxh)):
        r, mx, press, sw, second = [ref[k] * mask for k in range(5)]
        speed = mx / (1.0 + r)
        vx[pl.ds(16 if side else 7, NZ, stride=24), :] = speed
        own = vx[pl.ds(15 if side else 8, NZ, stride=24), :]
        slope = 0.5 * (second - own if side else own - second)
        squeeze = jnp.minimum(slope, 0.0)
        visc = sw * quad_viscosity * (1.0 + r) * squeeze
        cfh_ref[side] = 2.0 * visc
        f1 = mx * speed + press + visc * squeeze
        if side:
            ax[0, pl.ds(8, NZ, stride=16), :] = upper_part(mx, r)
            ax[1, pl.ds(8, NZ, stride=16), :] = upper_part(f1, mx)
        else:
            bx[0, pl.ds(7, NZ, stride=16), :] = lower_part(mx, r)
            bx[1, pl.ds(7, NZ, stride=16), :] = lower_part(f1, mx)
    for k in range(2):
        bz[k, layer(0), :] = zr[k] * mzl
        az[k, layer(NZ), :] = zr[k] * mzh
    yc[...] = columns_of(yl, yh, 2, myl, myh)
    for z in range(NZ):
        r, mx, my, mz, en = [u_ref[k, layer(z), :] for k in range(5)]
        ux, uy, uz, _, press = primitives(r, mx, my, mz, en, g_ref[layer(z), :])
        squeeze = jnp.minimum(0.5 * (vx[pl.ds(24 * z + 9, 8), :] - vx[pl.ds(24 * z + 7, 8), :]), 0.0)
        visc = s_ref[1, layer(z), :].astype(F32) * quad_viscosity * (1.0 + r) * squeeze
        cf_ref[layer(z), :] = 2.0 * visc
        f1 = mx * ux + press + visc * squeeze
        for k, st, fx, fy, fz in ((0, r, mx, my, mz), (1, mx, f1, mx * uy, mx * uz)):
            ax[k, pl.ds(16 * z, 8), :] = upper_part(fx, st)
            bx[k, pl.ds(16 * z + 8, 8), :] = lower_part(fx, st)
            az[k, layer(z), :] = upper_part(fz, st)
            bz[k, layer(z + 1), :] = lower_part(fz, st)
            ch[k, layer(z), :] = (
                3.0 * signal_speed * st
                + y_next(upper_part(fy, st), yc[layer(z), 2 + k : 3 + k], lane)
                - y_prev(lower_part(fy, st), yc[layer(z), k : k + 1], lane)
            )
    mis = jnp.zeros((NX, NY), F32)
    for z in range(NZ):
        new = []
        for k in range(2):
            change = (
                ch[k, layer(z), :]
                + (ax[k, pl.ds(16 * z + 1, 8), :] - bx[k, pl.ds(16 * z + 7, 8), :])
                + (az[k, layer(z + 1), :] - bz[k, layer(z), :])
            )
            new.append(u_ref[k, layer(z), :] - time_ratio * change)
        inv = 1.0 / (1.0 + new[0])
        speed = new[1] * inv
        off = speed - m_ref[layer(z), :]
        weight = n_ref[layer(z), :] * off
        mis = mis + weight * off
        lam_m = 2.0 * weight * inv
        lam_r = -lam_m * speed
        lam_ref[0, layer(z), :] = lam_r
        lam_ref[1, layer(z), :] = lam_m
        inv = 1.0 / (1.0 + u_ref[0, layer(z), :])
        extra = [u_ref[1, layer(z), :] * inv, u_ref[2, layer(z), :] * inv, g_ref[layer(z), :]]
        yp[layer(z), :] = pack_edges([lam_r, lam_m] + extra, lane)
    mis_ref[...] = mis
    za, zb = dyn_layer(face_layer(first, 0)), dyn_layer(face_layer(first, 1))
    inv = 1.0 / (1.0 + u_ref[0, za, :])
    ux = u_ref[1, za, :] * inv
    zs[0] = lam_ref[0, za, :]
    zs[1] = lam_ref[1, za, :]
    zs[2] = jnp.where(first, -HALF_T, HALF_T) * (lam_ref[0, zb, :] + lam_ref[1, zb, :] * ux)
    zs[3] = ux
    zs[4] = u_ref[3, za, :] * inv
    zs[5] = g_ref[za, :]
    rows = yp[...].T
    for out, edge, second, own, sign in ((yhi, 1, 0, 2, -HALF_T), (ylo, 2, 3, 0, HALF_T)):
        lam_r, lam_m, ux, uy, gamma = [rows[4 * i + edge : 4 * i + edge + 1] for i in range(5)]
        out[0:1] = lam_r
        out[1:2] = lam_m
        out[2:3] = sign * (rows[second : second + 1] + rows[4 + second : 5 + second] * ux)
        out[3:4] = ux
        out[4:5] = uy
        out[5:6] = gamma
        out[6:8] = jnp.zeros((2, NY), F32)
        yown[own : own + 1] = lam_r
        yown[own + 1 : own + 2] = lam_m
    yown[4:8] = jnp.zeros((4, NY), F32)


def edge_kernel(mesh, u_ref, lam_ref, cf_ref, yl, yh, zr, xlo, xhi, yc):
    _, (myl, myh), (mzl, mzh), _ = masks(mesh)
    low_y, high_y = yl[1:2] * myl, yh[1:2] * myh
    yc[:, 0:8] = jnp.concatenate([low_y, high_y, jnp.zeros((6, NY), F32)], axis=0).T
    lane = lax.broadcasted_iota(jnp.int32, (NZ, NY), 1)
    deep = lax.broadcasted_iota(jnp.int32, (NZ, NY), 0)
    for out, e, i, i2, sign in ((xhi, NX - 1, NX - 2, NX - 3, 1.0), (xlo, 0, 1, 2, -1.0)):
        r, my, mz = [u_ref[k, x_row(e), :] for k in (0, 2, 3)]
        inv = 1.0 / (1.0 + r)
        lm, lm_i = lam_ref[1, x_row(e), :], lam_ref[1, x_row(i), :]
        col = yc[x_row(e), :]
        side = zr[1, e : e + 1, :]
        up_y = jnp.where(lane == NY - 1, col[:, 1:2], pltpu.roll(lm, NY - 1, 1))
        down_y = jnp.where(lane == 0, col[:, 0:1], pltpu.roll(lm, 1, 1))
        up_z = jnp.where(deep == NZ - 1, side * mzh, pltpu.roll(lm, NZ - 1, 0))
        down_z = jnp.where(deep == 0, side * mzl, pltpu.roll(lm, 1, 0))
        slope = (sign * HALF_T) * (lm - lam_ref[1, x_row(i2), :]) * cf_ref[x_row(i), :]
        out[0] = lam_ref[0, x_row(e), :]
        out[1] = lm
        out[2] = lm_i
        out[3] = (
            STAY * lm
            + NEAR * (lm_i + (up_y + down_y) + (up_z + down_z))
            - (sign * HALF_T) * lam_ref[0, x_row(i), :]
            + HALF_T * ((up_y - down_y) * (my * inv) + (up_z - down_z) * (mz * inv))
            + (sign * 0.5) * slope * inv
        )
        out[4] = jnp.where(deep == 0, low_y, jnp.where(deep == 1, high_y, jnp.where(deep == 2, side, 0.0)))


def lean_kernel(mesh, u_ref, lam_ref, yl, yh, zr, base, vel, inv_ref, heat, lz, yc):
    _, (myl, myh), (mzl, mzh), _ = masks(mesh)
    lane = lanes()
    for k in range(2):
        for z in range(NZ):
            lz[k, layer(z + 1), :] = lam_ref[k, layer(z), :]
        lz[k, layer(0), :] = zr[k] * mzl
        lz[k, layer(NZ + 1), :] = zr[k] * mzh
    yc[...] = columns_of(yl, yh, 2, myl, myh)
    for z in range(NZ):
        r, mx, my, mz, en = [u_ref[k, layer(z), :] for k in range(5)]
        inv = 1.0 / (1.0 + r)
        ux, uy, uz = mx * inv, my * inv, mz * inv
        heat[layer(z), :] = en - 0.5 * (mx * ux + my * uy + mz * uz)
        inv_ref[layer(z), :] = inv
        for k, value in enumerate((ux, uy, uz)):
            vel[k, layer(z), :] = value
        lr, lm = lam_ref[0, layer(z), :], lam_ref[1, layer(z), :]
        lr_z = [lz[0, layer(z + s), :] for s in (0, 2)]
        lm_z = [lz[1, layer(z + s), :] for s in (0, 2)]
        lr_y = [y_prev(lr, yc[layer(z), 0:1], lane), y_next(lr, yc[layer(z), 2:3], lane)]
        lm_y = [y_prev(lm, yc[layer(z), 1:2], lane), y_next(lm, yc[layer(z), 3:4], lane)]
        phi_y1 = HALF_T * (lm_y[1] - lm_y[0])
        phi_z1 = HALF_T * (lm_z[1] - lm_z[0])
        near = (lm_y[0] + lm_y[1]) + (lm_z[0] + lm_z[1])
        base[0, layer(z), :] = STAY * lm + NEAR * near + phi_y1 * uy + phi_z1 * uz
        base[1, layer(z), :] = HALF_T * (lr_y[1] - lr_y[0]) + phi_y1 * ux
        base[2, layer(z), :] = HALF_T * (lr_z[1] - lr_z[0]) + phi_z1 * ux


def gradient_kernel(
    mesh, vel, heat_ref, u_ref, g_ref, base, vel_1, inv_1, heat_1, lam_ref, cf_ref, cfh_ref, xc, yown, yl, yh, zr, xl, xh, mis_ref, v_ref,
    grad_ref, row_ref,
    lx, px, dx, dg, yc, gx, gy, gz,
):
    (mxl, mxh), (myl, myh), (mzl, mzh), first = masks(mesh)
    lane = lanes()
    for k in range(2):
        for z in range(NZ):
            lx[k, pl.ds(24 * z + 8, 8), :] = lam_ref[k, layer(z), :]
        lx[k, pl.ds(7, NZ, stride=24), :] = xl[k] * mxl
        lx[k, pl.ds(16, NZ, stride=24), :] = xh[k] * mxh
    phi_low = HALF_T * (lam_ref[1, x_row(0), :] - xl[2] * mxl)
    phi_high = HALF_T * (xh[2] * mxh - lam_ref[1, x_row(NX - 1), :])
    dx[pl.ds(7, NZ, stride=24), :] = phi_low * cfh_ref[0]
    dx[pl.ds(16, NZ, stride=24), :] = phi_high * cfh_ref[1]
    for z in range(NZ):
        phi = HALF_T * (lx[1, pl.ds(24 * z + 9, 8), :] - lx[1, pl.ds(24 * z + 7, 8), :])
        px[layer(z), :] = phi
        dx[pl.ds(24 * z + 8, 8), :] = phi * cf_ref[layer(z), :]
    gx[1, pl.ds(7, NZ, stride=24), :] = mxl * phi_low * xc[2]
    gx[1, pl.ds(16, NZ, stride=24), :] = mxh * phi_high * xc[5]
    gx[0, pl.ds(7, NZ, stride=24), :] = mxl * (
        xl[3]
        + HALF_T * lam_ref[0, x_row(0), :]
        + NEAR * lam_ref[1, x_row(0), :]
        + phi_low * xc[0]
        - 0.5 * dx[pl.ds(8, NZ, stride=24), :] * xc[1]
    )
    gx[0, pl.ds(16, NZ, stride=24), :] = mxh * (
        xh[3]
        - HALF_T * lam_ref[0, x_row(NX - 1), :]
        + NEAR * lam_ref[1, x_row(NX - 1), :]
        + phi_high * xc[3]
        + 0.5 * dx[pl.ds(15, NZ, stride=24), :] * xc[4]
    )
    at_x = lax.bitwise_and(lax.broadcasted_iota(jnp.int32, (1, NY), 1), NX - 1)
    from_high, from_low = pltpu.roll(xh[4], NX - 1, 1) * mxh, pltpu.roll(xl[4], NY - NX + 1, 1) * mxl
    halo = []
    for side, ref, mask, sign in ((0, yl, myl, HALF_T), (1, yh, myh, -HALF_T)):
        items = ref[...]
        up = jnp.where(at_x == NX - 1, from_high[side : side + 1], pltpu.roll(items, NY - 1, 1)[1:2])
        down = jnp.where(at_x == 0, from_low[side : side + 1], pltpu.roll(items, 1, 1)[1:2])
        d_en = HALF_T * (up - down) * items[5:6]
        own_r, own_m = yown[2 * side : 2 * side + 1], yown[2 * side + 1 : 2 * side + 2]
        d_my = items[2:3] + sign * (own_r + own_m * items[3:4]) - d_en * items[4:5]
        halo += [d_my * mask, d_en * mask]
    yc[...] = jnp.concatenate(halo + [jnp.zeros((4, NY), F32)], axis=0).T
    deep = lax.broadcasted_iota(jnp.int32, (NX, NY), 0)
    up = jnp.where(deep == NX - 1, xh[4, 2:3, :] * mxh, pltpu.roll(zr[1], NX - 1, 0))
    down = jnp.where(deep == 0, xl[4, 2:3, :] * mxl, pltpu.roll(zr[1], 1, 0))
    d_en = HALF_T * (up - down) * zr[5]
    za = dyn_layer(face_layer(first, 0))
    d_mz = (
        zr[2]
        + jnp.where(first, -HALF_T, HALF_T) * (lam_ref[0, za, :] + lam_ref[1, za, :] * zr[3])
        - d_en * zr[4]
    )
    for k, value in ((0, d_mz), (1, d_en)):
        gz[k, layer(0), :] = value * mzl
        gz[k, layer(NZ + 1), :] = value * mzh
    for z in range(NZ):
        ux, uy, uz = [vel_1[k, layer(z), :] for k in range(3)]
        lr_x = [lx[0, pl.ds(24 * z + s, 8), :] for s in (7, 9)]
        lm_x = [lx[1, pl.ds(24 * z + s, 8), :] for s in (7, 9)]
        phi_x1 = px[layer(z), :]
        d_speed = phi_x1 * u_ref[1, layer(z), :] + 0.5 * (dx[pl.ds(24 * z + 7, 8), :] - dx[pl.ds(24 * z + 9, 8), :])
        d_en = phi_x1 * g_ref[layer(z), :]
        gx[0, pl.ds(24 * z + 8, 8), :] = (
            base[0, layer(z), :]
            + NEAR * (lm_x[0] + lm_x[1])
            + HALF_T * (lr_x[1] - lr_x[0])
            + (phi_x1 - d_en) * ux
            + d_speed * inv_1[layer(z), :]
        )
        gx[1, pl.ds(24 * z + 8, 8), :] = d_en
        gy[layer(z), :] = base[1, layer(z), :] - d_en * uy
        gz[0, layer(z + 1), :] = base[2, layer(z), :] - d_en * uz
        gz[1, layer(z + 1), :] = d_en
        dg[layer(z), :] = phi_x1 * heat_1[layer(z), :]
    acc = jnp.zeros((NX, NY), F32)
    for z in range(NZ):
        ux, uy, uz = [vel[k, layer(z), :] for k in range(3)]
        heat = heat_ref[layer(z), :]
        dif_x = [gx[k, pl.ds(24 * z + 9, 8), :] - gx[k, pl.ds(24 * z + 7, 8), :] for k in range(2)]
        dif_z = [gz[k, layer(z + 2), :] - gz[k, layer(z), :] for k in range(2)]
        dif_y = []
        for k, own in ((0, gy[layer(z), :]), (1, gz[1, layer(z + 1), :])):
            dif_y.append(
                y_next(own, yc[layer(z), 2 + k : 3 + k], lane) - y_prev(own, yc[layer(z), k : k + 1], lane)
            )
        d_press = HALF_T * (
            (dif_x[0] + ux * dif_x[1]) + (dif_y[0] + uy * dif_y[1]) + (dif_z[0] + uz * dif_z[1])
        )
        grad = dg[layer(z), :] + d_press * heat
        grad_ref[layer(z), :] = grad
        acc = acc + grad * grad
    total = jnp.sum(jnp.sum(acc, axis=0, keepdims=True), axis=1, keepdims=True)
    miss = jnp.sum(jnp.sum(mis_ref[...], axis=0, keepdims=True), axis=1, keepdims=True)
    miss = miss + jnp.sum(v_ref[...], axis=1, keepdims=True)
    row = jnp.where(lane == 0, total, jnp.where(lane == 1, miss, 0.0))
    for i in range(row_ref.shape[0] // NX):
        row_ref[layer(i), :] = row


def scale_kernel(devices, count, grad_ref, rows_ref, out_ref, misfit_ref):
    acc = rows_ref[layer(0), :]
    for i in range(1, devices // NX):
        acc = acc + rows_ref[layer(i), :]
    row = jnp.sum(acc, axis=0, keepdims=True)
    misfit_ref[0, 0] = row[0, 1] / (devices * count)
    scale = 1.0 / jnp.sqrt(row[0:1, 0:1] / (devices * CELLS * NY) + small_eps)
    out_ref[...] = grad_ref[...] * scale


def split3(value):
    hi = value.astype(jnp.bfloat16)
    rest = value - hi.astype(F32)
    mid = rest.astype(jnp.bfloat16)
    low = (rest - mid.astype(F32)).astype(jnp.bfloat16)
    return hi, mid, low


def probe_kernel(p_ref, o_ref, n_ref, m_ref, v_ref):
    count = p_ref.shape[1]
    probes, obs = p_ref[...], o_ref[...]
    row = lax.broadcasted_iota(jnp.int32, (CELLS, count), 0)
    on_a = row == lax.shift_right_logical(probes, 7)
    on_b = row == lax.bitwise_and(probes, NY - 1)
    one_a = jnp.where(on_a, 1.0, 0.0).astype(jnp.bfloat16)
    one_b = jnp.where(on_b, 1.0, 0.0).astype(jnp.bfloat16)

    def nt(a, b):
        return lax.dot_general(a, b, (((1,), (1,)), ((), ())), preferred_element_type=F32)

    parts = [jnp.where(on_a, part.astype(F32), 0.0).astype(jnp.bfloat16) for part in split3(obs)]
    hits = nt(one_a, one_b)
    sums = nt(parts[0], one_b) + (nt(parts[1], one_b) + nt(parts[2], one_b))
    n_ref[...] = hits
    mean = sums / jnp.maximum(hits, 1.0)
    m_ref[...] = mean
    mean_t = split3(mean.T)
    picked = sum(jnp.dot(part, one_a, preferred_element_type=F32) for part in reversed(mean_t))
    at_probe = jnp.sum(jnp.where(on_b, picked, 0.0), axis=0, keepdims=True)
    off = obs - at_probe
    v_ref[...] = off * off


SMALL = pltpu.CompilerParams(vmem_limit_bytes=12 * 1024 * 1024)

LARGE = pltpu.CompilerParams(vmem_limit_bytes=55168 * 1024)


def rows_of(*shape):
    return jax.ShapeDtypeStruct(shape, F32)


def vmem(*shape):
    return pltpu.VMEM(shape, F32)


def call(kernel, outs, scratch, params=SMALL):
    return pl.pallas_call(
        kernel,
        out_shape=outs,
        scratch_shapes=scratch,
        cost_estimate=pl.CostEstimate(flops=100000, bytes_accessed=100000, transcendentals=0),
        compiler_params=params,
    )


def ring(sizes, axis, step):
    n = sizes[axis]
    return [(i, (i + step) % n) for i in range(n)]


def exchange_x(sizes, xlo, xhi):
    return (
        lax.ppermute(xhi, "gx", ring(sizes, "gx", 1)),
        lax.ppermute(xlo, "gx", ring(sizes, "gx", -1)),
    )


def exchange_z(sizes, zs):
    return lax.ppermute(zs, "gz", ring(sizes, "gz", 1))


def exchange_yz(sizes, ylo, yhi, zs):
    zr = exchange_z(sizes, zs)
    yl = lax.ppermute(yhi, "gy", ring(sizes, "gy", 1))
    yh = lax.ppermute(ylo, "gy", ring(sizes, "gy", -1))
    return yl, yh, zr


def local(sizes, checkpoint, gruneisen, switch, probes, observed):
    bind = functools.partial
    state = checkpoint.reshape(5, CELLS, NY)
    gamma = gruneisen.reshape(CELLS, NY)
    sw = switch.reshape(2, CELLS, NY)
    plane = rows_of(8, NY)

    def x_slabs(items):
        return [rows_of(items, NZ, NY)] * 2

    pair = rows_of(16, NY)
    tall = (NZ + 2) * NX
    *sent_y, sent_z = call(
        bind(prep_kernel, sizes), [pair, pair, rows_of(11, NX, NY)], [vmem(CELLS, NY)], LARGE
    )(state, gamma, sw)
    got_yz = exchange_yz(sizes, *sent_y, sent_z)
    hits, mean, spread = call(
        probe_kernel,
        [rows_of(CELLS, NY), rows_of(CELLS, NY), rows_of(1, probes.shape[0])],
        [],
    )(probes.reshape(1, -1), observed.reshape(1, -1))
    grid = rows_of(CELLS, NY)
    vel, heat, press, slo, shi = call(still_kernel, [rows_of(3, CELLS, NY), grid, grid] + x_slabs(16), [])(
        state, gamma, sw
    )
    part, xlo, xhi, zz = call(
        bind(side_kernel, sizes),
        [rows_of(5, CELLS, NY)] + x_slabs(18) + [pair],
        [
            vmem(tall, NY), vmem(5, tall, NY), vmem(5, tall, NY), vmem(16, NY), vmem(CELLS, 16),
        ],
    )(state, sw, vel, press, slo, shi, *sent_y, *got_yz)
    got_x = exchange_x(sizes, xlo, xhi)
    zz = exchange_z(sizes, zz)
    state_1, lam_2, coef, coef_halo, mis, beside, *sent, yown = call(
        bind(forward_kernel, sizes),
        [rows_of(5, CELLS, NY), rows_of(2, CELLS, NY), rows_of(CELLS, NY), rows_of(2, NZ, NY), plane]
        + [rows_of(6, NZ, NY), plane, plane, rows_of(6, NX, NY), plane],
        [
            vmem(5, NZ, NY), vmem(5, NZ, NY), vmem(8, NY), vmem(8, NY), vmem(2, NX, NY),
            vmem(NZ * 24, NY), vmem(5, NZ * 16, NY), vmem(5, NZ * 16, NY), vmem(2, tall, NY), vmem(2, tall, NY),
            vmem(2, CELLS, NY), vmem(CELLS, 8), vmem(CELLS, NY), vmem(CELLS, 8),
        ],
    )(state, gamma, sw, vel, press, part, *sent_y, *got_yz, *got_x, zz, hits, mean)
    got_yz = exchange_yz(sizes, *sent)
    sent = call(bind(edge_kernel, sizes), x_slabs(5), [vmem(CELLS, NY)])(state_1, lam_2, coef, *got_yz)
    got_x = exchange_x(sizes, *sent)
    lean = call(
        bind(lean_kernel, sizes),
        [rows_of(3, CELLS, NY), rows_of(3, CELLS, NY), grid, grid],
        [vmem(2, tall, NY), vmem(CELLS, 8)],
    )(state_1, lam_2, *got_yz)
    devices = sizes["gx"] * sizes["gy"] * sizes["gz"]
    gradient, rows = call(
        bind(gradient_kernel, sizes),
        [rows_of(CELLS, NY), rows_of(devices, NY)],
        [
            vmem(2, NZ * 24, NY), vmem(CELLS, NY), vmem(NZ * 24, NY), vmem(CELLS, NY),
            vmem(CELLS, 8), vmem(2, NZ * 24, NY), vmem(CELLS, NY), vmem(2, tall, NY),
        ],
    )(vel, heat, state_1, gamma, *lean, lam_2, coef, coef_halo, beside, yown, *got_yz, *got_x, mis, spread)
    rows = lax.all_to_all(rows, ("gx", "gy", "gz"), 0, 0, tiled=True)
    direction, misfit = pl.pallas_call(
        bind(scale_kernel, devices, probes.shape[0]),
        out_shape=[rows_of(CELLS, NY), rows_of(1, 1)],
        out_specs=[pl.BlockSpec(memory_space=pltpu.VMEM), pl.BlockSpec(memory_space=pltpu.SMEM)],
        compiler_params=SMALL,
    )(gradient, rows)
    return direction.reshape(NZ, NX, NY), misfit.reshape(())


def solution(mesh):
    block = P("gz", "gx", "gy")
    parted = P(None, "gz", "gx", "gy")
    listed = P(("gx", "gy", "gz"))
    return jax.shard_map(
        functools.partial(local, dict(mesh.shape)),
        mesh=mesh,
        in_specs=(parted, block, parted, listed, listed),
        out_specs=(block, P()),
        check_vma=False,
    )
```

```python
import functools
import jax
import jax.numpy as jnp
from jax import lax
from jax.experimental import pallas as pl
from jax.experimental.pallas import tpu as pltpu
from jax.sharding import PartitionSpec as P

NZ, NX, NY = 16, 8, 128
CELLS = NZ * NX
bulk_modulus = 2.0
slope_coeff = 1.5
signal_speed = 2.5
time_ratio = 0.1
quad_viscosity = 4.0
small_eps = 1e-12
HALF_C = 0.5 * signal_speed
HALF_T = 0.5 * time_ratio
NEAR = time_ratio * HALF_C
STAY = 1.0 - 3.0 * time_ratio * signal_speed
F32 = jnp.float32


def primitives(r, mx, my, mz, en, gamma):
    inv = 1.0 / (1.0 + r)
    ux, uy, uz = mx * inv, my * inv, mz * inv
    heat = en - 0.5 * (mx * ux + my * uy + mz * uz)
    press = bulk_modulus * (r + slope_coeff * r * r) + gamma * heat
    return ux, uy, uz, heat, press


def total_pressure(press, sw, r, slope):
    squeeze = jnp.minimum(slope, 0.0)
    return press + sw * quad_viscosity * (1.0 + r) * squeeze * squeeze


def flux(state, axis, speed, total):
    rows = [state[1 + axis]] + [state[1 + k] * speed for k in range(3)]
    rows[1 + axis] = rows[1 + axis] + total
    return rows + [(state[4] + total) * speed]


def upper_part(f, u):
    return 0.5 * f - HALF_C * u


def lower_part(f, u):
    return 0.5 * f + HALF_C * u


def layer(z):
    return pl.ds(NX * z, NX)


def x_row(x):
    return pl.ds(x, NZ, stride=NX)


def lanes():
    return lax.broadcasted_iota(jnp.int32, (NX, NY), 1)


def y_next(value, column, lane):
    return jnp.where(lane == NY - 1, column, pltpu.roll(value, NY - 1, 1))


def y_prev(value, column, lane):
    return jnp.where(lane == 0, column, pltpu.roll(value, 1, 1))


def inside(flag):
    return jnp.where(flag, 1.0, 0.0).astype(F32)


def masks(mesh):
    ix, iy, iz = lax.axis_index("gx"), lax.axis_index("gy"), lax.axis_index("gz")
    return (
        (inside(ix > 0), inside(ix < mesh["gx"] - 1)),
        (inside(iy > 0), inside(iy < mesh["gy"] - 1)),
        (inside(iz > 0), inside(iz < mesh["gz"] - 1)),
        iz == 0,
    )


def face_layer(is_first, depth):
    return jnp.where(is_first, NZ - 1 - depth, depth)


def dyn_layer(z):
    return pl.ds(pl.multiple_of(NX * z, NX), NX)


def pack_edges(values, lane, depth=2):
    out = pltpu.roll(values[0], depth, 1)
    for i in range(1, len(values)):
        out = jnp.where(lane < 2 * depth * i, out, pltpu.roll(values[i], depth * (2 * i + 1), 1))
    return out


def begun(u, f, far, sign):
    return STAY * u + time_ratio * (sign * 0.5 * f + HALF_C * far)


def prep_kernel(mesh, u_ref, g_ref, s_ref, ylo, yhi, zs, yp):
    _, _, _, first = masks(mesh)
    lane = lanes()
    for z in range(NZ):
        vals = [u_ref[k, layer(z), :] for k in range(5)]
        vals += [g_ref[layer(z), :], s_ref[0, layer(z), :].astype(F32)]
        yp[layer(z), :] = pack_edges(vals, lane, 3)
    rows = yp[...].T
    for out, c1, c2, c3, sign in ((yhi, 2, 1, 0, 1.0), (ylo, 3, 4, 5, -1.0)):
        st, st2, st3 = [[rows[6 * k + c : 6 * k + c + 1] for k in range(7)] for c in (c1, c2, c3)]
        prim, prim2 = primitives(*st[:6]), primitives(*st2[:6])
        slope = (sign * 0.5) * (prim[1] - st3[2] / (1.0 + st3[0]))
        fl = flux(st2[:5], 1, prim2[1], total_pressure(prim2[4], st2[6], st2[0], slope))
        items = st[:5] + [prim[4], st[6], prim2[1]] + [begun(st[k], fl[k], st2[k], sign) for k in range(3)]
        for k in range(11):
            out[k : k + 1] = items[k]
        out[11:16] = jnp.zeros((5, NY), F32)
    za, zb, zc = [dyn_layer(face_layer(first, d)) for d in range(3)]
    sign = jnp.where(first, 1.0, -1.0)
    st, st2 = [[u_ref[k, at, :] for k in range(5)] for at in (za, zb)]
    prim, prim2 = primitives(*st, g_ref[za, :]), primitives(*st2, g_ref[zb, :])
    slope = (sign * 0.5) * (prim[2] - u_ref[3, zc, :] / (1.0 + u_ref[0, zc, :]))
    fl = flux(st2, 2, prim2[2], total_pressure(prim2[4], s_ref[0, zb, :].astype(F32), st2[0], slope))
    items = st + [prim[4], s_ref[0, za, :].astype(F32), prim2[2]]
    items += [begun(st[k], fl[k], st2[k], sign) for k in (0, 1, 3)]
    for k in range(11):
        zs[k] = items[k]


def still_kernel(u_ref, g_ref, s_ref, vel, heat, press, slo, shi, addlo, addhi):
    for z in range(NZ):
        prim = primitives(*[u_ref[k, layer(z), :] for k in range(5)], g_ref[layer(z), :])
        for k in range(3):
            vel[k, layer(z), :] = prim[k]
        heat[layer(z), :] = prim[3]
        press[layer(z), :] = prim[4]
    for out, add, e, i, j, last, sign in (
        (shi, addhi, NX - 1, NX - 2, NX - 3, NX - 4, 1.0),
        (slo, addlo, 0, 1, 2, 3, -1.0),
    ):
        for k in range(5):
            out[k] = u_ref[k, x_row(e), :]
        out[5] = g_ref[x_row(e), :]
        out[6] = s_ref[0, x_row(e), :].astype(F32)
        out[7] = vel[0, x_row(i), :]
        out[8] = s_ref[1, x_row(e), :].astype(F32)
        for at, before, after, base, count in ((i, e, j, 0, 5), (j, i, last, 5, 2)):
            st = [u_ref[k, x_row(at), :] for k in range(5)]
            slope = (sign * 0.5) * (vel[0, x_row(before), :] - vel[0, x_row(after), :])
            total = total_pressure(press[x_row(at), :], s_ref[0, x_row(at), :].astype(F32), st[0], slope)
            fl = flux(st, 0, vel[0, x_row(at), :], total)
            for k in range(count):
                add[base + k] = time_ratio * (sign * 0.5 * fl[k] + HALF_C * st[k])


def side_kernel(
    mesh, u_ref, s_ref, vel, pr, addlo, addhi, ylo, yhi, yl, yh, zr,
    part, xlo, xhi, zz,
    vz, az, bz, yr, yc,
):
    _, (myl, myh), (mzl, mzh), first = masks(mesh)
    lane = lanes()
    for z in range(NZ):
        vz[layer(z + 1), :] = vel[2, layer(z), :]
    far = [zr[k] for k in range(8)]
    speed = far[3] / (1.0 + far[0])
    own = vel[2, dyn_layer(face_layer(first, 0)), :]
    slope = (far[7] - own) * jnp.where(first, 0.5, -0.5)
    fl = flux(far[:5], 2, speed, total_pressure(far[5], far[6], far[0], slope))
    for k in range(5):
        bz[k, layer(0), :] = lower_part(fl[k], far[k]) * mzl
        az[k, layer(NZ), :] = upper_part(fl[k], far[k]) * mzh
    vz[layer(0), :] = speed * mzl
    vz[layer(NZ + 1), :] = speed * mzh
    low = [yl[k : k + 1] * myl for k in range(8)]
    high = [yh[k : k + 1] * myh for k in range(8)]
    speed = low[2] / (1.0 + low[0])
    yr[10:11, :] = speed
    slope = 0.5 * (ylo[2:3] / (1.0 + ylo[0:1]) - low[7])
    fl = flux(low[:5], 1, speed, total_pressure(low[5], low[6], low[0], slope))
    for k in range(5):
        yr[k : k + 1, :] = lower_part(fl[k], low[k])
    speed = high[2] / (1.0 + high[0])
    yr[11:12, :] = speed
    slope = 0.5 * (high[7] - yhi[2:3] / (1.0 + yhi[0:1]))
    fl = flux(high[:5], 1, speed, total_pressure(high[5], high[6], high[0], slope))
    for k in range(5):
        yr[5 + k : 6 + k, :] = upper_part(fl[k], high[k])
    yr[12:16, :] = jnp.zeros((4, NY), F32)
    yc[...] = yr[...].T
    for z in range(NZ):
        st = [u_ref[k, layer(z), :] for k in range(5)]
        press = pr[layer(z), :]
        visc = s_ref[0, layer(z), :].astype(F32) * quad_viscosity * (1.0 + st[0])
        uy, uz = vel[1, layer(z), :], vel[2, layer(z), :]

        def col(i):
            return yc[layer(z), i : i + 1]

        def total(up, down):
            squeeze = jnp.minimum(0.5 * (up - down), 0.0)
            return press + visc * squeeze * squeeze

        fy = flux(st, 1, uy, total(y_next(uy, col(11), lane), y_prev(uy, col(10), lane)))
        fz = flux(st, 2, uz, total(vz[layer(z + 2), :], vz[layer(z), :]))
        for k in range(5):
            az[k, layer(z), :] = upper_part(fz[k], st[k])
            bz[k, layer(z + 1), :] = lower_part(fz[k], st[k])
            part[k, layer(z), :] = STAY * st[k] - time_ratio * (
                y_next(upper_part(fy[k], st[k]), col(5 + k), lane)
                - y_prev(lower_part(fy[k], st[k]), col(k), lane)
            )
    for z in range(NZ):
        for k in range(5):
            part[k, layer(z), :] = part[k, layer(z), :] - time_ratio * (
                az[k, layer(z + 1), :] - bz[k, layer(z), :]
            )
    for k in range(8):
        zz[k : k + 1, :] = low[k]
        zz[8 + k : 9 + k, :] = high[k]
    for out, add, e, i in ((xhi, addhi, NX - 1, NX - 2), (xlo, addlo, 0, 1)):
        for k in range(5):
            out[k] = part[k, x_row(e), :] + add[k]
        for k in range(2):
            out[5 + k] = part[k, x_row(i), :] + add[5 + k]
        out[7] = zz[...]
        for k in range(8):
            out[8, k : k + 1, :] = zr[k, e : e + 1, :]
        out[8, 8:9, :] = zr[1, i : i + 1, :] / (1.0 + zr[0, i : i + 1, :])
        out[8, 9:16, :] = jnp.zeros((7, NY), F32)


def shifted_x(own, low, high, at_x):
    up = jnp.where(at_x == NX - 1, pltpu.roll(high, NX - 1, 1), pltpu.roll(own, NY - 1, 1))
    down = jnp.where(at_x == 0, pltpu.roll(low, NY - NX + 1, 1), pltpu.roll(own, 1, 1))
    return up, down


def halo_step(
    mesh, u_ref, g_ref, s_ref, vel, pr, part, ylo, yhi, yl, yh, zr, xl, xh, wl, wh, zz,
    o_ref, xc, hxl, hxh, hyl, hyh, hz, vx, ax, bx, zc,
):
    (mxl, mxh), (myl, myh), (mzl, mzh), first = masks(mesh)
    for z in range(NZ):
        vx[pl.ds(24 * z + 8, 8), :] = vel[0, layer(z), :]
    low = [xl[k] * mxl for k in range(8)]
    high = [xh[k] * mxh for k in range(8)]
    prim = primitives(*low[:6])
    vx[pl.ds(7, NZ, stride=24), :] = prim[0]
    slope = 0.5 * (vx[pl.ds(8, NZ, stride=24), :] - low[7])
    f_low = flux(low[:5], 0, prim[0], total_pressure(prim[4], low[6], low[0], slope))
    prim = primitives(*high[:6])
    vx[pl.ds(16, NZ, stride=24), :] = prim[0]
    slope = 0.5 * (high[7] - vx[pl.ds(15, NZ, stride=24), :])
    f_high = flux(high[:5], 0, prim[0], total_pressure(prim[4], high[6], high[0], slope))
    for k in range(5):
        bx[k, pl.ds(7, NZ, stride=16), :] = lower_part(f_low[k], low[k])
        ax[k, pl.ds(8, NZ, stride=16), :] = upper_part(f_high[k], high[k])
    for z in range(NZ):
        st = [u_ref[k, layer(z), :] for k in range(5)]
        ux, press = vel[0, layer(z), :], pr[layer(z), :]
        slope = 0.5 * (vx[pl.ds(24 * z + 9, 8), :] - vx[pl.ds(24 * z + 7, 8), :])
        fx = flux(st, 0, ux, total_pressure(press, s_ref[0, layer(z), :].astype(F32), st[0], slope))
        for k in range(5):
            ax[k, pl.ds(16 * z, 8), :] = upper_part(fx[k], st[k])
            bx[k, pl.ds(16 * z + 8, 8), :] = lower_part(fx[k], st[k])
    for z in range(NZ):
        for k in range(5):
            o_ref[k, layer(z), :] = part[k, layer(z), :] - time_ratio * (
                ax[k, pl.ds(16 * z + 1, 8), :] - bx[k, pl.ds(16 * z + 7, 8), :]
            )
    for out, ref, begun_ref, mask in ((hxl, xl, wl, mxl), (hxh, xh, wh, mxh)):
        if ref is xl:
            near = [-ax[k, pl.ds(0, NZ, stride=16), :] for k in range(5)]
            next_ = [-upper_part(f_low[k], low[k]) for k in range(2)]
        else:
            near = [bx[k, pl.ds(15, NZ, stride=16), :] for k in range(5)]
            next_ = [lower_part(f_high[k], high[k]) for k in range(2)]
        st = [(begun_ref[k] + time_ratio * near[k]) * mask for k in range(5)]
        st2 = [(begun_ref[5 + k] + time_ratio * next_[k]) * mask for k in range(2)]
        out[0] = st[0]
        out[1] = st[1]
        out[2] = primitives(*st, ref[5] * mask)[4]
        out[3] = ref[8] * mask
        out[4] = st2[1] / (1.0 + st2[0])
        base = 0 if ref is xl else 3
        inv, gamma = 1.0 / (1.0 + st[0]), ref[5] * mask
        xc[base] = (2.0 - gamma) * (st[1] * inv)
        xc[base + 1] = inv
        xc[base + 2] = gamma
    lane = lax.broadcasted_iota(jnp.int32, (1, NY), 1)
    at_x = lax.bitwise_and(lane, NX - 1)
    for side, ref, mask, own, out, sign in ((0, yl, myl, ylo, hyl, -1.0), (1, yh, myh, yhi, hyh, 1.0)):

        def items(values, m):
            return [values[k : k + 1] * m for k in range(8)]

        here = items(ref, mask)
        near_l, near_h = items(wl[7, 8 * side : 8 * side + 8, :], mxl), items(wh[7, 8 * side : 8 * side + 8, :], mxh)
        ux, ux_l, ux_h = [v[1] / (1.0 + v[0]) for v in (here, near_l, near_h)]
        up, down = shifted_x(ux, ux_l, ux_h, at_x)
        slope = 0.5 * (up - down)
        slope_h = 0.5 * (pltpu.roll(ux_h, NY - 1, 1) - pltpu.roll(ux, NY - NX + 1, 1))
        slope_l = 0.5 * (pltpu.roll(ux, NX - 1, 1) - pltpu.roll(ux_l, 1, 1))

        def fx_of(v, speed, slope):
            return [v[1], v[1] * speed + total_pressure(v[5], v[6], v[0], slope), v[2] * speed]

        f_here, f_l, f_h = fx_of(here, ux, slope), fx_of(near_l, ux_l, slope_l), fx_of(near_h, ux_h, slope_h)
        uz = here[3] / (1.0 + here[0])
        near_z = items(zz[8 * side : 8 * side + 8, :], 1.0)
        uz_z = near_z[3] / (1.0 + near_z[0])
        fz, fz_z = [[v[3], v[1] * w, v[2] * w] for v, w in ((here, uz), (near_z, uz_z))]
        self_ = items(own, 1.0)
        uy = self_[2] / (1.0 + self_[0])
        uy_here = here[2] / (1.0 + here[0])
        slope = 0.5 * (self_[7] - uy_here if side == 0 else uy_here - self_[7])
        fy = [self_[2], self_[1] * uy, self_[2] * uy + total_pressure(self_[5], self_[6], self_[0], slope)]
        new = []
        for k in range(3):
            a_x, _ = shifted_x(upper_part(f_here[k], here[k]), ux_l, upper_part(f_h[k], near_h[k]), at_x)
            _, b_x = shifted_x(lower_part(f_here[k], here[k]), lower_part(f_l[k], near_l[k]), ux_h, at_x)
            a_z = jnp.where(
                lane >= NY - NX,
                pltpu.roll(upper_part(fz_z[k], near_z[k]), NY - NX, 1) * mzh,
                pltpu.roll(upper_part(fz[k], here[k]), NY - NX, 1),
            )
            b_z = jnp.where(
                lane < NX,
                pltpu.roll(lower_part(fz_z[k], near_z[k]), NX, 1) * mzl,
                pltpu.roll(lower_part(fz[k], here[k]), NX, 1),
            )
            facing = sign * 0.5 * fy[k] + HALF_C * self_[k]
            new.append(mask * (ref[8 + k : 9 + k] + time_ratio * (facing - (a_x - b_x) - (a_z - b_z))))
        r, mx, my = new
        combine = lower_part if side == 0 else upper_part
        out[0:1, :] = combine(my, r)
        out[1:2, :] = combine(mx * (my / (1.0 + r)), mx)
        out[2:8, :] = jnp.zeros((6, NY), F32)
    rows = []
    for side in range(2):
        v = [zz[8 * side + k : 8 * side + k + 1, :] for k in range(8)]
        speed = v[2] / (1.0 + v[0])
        fy = [v[2], v[1] * speed, v[3] * speed]
        combine = upper_part if side else lower_part
        rows += [combine(f, v[k]) for f, k in zip(fy, (0, 1, 3))]
    zc[...] = jnp.concatenate(rows + [jnp.zeros((2, NY), F32)], axis=0).T
    cols = zc[dyn_layer(jnp.where(first, 0, NZ - 1)), :]
    full = lanes()
    deep = lax.broadcasted_iota(jnp.int32, (NX, NY), 0)
    here = [zr[k] for k in range(8)]
    near_l = [wl[8, k : k + 1, :] * mxl for k in range(9)]
    near_h = [wh[8, k : k + 1, :] * mxh for k in range(9)]
    ux, ux_l, ux_h = [v[1] / (1.0 + v[0]) for v in (here, near_l, near_h)]

    def next_x(value, row):
        return jnp.where(deep == NX - 1, row, pltpu.roll(value, NX - 1, 0))

    def prev_x(value, row):
        return jnp.where(deep == 0, row, pltpu.roll(value, 1, 0))

    slope = 0.5 * (next_x(ux, ux_h) - prev_x(ux, ux_l))
    slope_h = 0.5 * (near_h[8] - ux[NX - 1 : NX])
    slope_l = 0.5 * (ux[0:1] - near_l[8])

    def fx_layer(v, speed, slope):
        return [v[1], v[1] * speed + total_pressure(v[5], v[6], v[0], slope), v[3] * speed]

    f_here, f_l, f_h = fx_layer(here, ux, slope), fx_layer(near_l, ux_l, slope_l), fx_layer(near_h, ux_h, slope_h)
    uy = here[2] / (1.0 + here[0])
    fy = [here[2], here[1] * uy, here[3] * uy]
    za, zb = dyn_layer(face_layer(first, 0)), dyn_layer(face_layer(first, 1))
    sign = jnp.where(first, 1.0, -1.0)
    st = [u_ref[k, za, :] for k in range(5)]
    slope = (sign * 0.5) * (here[3] / (1.0 + here[0]) - vel[2, zb, :])
    fz = flux(st, 2, vel[2, za, :], total_pressure(pr[za, :], s_ref[0, za, :].astype(F32), st[0], slope))
    new = []
    for n, k in enumerate((0, 1, 3)):
        a_x = next_x(upper_part(f_here[n], here[k]), upper_part(f_h[n], near_h[k]))
        b_x = prev_x(lower_part(f_here[n], here[k]), lower_part(f_l[n], near_l[k]))
        a_y = y_next(upper_part(fy[n], here[k]), cols[:, 3 + n : 4 + n], full)
        b_y = y_prev(lower_part(fy[n], here[k]), cols[:, n : n + 1], full)
        facing = sign * 0.5 * fz[k] + HALF_C * st[k]
        new.append(zr[8 + n] + time_ratio * (facing - (a_x - b_x) - (a_y - b_y)))
    r, mx, mz = new
    hz[0] = 0.5 * mz - (sign * HALF_C) * r
    hz[1] = 0.5 * mx * (mz / (1.0 + r)) - (sign * HALF_C) * mx


def forward_kernel(
    mesh, u0_ref, g_ref, s_ref, vel, pr, part, ylo_in, yhi_in, yl, yh, zr, xl, xh, wl, wh, zz, n_ref, m_ref,
    u_ref, lam_ref, cf_ref, cfh_ref, mis_ref, xc, ylo, yhi, zs, yown,
    hxl, hxh, hyl, hyh, hz, vx, ax, bx, az, bz, ch, yc, yp, zc,
):
    halo_step(
        mesh, u0_ref, g_ref, s_ref, vel, pr, part, ylo_in, yhi_in, yl, yh, zr, xl, xh, wl, wh, zz,
        u_ref, xc, hxl, hxh, hyl, hyh, hz, vx, ax, bx, zc,
    )
    speed_kernel(
        mesh, u_ref, g_ref, s_ref, hxl, hxh, hyl, hyh, hz, n_ref, m_ref,
        lam_ref, cf_ref, cfh_ref, mis_ref, ylo, yhi, zs, yown,
        vx, ax, bx, az, bz, ch, yc, yp,
    )


def columns_of(low, high, count, low_mask, high_mask):
    rows = [low[k : k + 1] * low_mask for k in range(count)]
    rows += [high[k : k + 1] * high_mask for k in range(count)]
    rows.append(jnp.zeros((8 - 2 * count, NY), F32))
    return jnp.concatenate(rows, axis=0).T


def speed_kernel(
    mesh, u_ref, g_ref, s_ref, xl, xh, yl, yh, zr, n_ref, m_ref,
    lam_ref, cf_ref, cfh_ref, mis_ref, ylo, yhi, zs, yown,
    vx, ax, bx, az, bz, ch, yc, yp,
):
    (mxl, mxh), (myl, myh), (mzl, mzh), first = masks(mesh)
    lane = lanes()
    for z in range(NZ):
        vx[pl.ds(24 * z + 8, 8), :] = u_ref[1, layer(z), :] / (1.0 + u_ref[0, layer(z), :])
    for side, ref, mask in ((0, xl, mxl), (1, xh, mxh)):
        r, mx, press, sw, second = [ref[k] * mask for k in range(5)]
        speed = mx / (1.0 + r)
        vx[pl.ds(16 if side else 7, NZ, stride=24), :] = speed
        own = vx[pl.ds(15 if side else 8, NZ, stride=24), :]
        slope = 0.5 * (second - own if side else own - second)
        squeeze = jnp.minimum(slope, 0.0)
        visc = sw * quad_viscosity * (1.0 + r) * squeeze
        cfh_ref[side] = 2.0 * visc
        f1 = mx * speed + press + visc * squeeze
        if side:
            ax[0, pl.ds(8, NZ, stride=16), :] = upper_part(mx, r)
            ax[1, pl.ds(8, NZ, stride=16), :] = upper_part(f1, mx)
        else:
            bx[0, pl.ds(7, NZ, stride=16), :] = lower_part(mx, r)
            bx[1, pl.ds(7, NZ, stride=16), :] = lower_part(f1, mx)
    for k in range(2):
        bz[k, layer(0), :] = zr[k] * mzl
        az[k, layer(NZ), :] = zr[k] * mzh
    yc[...] = columns_of(yl, yh, 2, myl, myh)
    for z in range(NZ):
        r, mx, my, mz, en = [u_ref[k, layer(z), :] for k in range(5)]
        ux, uy, uz, _, press = primitives(r, mx, my, mz, en, g_ref[layer(z), :])
        squeeze = jnp.minimum(0.5 * (vx[pl.ds(24 * z + 9, 8), :] - vx[pl.ds(24 * z + 7, 8), :]), 0.0)
        visc = s_ref[1, layer(z), :].astype(F32) * quad_viscosity * (1.0 + r) * squeeze
        cf_ref[layer(z), :] = 2.0 * visc
        f1 = mx * ux + press + visc * squeeze
        for k, st, fx, fy, fz in ((0, r, mx, my, mz), (1, mx, f1, mx * uy, mx * uz)):
            ax[k, pl.ds(16 * z, 8), :] = upper_part(fx, st)
            bx[k, pl.ds(16 * z + 8, 8), :] = lower_part(fx, st)
            az[k, layer(z), :] = upper_part(fz, st)
            bz[k, layer(z + 1), :] = lower_part(fz, st)
            ch[k, layer(z), :] = (
                3.0 * signal_speed * st
                + y_next(upper_part(fy, st), yc[layer(z), 2 + k : 3 + k], lane)
                - y_prev(lower_part(fy, st), yc[layer(z), k : k + 1], lane)
            )
    mis = jnp.zeros((NX, NY), F32)
    for z in range(NZ):
        new = []
        for k in range(2):
            change = (
                ch[k, layer(z), :]
                + (ax[k, pl.ds(16 * z + 1, 8), :] - bx[k, pl.ds(16 * z + 7, 8), :])
                + (az[k, layer(z + 1), :] - bz[k, layer(z), :])
            )
            new.append(u_ref[k, layer(z), :] - time_ratio * change)
        inv = 1.0 / (1.0 + new[0])
        speed = new[1] * inv
        off = speed - m_ref[layer(z), :]
        weight = n_ref[layer(z), :] * off
        mis = mis + weight * off
        lam_m = 2.0 * weight * inv
        lam_r = -lam_m * speed
        lam_ref[0, layer(z), :] = lam_r
        lam_ref[1, layer(z), :] = lam_m
        inv = 1.0 / (1.0 + u_ref[0, layer(z), :])
        extra = [u_ref[1, layer(z), :] * inv, u_ref[2, layer(z), :] * inv, g_ref[layer(z), :]]
        yp[layer(z), :] = pack_edges([lam_r, lam_m] + extra, lane)
    mis_ref[...] = mis
    za, zb = dyn_layer(face_layer(first, 0)), dyn_layer(face_layer(first, 1))
    inv = 1.0 / (1.0 + u_ref[0, za, :])
    ux = u_ref[1, za, :] * inv
    zs[0] = lam_ref[0, za, :]
    zs[1] = lam_ref[1, za, :]
    zs[2] = jnp.where(first, -HALF_T, HALF_T) * (lam_ref[0, zb, :] + lam_ref[1, zb, :] * ux)
    zs[3] = ux
    zs[4] = u_ref[3, za, :] * inv
    zs[5] = g_ref[za, :]
    rows = yp[...].T
    for out, edge, second, own, sign in ((yhi, 1, 0, 2, -HALF_T), (ylo, 2, 3, 0, HALF_T)):
        lam_r, lam_m, ux, uy, gamma = [rows[4 * i + edge : 4 * i + edge + 1] for i in range(5)]
        out[0:1] = lam_r
        out[1:2] = lam_m
        out[2:3] = sign * (rows[second : second + 1] + rows[4 + second : 5 + second] * ux)
        out[3:4] = ux
        out[4:5] = uy
        out[5:6] = gamma
        out[6:8] = jnp.zeros((2, NY), F32)
        yown[own : own + 1] = lam_r
        yown[own + 1 : own + 2] = lam_m
    yown[4:8] = jnp.zeros((4, NY), F32)


def edge_kernel(mesh, u_ref, lam_ref, cf_ref, yl, yh, zr, xlo, xhi, yc):
    _, (myl, myh), (mzl, mzh), _ = masks(mesh)
    low_y, high_y = yl[1:2] * myl, yh[1:2] * myh
    yc[:, 0:8] = jnp.concatenate([low_y, high_y, jnp.zeros((6, NY), F32)], axis=0).T
    lane = lax.broadcasted_iota(jnp.int32, (NZ, NY), 1)
    deep = lax.broadcasted_iota(jnp.int32, (NZ, NY), 0)
    for out, e, i, i2, sign in ((xhi, NX - 1, NX - 2, NX - 3, 1.0), (xlo, 0, 1, 2, -1.0)):
        r, my, mz = [u_ref[k, x_row(e), :] for k in (0, 2, 3)]
        inv = 1.0 / (1.0 + r)
        lm, lm_i = lam_ref[1, x_row(e), :], lam_ref[1, x_row(i), :]
        col = yc[x_row(e), :]
        side = zr[1, e : e + 1, :]
        up_y = jnp.where(lane == NY - 1, col[:, 1:2], pltpu.roll(lm, NY - 1, 1))
        down_y = jnp.where(lane == 0, col[:, 0:1], pltpu.roll(lm, 1, 1))
        up_z = jnp.where(deep == NZ - 1, side * mzh, pltpu.roll(lm, NZ - 1, 0))
        down_z = jnp.where(deep == 0, side * mzl, pltpu.roll(lm, 1, 0))
        slope = (sign * HALF_T) * (lm - lam_ref[1, x_row(i2), :]) * cf_ref[x_row(i), :]
        out[0] = lam_ref[0, x_row(e), :]
        out[1] = lm
        out[2] = lm_i
        out[3] = (
            STAY * lm
            + NEAR * (lm_i + (up_y + down_y) + (up_z + down_z))
            - (sign * HALF_T) * lam_ref[0, x_row(i), :]
            + HALF_T * ((up_y - down_y) * (my * inv) + (up_z - down_z) * (mz * inv))
            + (sign * 0.5) * slope * inv
        )
        out[4] = jnp.where(deep == 0, low_y, jnp.where(deep == 1, high_y, jnp.where(deep == 2, side, 0.0)))


def lean_kernel(mesh, u_ref, lam_ref, yl, yh, zr, base, vel, inv_ref, heat, lz, yc):
    _, (myl, myh), (mzl, mzh), _ = masks(mesh)
    lane = lanes()
    for k in range(2):
        for z in range(NZ):
            lz[k, layer(z + 1), :] = lam_ref[k, layer(z), :]
        lz[k, layer(0), :] = zr[k] * mzl
        lz[k, layer(NZ + 1), :] = zr[k] * mzh
    yc[...] = columns_of(yl, yh, 2, myl, myh)
    for z in range(NZ):
        r, mx, my, mz, en = [u_ref[k, layer(z), :] for k in range(5)]
        inv = 1.0 / (1.0 + r)
        ux, uy, uz = mx * inv, my * inv, mz * inv
        heat[layer(z), :] = en - 0.5 * (mx * ux + my * uy + mz * uz)
        inv_ref[layer(z), :] = inv
        for k, value in enumerate((ux, uy, uz)):
            vel[k, layer(z), :] = value
        lr, lm = lam_ref[0, layer(z), :], lam_ref[1, layer(z), :]
        lr_z = [lz[0, layer(z + s), :] for s in (0, 2)]
        lm_z = [lz[1, layer(z + s), :] for s in (0, 2)]
        lr_y = [y_prev(lr, yc[layer(z), 0:1], lane), y_next(lr, yc[layer(z), 2:3], lane)]
        lm_y = [y_prev(lm, yc[layer(z), 1:2], lane), y_next(lm, yc[layer(z), 3:4], lane)]
        phi_y1 = HALF_T * (lm_y[1] - lm_y[0])
        phi_z1 = HALF_T * (lm_z[1] - lm_z[0])
        near = (lm_y[0] + lm_y[1]) + (lm_z[0] + lm_z[1])
        base[0, layer(z), :] = STAY * lm + NEAR * near + phi_y1 * uy + phi_z1 * uz
        base[1, layer(z), :] = HALF_T * (lr_y[1] - lr_y[0]) + phi_y1 * ux
        base[2, layer(z), :] = HALF_T * (lr_z[1] - lr_z[0]) + phi_z1 * ux


def gradient_kernel(
    mesh, vel, heat_ref, u_ref, g_ref, base, vel_1, inv_1, heat_1, lam_ref, cf_ref, cfh_ref, xc, yown, yl, yh, zr, xl, xh, mis_ref, v_ref,
    grad_ref, row_ref,
    lx, px, dx, dg, yc, gx, gy, gz,
):
    (mxl, mxh), (myl, myh), (mzl, mzh), first = masks(mesh)
    lane = lanes()
    for k in range(2):
        for z in range(NZ):
            lx[k, pl.ds(24 * z + 8, 8), :] = lam_ref[k, layer(z), :]
        lx[k, pl.ds(7, NZ, stride=24), :] = xl[k] * mxl
        lx[k, pl.ds(16, NZ, stride=24), :] = xh[k] * mxh
    phi_low = HALF_T * (lam_ref[1, x_row(0), :] - xl[2] * mxl)
    phi_high = HALF_T * (xh[2] * mxh - lam_ref[1, x_row(NX - 1), :])
    dx[pl.ds(7, NZ, stride=24), :] = phi_low * cfh_ref[0]
    dx[pl.ds(16, NZ, stride=24), :] = phi_high * cfh_ref[1]
    for z in range(NZ):
        phi = HALF_T * (lx[1, pl.ds(24 * z + 9, 8), :] - lx[1, pl.ds(24 * z + 7, 8), :])
        px[layer(z), :] = phi
        dx[pl.ds(24 * z + 8, 8), :] = phi * cf_ref[layer(z), :]
    gx[1, pl.ds(7, NZ, stride=24), :] = mxl * phi_low * xc[2]
    gx[1, pl.ds(16, NZ, stride=24), :] = mxh * phi_high * xc[5]
    gx[0, pl.ds(7, NZ, stride=24), :] = mxl * (
        xl[3]
        + HALF_T * lam_ref[0, x_row(0), :]
        + NEAR * lam_ref[1, x_row(0), :]
        + phi_low * xc[0]
        - 0.5 * dx[pl.ds(8, NZ, stride=24), :] * xc[1]
    )
    gx[0, pl.ds(16, NZ, stride=24), :] = mxh * (
        xh[3]
        - HALF_T * lam_ref[0, x_row(NX - 1), :]
        + NEAR * lam_ref[1, x_row(NX - 1), :]
        + phi_high * xc[3]
        + 0.5 * dx[pl.ds(15, NZ, stride=24), :] * xc[4]
    )
    at_x = lax.bitwise_and(lax.broadcasted_iota(jnp.int32, (1, NY), 1), NX - 1)
    from_high, from_low = pltpu.roll(xh[4], NX - 1, 1) * mxh, pltpu.roll(xl[4], NY - NX + 1, 1) * mxl
    halo = []
    for side, ref, mask, sign in ((0, yl, myl, HALF_T), (1, yh, myh, -HALF_T)):
        items = ref[...]
        up = jnp.where(at_x == NX - 1, from_high[side : side + 1], pltpu.roll(items, NY - 1, 1)[1:2])
        down = jnp.where(at_x == 0, from_low[side : side + 1], pltpu.roll(items, 1, 1)[1:2])
        d_en = HALF_T * (up - down) * items[5:6]
        own_r, own_m = yown[2 * side : 2 * side + 1], yown[2 * side + 1 : 2 * side + 2]
        d_my = items[2:3] + sign * (own_r + own_m * items[3:4]) - d_en * items[4:5]
        halo += [d_my * mask, d_en * mask]
    yc[...] = jnp.concatenate(halo + [jnp.zeros((4, NY), F32)], axis=0).T
    deep = lax.broadcasted_iota(jnp.int32, (NX, NY), 0)
    up = jnp.where(deep == NX - 1, xh[4, 2:3, :] * mxh, pltpu.roll(zr[1], NX - 1, 0))
    down = jnp.where(deep == 0, xl[4, 2:3, :] * mxl, pltpu.roll(zr[1], 1, 0))
    d_en = HALF_T * (up - down) * zr[5]
    za = dyn_layer(face_layer(first, 0))
    d_mz = (
        zr[2]
        + jnp.where(first, -HALF_T, HALF_T) * (lam_ref[0, za, :] + lam_ref[1, za, :] * zr[3])
        - d_en * zr[4]
    )
    for k, value in ((0, d_mz), (1, d_en)):
        gz[k, layer(0), :] = value * mzl
        gz[k, layer(NZ + 1), :] = value * mzh
    for z in range(NZ):
        ux, uy, uz = [vel_1[k, layer(z), :] for k in range(3)]
        lr_x = [lx[0, pl.ds(24 * z + s, 8), :] for s in (7, 9)]
        lm_x = [lx[1, pl.ds(24 * z + s, 8), :] for s in (7, 9)]
        phi_x1 = px[layer(z), :]
        d_speed = phi_x1 * u_ref[1, layer(z), :] + 0.5 * (dx[pl.ds(24 * z + 7, 8), :] - dx[pl.ds(24 * z + 9, 8), :])
        d_en = phi_x1 * g_ref[layer(z), :]
        gx[0, pl.ds(24 * z + 8, 8), :] = (
            base[0, layer(z), :]
            + NEAR * (lm_x[0] + lm_x[1])
            + HALF_T * (lr_x[1] - lr_x[0])
            + (phi_x1 - d_en) * ux
            + d_speed * inv_1[layer(z), :]
        )
        gx[1, pl.ds(24 * z + 8, 8), :] = d_en
        gy[layer(z), :] = base[1, layer(z), :] - d_en * uy
        gz[0, layer(z + 1), :] = base[2, layer(z), :] - d_en * uz
        gz[1, layer(z + 1), :] = d_en
        dg[layer(z), :] = phi_x1 * heat_1[layer(z), :]
    acc = jnp.zeros((NX, NY), F32)
    for z in range(NZ):
        ux, uy, uz = [vel[k, layer(z), :] for k in range(3)]
        heat = heat_ref[layer(z), :]
        dif_x = [gx[k, pl.ds(24 * z + 9, 8), :] - gx[k, pl.ds(24 * z + 7, 8), :] for k in range(2)]
        dif_z = [gz[k, layer(z + 2), :] - gz[k, layer(z), :] for k in range(2)]
        dif_y = []
        for k, own in ((0, gy[layer(z), :]), (1, gz[1, layer(z + 1), :])):
            dif_y.append(
                y_next(own, yc[layer(z), 2 + k : 3 + k], lane) - y_prev(own, yc[layer(z), k : k + 1], lane)
            )
        d_press = HALF_T * (
            (dif_x[0] + ux * dif_x[1]) + (dif_y[0] + uy * dif_y[1]) + (dif_z[0] + uz * dif_z[1])
        )
        grad = dg[layer(z), :] + d_press * heat
        grad_ref[layer(z), :] = grad
        acc = acc + grad * grad
    total = jnp.sum(jnp.sum(acc, axis=0, keepdims=True), axis=1, keepdims=True)
    miss = jnp.sum(jnp.sum(mis_ref[...], axis=0, keepdims=True), axis=1, keepdims=True)
    miss = miss + jnp.sum(v_ref[...], axis=1, keepdims=True)
    row = jnp.where(lane == 0, total, jnp.where(lane == 1, miss, 0.0))
    for i in range(row_ref.shape[0] // NX):
        row_ref[layer(i), :] = row


def scale_kernel(devices, count, grad_ref, rows_ref, out_ref, misfit_ref):
    acc = rows_ref[layer(0), :]
    for i in range(1, devices // NX):
        acc = acc + rows_ref[layer(i), :]
    row = jnp.sum(acc, axis=0, keepdims=True)
    misfit_ref[0, 0] = row[0, 1] / (devices * count)
    scale = 1.0 / jnp.sqrt(row[0:1, 0:1] / (devices * CELLS * NY) + small_eps)
    out_ref[...] = grad_ref[...] * scale


def split3(value):
    hi = value.astype(jnp.bfloat16)
    rest = value - hi.astype(F32)
    mid = rest.astype(jnp.bfloat16)
    low = (rest - mid.astype(F32)).astype(jnp.bfloat16)
    return hi, mid, low


def probe_kernel(p_ref, o_ref, n_ref, m_ref, v_ref):
    count = p_ref.shape[1]
    probes, obs = p_ref[...], o_ref[...]
    row = lax.broadcasted_iota(jnp.int32, (CELLS, count), 0)
    on_a = row == lax.shift_right_logical(probes, 7)
    on_b = row == lax.bitwise_and(probes, NY - 1)
    one_a = jnp.where(on_a, 1.0, 0.0).astype(jnp.bfloat16)
    one_b = jnp.where(on_b, 1.0, 0.0).astype(jnp.bfloat16)

    def nt(a, b):
        return lax.dot_general(a, b, (((1,), (1,)), ((), ())), preferred_element_type=F32)

    parts = [jnp.where(on_a, part.astype(F32), 0.0).astype(jnp.bfloat16) for part in split3(obs)]
    hits = nt(one_a, one_b)
    sums = nt(parts[0], one_b) + (nt(parts[1], one_b) + nt(parts[2], one_b))
    n_ref[...] = hits
    mean = sums / jnp.maximum(hits, 1.0)
    m_ref[...] = mean
    mean_t = split3(mean.T)
    picked = sum(jnp.dot(part, one_a, preferred_element_type=F32) for part in reversed(mean_t))
    at_probe = jnp.sum(jnp.where(on_b, picked, 0.0), axis=0, keepdims=True)
    off = obs - at_probe
    v_ref[...] = off * off


SMALL = pltpu.CompilerParams(vmem_limit_bytes=12 * 1024 * 1024)

LARGE = pltpu.CompilerParams(vmem_limit_bytes=55168 * 1024)


def rows_of(*shape):
    return jax.ShapeDtypeStruct(shape, F32)


def vmem(*shape):
    return pltpu.VMEM(shape, F32)


def call(kernel, outs, scratch, params=SMALL):
    return pl.pallas_call(
        kernel,
        out_shape=outs,
        scratch_shapes=scratch,
        cost_estimate=pl.CostEstimate(flops=100000, bytes_accessed=100000, transcendentals=0),
        compiler_params=params,
    )


def ring(sizes, axis, step):
    n = sizes[axis]
    return [(i, (i + step) % n) for i in range(n)]


def exchange_x(sizes, xlo, xhi):
    return (
        lax.ppermute(xhi, "gx", ring(sizes, "gx", 1)),
        lax.ppermute(xlo, "gx", ring(sizes, "gx", -1)),
    )


def exchange_z(sizes, zs):
    return lax.ppermute(zs, "gz", ring(sizes, "gz", 1))


def exchange_yz(sizes, ylo, yhi, zs):
    zr = exchange_z(sizes, zs)
    yl = lax.ppermute(yhi, "gy", ring(sizes, "gy", 1))
    yh = lax.ppermute(ylo, "gy", ring(sizes, "gy", -1))
    return yl, yh, zr


def local(sizes, checkpoint, gruneisen, switch, probes, observed):
    bind = functools.partial
    state = checkpoint.reshape(5, CELLS, NY)
    gamma = gruneisen.reshape(CELLS, NY)
    sw = switch.reshape(2, CELLS, NY)
    plane = rows_of(8, NY)

    def x_slabs(items):
        return [rows_of(items, NZ, NY)] * 2

    pair = rows_of(16, NY)
    tall = (NZ + 2) * NX
    *sent_y, sent_z = call(
        bind(prep_kernel, sizes), [pair, pair, rows_of(11, NX, NY)], [vmem(CELLS, NY)], LARGE
    )(state, gamma, sw)
    got_yz = exchange_yz(sizes, *sent_y, sent_z)
    hits, mean, spread = call(
        probe_kernel,
        [rows_of(CELLS, NY), rows_of(CELLS, NY), rows_of(1, probes.shape[0])],
        [],
    )(probes.reshape(1, -1), observed.reshape(1, -1))
    grid = rows_of(CELLS, NY)
    vel, heat, press, slo, shi, *adds = call(still_kernel, [rows_of(3, CELLS, NY), grid, grid] + x_slabs(9) + x_slabs(7), [])(
        state, gamma, sw
    )
    got_still = exchange_x(sizes, slo, shi)
    part, xlo, xhi, zz = call(
        bind(side_kernel, sizes),
        [rows_of(5, CELLS, NY)] + x_slabs(9) + [pair],
        [
            vmem(tall, NY), vmem(5, tall, NY), vmem(5, tall, NY), vmem(16, NY), vmem(CELLS, 16),
        ],
    )(state, sw, vel, press, *adds, *sent_y, *got_yz)
    got_x = exchange_x(sizes, xlo, xhi)
    zz = exchange_z(sizes, zz)
    state_1, lam_2, coef, coef_halo, mis, beside, *sent, yown = call(
        bind(forward_kernel, sizes),
        [rows_of(5, CELLS, NY), rows_of(2, CELLS, NY), rows_of(CELLS, NY), rows_of(2, NZ, NY), plane]
        + [rows_of(6, NZ, NY), plane, plane, rows_of(6, NX, NY), plane],
        [
            vmem(5, NZ, NY), vmem(5, NZ, NY), vmem(8, NY), vmem(8, NY), vmem(2, NX, NY),
            vmem(NZ * 24, NY), vmem(5, NZ * 16, NY), vmem(5, NZ * 16, NY), vmem(2, tall, NY), vmem(2, tall, NY),
            vmem(2, CELLS, NY), vmem(CELLS, 8), vmem(CELLS, NY), vmem(CELLS, 8),
        ],
    )(state, gamma, sw, vel, press, part, *sent_y, *got_yz, *got_still, *got_x, zz, hits, mean)
    got_yz = exchange_yz(sizes, *sent)
    sent = call(bind(edge_kernel, sizes), x_slabs(5), [vmem(CELLS, NY)])(state_1, lam_2, coef, *got_yz)
    got_x = exchange_x(sizes, *sent)
    lean = call(
        bind(lean_kernel, sizes),
        [rows_of(3, CELLS, NY), rows_of(3, CELLS, NY), grid, grid],
        [vmem(2, tall, NY), vmem(CELLS, 8)],
    )(state_1, lam_2, *got_yz)
    devices = sizes["gx"] * sizes["gy"] * sizes["gz"]
    gradient, rows = call(
        bind(gradient_kernel, sizes),
        [rows_of(CELLS, NY), rows_of(devices, NY)],
        [
            vmem(2, NZ * 24, NY), vmem(CELLS, NY), vmem(NZ * 24, NY), vmem(CELLS, NY),
            vmem(CELLS, 8), vmem(2, NZ * 24, NY), vmem(CELLS, NY), vmem(2, tall, NY),
        ],
    )(vel, heat, state_1, gamma, *lean, lam_2, coef, coef_halo, beside, yown, *got_yz, *got_x, mis, spread)
    rows = lax.all_to_all(rows, ("gx", "gy", "gz"), 0, 0, tiled=True)
    direction, misfit = pl.pallas_call(
        bind(scale_kernel, devices, probes.shape[0]),
        out_shape=[rows_of(CELLS, NY), rows_of(1, 1)],
        out_specs=[pl.BlockSpec(memory_space=pltpu.VMEM), pl.BlockSpec(memory_space=pltpu.SMEM)],
        compiler_params=SMALL,
    )(gradient, rows)
    return direction.reshape(NZ, NX, NY), misfit.reshape(())


def solution(mesh):
    block = P("gz", "gx", "gy")
    parted = P(None, "gz", "gx", "gy")
    listed = P(("gx", "gy", "gz"))
    return jax.shard_map(
        functools.partial(local, dict(mesh.shape)),
        mesh=mesh,
        in_specs=(parted, block, parted, listed, listed),
        out_specs=(block, P()),
        check_vma=False,
    )
```

```python
import functools
import jax
import jax.numpy as jnp
from jax import lax
from jax.experimental import pallas as pl
from jax.experimental.pallas import tpu as pltpu
from jax.sharding import PartitionSpec as P

NZ, NX, NY = 16, 8, 128
CELLS = NZ * NX
bulk_modulus = 2.0
slope_coeff = 1.5
signal_speed = 2.5
time_ratio = 0.1
quad_viscosity = 4.0
small_eps = 1e-12
HALF_C = 0.5 * signal_speed
HALF_T = 0.5 * time_ratio
NEAR = time_ratio * HALF_C
STAY = 1.0 - 3.0 * time_ratio * signal_speed
F32 = jnp.float32
NARROW = 8


def primitives(r, mx, my, mz, en, gamma):
    inv = 1.0 / (1.0 + r)
    ux, uy, uz = mx * inv, my * inv, mz * inv
    heat = en - 0.5 * (mx * ux + my * uy + mz * uz)
    press = bulk_modulus * (r + slope_coeff * r * r) + gamma * heat
    return ux, uy, uz, heat, press


def total_pressure(press, sw, r, slope):
    squeeze = jnp.minimum(slope, 0.0)
    return press + sw * quad_viscosity * (1.0 + r) * squeeze * squeeze


def flux(state, axis, speed, total):
    rows = [state[1 + axis]] + [state[1 + k] * speed for k in range(3)]
    rows[1 + axis] = rows[1 + axis] + total
    return rows + [(state[4] + total) * speed]


def upper_part(f, u):
    return 0.5 * f - HALF_C * u


def lower_part(f, u):
    return 0.5 * f + HALF_C * u


def layer(z):
    return pl.ds(NX * z, NX)


def x_row(x):
    return pl.ds(x, NZ, stride=NX)


def lanes():
    return lax.broadcasted_iota(jnp.int32, (NX, NY), 1)


def y_next(value, column, lane):
    return jnp.where(lane == NY - 1, column, pltpu.roll(value, NY - 1, 1))


def y_prev(value, column, lane):
    return jnp.where(lane == 0, column, pltpu.roll(value, 1, 1))


def inside(flag):
    return jnp.where(flag, 1.0, 0.0).astype(F32)


def masks(mesh):
    ix, iy, iz = lax.axis_index("gx"), lax.axis_index("gy"), lax.axis_index("gz")
    return (
        (inside(ix > 0), inside(ix < mesh["gx"] - 1)),
        (inside(iy > 0), inside(iy < mesh["gy"] - 1)),
        (inside(iz > 0), inside(iz < mesh["gz"] - 1)),
        iz == 0,
    )


def face_layer(is_first, depth):
    return jnp.where(is_first, NZ - 1 - depth, depth)


def dyn_layer(z):
    return pl.ds(pl.multiple_of(NX * z, NX), NX)


def pack_edges(values, lane, depth=2):
    out = pltpu.roll(values[0], depth, 1)
    for i in range(1, len(values)):
        out = jnp.where(lane < 2 * depth * i, out, pltpu.roll(values[i], depth * (2 * i + 1), 1))
    return out


def begun(u, f, far, sign):
    return STAY * u + time_ratio * (sign * 0.5 * f + HALF_C * far)


def prep_kernel(mesh, u_ref, g_ref, s_ref, ylo, yhi, zs, yp):
    _, _, _, first = masks(mesh)
    lane = lanes()
    for z in range(NZ):
        vals = [u_ref[k, layer(z), :] for k in range(5)]
        vals += [g_ref[layer(z), :], s_ref[0, layer(z), :].astype(F32)]
        yp[layer(z), :] = pack_edges(vals, lane, 3)
    rows = yp[...].T
    for out, c1, c2, c3, sign in ((yhi, 2, 1, 0, 1.0), (ylo, 3, 4, 5, -1.0)):
        st, st2, st3 = [[rows[6 * k + c : 6 * k + c + 1] for k in range(7)] for c in (c1, c2, c3)]
        prim, prim2 = primitives(*st[:6]), primitives(*st2[:6])
        slope = (sign * 0.5) * (prim[1] - st3[2] / (1.0 + st3[0]))
        fl = flux(st2[:5], 1, prim2[1], total_pressure(prim2[4], st2[6], st2[0], slope))
        items = st[:5] + [prim[4], st[6], prim2[1]] + [begun(st[k], fl[k], st2[k], sign) for k in range(3)]
        for k in range(11):
            out[k : k + 1] = items[k]
        out[11:16] = jnp.zeros((5, NY), F32)
    za, zb, zc = [dyn_layer(face_layer(first, d)) for d in range(3)]
    sign = jnp.where(first, 1.0, -1.0)
    st, st2 = [[u_ref[k, at, :] for k in range(5)] for at in (za, zb)]
    prim, prim2 = primitives(*st, g_ref[za, :]), primitives(*st2, g_ref[zb, :])
    slope = (sign * 0.5) * (prim[2] - u_ref[3, zc, :] / (1.0 + u_ref[0, zc, :]))
    fl = flux(st2, 2, prim2[2], total_pressure(prim2[4], s_ref[0, zb, :].astype(F32), st2[0], slope))
    items = st + [prim[4], s_ref[0, za, :].astype(F32), prim2[2]]
    items += [begun(st[k], fl[k], st2[k], sign) for k in (0, 1, 3)]
    for k in range(11):
        zs[k] = items[k]


def still_kernel(u_ref, g_ref, s_ref, vel, heat, press, inner, slo, shi):
    lane = lanes()
    for z in range(NZ):
        prim = primitives(*[u_ref[k, layer(z), :] for k in range(5)], g_ref[layer(z), :])
        for k in range(3):
            vel[k, layer(z), :] = prim[k]
        heat[layer(z), :] = prim[3]
        press[layer(z), :] = prim[4]
        st = [u_ref[k, layer(z), :] for k in range(5)]
        uy = prim[1]
        squeeze = jnp.minimum(0.5 * (pltpu.roll(uy, NY - 1, 1) - pltpu.roll(uy, 1, 1)), 0.0)
        squeeze = jnp.where((lane == 0) | (lane == NY - 1), 0.0, squeeze)
        visc = s_ref[0, layer(z), :].astype(F32) * quad_viscosity * (1.0 + st[0])
        fy = flux(st, 1, uy, prim[4] + visc * squeeze * squeeze)
        for k in range(5):
            inner[k, layer(z), :] = STAY * st[k] - time_ratio * (
                y_next(upper_part(fy[k], st[k]), 0.0, lane) - y_prev(lower_part(fy[k], st[k]), 0.0, lane)
            )
    for out, e, i, j, last, sign in ((shi, NX - 1, NX - 2, NX - 3, NX - 4, 1.0), (slo, 0, 1, 2, 3, -1.0)):
        for k in range(5):
            out[k] = u_ref[k, x_row(e), :]
        out[5] = g_ref[x_row(e), :]
        out[6] = s_ref[0, x_row(e), :].astype(F32)
        out[7] = vel[0, x_row(i), :]
        out[8] = s_ref[1, x_row(e), :].astype(F32)
        for at, before, after, base, count in ((i, e, j, 9, 5), (j, i, last, 14, 2)):
            st = [u_ref[k, x_row(at), :] for k in range(5)]
            slope = (sign * 0.5) * (vel[0, x_row(before), :] - vel[0, x_row(after), :])
            total = total_pressure(press[x_row(at), :], s_ref[0, x_row(at), :].astype(F32), st[0], slope)
            fl = flux(st, 0, vel[0, x_row(at), :], total)
            for k in range(count):
                out[base + k] = time_ratio * (sign * 0.5 * fl[k] + HALF_C * st[k])


def side_kernel(
    mesh, u_ref, s_ref, vel, pr, inner, slo, shi, ylo, yhi, yl, yh, zr,
    part, xlo, xhi, zz,
    vz, az, bz, yr,
):
    _, (myl, myh), (mzl, mzh), first = masks(mesh)
    for z in range(NZ):
        vz[layer(z + 1), :] = vel[2, layer(z), :]
    far = [zr[k] for k in range(8)]
    speed = far[3] / (1.0 + far[0])
    own = vel[2, dyn_layer(face_layer(first, 0)), :]
    slope = (far[7] - own) * jnp.where(first, 0.5, -0.5)
    fl = flux(far[:5], 2, speed, total_pressure(far[5], far[6], far[0], slope))
    for k in range(5):
        bz[k, layer(0), :] = lower_part(fl[k], far[k]) * mzl
        az[k, layer(NZ), :] = upper_part(fl[k], far[k]) * mzh
    vz[layer(0), :] = speed * mzl
    vz[layer(NZ + 1), :] = speed * mzh
    yr[...] = jnp.zeros(yr.shape, F32)
    sides = []
    for side, ref, mask, own, sign in ((0, yl, myl, ylo, 1.0), (1, yh, myh, yhi, -1.0)):
        items = [ref[k : k + 1] * mask for k in range(8)]
        sides.append(items)
        speed = items[2] / (1.0 + items[0])
        uy = own[2:3] / (1.0 + own[0:1])
        slope = (sign * 0.5) * (uy - items[7])
        fl = flux(items[:5], 1, speed, total_pressure(items[5], items[6], items[0], slope))
        squeeze = jnp.minimum((sign * 0.5) * (own[7:8] - speed), 0.0)
        visc = own[6:7] * quad_viscosity * (1.0 + own[0:1]) * squeeze * squeeze
        for k in range(5):
            at = 4 * k + side
            yr[at : at + 1, :] = time_ratio * (sign * 0.5 * fl[k] + HALF_C * items[k])
        yr[10 + side : 11 + side, :] = (sign * HALF_T) * visc
        yr[18 + side : 19 + side, :] = (sign * HALF_T) * visc * uy
    low, high = sides
    parts = jnp.concatenate([piece.astype(F32) for piece in split3(yr[...].T)], axis=1).astype(jnp.bfloat16)
    item = lax.bitwise_and(lax.broadcasted_iota(jnp.int32, (3 * yr.shape[0], NY), 0), yr.shape[0] - 1)
    column = lax.broadcasted_iota(jnp.int32, (3 * yr.shape[0], NY), 1)
    for k in range(5):
        place = (item == 4 * k) & (column == 0) | (item == 4 * k + 1) & (column == NY - 1)
        place = place | (item == 4 * k + 2) & (column == 1) | (item == 4 * k + 3) & (column == NY - 2)
        spread = jnp.where(place, 1.0, 0.0).astype(jnp.bfloat16)
        part[k] = inner[k] + jnp.dot(parts, spread, preferred_element_type=F32)
    for z in range(NZ):
        st = [u_ref[k, layer(z), :] for k in range(5)]
        squeeze = jnp.minimum(0.5 * (vz[layer(z + 2), :] - vz[layer(z), :]), 0.0)
        visc = s_ref[0, layer(z), :].astype(F32) * quad_viscosity * (1.0 + st[0])
        fz = flux(st, 2, vel[2, layer(z), :], pr[layer(z), :] + visc * squeeze * squeeze)
        for k in range(5):
            az[k, layer(z), :] = upper_part(fz[k], st[k])
            bz[k, layer(z + 1), :] = lower_part(fz[k], st[k])
    for z in range(NZ):
        for k in range(5):
            part[k, layer(z), :] = part[k, layer(z), :] - time_ratio * (
                az[k, layer(z + 1), :] - bz[k, layer(z), :]
            )
    for k in range(8):
        zz[k : k + 1, :] = low[k]
        zz[8 + k : 9 + k, :] = high[k]
    for out, still, e, i in ((xhi, shi, NX - 1, NX - 2), (xlo, slo, 0, 1)):
        for k in range(9):
            out[k] = still[k]
        for k in range(5):
            out[9 + k] = part[k, x_row(e), :] + still[9 + k]
        for k in range(2):
            out[14 + k] = part[k, x_row(i), :] + still[14 + k]
        out[16] = zz[...]
        for k in range(8):
            out[17, k : k + 1, :] = zr[k, e : e + 1, :]
        out[17, 8:9, :] = zr[1, i : i + 1, :] / (1.0 + zr[0, i : i + 1, :])
        out[17, 9:16, :] = jnp.zeros((7, NY), F32)


def shifted_x(own, low, high, at_x):
    up = jnp.where(at_x == NX - 1, pltpu.roll(high, NX - 1, 1), pltpu.roll(own, NY - 1, 1))
    down = jnp.where(at_x == 0, pltpu.roll(low, NY - NX + 1, 1), pltpu.roll(own, 1, 1))
    return up, down


def halo_step(
    mesh, u_ref, g_ref, s_ref, vel, pr, part, ylo, yhi, yl, yh, zr, xl, xh, zz,
    o_ref, xc, hxl, hxh, hyl, hyh, hz, vx, ax, bx, zc,
):
    (mxl, mxh), (myl, myh), (mzl, mzh), first = masks(mesh)
    for z in range(NZ):
        vx[pl.ds(24 * z + 8, 8), :] = vel[0, layer(z), :]
    low = [xl[k] * mxl for k in range(8)]
    high = [xh[k] * mxh for k in range(8)]
    prim = primitives(*low[:6])
    vx[pl.ds(7, NZ, stride=24), :] = prim[0]
    slope = 0.5 * (vx[pl.ds(8, NZ, stride=24), :] - low[7])
    f_low = flux(low[:5], 0, prim[0], total_pressure(prim[4], low[6], low[0], slope))
    prim = primitives(*high[:6])
    vx[pl.ds(16, NZ, stride=24), :] = prim[0]
    slope = 0.5 * (high[7] - vx[pl.ds(15, NZ, stride=24), :])
    f_high = flux(high[:5], 0, prim[0], total_pressure(prim[4], high[6], high[0], slope))
    for k in range(5):
        bx[k, pl.ds(7, NZ, stride=16), :] = lower_part(f_low[k], low[k])
        ax[k, pl.ds(8, NZ, stride=16), :] = upper_part(f_high[k], high[k])
    for z in range(NZ):
        st = [u_ref[k, layer(z), :] for k in range(5)]
        ux, press = vel[0, layer(z), :], pr[layer(z), :]
        slope = 0.5 * (vx[pl.ds(24 * z + 9, 8), :] - vx[pl.ds(24 * z + 7, 8), :])
        fx = flux(st, 0, ux, total_pressure(press, s_ref[0, layer(z), :].astype(F32), st[0], slope))
        for k in range(5):
            ax[k, pl.ds(16 * z, 8), :] = upper_part(fx[k], st[k])
            bx[k, pl.ds(16 * z + 8, 8), :] = lower_part(fx[k], st[k])
    for z in range(NZ):
        for k in range(5):
            o_ref[k, layer(z), :] = part[k, layer(z), :] - time_ratio * (
                ax[k, pl.ds(16 * z + 1, 8), :] - bx[k, pl.ds(16 * z + 7, 8), :]
            )
    for out, ref, mask in ((hxl, xl, mxl), (hxh, xh, mxh)):
        if ref is xl:
            near = [-ax[k, pl.ds(0, NZ, stride=16), :] for k in range(5)]
            next_ = [-upper_part(f_low[k], low[k]) for k in range(2)]
        else:
            near = [bx[k, pl.ds(15, NZ, stride=16), :] for k in range(5)]
            next_ = [lower_part(f_high[k], high[k]) for k in range(2)]
        st = [(ref[9 + k] + time_ratio * near[k]) * mask for k in range(5)]
        st2 = [(ref[14 + k] + time_ratio * next_[k]) * mask for k in range(2)]
        out[0] = st[0]
        out[1] = st[1]
        out[2] = primitives(*st, ref[5] * mask)[4]
        out[3] = ref[8] * mask
        out[4] = st2[1] / (1.0 + st2[0])
        base = 0 if ref is xl else 3
        inv, gamma = 1.0 / (1.0 + st[0]), ref[5] * mask
        xc[base] = (2.0 - gamma) * (st[1] * inv)
        xc[base + 1] = inv
        xc[base + 2] = gamma
    lane = lax.broadcasted_iota(jnp.int32, (1, NY), 1)
    at_x = lax.bitwise_and(lane, NX - 1)
    for side, ref, mask, own, out, sign in ((0, yl, myl, ylo, hyl, -1.0), (1, yh, myh, yhi, hyh, 1.0)):

        def items(values, m):
            return [values[k : k + 1] * m for k in range(8)]

        here = items(ref, mask)
        near_l, near_h = items(xl[16, 8 * side : 8 * side + 8, :], mxl), items(xh[16, 8 * side : 8 * side + 8, :], mxh)
        ux, ux_l, ux_h = [v[1] / (1.0 + v[0]) for v in (here, near_l, near_h)]
        up, down = shifted_x(ux, ux_l, ux_h, at_x)
        slope = 0.5 * (up - down)
        slope_h = 0.5 * (pltpu.roll(ux_h, NY - 1, 1) - pltpu.roll(ux, NY - NX + 1, 1))
        slope_l = 0.5 * (pltpu.roll(ux, NX - 1, 1) - pltpu.roll(ux_l, 1, 1))

        def fx_of(v, speed, slope):
            return [v[1], v[1] * speed + total_pressure(v[5], v[6], v[0], slope), v[2] * speed]

        f_here, f_l, f_h = fx_of(here, ux, slope), fx_of(near_l, ux_l, slope_l), fx_of(near_h, ux_h, slope_h)
        uz = here[3] / (1.0 + here[0])
        near_z = items(zz[8 * side : 8 * side + 8, :], 1.0)
        uz_z = near_z[3] / (1.0 + near_z[0])
        fz, fz_z = [[v[3], v[1] * w, v[2] * w] for v, w in ((here, uz), (near_z, uz_z))]
        self_ = items(own, 1.0)
        uy = self_[2] / (1.0 + self_[0])
        uy_here = here[2] / (1.0 + here[0])
        slope = 0.5 * (self_[7] - uy_here if side == 0 else uy_here - self_[7])
        fy = [self_[2], self_[1] * uy, self_[2] * uy + total_pressure(self_[5], self_[6], self_[0], slope)]
        new = []
        for k in range(3):
            a_x, _ = shifted_x(upper_part(f_here[k], here[k]), ux_l, upper_part(f_h[k], near_h[k]), at_x)
            _, b_x = shifted_x(lower_part(f_here[k], here[k]), lower_part(f_l[k], near_l[k]), ux_h, at_x)
            a_z = jnp.where(
                lane >= NY - NX,
                pltpu.roll(upper_part(fz_z[k], near_z[k]), NY - NX, 1) * mzh,
                pltpu.roll(upper_part(fz[k], here[k]), NY - NX, 1),
            )
            b_z = jnp.where(
                lane < NX,
                pltpu.roll(lower_part(fz_z[k], near_z[k]), NX, 1) * mzl,
                pltpu.roll(lower_part(fz[k], here[k]), NX, 1),
            )
            facing = sign * 0.5 * fy[k] + HALF_C * self_[k]
            new.append(mask * (ref[8 + k : 9 + k] + time_ratio * (facing - (a_x - b_x) - (a_z - b_z))))
        r, mx, my = new
        combine = lower_part if side == 0 else upper_part
        out[0:1, :] = combine(my, r)
        out[1:2, :] = combine(mx * (my / (1.0 + r)), mx)
        out[2:8, :] = jnp.zeros((6, NY), F32)
    rows = []
    for side in range(2):
        v = [zz[8 * side + k : 8 * side + k + 1, :] for k in range(8)]
        speed = v[2] / (1.0 + v[0])
        fy = [v[2], v[1] * speed, v[3] * speed]
        combine = upper_part if side else lower_part
        rows += [combine(f, v[k]) for f, k in zip(fy, (0, 1, 3))]
    zc[...] = jnp.concatenate(rows + [jnp.zeros((2, NY), F32)], axis=0).T
    cols = zc[dyn_layer(jnp.where(first, 0, NZ - 1)), :]
    full = lanes()
    deep = lax.broadcasted_iota(jnp.int32, (NX, NY), 0)
    here = [zr[k] for k in range(8)]
    near_l = [xl[17, k : k + 1, :] * mxl for k in range(9)]
    near_h = [xh[17, k : k + 1, :] * mxh for k in range(9)]
    ux, ux_l, ux_h = [v[1] / (1.0 + v[0]) for v in (here, near_l, near_h)]

    def next_x(value, row):
        return jnp.where(deep == NX - 1, row, pltpu.roll(value, NX - 1, 0))

    def prev_x(value, row):
        return jnp.where(deep == 0, row, pltpu.roll(value, 1, 0))

    slope = 0.5 * (next_x(ux, ux_h) - prev_x(ux, ux_l))
    slope_h = 0.5 * (near_h[8] - ux[NX - 1 : NX])
    slope_l = 0.5 * (ux[0:1] - near_l[8])

    def fx_layer(v, speed, slope):
        return [v[1], v[1] * speed + total_pressure(v[5], v[6], v[0], slope), v[3] * speed]

    f_here, f_l, f_h = fx_layer(here, ux, slope), fx_layer(near_l, ux_l, slope_l), fx_layer(near_h, ux_h, slope_h)
    uy = here[2] / (1.0 + here[0])
    fy = [here[2], here[1] * uy, here[3] * uy]
    za, zb = dyn_layer(face_layer(first, 0)), dyn_layer(face_layer(first, 1))
    sign = jnp.where(first, 1.0, -1.0)
    st = [u_ref[k, za, :] for k in range(5)]
    slope = (sign * 0.5) * (here[3] / (1.0 + here[0]) - vel[2, zb, :])
    fz = flux(st, 2, vel[2, za, :], total_pressure(pr[za, :], s_ref[0, za, :].astype(F32), st[0], slope))
    new = []
    for n, k in enumerate((0, 1, 3)):
        a_x = next_x(upper_part(f_here[n], here[k]), upper_part(f_h[n], near_h[k]))
        b_x = prev_x(lower_part(f_here[n], here[k]), lower_part(f_l[n], near_l[k]))
        a_y = y_next(upper_part(fy[n], here[k]), cols[:, 3 + n : 4 + n], full)
        b_y = y_prev(lower_part(fy[n], here[k]), cols[:, n : n + 1], full)
        facing = sign * 0.5 * fz[k] + HALF_C * st[k]
        new.append(zr[8 + n] + time_ratio * (facing - (a_x - b_x) - (a_y - b_y)))
    r, mx, mz = new
    hz[0] = 0.5 * mz - (sign * HALF_C) * r
    hz[1] = 0.5 * mx * (mz / (1.0 + r)) - (sign * HALF_C) * mx


def forward_kernel(
    mesh, u0_ref, g_ref, s_ref, vel, pr, part, ylo_in, yhi_in, yl, yh, zr, xl, xh, zz, n_ref, m_ref,
    u_ref, lam_ref, cf_ref, cfh_ref, mis_ref, xc, ylo, yhi, zs, yown,
    hxl, hxh, hyl, hyh, hz, vx, ax, bx, az, bz, ch, yc, yp, zc,
):
    halo_step(
        mesh, u0_ref, g_ref, s_ref, vel, pr, part, ylo_in, yhi_in, yl, yh, zr, xl, xh, zz,
        u_ref, xc, hxl, hxh, hyl, hyh, hz, vx, ax, bx, zc,
    )
    speed_kernel(
        mesh, u_ref, g_ref, s_ref, hxl, hxh, hyl, hyh, hz, n_ref, m_ref,
        lam_ref, cf_ref, cfh_ref, mis_ref, ylo, yhi, zs, yown,
        vx, ax, bx, az, bz, ch, yc, yp,
    )


def columns_of(low, high, count, low_mask, high_mask):
    rows = [low[k : k + 1] * low_mask for k in range(count)]
    rows += [high[k : k + 1] * high_mask for k in range(count)]
    rows.append(jnp.zeros((8 - 2 * count, NY), F32))
    return jnp.concatenate(rows, axis=0).T


def speed_kernel(
    mesh, u_ref, g_ref, s_ref, xl, xh, yl, yh, zr, n_ref, m_ref,
    lam_ref, cf_ref, cfh_ref, mis_ref, ylo, yhi, zs, yown,
    vx, ax, bx, az, bz, ch, yc, yp,
):
    (mxl, mxh), (myl, myh), (mzl, mzh), first = masks(mesh)
    lane = lanes()
    for z in range(NZ):
        vx[pl.ds(24 * z + 8, 8), :] = u_ref[1, layer(z), :] / (1.0 + u_ref[0, layer(z), :])
    for side, ref, mask in ((0, xl, mxl), (1, xh, mxh)):
        r, mx, press, sw, second = [ref[k] * mask for k in range(5)]
        speed = mx / (1.0 + r)
        vx[pl.ds(16 if side else 7, NZ, stride=24), :] = speed
        own = vx[pl.ds(15 if side else 8, NZ, stride=24), :]
        slope = 0.5 * (second - own if side else own - second)
        squeeze = jnp.minimum(slope, 0.0)
        visc = sw * quad_viscosity * (1.0 + r) * squeeze
        cfh_ref[side] = 2.0 * visc
        f1 = mx * speed + press + visc * squeeze
        if side:
            ax[0, pl.ds(8, NZ, stride=16), :] = upper_part(mx, r)
            ax[1, pl.ds(8, NZ, stride=16), :] = upper_part(f1, mx)
        else:
            bx[0, pl.ds(7, NZ, stride=16), :] = lower_part(mx, r)
            bx[1, pl.ds(7, NZ, stride=16), :] = lower_part(f1, mx)
    for k in range(2):
        bz[k, layer(0), :] = zr[k] * mzl
        az[k, layer(NZ), :] = zr[k] * mzh
    yc[...] = columns_of(yl, yh, 2, myl, myh)
    for z in range(NZ):
        r, mx, my, mz, en = [u_ref[k, layer(z), :] for k in range(5)]
        ux, uy, uz, _, press = primitives(r, mx, my, mz, en, g_ref[layer(z), :])
        squeeze = jnp.minimum(0.5 * (vx[pl.ds(24 * z + 9, 8), :] - vx[pl.ds(24 * z + 7, 8), :]), 0.0)
        visc = s_ref[1, layer(z), :].astype(F32) * quad_viscosity * (1.0 + r) * squeeze
        cf_ref[layer(z), :] = 2.0 * visc
        f1 = mx * ux + press + visc * squeeze
        for k, st, fx, fy, fz in ((0, r, mx, my, mz), (1, mx, f1, mx * uy, mx * uz)):
            ax[k, pl.ds(16 * z, 8), :] = upper_part(fx, st)
            bx[k, pl.ds(16 * z + 8, 8), :] = lower_part(fx, st)
            az[k, layer(z), :] = upper_part(fz, st)
            bz[k, layer(z + 1), :] = lower_part(fz, st)
            ch[k, layer(z), :] = (
                3.0 * signal_speed * st
                + y_next(upper_part(fy, st), yc[layer(z), 2 + k : 3 + k], lane)
                - y_prev(lower_part(fy, st), yc[layer(z), k : k + 1], lane)
            )
    mis = jnp.zeros((NX, NY), F32)
    for z in range(NZ):
        new = []
        for k in range(2):
            change = (
                ch[k, layer(z), :]
                + (ax[k, pl.ds(16 * z + 1, 8), :] - bx[k, pl.ds(16 * z + 7, 8), :])
                + (az[k, layer(z + 1), :] - bz[k, layer(z), :])
            )
            new.append(u_ref[k, layer(z), :] - time_ratio * change)
        inv = 1.0 / (1.0 + new[0])
        speed = new[1] * inv
        off = speed - m_ref[layer(z), :]
        weight = n_ref[layer(z), :] * off
        mis = mis + weight * off
        lam_m = 2.0 * weight * inv
        lam_r = -lam_m * speed
        lam_ref[0, layer(z), :] = lam_r
        lam_ref[1, layer(z), :] = lam_m
        inv = 1.0 / (1.0 + u_ref[0, layer(z), :])
        extra = [u_ref[1, layer(z), :] * inv, u_ref[2, layer(z), :] * inv, g_ref[layer(z), :]]
        yp[layer(z), :] = pack_edges([lam_r, lam_m] + extra, lane)
    mis_ref[...] = mis
    za, zb = dyn_layer(face_layer(first, 0)), dyn_layer(face_layer(first, 1))
    inv = 1.0 / (1.0 + u_ref[0, za, :])
    ux = u_ref[1, za, :] * inv
    zs[0] = lam_ref[0, za, :]
    zs[1] = lam_ref[1, za, :]
    zs[2] = jnp.where(first, -HALF_T, HALF_T) * (lam_ref[0, zb, :] + lam_ref[1, zb, :] * ux)
    zs[3] = ux
    zs[4] = u_ref[3, za, :] * inv
    zs[5] = g_ref[za, :]
    rows = yp[...].T
    for out, edge, second, own, sign in ((yhi, 1, 0, 2, -HALF_T), (ylo, 2, 3, 0, HALF_T)):
        lam_r, lam_m, ux, uy, gamma = [rows[4 * i + edge : 4 * i + edge + 1] for i in range(5)]
        out[0:1] = lam_r
        out[1:2] = lam_m
        out[2:3] = sign * (rows[second : second + 1] + rows[4 + second : 5 + second] * ux)
        out[3:4] = ux
        out[4:5] = uy
        out[5:6] = gamma
        out[6:8] = jnp.zeros((2, NY), F32)
        yown[own : own + 1] = lam_r
        yown[own + 1 : own + 2] = lam_m
    yown[4:8] = jnp.zeros((4, NY), F32)


def edge_kernel(mesh, u_ref, lam_ref, cf_ref, yl, yh, zr, xlo, xhi, yc):
    _, (myl, myh), (mzl, mzh), _ = masks(mesh)
    low_y, high_y = yl[1:2] * myl, yh[1:2] * myh
    yc[:, 0:8] = jnp.concatenate([low_y, high_y, jnp.zeros((6, NY), F32)], axis=0).T
    lane = lax.broadcasted_iota(jnp.int32, (NZ, NY), 1)
    deep = lax.broadcasted_iota(jnp.int32, (NZ, NY), 0)
    for out, e, i, i2, sign in ((xhi, NX - 1, NX - 2, NX - 3, 1.0), (xlo, 0, 1, 2, -1.0)):
        r, my, mz = [u_ref[k, x_row(e), :] for k in (0, 2, 3)]
        inv = 1.0 / (1.0 + r)
        lm, lm_i = lam_ref[1, x_row(e), :], lam_ref[1, x_row(i), :]
        col = yc[x_row(e), :]
        side = zr[1, e : e + 1, :]
        up_y = jnp.where(lane == NY - 1, col[:, 1:2], pltpu.roll(lm, NY - 1, 1))
        down_y = jnp.where(lane == 0, col[:, 0:1], pltpu.roll(lm, 1, 1))
        up_z = jnp.where(deep == NZ - 1, side * mzh, pltpu.roll(lm, NZ - 1, 0))
        down_z = jnp.where(deep == 0, side * mzl, pltpu.roll(lm, 1, 0))
        slope = (sign * HALF_T) * (lm - lam_ref[1, x_row(i2), :]) * cf_ref[x_row(i), :]
        out[0] = lam_ref[0, x_row(e), :]
        out[1] = lm
        out[2] = lm_i
        out[3] = (
            STAY * lm
            + NEAR * (lm_i + (up_y + down_y) + (up_z + down_z))
            - (sign * HALF_T) * lam_ref[0, x_row(i), :]
            + HALF_T * ((up_y - down_y) * (my * inv) + (up_z - down_z) * (mz * inv))
            + (sign * 0.5) * slope * inv
        )
        out[4] = jnp.where(deep == 0, low_y, jnp.where(deep == 1, high_y, jnp.where(deep == 2, side, 0.0)))


def lean_kernel(mesh, u_ref, lam_ref, yl, yh, zr, base, vel, inv_ref, heat, lz, yc):
    _, (myl, myh), (mzl, mzh), _ = masks(mesh)
    lane = lanes()
    for k in range(2):
        for z in range(NZ):
            lz[k, layer(z + 1), :] = lam_ref[k, layer(z), :]
        lz[k, layer(0), :] = zr[k] * mzl
        lz[k, layer(NZ + 1), :] = zr[k] * mzh
    yc[...] = columns_of(yl, yh, 2, myl, myh)
    for z in range(NZ):
        r, mx, my, mz, en = [u_ref[k, layer(z), :] for k in range(5)]
        inv = 1.0 / (1.0 + r)
        ux, uy, uz = mx * inv, my * inv, mz * inv
        heat[layer(z), :] = en - 0.5 * (mx * ux + my * uy + mz * uz)
        inv_ref[layer(z), :] = inv
        for k, value in enumerate((ux, uy, uz)):
            vel[k, layer(z), :] = value
        lr, lm = lam_ref[0, layer(z), :], lam_ref[1, layer(z), :]
        lr_z = [lz[0, layer(z + s), :] for s in (0, 2)]
        lm_z = [lz[1, layer(z + s), :] for s in (0, 2)]
        lr_y = [y_prev(lr, yc[layer(z), 0:1], lane), y_next(lr, yc[layer(z), 2:3], lane)]
        lm_y = [y_prev(lm, yc[layer(z), 1:2], lane), y_next(lm, yc[layer(z), 3:4], lane)]
        phi_y1 = HALF_T * (lm_y[1] - lm_y[0])
        phi_z1 = HALF_T * (lm_z[1] - lm_z[0])
        near = (lm_y[0] + lm_y[1]) + (lm_z[0] + lm_z[1])
        base[0, layer(z), :] = STAY * lm + NEAR * near + phi_y1 * uy + phi_z1 * uz
        base[1, layer(z), :] = HALF_T * (lr_y[1] - lr_y[0]) + phi_y1 * ux
        base[2, layer(z), :] = HALF_T * (lr_z[1] - lr_z[0]) + phi_z1 * ux


def gradient_kernel(
    mesh, vel, heat_ref, u_ref, g_ref, base, vel_1, inv_1, heat_1, lam_ref, cf_ref, cfh_ref, xc, yown, yl, yh, zr, xl, xh, mis_ref, v_ref,
    grad_ref, row_ref,
    lx, px, dx, dg, yc, gx, gy, gz,
):
    (mxl, mxh), (myl, myh), (mzl, mzh), first = masks(mesh)
    lane = lanes()
    for k in range(2):
        for z in range(NZ):
            lx[k, pl.ds(24 * z + 8, 8), :] = lam_ref[k, layer(z), :]
        lx[k, pl.ds(7, NZ, stride=24), :] = xl[k] * mxl
        lx[k, pl.ds(16, NZ, stride=24), :] = xh[k] * mxh
    phi_low = HALF_T * (lam_ref[1, x_row(0), :] - xl[2] * mxl)
    phi_high = HALF_T * (xh[2] * mxh - lam_ref[1, x_row(NX - 1), :])
    dx[pl.ds(7, NZ, stride=24), :] = phi_low * cfh_ref[0]
    dx[pl.ds(16, NZ, stride=24), :] = phi_high * cfh_ref[1]
    for z in range(NZ):
        phi = HALF_T * (lx[1, pl.ds(24 * z + 9, 8), :] - lx[1, pl.ds(24 * z + 7, 8), :])
        px[layer(z), :] = phi
        dx[pl.ds(24 * z + 8, 8), :] = phi * cf_ref[layer(z), :]
    gx[1, pl.ds(7, NZ, stride=24), :] = mxl * phi_low * xc[2]
    gx[1, pl.ds(16, NZ, stride=24), :] = mxh * phi_high * xc[5]
    gx[0, pl.ds(7, NZ, stride=24), :] = mxl * (
        xl[3]
        + HALF_T * lam_ref[0, x_row(0), :]
        + NEAR * lam_ref[1, x_row(0), :]
        + phi_low * xc[0]
        - 0.5 * dx[pl.ds(8, NZ, stride=24), :] * xc[1]
    )
    gx[0, pl.ds(16, NZ, stride=24), :] = mxh * (
        xh[3]
        - HALF_T * lam_ref[0, x_row(NX - 1), :]
        + NEAR * lam_ref[1, x_row(NX - 1), :]
        + phi_high * xc[3]
        + 0.5 * dx[pl.ds(15, NZ, stride=24), :] * xc[4]
    )
    at_x = lax.bitwise_and(lax.broadcasted_iota(jnp.int32, (1, NY), 1), NX - 1)
    from_high, from_low = pltpu.roll(xh[4], NX - 1, 1) * mxh, pltpu.roll(xl[4], NY - NX + 1, 1) * mxl
    halo = []
    for side, ref, mask, sign in ((0, yl, myl, HALF_T), (1, yh, myh, -HALF_T)):
        items = ref[...]
        up = jnp.where(at_x == NX - 1, from_high[side : side + 1], pltpu.roll(items, NY - 1, 1)[1:2])
        down = jnp.where(at_x == 0, from_low[side : side + 1], pltpu.roll(items, 1, 1)[1:2])
        d_en = HALF_T * (up - down) * items[5:6]
        own_r, own_m = yown[2 * side : 2 * side + 1], yown[2 * side + 1 : 2 * side + 2]
        d_my = items[2:3] + sign * (own_r + own_m * items[3:4]) - d_en * items[4:5]
        halo += [d_my * mask, d_en * mask]
    yc[...] = jnp.concatenate(halo + [jnp.zeros((4, NY), F32)], axis=0).T
    deep = lax.broadcasted_iota(jnp.int32, (NX, NY), 0)
    up = jnp.where(deep == NX - 1, xh[4, 2:3, :] * mxh, pltpu.roll(zr[1], NX - 1, 0))
    down = jnp.where(deep == 0, xl[4, 2:3, :] * mxl, pltpu.roll(zr[1], 1, 0))
    d_en = HALF_T * (up - down) * zr[5]
    za = dyn_layer(face_layer(first, 0))
    d_mz = (
        zr[2]
        + jnp.where(first, -HALF_T, HALF_T) * (lam_ref[0, za, :] + lam_ref[1, za, :] * zr[3])
        - d_en * zr[4]
    )
    for k, value in ((0, d_mz), (1, d_en)):
        gz[k, layer(0), :] = value * mzl
        gz[k, layer(NZ + 1), :] = value * mzh
    for z in range(NZ):
        ux, uy, uz = [vel_1[k, layer(z), :] for k in range(3)]
        lr_x = [lx[0, pl.ds(24 * z + s, 8), :] for s in (7, 9)]
        lm_x = [lx[1, pl.ds(24 * z + s, 8), :] for s in (7, 9)]
        phi_x1 = px[layer(z), :]
        d_speed = phi_x1 * u_ref[1, layer(z), :] + 0.5 * (dx[pl.ds(24 * z + 7, 8), :] - dx[pl.ds(24 * z + 9, 8), :])
        d_en = phi_x1 * g_ref[layer(z), :]
        gx[0, pl.ds(24 * z + 8, 8), :] = (
            base[0, layer(z), :]
            + NEAR * (lm_x[0] + lm_x[1])
            + HALF_T * (lr_x[1] - lr_x[0])
            + (phi_x1 - d_en) * ux
            + d_speed * inv_1[layer(z), :]
        )
        gx[1, pl.ds(24 * z + 8, 8), :] = d_en
        gy[layer(z), :] = base[1, layer(z), :] - d_en * uy
        gz[0, layer(z + 1), :] = base[2, layer(z), :] - d_en * uz
        gz[1, layer(z + 1), :] = d_en
        dg[layer(z), :] = phi_x1 * heat_1[layer(z), :]
    acc = jnp.zeros((NX, NY), F32)
    for z in range(NZ):
        ux, uy, uz = [vel[k, layer(z), :] for k in range(3)]
        heat = heat_ref[layer(z), :]
        dif_x = [gx[k, pl.ds(24 * z + 9, 8), :] - gx[k, pl.ds(24 * z + 7, 8), :] for k in range(2)]
        dif_z = [gz[k, layer(z + 2), :] - gz[k, layer(z), :] for k in range(2)]
        dif_y = []
        for k, own in ((0, gy[layer(z), :]), (1, gz[1, layer(z + 1), :])):
            dif_y.append(
                y_next(own, yc[layer(z), 2 + k : 3 + k], lane) - y_prev(own, yc[layer(z), k : k + 1], lane)
            )
        d_press = HALF_T * (
            (dif_x[0] + ux * dif_x[1]) + (dif_y[0] + uy * dif_y[1]) + (dif_z[0] + uz * dif_z[1])
        )
        grad = dg[layer(z), :] + d_press * heat
        grad_ref[layer(z), :] = grad
        acc = acc + grad * grad
    total = jnp.sum(jnp.sum(acc, axis=0, keepdims=True), axis=1, keepdims=True)
    miss = jnp.sum(jnp.sum(mis_ref[...], axis=0, keepdims=True), axis=1, keepdims=True)
    miss = miss + jnp.sum(v_ref[...], axis=1, keepdims=True)
    row = jnp.where(lane == 0, total, jnp.where(lane == 1, miss, 0.0))
    for i in range(row_ref.shape[0] // NX):
        row_ref[layer(i), :] = row[:, :NARROW]


def scale_kernel(devices, count, grad_ref, rows_ref, out_ref, misfit_ref):
    acc = rows_ref[layer(0), :]
    for i in range(1, devices // NX):
        acc = acc + rows_ref[layer(i), :]
    row = jnp.sum(acc, axis=0, keepdims=True)
    misfit_ref[0, 0] = row[0, 1] / (devices * count)
    scale = 1.0 / jnp.sqrt(row[0:1, 0:1] / (devices * CELLS * NY) + small_eps)
    out_ref[...] = grad_ref[...] * scale


def split3(value):
    hi = value.astype(jnp.bfloat16)
    rest = value - hi.astype(F32)
    mid = rest.astype(jnp.bfloat16)
    low = (rest - mid.astype(F32)).astype(jnp.bfloat16)
    return hi, mid, low


def probe_kernel(p_ref, o_ref, n_ref, m_ref, v_ref):
    count = p_ref.shape[1]
    probes, obs = p_ref[...], o_ref[...]
    row = lax.broadcasted_iota(jnp.int32, (CELLS, count), 0)
    on_a = row == lax.shift_right_logical(probes, 7)
    on_b = row == lax.bitwise_and(probes, NY - 1)
    one_a = jnp.where(on_a, 1.0, 0.0).astype(jnp.bfloat16)
    one_b = jnp.where(on_b, 1.0, 0.0).astype(jnp.bfloat16)

    def nt(a, b):
        return lax.dot_general(a, b, (((1,), (1,)), ((), ())), preferred_element_type=F32)

    parts = [jnp.where(on_a, part.astype(F32), 0.0).astype(jnp.bfloat16) for part in split3(obs)]
    hits = nt(one_a, one_b)
    sums = nt(parts[0], one_b) + (nt(parts[1], one_b) + nt(parts[2], one_b))
    n_ref[...] = hits
    mean = sums / jnp.maximum(hits, 1.0)
    m_ref[...] = mean
    mean_t = split3(mean.T)
    picked = sum(jnp.dot(part, one_a, preferred_element_type=F32) for part in reversed(mean_t))
    at_probe = jnp.sum(jnp.where(on_b, picked, 0.0), axis=0, keepdims=True)
    off = obs - at_probe
    v_ref[...] = off * off


SMALL = pltpu.CompilerParams(vmem_limit_bytes=12 * 1024 * 1024)

LARGE = pltpu.CompilerParams(vmem_limit_bytes=55168 * 1024)


def rows_of(*shape):
    return jax.ShapeDtypeStruct(shape, F32)


def vmem(*shape):
    return pltpu.VMEM(shape, F32)


def call(kernel, outs, scratch, params=SMALL):
    return pl.pallas_call(
        kernel,
        out_shape=outs,
        scratch_shapes=scratch,
        cost_estimate=pl.CostEstimate(flops=100000, bytes_accessed=100000, transcendentals=0),
        compiler_params=params,
    )


def ring(sizes, axis, step):
    n = sizes[axis]
    return [(i, (i + step) % n) for i in range(n)]


def exchange_x(sizes, xlo, xhi):
    return (
        lax.ppermute(xhi, "gx", ring(sizes, "gx", 1)),
        lax.ppermute(xlo, "gx", ring(sizes, "gx", -1)),
    )


def exchange_z(sizes, zs):
    return lax.ppermute(zs, "gz", ring(sizes, "gz", 1))


def exchange_yz(sizes, ylo, yhi, zs):
    zr = exchange_z(sizes, zs)
    yl = lax.ppermute(yhi, "gy", ring(sizes, "gy", 1))
    yh = lax.ppermute(ylo, "gy", ring(sizes, "gy", -1))
    return yl, yh, zr


def local(sizes, checkpoint, gruneisen, switch, probes, observed):
    bind = functools.partial
    state = checkpoint.reshape(5, CELLS, NY)
    gamma = gruneisen.reshape(CELLS, NY)
    sw = switch.reshape(2, CELLS, NY)
    plane = rows_of(8, NY)

    def x_slabs(items):
        return [rows_of(items, NZ, NY)] * 2

    pair = rows_of(16, NY)
    tall = (NZ + 2) * NX
    *sent_y, sent_z = call(
        bind(prep_kernel, sizes), [pair, pair, rows_of(11, NX, NY)], [vmem(CELLS, NY)], LARGE
    )(state, gamma, sw)
    got_yz = exchange_yz(sizes, *sent_y, sent_z)
    hits, mean, spread = call(
        probe_kernel,
        [rows_of(CELLS, NY), rows_of(CELLS, NY), rows_of(1, probes.shape[0])],
        [],
    )(probes.reshape(1, -1), observed.reshape(1, -1))
    grid = rows_of(CELLS, NY)
    vel, heat, press, inner, slo, shi = call(still_kernel, [rows_of(3, CELLS, NY), grid, grid, rows_of(5, CELLS, NY)] + x_slabs(16), [])(
        state, gamma, sw
    )
    part, xlo, xhi, zz = call(
        bind(side_kernel, sizes),
        [rows_of(5, CELLS, NY)] + x_slabs(18) + [pair],
        [
            vmem(tall, NY), vmem(5, tall, NY), vmem(5, tall, NY), vmem(32, NY),
        ],
    )(state, sw, vel, press, inner, slo, shi, *sent_y, *got_yz)
    got_x = exchange_x(sizes, xlo, xhi)
    zz = exchange_z(sizes, zz)
    state_1, lam_2, coef, coef_halo, mis, beside, *sent, yown = call(
        bind(forward_kernel, sizes),
        [rows_of(5, CELLS, NY), rows_of(2, CELLS, NY), rows_of(CELLS, NY), rows_of(2, NZ, NY), plane]
        + [rows_of(6, NZ, NY), plane, plane, rows_of(6, NX, NY), plane],
        [
            vmem(5, NZ, NY), vmem(5, NZ, NY), vmem(8, NY), vmem(8, NY), vmem(2, NX, NY),
            vmem(NZ * 24, NY), vmem(5, NZ * 16, NY), vmem(5, NZ * 16, NY), vmem(2, tall, NY), vmem(2, tall, NY),
            vmem(2, CELLS, NY), vmem(CELLS, 8), vmem(CELLS, NY), vmem(CELLS, 8),
        ],
    )(state, gamma, sw, vel, press, part, *sent_y, *got_yz, *got_x, zz, hits, mean)
    got_yz = exchange_yz(sizes, *sent)
    sent = call(bind(edge_kernel, sizes), x_slabs(5), [vmem(CELLS, NY)])(state_1, lam_2, coef, *got_yz)
    got_x = exchange_x(sizes, *sent)
    lean = call(
        bind(lean_kernel, sizes),
        [rows_of(3, CELLS, NY), rows_of(3, CELLS, NY), grid, grid],
        [vmem(2, tall, NY), vmem(CELLS, 8)],
    )(state_1, lam_2, *got_yz)
    devices = sizes["gx"] * sizes["gy"] * sizes["gz"]
    gradient, rows = call(
        bind(gradient_kernel, sizes),
        [rows_of(CELLS, NY), rows_of(devices, NARROW)],
        [
            vmem(2, NZ * 24, NY), vmem(CELLS, NY), vmem(NZ * 24, NY), vmem(CELLS, NY),
            vmem(CELLS, 8), vmem(2, NZ * 24, NY), vmem(CELLS, NY), vmem(2, tall, NY),
        ],
    )(vel, heat, state_1, gamma, *lean, lam_2, coef, coef_halo, beside, yown, *got_yz, *got_x, mis, spread)
    rows = lax.all_to_all(rows, ("gx", "gy", "gz"), 0, 0, tiled=True)
    direction, misfit = pl.pallas_call(
        bind(scale_kernel, devices, probes.shape[0]),
        out_shape=[rows_of(CELLS, NY), rows_of(1, 1)],
        out_specs=[pl.BlockSpec(memory_space=pltpu.VMEM), pl.BlockSpec(memory_space=pltpu.SMEM)],
        compiler_params=SMALL,
    )(gradient, rows)
    return direction.reshape(NZ, NX, NY), misfit.reshape(())


def solution(mesh):
    block = P("gz", "gx", "gy")
    parted = P(None, "gz", "gx", "gy")
    listed = P(("gx", "gy", "gz"))
    return jax.shard_map(
        functools.partial(local, dict(mesh.shape)),
        mesh=mesh,
        in_specs=(parted, block, parted, listed, listed),
        out_specs=(block, P()),
        check_vma=False,
    )
```

```python
import functools
import jax
import jax.numpy as jnp
from jax import lax
from jax.experimental import pallas as pl
from jax.experimental.pallas import tpu as pltpu
from jax.sharding import PartitionSpec as P

NZ, NX, NY = 16, 8, 128
CELLS = NZ * NX
bulk_modulus = 2.0
slope_coeff = 1.5
signal_speed = 2.5
time_ratio = 0.1
quad_viscosity = 4.0
small_eps = 1e-12
HALF_C = 0.5 * signal_speed
HALF_T = 0.5 * time_ratio
NEAR = time_ratio * HALF_C
STAY = 1.0 - 3.0 * time_ratio * signal_speed
F32 = jnp.float32
NARROW = 8


def primitives(r, mx, my, mz, en, gamma):
    inv = 1.0 / (1.0 + r)
    ux, uy, uz = mx * inv, my * inv, mz * inv
    heat = en - 0.5 * (mx * ux + my * uy + mz * uz)
    press = bulk_modulus * (r + slope_coeff * r * r) + gamma * heat
    return ux, uy, uz, heat, press


def total_pressure(press, sw, r, slope):
    squeeze = jnp.minimum(slope, 0.0)
    return press + sw * quad_viscosity * (1.0 + r) * squeeze * squeeze


def flux(state, axis, speed, total):
    rows = [state[1 + axis]] + [state[1 + k] * speed for k in range(3)]
    rows[1 + axis] = rows[1 + axis] + total
    return rows + [(state[4] + total) * speed]


def upper_part(f, u):
    return 0.5 * f - HALF_C * u


def lower_part(f, u):
    return 0.5 * f + HALF_C * u


def layer(z):
    return pl.ds(NX * z, NX)


def x_row(x):
    return pl.ds(x, NZ, stride=NX)


def lanes():
    return lax.broadcasted_iota(jnp.int32, (NX, NY), 1)


def y_next(value, column, lane):
    return jnp.where(lane == NY - 1, column, pltpu.roll(value, NY - 1, 1))


def y_prev(value, column, lane):
    return jnp.where(lane == 0, column, pltpu.roll(value, 1, 1))


def inside(flag):
    return jnp.where(flag, 1.0, 0.0).astype(F32)


def masks(mesh):
    ix, iy, iz = lax.axis_index("gx"), lax.axis_index("gy"), lax.axis_index("gz")
    return (
        (inside(ix > 0), inside(ix < mesh["gx"] - 1)),
        (inside(iy > 0), inside(iy < mesh["gy"] - 1)),
        (inside(iz > 0), inside(iz < mesh["gz"] - 1)),
        iz == 0,
    )


def face_layer(is_first, depth):
    return jnp.where(is_first, NZ - 1 - depth, depth)


def dyn_layer(z):
    return pl.ds(pl.multiple_of(NX * z, NX), NX)


def pack_edges(values, lane, depth=2):
    out = pltpu.roll(values[0], depth, 1)
    for i in range(1, len(values)):
        out = jnp.where(lane < 2 * depth * i, out, pltpu.roll(values[i], depth * (2 * i + 1), 1))
    return out


def begun(u, f, far, sign):
    return STAY * u + time_ratio * (sign * 0.5 * f + HALF_C * far)


def prep_kernel(mesh, u_ref, g_ref, s_ref, ylo, yhi, zs, yp):
    _, _, _, first = masks(mesh)
    lane = lanes()
    for z in range(NZ):
        vals = [u_ref[k, layer(z), :] for k in range(5)]
        vals += [g_ref[layer(z), :], s_ref[0, layer(z), :].astype(F32)]
        yp[layer(z), :] = pack_edges(vals, lane, 3)
    rows = yp[...].T
    for out, c1, c2, c3, sign in ((yhi, 2, 1, 0, 1.0), (ylo, 3, 4, 5, -1.0)):
        st, st2, st3 = [[rows[6 * k + c : 6 * k + c + 1] for k in range(7)] for c in (c1, c2, c3)]
        prim, prim2 = primitives(*st[:6]), primitives(*st2[:6])
        slope = (sign * 0.5) * (prim[1] - st3[2] / (1.0 + st3[0]))
        fl = flux(st2[:5], 1, prim2[1], total_pressure(prim2[4], st2[6], st2[0], slope))
        items = st[:5] + [prim[4], st[6], prim2[1]] + [begun(st[k], fl[k], st2[k], sign) for k in range(3)]
        for k in range(11):
            out[k : k + 1] = items[k]
        out[11:16] = jnp.zeros((5, NY), F32)
    za, zb, zc = [dyn_layer(face_layer(first, d)) for d in range(3)]
    sign = jnp.where(first, 1.0, -1.0)
    st, st2 = [[u_ref[k, at, :] for k in range(5)] for at in (za, zb)]
    prim, prim2 = primitives(*st, g_ref[za, :]), primitives(*st2, g_ref[zb, :])
    slope = (sign * 0.5) * (prim[2] - u_ref[3, zc, :] / (1.0 + u_ref[0, zc, :]))
    fl = flux(st2, 2, prim2[2], total_pressure(prim2[4], s_ref[0, zb, :].astype(F32), st2[0], slope))
    items = st + [prim[4], s_ref[0, za, :].astype(F32), prim2[2]]
    items += [begun(st[k], fl[k], st2[k], sign) for k in (0, 1, 3)]
    for k in range(11):
        zs[k] = items[k]


def still_kernel(u_ref, g_ref, s_ref, vel, heat, press, inner, slo, shi):
    lane = lanes()
    for z in range(NZ):
        prim = primitives(*[u_ref[k, layer(z), :] for k in range(5)], g_ref[layer(z), :])
        for k in range(3):
            vel[k, layer(z), :] = prim[k]
        heat[layer(z), :] = prim[3]
        press[layer(z), :] = prim[4]
        st = [u_ref[k, layer(z), :] for k in range(5)]
        uy = prim[1]
        squeeze = jnp.minimum(0.5 * (pltpu.roll(uy, NY - 1, 1) - pltpu.roll(uy, 1, 1)), 0.0)
        squeeze = jnp.where((lane == 0) | (lane == NY - 1), 0.0, squeeze)
        visc = s_ref[0, layer(z), :].astype(F32) * quad_viscosity * (1.0 + st[0])
        fy = flux(st, 1, uy, prim[4] + visc * squeeze * squeeze)
        for k in range(5):
            inner[k, layer(z), :] = STAY * st[k] - time_ratio * (
                y_next(upper_part(fy[k], st[k]), 0.0, lane) - y_prev(lower_part(fy[k], st[k]), 0.0, lane)
            )
    for out, e, i, j, last, sign in ((shi, NX - 1, NX - 2, NX - 3, NX - 4, 1.0), (slo, 0, 1, 2, 3, -1.0)):
        for k in range(5):
            out[k] = u_ref[k, x_row(e), :]
        out[5] = g_ref[x_row(e), :]
        out[6] = s_ref[0, x_row(e), :].astype(F32)
        out[7] = vel[0, x_row(i), :]
        out[8] = s_ref[1, x_row(e), :].astype(F32)
        for at, before, after, base, count in ((i, e, j, 9, 5), (j, i, last, 14, 2)):
            st = [u_ref[k, x_row(at), :] for k in range(5)]
            slope = (sign * 0.5) * (vel[0, x_row(before), :] - vel[0, x_row(after), :])
            total = total_pressure(press[x_row(at), :], s_ref[0, x_row(at), :].astype(F32), st[0], slope)
            fl = flux(st, 0, vel[0, x_row(at), :], total)
            for k in range(count):
                out[base + k] = time_ratio * (sign * 0.5 * fl[k] + HALF_C * st[k])


def side_kernel(
    mesh, u_ref, s_ref, vel, pr, inner, slo, shi, ylo, yhi, yl, yh, zr,
    part, xlo, xhi, zz,
    vz, az, bz, yr,
):
    _, (myl, myh), (mzl, mzh), first = masks(mesh)
    for z in range(NZ):
        vz[layer(z + 1), :] = vel[2, layer(z), :]
    far = [zr[k] for k in range(8)]
    speed = far[3] / (1.0 + far[0])
    own = vel[2, dyn_layer(face_layer(first, 0)), :]
    slope = (far[7] - own) * jnp.where(first, 0.5, -0.5)
    fl = flux(far[:5], 2, speed, total_pressure(far[5], far[6], far[0], slope))
    for k in range(5):
        bz[k, layer(0), :] = lower_part(fl[k], far[k]) * mzl
        az[k, layer(NZ), :] = upper_part(fl[k], far[k]) * mzh
    vz[layer(0), :] = speed * mzl
    vz[layer(NZ + 1), :] = speed * mzh
    yr[...] = jnp.zeros(yr.shape, F32)
    sides = []
    for side, ref, mask, own, sign in ((0, yl, myl, ylo, 1.0), (1, yh, myh, yhi, -1.0)):
        items = [ref[k : k + 1] * mask for k in range(8)]
        sides.append(items)
        speed = items[2] / (1.0 + items[0])
        uy = own[2:3] / (1.0 + own[0:1])
        slope = (sign * 0.5) * (uy - items[7])
        fl = flux(items[:5], 1, speed, total_pressure(items[5], items[6], items[0], slope))
        squeeze = jnp.minimum((sign * 0.5) * (own[7:8] - speed), 0.0)
        visc = own[6:7] * quad_viscosity * (1.0 + own[0:1]) * squeeze * squeeze
        for k in range(5):
            at = 4 * k + side
            yr[at : at + 1, :] = time_ratio * (sign * 0.5 * fl[k] + HALF_C * items[k])
        yr[10 + side : 11 + side, :] = (sign * HALF_T) * visc
        yr[18 + side : 19 + side, :] = (sign * HALF_T) * visc * uy
    low, high = sides
    parts = jnp.concatenate([piece.astype(F32) for piece in split3(yr[...].T)], axis=1).astype(jnp.bfloat16)
    item = lax.bitwise_and(lax.broadcasted_iota(jnp.int32, (3 * yr.shape[0], NY), 0), yr.shape[0] - 1)
    column = lax.broadcasted_iota(jnp.int32, (3 * yr.shape[0], NY), 1)
    for k in range(5):
        place = (item == 4 * k) & (column == 0) | (item == 4 * k + 1) & (column == NY - 1)
        place = place | (item == 4 * k + 2) & (column == 1) | (item == 4 * k + 3) & (column == NY - 2)
        spread = jnp.where(place, 1.0, 0.0).astype(jnp.bfloat16)
        part[k] = inner[k] + jnp.dot(parts, spread, preferred_element_type=F32)
    for z in range(NZ):
        st = [u_ref[k, layer(z), :] for k in range(5)]
        squeeze = jnp.minimum(0.5 * (vz[layer(z + 2), :] - vz[layer(z), :]), 0.0)
        visc = s_ref[0, layer(z), :].astype(F32) * quad_viscosity * (1.0 + st[0])
        fz = flux(st, 2, vel[2, layer(z), :], pr[layer(z), :] + visc * squeeze * squeeze)
        for k in range(5):
            az[k, layer(z), :] = upper_part(fz[k], st[k])
            bz[k, layer(z + 1), :] = lower_part(fz[k], st[k])
    for z in range(NZ):
        for k in range(5):
            part[k, layer(z), :] = part[k, layer(z), :] - time_ratio * (
                az[k, layer(z + 1), :] - bz[k, layer(z), :]
            )
    for k in range(8):
        zz[k : k + 1, :] = low[k]
        zz[8 + k : 9 + k, :] = high[k]
    for out, still, e, i in ((xhi, shi, NX - 1, NX - 2), (xlo, slo, 0, 1)):
        for k in range(9):
            out[k] = still[k]
        for k in range(5):
            out[9 + k] = part[k, x_row(e), :] + still[9 + k]
        for k in range(2):
            out[14 + k] = part[k, x_row(i), :] + still[14 + k]
        out[16] = zz[...]
        for k in range(8):
            out[17, k : k + 1, :] = zr[k, e : e + 1, :]
        out[17, 8:9, :] = zr[1, i : i + 1, :] / (1.0 + zr[0, i : i + 1, :])
        out[17, 9:16, :] = jnp.zeros((7, NY), F32)


def shifted_x(own, low, high, at_x):
    up = jnp.where(at_x == NX - 1, pltpu.roll(high, NX - 1, 1), pltpu.roll(own, NY - 1, 1))
    down = jnp.where(at_x == 0, pltpu.roll(low, NY - NX + 1, 1), pltpu.roll(own, 1, 1))
    return up, down


def halo_step(
    mesh, u_ref, g_ref, s_ref, vel, pr, part, ylo, yhi, yl, yh, zr, xl, xh, zz,
    o_ref, xc, hxl, hxh, hyl, hyh, hz, vx, ax, bx, zc,
):
    (mxl, mxh), (myl, myh), (mzl, mzh), first = masks(mesh)
    for z in range(NZ):
        vx[pl.ds(24 * z + 8, 8), :] = vel[0, layer(z), :]
    low = [xl[k] * mxl for k in range(8)]
    high = [xh[k] * mxh for k in range(8)]
    prim = primitives(*low[:6])
    vx[pl.ds(7, NZ, stride=24), :] = prim[0]
    slope = 0.5 * (vx[pl.ds(8, NZ, stride=24), :] - low[7])
    f_low = flux(low[:5], 0, prim[0], total_pressure(prim[4], low[6], low[0], slope))
    prim = primitives(*high[:6])
    vx[pl.ds(16, NZ, stride=24), :] = prim[0]
    slope = 0.5 * (high[7] - vx[pl.ds(15, NZ, stride=24), :])
    f_high = flux(high[:5], 0, prim[0], total_pressure(prim[4], high[6], high[0], slope))
    for k in range(5):
        bx[k, pl.ds(7, NZ, stride=16), :] = lower_part(f_low[k], low[k])
        ax[k, pl.ds(8, NZ, stride=16), :] = upper_part(f_high[k], high[k])
    for z in range(NZ):
        st = [u_ref[k, layer(z), :] for k in range(5)]
        ux, press = vel[0, layer(z), :], pr[layer(z), :]
        slope = 0.5 * (vx[pl.ds(24 * z + 9, 8), :] - vx[pl.ds(24 * z + 7, 8), :])
        fx = flux(st, 0, ux, total_pressure(press, s_ref[0, layer(z), :].astype(F32), st[0], slope))
        for k in range(5):
            ax[k, pl.ds(16 * z, 8), :] = upper_part(fx[k], st[k])
            bx[k, pl.ds(16 * z + 8, 8), :] = lower_part(fx[k], st[k])
    for z in range(NZ):
        for k in range(5):
            o_ref[k, layer(z), :] = part[k, layer(z), :] - time_ratio * (
                ax[k, pl.ds(16 * z + 1, 8), :] - bx[k, pl.ds(16 * z + 7, 8), :]
            )
    for out, ref, mask in ((hxl, xl, mxl), (hxh, xh, mxh)):
        if ref is xl:
            near = [-ax[k, pl.ds(0, NZ, stride=16), :] for k in range(5)]
            next_ = [-upper_part(f_low[k], low[k]) for k in range(2)]
        else:
            near = [bx[k, pl.ds(15, NZ, stride=16), :] for k in range(5)]
            next_ = [lower_part(f_high[k], high[k]) for k in range(2)]
        st = [(ref[9 + k] + time_ratio * near[k]) * mask for k in range(5)]
        st2 = [(ref[14 + k] + time_ratio * next_[k]) * mask for k in range(2)]
        out[0] = st[0]
        out[1] = st[1]
        out[2] = primitives(*st, ref[5] * mask)[4]
        out[3] = ref[8] * mask
        out[4] = st2[1] / (1.0 + st2[0])
        base = 0 if ref is xl else 3
        inv, gamma = 1.0 / (1.0 + st[0]), ref[5] * mask
        xc[base] = (2.0 - gamma) * (st[1] * inv)
        xc[base + 1] = inv
        xc[base + 2] = gamma
    lane = lax.broadcasted_iota(jnp.int32, (1, NY), 1)
    at_x = lax.bitwise_and(lane, NX - 1)
    for side, ref, mask, own, out, sign in ((0, yl, myl, ylo, hyl, -1.0), (1, yh, myh, yhi, hyh, 1.0)):

        def items(values, m):
            return [values[k : k + 1] * m for k in range(8)]

        here = items(ref, mask)
        near_l, near_h = items(xl[16, 8 * side : 8 * side + 8, :], mxl), items(xh[16, 8 * side : 8 * side + 8, :], mxh)
        ux, ux_l, ux_h = [v[1] / (1.0 + v[0]) for v in (here, near_l, near_h)]
        up, down = shifted_x(ux, ux_l, ux_h, at_x)
        slope = 0.5 * (up - down)
        slope_h = 0.5 * (pltpu.roll(ux_h, NY - 1, 1) - pltpu.roll(ux, NY - NX + 1, 1))
        slope_l = 0.5 * (pltpu.roll(ux, NX - 1, 1) - pltpu.roll(ux_l, 1, 1))

        def fx_of(v, speed, slope):
            return [v[1], v[1] * speed + total_pressure(v[5], v[6], v[0], slope), v[2] * speed]

        f_here, f_l, f_h = fx_of(here, ux, slope), fx_of(near_l, ux_l, slope_l), fx_of(near_h, ux_h, slope_h)
        uz = here[3] / (1.0 + here[0])
        near_z = items(zz[8 * side : 8 * side + 8, :], 1.0)
        uz_z = near_z[3] / (1.0 + near_z[0])
        fz, fz_z = [[v[3], v[1] * w, v[2] * w] for v, w in ((here, uz), (near_z, uz_z))]
        self_ = items(own, 1.0)
        uy = self_[2] / (1.0 + self_[0])
        uy_here = here[2] / (1.0 + here[0])
        slope = 0.5 * (self_[7] - uy_here if side == 0 else uy_here - self_[7])
        fy = [self_[2], self_[1] * uy, self_[2] * uy + total_pressure(self_[5], self_[6], self_[0], slope)]
        new = []
        for k in range(3):
            a_x, _ = shifted_x(upper_part(f_here[k], here[k]), ux_l, upper_part(f_h[k], near_h[k]), at_x)
            _, b_x = shifted_x(lower_part(f_here[k], here[k]), lower_part(f_l[k], near_l[k]), ux_h, at_x)
            a_z = jnp.where(
                lane >= NY - NX,
                pltpu.roll(upper_part(fz_z[k], near_z[k]), NY - NX, 1) * mzh,
                pltpu.roll(upper_part(fz[k], here[k]), NY - NX, 1),
            )
            b_z = jnp.where(
                lane < NX,
                pltpu.roll(lower_part(fz_z[k], near_z[k]), NX, 1) * mzl,
                pltpu.roll(lower_part(fz[k], here[k]), NX, 1),
            )
            facing = sign * 0.5 * fy[k] + HALF_C * self_[k]
            new.append(mask * (ref[8 + k : 9 + k] + time_ratio * (facing - (a_x - b_x) - (a_z - b_z))))
        r, mx, my = new
        combine = lower_part if side == 0 else upper_part
        out[0:1, :] = combine(my, r)
        out[1:2, :] = combine(mx * (my / (1.0 + r)), mx)
        out[2:8, :] = jnp.zeros((6, NY), F32)
    rows = []
    for side in range(2):
        v = [zz[8 * side + k : 8 * side + k + 1, :] for k in range(8)]
        speed = v[2] / (1.0 + v[0])
        fy = [v[2], v[1] * speed, v[3] * speed]
        combine = upper_part if side else lower_part
        rows += [combine(f, v[k]) for f, k in zip(fy, (0, 1, 3))]
    zc[...] = jnp.concatenate(rows + [jnp.zeros((2, NY), F32)], axis=0).T
    cols = zc[dyn_layer(jnp.where(first, 0, NZ - 1)), :]
    full = lanes()
    deep = lax.broadcasted_iota(jnp.int32, (NX, NY), 0)
    here = [zr[k] for k in range(8)]
    near_l = [xl[17, k : k + 1, :] * mxl for k in range(9)]
    near_h = [xh[17, k : k + 1, :] * mxh for k in range(9)]
    ux, ux_l, ux_h = [v[1] / (1.0 + v[0]) for v in (here, near_l, near_h)]

    def next_x(value, row):
        return jnp.where(deep == NX - 1, row, pltpu.roll(value, NX - 1, 0))

    def prev_x(value, row):
        return jnp.where(deep == 0, row, pltpu.roll(value, 1, 0))

    slope = 0.5 * (next_x(ux, ux_h) - prev_x(ux, ux_l))
    slope_h = 0.5 * (near_h[8] - ux[NX - 1 : NX])
    slope_l = 0.5 * (ux[0:1] - near_l[8])

    def fx_layer(v, speed, slope):
        return [v[1], v[1] * speed + total_pressure(v[5], v[6], v[0], slope), v[3] * speed]

    f_here, f_l, f_h = fx_layer(here, ux, slope), fx_layer(near_l, ux_l, slope_l), fx_layer(near_h, ux_h, slope_h)
    uy = here[2] / (1.0 + here[0])
    fy = [here[2], here[1] * uy, here[3] * uy]
    za, zb = dyn_layer(face_layer(first, 0)), dyn_layer(face_layer(first, 1))
    sign = jnp.where(first, 1.0, -1.0)
    st = [u_ref[k, za, :] for k in range(5)]
    slope = (sign * 0.5) * (here[3] / (1.0 + here[0]) - vel[2, zb, :])
    fz = flux(st, 2, vel[2, za, :], total_pressure(pr[za, :], s_ref[0, za, :].astype(F32), st[0], slope))
    new = []
    for n, k in enumerate((0, 1, 3)):
        a_x = next_x(upper_part(f_here[n], here[k]), upper_part(f_h[n], near_h[k]))
        b_x = prev_x(lower_part(f_here[n], here[k]), lower_part(f_l[n], near_l[k]))
        a_y = y_next(upper_part(fy[n], here[k]), cols[:, 3 + n : 4 + n], full)
        b_y = y_prev(lower_part(fy[n], here[k]), cols[:, n : n + 1], full)
        facing = sign * 0.5 * fz[k] + HALF_C * st[k]
        new.append(zr[8 + n] + time_ratio * (facing - (a_x - b_x) - (a_y - b_y)))
    r, mx, mz = new
    hz[0] = 0.5 * mz - (sign * HALF_C) * r
    hz[1] = 0.5 * mx * (mz / (1.0 + r)) - (sign * HALF_C) * mx


def forward_kernel(
    mesh, u0_ref, g_ref, s_ref, vel, pr, part, ylo_in, yhi_in, yl, yh, zr, xl, xh, zz, n_ref, m_ref,
    u_ref, lam_ref, cf_ref, cfh_ref, mis_ref, xc, ylo, yhi, zs, yown,
    hxl, hxh, hyl, hyh, hz, vx, ax, bx, az, bz, ch, yc, yp, zc,
):
    halo_step(
        mesh, u0_ref, g_ref, s_ref, vel, pr, part, ylo_in, yhi_in, yl, yh, zr, xl, xh, zz,
        u_ref, xc, hxl, hxh, hyl, hyh, hz, vx, ax, bx, zc,
    )
    speed_kernel(
        mesh, u_ref, g_ref, s_ref, hxl, hxh, hyl, hyh, hz, n_ref, m_ref,
        lam_ref, cf_ref, cfh_ref, mis_ref, ylo, yhi, zs, yown,
        vx, ax, bx, az, bz, ch, yc, yp,
    )


def columns_of(low, high, count, low_mask, high_mask):
    rows = [low[k : k + 1] * low_mask for k in range(count)]
    rows += [high[k : k + 1] * high_mask for k in range(count)]
    rows.append(jnp.zeros((8 - 2 * count, NY), F32))
    return jnp.concatenate(rows, axis=0).T


def speed_kernel(
    mesh, u_ref, g_ref, s_ref, xl, xh, yl, yh, zr, n_ref, m_ref,
    lam_ref, cf_ref, cfh_ref, mis_ref, ylo, yhi, zs, yown,
    vx, ax, bx, az, bz, ch, yc, yp,
):
    (mxl, mxh), (myl, myh), (mzl, mzh), first = masks(mesh)
    lane = lanes()
    for z in range(NZ):
        vx[pl.ds(24 * z + 8, 8), :] = u_ref[1, layer(z), :] / (1.0 + u_ref[0, layer(z), :])
    for side, ref, mask in ((0, xl, mxl), (1, xh, mxh)):
        r, mx, press, sw, second = [ref[k] * mask for k in range(5)]
        speed = mx / (1.0 + r)
        vx[pl.ds(16 if side else 7, NZ, stride=24), :] = speed
        own = vx[pl.ds(15 if side else 8, NZ, stride=24), :]
        slope = 0.5 * (second - own if side else own - second)
        squeeze = jnp.minimum(slope, 0.0)
        visc = sw * quad_viscosity * (1.0 + r) * squeeze
        cfh_ref[side] = 2.0 * visc
        f1 = mx * speed + press + visc * squeeze
        if side:
            ax[0, pl.ds(8, NZ, stride=16), :] = upper_part(mx, r)
            ax[1, pl.ds(8, NZ, stride=16), :] = upper_part(f1, mx)
        else:
            bx[0, pl.ds(7, NZ, stride=16), :] = lower_part(mx, r)
            bx[1, pl.ds(7, NZ, stride=16), :] = lower_part(f1, mx)
    for k in range(2):
        bz[k, layer(0), :] = zr[k] * mzl
        az[k, layer(NZ), :] = zr[k] * mzh
    yc[...] = columns_of(yl, yh, 2, myl, myh)
    for z in range(NZ):
        r, mx, my, mz, en = [u_ref[k, layer(z), :] for k in range(5)]
        ux, uy, uz, _, press = primitives(r, mx, my, mz, en, g_ref[layer(z), :])
        squeeze = jnp.minimum(0.5 * (vx[pl.ds(24 * z + 9, 8), :] - vx[pl.ds(24 * z + 7, 8), :]), 0.0)
        visc = s_ref[1, layer(z), :].astype(F32) * quad_viscosity * (1.0 + r) * squeeze
        cf_ref[layer(z), :] = 2.0 * visc
        f1 = mx * ux + press + visc * squeeze
        for k, st, fx, fy, fz in ((0, r, mx, my, mz), (1, mx, f1, mx * uy, mx * uz)):
            ax[k, pl.ds(16 * z, 8), :] = upper_part(fx, st)
            bx[k, pl.ds(16 * z + 8, 8), :] = lower_part(fx, st)
            az[k, layer(z), :] = upper_part(fz, st)
            bz[k, layer(z + 1), :] = lower_part(fz, st)
            ch[k, layer(z), :] = (
                3.0 * signal_speed * st
                + y_next(upper_part(fy, st), yc[layer(z), 2 + k : 3 + k], lane)
                - y_prev(lower_part(fy, st), yc[layer(z), k : k + 1], lane)
            )
    mis = jnp.zeros((NX, NY), F32)
    for z in range(NZ):
        new = []
        for k in range(2):
            change = (
                ch[k, layer(z), :]
                + (ax[k, pl.ds(16 * z + 1, 8), :] - bx[k, pl.ds(16 * z + 7, 8), :])
                + (az[k, layer(z + 1), :] - bz[k, layer(z), :])
            )
            new.append(u_ref[k, layer(z), :] - time_ratio * change)
        inv = 1.0 / (1.0 + new[0])
        speed = new[1] * inv
        off = speed - m_ref[layer(z), :]
        weight = n_ref[layer(z), :] * off
        mis = mis + weight * off
        lam_m = 2.0 * weight * inv
        lam_r = -lam_m * speed
        lam_ref[0, layer(z), :] = lam_r
        lam_ref[1, layer(z), :] = lam_m
        inv = 1.0 / (1.0 + u_ref[0, layer(z), :])
        extra = [u_ref[1, layer(z), :] * inv, u_ref[2, layer(z), :] * inv, g_ref[layer(z), :]]
        yp[layer(z), :] = pack_edges([lam_r, lam_m] + extra, lane)
    mis_ref[...] = mis
    za, zb = dyn_layer(face_layer(first, 0)), dyn_layer(face_layer(first, 1))
    inv = 1.0 / (1.0 + u_ref[0, za, :])
    ux = u_ref[1, za, :] * inv
    zs[0] = lam_ref[0, za, :]
    zs[1] = lam_ref[1, za, :]
    zs[2] = jnp.where(first, -HALF_T, HALF_T) * (lam_ref[0, zb, :] + lam_ref[1, zb, :] * ux)
    zs[3] = ux
    zs[4] = u_ref[3, za, :] * inv
    zs[5] = g_ref[za, :]
    rows = yp[...].T
    for out, edge, second, own, sign in ((yhi, 1, 0, 2, -HALF_T), (ylo, 2, 3, 0, HALF_T)):
        lam_r, lam_m, ux, uy, gamma = [rows[4 * i + edge : 4 * i + edge + 1] for i in range(5)]
        out[0:1] = lam_r
        out[1:2] = lam_m
        out[2:3] = sign * (rows[second : second + 1] + rows[4 + second : 5 + second] * ux)
        out[3:4] = ux
        out[4:5] = uy
        out[5:6] = gamma
        out[6:] = jnp.zeros((out.shape[0] - 6, NY), F32)
        yown[own : own + 1] = lam_r
        yown[own + 1 : own + 2] = lam_m
    yown[4:8] = jnp.zeros((4, NY), F32)


def edge_kernel(mesh, u_ref, lam_ref, cf_ref, yl, yh, zr, xlo, xhi, yc):
    _, (myl, myh), (mzl, mzh), _ = masks(mesh)
    low_y, high_y = yl[1:2] * myl, yh[1:2] * myh
    yc[:, 0:8] = jnp.concatenate([low_y, high_y, jnp.zeros((6, NY), F32)], axis=0).T
    lane = lax.broadcasted_iota(jnp.int32, (NZ, NY), 1)
    deep = lax.broadcasted_iota(jnp.int32, (NZ, NY), 0)
    for out, e, i, i2, sign in ((xhi, NX - 1, NX - 2, NX - 3, 1.0), (xlo, 0, 1, 2, -1.0)):
        r, my, mz = [u_ref[k, x_row(e), :] for k in (0, 2, 3)]
        inv = 1.0 / (1.0 + r)
        lm, lm_i = lam_ref[1, x_row(e), :], lam_ref[1, x_row(i), :]
        col = yc[x_row(e), :]
        side = zr[1, e : e + 1, :]
        up_y = jnp.where(lane == NY - 1, col[:, 1:2], pltpu.roll(lm, NY - 1, 1))
        down_y = jnp.where(lane == 0, col[:, 0:1], pltpu.roll(lm, 1, 1))
        up_z = jnp.where(deep == NZ - 1, side * mzh, pltpu.roll(lm, NZ - 1, 0))
        down_z = jnp.where(deep == 0, side * mzl, pltpu.roll(lm, 1, 0))
        slope = (sign * HALF_T) * (lm - lam_ref[1, x_row(i2), :]) * cf_ref[x_row(i), :]
        out[0] = lam_ref[0, x_row(e), :]
        out[1] = lm
        out[2] = lm_i
        out[3] = (
            STAY * lm
            + NEAR * (lm_i + (up_y + down_y) + (up_z + down_z))
            - (sign * HALF_T) * lam_ref[0, x_row(i), :]
            + HALF_T * ((up_y - down_y) * (my * inv) + (up_z - down_z) * (mz * inv))
            + (sign * 0.5) * slope * inv
        )
        out[4] = jnp.where(deep == 0, low_y, jnp.where(deep == 1, high_y, jnp.where(deep == 2, side, 0.0)))


def lean_kernel(mesh, u_ref, lam_ref, yl, yh, zr, base, vel, inv_ref, heat, lz, yc):
    _, (myl, myh), (mzl, mzh), _ = masks(mesh)
    lane = lanes()
    for k in range(2):
        for z in range(NZ):
            lz[k, layer(z + 1), :] = lam_ref[k, layer(z), :]
        lz[k, layer(0), :] = zr[k] * mzl
        lz[k, layer(NZ + 1), :] = zr[k] * mzh
    yc[...] = columns_of(yl, yh, 2, myl, myh)
    for z in range(NZ):
        r, mx, my, mz, en = [u_ref[k, layer(z), :] for k in range(5)]
        inv = 1.0 / (1.0 + r)
        ux, uy, uz = mx * inv, my * inv, mz * inv
        heat[layer(z), :] = en - 0.5 * (mx * ux + my * uy + mz * uz)
        inv_ref[layer(z), :] = inv
        for k, value in enumerate((ux, uy, uz)):
            vel[k, layer(z), :] = value
        lr, lm = lam_ref[0, layer(z), :], lam_ref[1, layer(z), :]
        lr_z = [lz[0, layer(z + s), :] for s in (0, 2)]
        lm_z = [lz[1, layer(z + s), :] for s in (0, 2)]
        lr_y = [y_prev(lr, yc[layer(z), 0:1], lane), y_next(lr, yc[layer(z), 2:3], lane)]
        lm_y = [y_prev(lm, yc[layer(z), 1:2], lane), y_next(lm, yc[layer(z), 3:4], lane)]
        phi_y1 = HALF_T * (lm_y[1] - lm_y[0])
        phi_z1 = HALF_T * (lm_z[1] - lm_z[0])
        near = (lm_y[0] + lm_y[1]) + (lm_z[0] + lm_z[1])
        base[0, layer(z), :] = STAY * lm + NEAR * near + phi_y1 * uy + phi_z1 * uz
        base[1, layer(z), :] = HALF_T * (lr_y[1] - lr_y[0]) + phi_y1 * ux
        base[2, layer(z), :] = HALF_T * (lr_z[1] - lr_z[0]) + phi_z1 * ux


def gradient_kernel(
    mesh, vel, heat_ref, u_ref, g_ref, base, vel_1, inv_1, heat_1, lam_ref, cf_ref, cfh_ref, xc, yown, yl, yh, zr, xl, xh, mis_ref, v_ref,
    grad_ref, row_ref,
    lx, px, dx, dg, yc, gx, gy, gz,
):
    (mxl, mxh), (myl, myh), (mzl, mzh), first = masks(mesh)
    lane = lanes()
    for k in range(2):
        for z in range(NZ):
            lx[k, pl.ds(24 * z + 8, 8), :] = lam_ref[k, layer(z), :]
        lx[k, pl.ds(7, NZ, stride=24), :] = xl[k] * mxl
        lx[k, pl.ds(16, NZ, stride=24), :] = xh[k] * mxh
    phi_low = HALF_T * (lam_ref[1, x_row(0), :] - xl[2] * mxl)
    phi_high = HALF_T * (xh[2] * mxh - lam_ref[1, x_row(NX - 1), :])
    dx[pl.ds(7, NZ, stride=24), :] = phi_low * cfh_ref[0]
    dx[pl.ds(16, NZ, stride=24), :] = phi_high * cfh_ref[1]
    for z in range(NZ):
        phi = HALF_T * (lx[1, pl.ds(24 * z + 9, 8), :] - lx[1, pl.ds(24 * z + 7, 8), :])
        px[layer(z), :] = phi
        dx[pl.ds(24 * z + 8, 8), :] = phi * cf_ref[layer(z), :]
    gx[1, pl.ds(7, NZ, stride=24), :] = mxl * phi_low * xc[2]
    gx[1, pl.ds(16, NZ, stride=24), :] = mxh * phi_high * xc[5]
    gx[0, pl.ds(7, NZ, stride=24), :] = mxl * (
        xl[3]
        + HALF_T * lam_ref[0, x_row(0), :]
        + NEAR * lam_ref[1, x_row(0), :]
        + phi_low * xc[0]
        - 0.5 * dx[pl.ds(8, NZ, stride=24), :] * xc[1]
    )
    gx[0, pl.ds(16, NZ, stride=24), :] = mxh * (
        xh[3]
        - HALF_T * lam_ref[0, x_row(NX - 1), :]
        + NEAR * lam_ref[1, x_row(NX - 1), :]
        + phi_high * xc[3]
        + 0.5 * dx[pl.ds(15, NZ, stride=24), :] * xc[4]
    )
    at_x = lax.bitwise_and(lax.broadcasted_iota(jnp.int32, (1, NY), 1), NX - 1)
    from_high, from_low = pltpu.roll(xh[4], NX - 1, 1) * mxh, pltpu.roll(xl[4], NY - NX + 1, 1) * mxl
    halo = []
    for side, ref, mask, sign in ((0, yl, myl, HALF_T), (1, yh, myh, -HALF_T)):
        items = ref[0:8]
        up = jnp.where(at_x == NX - 1, from_high[side : side + 1], pltpu.roll(items, NY - 1, 1)[1:2])
        down = jnp.where(at_x == 0, from_low[side : side + 1], pltpu.roll(items, 1, 1)[1:2])
        d_en = HALF_T * (up - down) * items[5:6]
        own_r, own_m = yown[2 * side : 2 * side + 1], yown[2 * side + 1 : 2 * side + 2]
        d_my = items[2:3] + sign * (own_r + own_m * items[3:4]) - d_en * items[4:5]
        halo += [d_my * mask, d_en * mask]
    yc[...] = jnp.concatenate(halo + [jnp.zeros((4, NY), F32)], axis=0).T
    deep = lax.broadcasted_iota(jnp.int32, (NX, NY), 0)
    up = jnp.where(deep == NX - 1, xh[4, 2:3, :] * mxh, pltpu.roll(zr[1], NX - 1, 0))
    down = jnp.where(deep == 0, xl[4, 2:3, :] * mxl, pltpu.roll(zr[1], 1, 0))
    d_en = HALF_T * (up - down) * zr[5]
    za = dyn_layer(face_layer(first, 0))
    d_mz = (
        zr[2]
        + jnp.where(first, -HALF_T, HALF_T) * (lam_ref[0, za, :] + lam_ref[1, za, :] * zr[3])
        - d_en * zr[4]
    )
    for k, value in ((0, d_mz), (1, d_en)):
        gz[k, layer(0), :] = value * mzl
        gz[k, layer(NZ + 1), :] = value * mzh
    for z in range(NZ):
        ux, uy, uz = [vel_1[k, layer(z), :] for k in range(3)]
        lr_x = [lx[0, pl.ds(24 * z + s, 8), :] for s in (7, 9)]
        lm_x = [lx[1, pl.ds(24 * z + s, 8), :] for s in (7, 9)]
        phi_x1 = px[layer(z), :]
        d_speed = phi_x1 * u_ref[1, layer(z), :] + 0.5 * (dx[pl.ds(24 * z + 7, 8), :] - dx[pl.ds(24 * z + 9, 8), :])
        d_en = phi_x1 * g_ref[layer(z), :]
        gx[0, pl.ds(24 * z + 8, 8), :] = (
            base[0, layer(z), :]
            + NEAR * (lm_x[0] + lm_x[1])
            + HALF_T * (lr_x[1] - lr_x[0])
            + (phi_x1 - d_en) * ux
            + d_speed * inv_1[layer(z), :]
        )
        gx[1, pl.ds(24 * z + 8, 8), :] = d_en
        gy[layer(z), :] = base[1, layer(z), :] - d_en * uy
        gz[0, layer(z + 1), :] = base[2, layer(z), :] - d_en * uz
        gz[1, layer(z + 1), :] = d_en
        dg[layer(z), :] = phi_x1 * heat_1[layer(z), :]
    acc = jnp.zeros((NX, NY), F32)
    for z in range(NZ):
        ux, uy, uz = [vel[k, layer(z), :] for k in range(3)]
        heat = heat_ref[layer(z), :]
        dif_x = [gx[k, pl.ds(24 * z + 9, 8), :] - gx[k, pl.ds(24 * z + 7, 8), :] for k in range(2)]
        dif_z = [gz[k, layer(z + 2), :] - gz[k, layer(z), :] for k in range(2)]
        dif_y = []
        for k, own in ((0, gy[layer(z), :]), (1, gz[1, layer(z + 1), :])):
            dif_y.append(
                y_next(own, yc[layer(z), 2 + k : 3 + k], lane) - y_prev(own, yc[layer(z), k : k + 1], lane)
            )
        d_press = HALF_T * (
            (dif_x[0] + ux * dif_x[1]) + (dif_y[0] + uy * dif_y[1]) + (dif_z[0] + uz * dif_z[1])
        )
        grad = dg[layer(z), :] + d_press * heat
        grad_ref[layer(z), :] = grad
        acc = acc + grad * grad
    total = jnp.sum(jnp.sum(acc, axis=0, keepdims=True), axis=1, keepdims=True)
    miss = jnp.sum(jnp.sum(mis_ref[...], axis=0, keepdims=True), axis=1, keepdims=True)
    miss = miss + jnp.sum(v_ref[...], axis=1, keepdims=True)
    row = jnp.where(lane == 0, total, jnp.where(lane == 1, miss, 0.0))
    for i in range(row_ref.shape[0] // NX):
        row_ref[layer(i), :] = row[:, :NARROW]


def scale_kernel(devices, count, grad_ref, rows_ref, out_ref, misfit_ref):
    acc = rows_ref[layer(0), :]
    for i in range(1, devices // NX):
        acc = acc + rows_ref[layer(i), :]
    row = jnp.sum(acc, axis=0, keepdims=True)
    misfit_ref[0, 0] = row[0, 1] / (devices * count)
    scale = 1.0 / jnp.sqrt(row[0:1, 0:1] / (devices * CELLS * NY) + small_eps)
    out_ref[...] = grad_ref[...] * scale


def split3(value):
    hi = value.astype(jnp.bfloat16)
    rest = value - hi.astype(F32)
    mid = rest.astype(jnp.bfloat16)
    low = (rest - mid.astype(F32)).astype(jnp.bfloat16)
    return hi, mid, low


def probe_kernel(p_ref, o_ref, n_ref, m_ref, v_ref):
    count = p_ref.shape[1]
    probes, obs = p_ref[...], o_ref[...]
    row = lax.broadcasted_iota(jnp.int32, (CELLS, count), 0)
    on_a = row == lax.shift_right_logical(probes, 7)
    on_b = row == lax.bitwise_and(probes, NY - 1)
    one_a = jnp.where(on_a, 1.0, 0.0).astype(jnp.bfloat16)
    one_b = jnp.where(on_b, 1.0, 0.0).astype(jnp.bfloat16)

    def nt(a, b):
        return lax.dot_general(a, b, (((1,), (1,)), ((), ())), preferred_element_type=F32)

    parts = [jnp.where(on_a, part.astype(F32), 0.0).astype(jnp.bfloat16) for part in split3(obs)]
    hits = nt(one_a, one_b)
    sums = nt(parts[0], one_b) + (nt(parts[1], one_b) + nt(parts[2], one_b))
    n_ref[...] = hits
    mean = sums / jnp.maximum(hits, 1.0)
    m_ref[...] = mean
    mean_t = split3(mean.T)
    picked = sum(jnp.dot(part, one_a, preferred_element_type=F32) for part in reversed(mean_t))
    at_probe = jnp.sum(jnp.where(on_b, picked, 0.0), axis=0, keepdims=True)
    off = obs - at_probe
    v_ref[...] = off * off


SMALL = pltpu.CompilerParams(vmem_limit_bytes=12 * 1024 * 1024)

LARGE = pltpu.CompilerParams(vmem_limit_bytes=55168 * 1024)


def rows_of(*shape):
    return jax.ShapeDtypeStruct(shape, F32)


def vmem(*shape):
    return pltpu.VMEM(shape, F32)


def call(kernel, outs, scratch, params=SMALL):
    return pl.pallas_call(
        kernel,
        out_shape=outs,
        scratch_shapes=scratch,
        cost_estimate=pl.CostEstimate(flops=100000, bytes_accessed=100000, transcendentals=0),
        compiler_params=params,
    )


def ring(sizes, axis, step):
    n = sizes[axis]
    return [(i, (i + step) % n) for i in range(n)]


def exchange_x(sizes, xlo, xhi):
    return (
        lax.ppermute(xhi, "gx", ring(sizes, "gx", 1)),
        lax.ppermute(xlo, "gx", ring(sizes, "gx", -1)),
    )


def exchange_z(sizes, zs):
    return lax.ppermute(zs, "gz", ring(sizes, "gz", 1))


def exchange_yz(sizes, ylo, yhi, zs):
    zr = exchange_z(sizes, zs)
    yl = lax.ppermute(yhi, "gy", ring(sizes, "gy", 1))
    yh = lax.ppermute(ylo, "gy", ring(sizes, "gy", -1))
    return yl, yh, zr


def local(sizes, checkpoint, gruneisen, switch, probes, observed):
    bind = functools.partial
    state = checkpoint.reshape(5, CELLS, NY)
    gamma = gruneisen.reshape(CELLS, NY)
    sw = switch.reshape(2, CELLS, NY)
    plane = rows_of(8, NY)

    def x_slabs(items):
        return [rows_of(items, NZ, NY)] * 2

    pair = rows_of(16, NY)
    tall = (NZ + 2) * NX
    *sent_y, sent_z = call(
        bind(prep_kernel, sizes), [pair, pair, rows_of(11, NX, NY)], [vmem(CELLS, NY)], LARGE
    )(state, gamma, sw)
    got_yz = exchange_yz(sizes, *sent_y, sent_z)
    hits, mean, spread = call(
        probe_kernel,
        [rows_of(CELLS, NY), rows_of(CELLS, NY), rows_of(1, probes.shape[0])],
        [],
    )(probes.reshape(1, -1), observed.reshape(1, -1))
    grid = rows_of(CELLS, NY)
    vel, heat, press, inner, slo, shi = call(still_kernel, [rows_of(3, CELLS, NY), grid, grid, rows_of(5, CELLS, NY)] + x_slabs(16), [])(
        state, gamma, sw
    )
    part, xlo, xhi, zz = call(
        bind(side_kernel, sizes),
        [rows_of(5, CELLS, NY)] + x_slabs(18) + [pair],
        [
            vmem(tall, NY), vmem(5, tall, NY), vmem(5, tall, NY), vmem(32, NY),
        ],
    )(state, sw, vel, press, inner, slo, shi, *sent_y, *got_yz)
    got_x = exchange_x(sizes, xlo, xhi)
    zz = exchange_z(sizes, zz)
    tied = rows_of(6 * NX, NY)
    state_1, lam_2, coef, coef_halo, mis, beside, *sent, yown = call(
        bind(forward_kernel, sizes),
        [rows_of(5, CELLS, NY), rows_of(2, CELLS, NY), rows_of(CELLS, NY), rows_of(2, NZ, NY), plane]
        + [rows_of(6, NZ, NY), tied, tied, rows_of(6, NX, NY), plane],
        [
            vmem(5, NZ, NY), vmem(5, NZ, NY), vmem(8, NY), vmem(8, NY), vmem(2, NX, NY),
            vmem(NZ * 24, NY), vmem(5, NZ * 16, NY), vmem(5, NZ * 16, NY), vmem(2, tall, NY), vmem(2, tall, NY),
            vmem(2, CELLS, NY), vmem(CELLS, 8), vmem(CELLS, NY), vmem(CELLS, 8),
        ],
    )(state, gamma, sw, vel, press, part, *sent_y, *got_yz, *got_x, zz, hits, mean)
    got_yz = exchange_yz(sizes, *sent)
    sent = call(bind(edge_kernel, sizes), x_slabs(5), [vmem(CELLS, NY)])(state_1, lam_2, coef, *got_yz)
    got_x = exchange_x(sizes, *sent)
    lean = call(
        bind(lean_kernel, sizes),
        [rows_of(3, CELLS, NY), rows_of(3, CELLS, NY), grid, grid],
        [vmem(2, tall, NY), vmem(CELLS, 8)],
    )(state_1, lam_2, *got_yz)
    devices = sizes["gx"] * sizes["gy"] * sizes["gz"]
    gradient, rows = call(
        bind(gradient_kernel, sizes),
        [rows_of(CELLS, NY), rows_of(devices, NARROW)],
        [
            vmem(2, NZ * 24, NY), vmem(CELLS, NY), vmem(NZ * 24, NY), vmem(CELLS, NY),
            vmem(CELLS, 8), vmem(2, NZ * 24, NY), vmem(CELLS, NY), vmem(2, tall, NY),
        ],
    )(vel, heat, state_1, gamma, *lean, lam_2, coef, coef_halo, beside, yown, *got_yz, *got_x, mis, spread)
    rows = lax.all_to_all(rows, ("gx", "gy", "gz"), 0, 0, tiled=True)
    direction, misfit = pl.pallas_call(
        bind(scale_kernel, devices, probes.shape[0]),
        out_shape=[rows_of(CELLS, NY), rows_of(1, 1)],
        out_specs=[pl.BlockSpec(memory_space=pltpu.VMEM), pl.BlockSpec(memory_space=pltpu.SMEM)],
        compiler_params=SMALL,
    )(gradient, rows)
    return direction.reshape(NZ, NX, NY), misfit.reshape(())


def solution(mesh):
    block = P("gz", "gx", "gy")
    parted = P(None, "gz", "gx", "gy")
    listed = P(("gx", "gy", "gz"))
    return jax.shard_map(
        functools.partial(local, dict(mesh.shape)),
        mesh=mesh,
        in_specs=(parted, block, parted, listed, listed),
        out_specs=(block, P()),
        check_vma=False,
    )
```

```python
import functools
import jax
import jax.numpy as jnp
from jax import lax
from jax.experimental import pallas as pl
from jax.experimental.pallas import tpu as pltpu
from jax.sharding import PartitionSpec as P

NZ, NX, NY = 16, 8, 128
CELLS = NZ * NX
bulk_modulus = 2.0
slope_coeff = 1.5
signal_speed = 2.5
time_ratio = 0.1
quad_viscosity = 4.0
small_eps = 1e-12
HALF_C = 0.5 * signal_speed
HALF_T = 0.5 * time_ratio
NEAR = time_ratio * HALF_C
STAY = 1.0 - 3.0 * time_ratio * signal_speed
F32 = jnp.float32
NARROW = 8


def primitives(r, mx, my, mz, en, gamma):
    inv = 1.0 / (1.0 + r)
    ux, uy, uz = mx * inv, my * inv, mz * inv
    heat = en - 0.5 * (mx * ux + my * uy + mz * uz)
    press = bulk_modulus * (r + slope_coeff * r * r) + gamma * heat
    return ux, uy, uz, heat, press


def total_pressure(press, sw, r, slope):
    squeeze = jnp.minimum(slope, 0.0)
    return press + sw * quad_viscosity * (1.0 + r) * squeeze * squeeze


def flux(state, axis, speed, total):
    rows = [state[1 + axis]] + [state[1 + k] * speed for k in range(3)]
    rows[1 + axis] = rows[1 + axis] + total
    return rows + [(state[4] + total) * speed]


def upper_part(f, u):
    return 0.5 * f - HALF_C * u


def lower_part(f, u):
    return 0.5 * f + HALF_C * u


def layer(z):
    return pl.ds(NX * z, NX)


def x_row(x):
    return pl.ds(x, NZ, stride=NX)


def lanes():
    return lax.broadcasted_iota(jnp.int32, (NX, NY), 1)


def y_next(value, column, lane):
    return jnp.where(lane == NY - 1, column, pltpu.roll(value, NY - 1, 1))


def y_prev(value, column, lane):
    return jnp.where(lane == 0, column, pltpu.roll(value, 1, 1))


def inside(flag):
    return jnp.where(flag, 1.0, 0.0).astype(F32)


def masks(mesh):
    ix, iy, iz = lax.axis_index("gx"), lax.axis_index("gy"), lax.axis_index("gz")
    return (
        (inside(ix > 0), inside(ix < mesh["gx"] - 1)),
        (inside(iy > 0), inside(iy < mesh["gy"] - 1)),
        (inside(iz > 0), inside(iz < mesh["gz"] - 1)),
        iz == 0,
    )


def face_layer(is_first, depth):
    return jnp.where(is_first, NZ - 1 - depth, depth)


def dyn_layer(z):
    return pl.ds(pl.multiple_of(NX * z, NX), NX)


def pack_edges(values, lane, depth=2):
    out = pltpu.roll(values[0], depth, 1)
    for i in range(1, len(values)):
        out = jnp.where(lane < 2 * depth * i, out, pltpu.roll(values[i], depth * (2 * i + 1), 1))
    return out


def begun(u, f, far, sign):
    return STAY * u + time_ratio * (sign * 0.5 * f + HALF_C * far)


def prep_kernel(mesh, u_ref, g_ref, s_ref, ylo, yhi, zs, yp):
    _, _, _, first = masks(mesh)
    lane = lanes()
    for z in range(NZ):
        vals = [u_ref[k, layer(z), :] for k in range(5)]
        vals += [g_ref[layer(z), :], s_ref[0, layer(z), :].astype(F32)]
        yp[layer(z), :] = pack_edges(vals, lane, 3)
    rows = yp[...].T
    for out, c1, c2, c3, sign in ((yhi, 2, 1, 0, 1.0), (ylo, 3, 4, 5, -1.0)):
        st, st2, st3 = [[rows[6 * k + c : 6 * k + c + 1] for k in range(7)] for c in (c1, c2, c3)]
        prim, prim2 = primitives(*st[:6]), primitives(*st2[:6])
        slope = (sign * 0.5) * (prim[1] - st3[2] / (1.0 + st3[0]))
        fl = flux(st2[:5], 1, prim2[1], total_pressure(prim2[4], st2[6], st2[0], slope))
        items = st[:5] + [prim[4], st[6], prim2[1]] + [begun(st[k], fl[k], st2[k], sign) for k in range(3)]
        for k in range(11):
            out[k : k + 1] = items[k]
        out[11:16] = jnp.zeros((5, NY), F32)
    za, zb, zc = [dyn_layer(face_layer(first, d)) for d in range(3)]
    sign = jnp.where(first, 1.0, -1.0)
    st, st2 = [[u_ref[k, at, :] for k in range(5)] for at in (za, zb)]
    prim, prim2 = primitives(*st, g_ref[za, :]), primitives(*st2, g_ref[zb, :])
    slope = (sign * 0.5) * (prim[2] - u_ref[3, zc, :] / (1.0 + u_ref[0, zc, :]))
    fl = flux(st2, 2, prim2[2], total_pressure(prim2[4], s_ref[0, zb, :].astype(F32), st2[0], slope))
    items = st + [prim[4], s_ref[0, za, :].astype(F32), prim2[2]]
    items += [begun(st[k], fl[k], st2[k], sign) for k in (0, 1, 3)]
    for k in range(11):
        zs[k] = items[k]


def still_kernel(u_ref, g_ref, s_ref, vel, heat, press, inner, slo, shi):
    lane = lanes()
    for z in range(NZ):
        prim = primitives(*[u_ref[k, layer(z), :] for k in range(5)], g_ref[layer(z), :])
        for k in range(3):
            vel[k, layer(z), :] = prim[k]
        heat[layer(z), :] = prim[3]
        press[layer(z), :] = prim[4]
        st = [u_ref[k, layer(z), :] for k in range(5)]
        uy = prim[1]
        squeeze = jnp.minimum(0.5 * (pltpu.roll(uy, NY - 1, 1) - pltpu.roll(uy, 1, 1)), 0.0)
        squeeze = jnp.where((lane == 0) | (lane == NY - 1), 0.0, squeeze)
        visc = s_ref[0, layer(z), :].astype(F32) * quad_viscosity * (1.0 + st[0])
        fy = flux(st, 1, uy, prim[4] + visc * squeeze * squeeze)
        for k in range(5):
            inner[k, layer(z), :] = STAY * st[k] - time_ratio * (
                y_next(upper_part(fy[k], st[k]), 0.0, lane) - y_prev(lower_part(fy[k], st[k]), 0.0, lane)
            )
    for out, e, i, j, last, sign in ((shi, NX - 1, NX - 2, NX - 3, NX - 4, 1.0), (slo, 0, 1, 2, 3, -1.0)):
        for k in range(5):
            out[k] = u_ref[k, x_row(e), :]
        out[5] = g_ref[x_row(e), :]
        out[6] = s_ref[0, x_row(e), :].astype(F32)
        out[7] = vel[0, x_row(i), :]
        out[8] = s_ref[1, x_row(e), :].astype(F32)
        for at, before, after, base, count in ((i, e, j, 9, 5), (j, i, last, 14, 2)):
            st = [u_ref[k, x_row(at), :] for k in range(5)]
            slope = (sign * 0.5) * (vel[0, x_row(before), :] - vel[0, x_row(after), :])
            total = total_pressure(press[x_row(at), :], s_ref[0, x_row(at), :].astype(F32), st[0], slope)
            fl = flux(st, 0, vel[0, x_row(at), :], total)
            for k in range(count):
                out[base + k] = time_ratio * (sign * 0.5 * fl[k] + HALF_C * st[k])


def side_kernel(
    mesh, u_ref, s_ref, vel, pr, inner, slo, shi, ylo, yhi, yl, yh, zr,
    part, xlo, xhi, zz,
    vz, az, bz, yr,
):
    _, (myl, myh), (mzl, mzh), first = masks(mesh)
    for z in range(NZ):
        vz[layer(z + 1), :] = vel[2, layer(z), :]
    far = [zr[k] for k in range(8)]
    speed = far[3] / (1.0 + far[0])
    own = vel[2, dyn_layer(face_layer(first, 0)), :]
    slope = (far[7] - own) * jnp.where(first, 0.5, -0.5)
    fl = flux(far[:5], 2, speed, total_pressure(far[5], far[6], far[0], slope))
    for k in range(5):
        bz[k, layer(0), :] = lower_part(fl[k], far[k]) * mzl
        az[k, layer(NZ), :] = upper_part(fl[k], far[k]) * mzh
    vz[layer(0), :] = speed * mzl
    vz[layer(NZ + 1), :] = speed * mzh
    yr[...] = jnp.zeros(yr.shape, F32)
    sides = []
    for side, ref, mask, own, sign in ((0, yl, myl, ylo, 1.0), (1, yh, myh, yhi, -1.0)):
        items = [ref[k : k + 1] * mask for k in range(8)]
        sides.append(items)
        speed = items[2] / (1.0 + items[0])
        uy = own[2:3] / (1.0 + own[0:1])
        slope = (sign * 0.5) * (uy - items[7])
        fl = flux(items[:5], 1, speed, total_pressure(items[5], items[6], items[0], slope))
        squeeze = jnp.minimum((sign * 0.5) * (own[7:8] - speed), 0.0)
        visc = own[6:7] * quad_viscosity * (1.0 + own[0:1]) * squeeze * squeeze
        for k in range(5):
            at = 4 * k + side
            yr[at : at + 1, :] = time_ratio * (sign * 0.5 * fl[k] + HALF_C * items[k])
        yr[10 + side : 11 + side, :] = (sign * HALF_T) * visc
        yr[18 + side : 19 + side, :] = (sign * HALF_T) * visc * uy
    low, high = sides
    parts = jnp.concatenate([piece.astype(F32) for piece in split3(yr[...].T)], axis=1).astype(jnp.bfloat16)
    item = lax.bitwise_and(lax.broadcasted_iota(jnp.int32, (3 * yr.shape[0], NY), 0), yr.shape[0] - 1)
    column = lax.broadcasted_iota(jnp.int32, (3 * yr.shape[0], NY), 1)
    for k in range(5):
        place = (item == 4 * k) & (column == 0) | (item == 4 * k + 1) & (column == NY - 1)
        place = place | (item == 4 * k + 2) & (column == 1) | (item == 4 * k + 3) & (column == NY - 2)
        spread = jnp.where(place, 1.0, 0.0).astype(jnp.bfloat16)
        part[k] = inner[k] + jnp.dot(parts, spread, preferred_element_type=F32)
    for z in range(NZ):
        st = [u_ref[k, layer(z), :] for k in range(5)]
        squeeze = jnp.minimum(0.5 * (vz[layer(z + 2), :] - vz[layer(z), :]), 0.0)
        visc = s_ref[0, layer(z), :].astype(F32) * quad_viscosity * (1.0 + st[0])
        fz = flux(st, 2, vel[2, layer(z), :], pr[layer(z), :] + visc * squeeze * squeeze)
        for k in range(5):
            az[k, layer(z), :] = upper_part(fz[k], st[k])
            bz[k, layer(z + 1), :] = lower_part(fz[k], st[k])
    for z in range(NZ):
        for k in range(5):
            part[k, layer(z), :] = part[k, layer(z), :] - time_ratio * (
                az[k, layer(z + 1), :] - bz[k, layer(z), :]
            )
    for k in range(8):
        zz[k : k + 1, :] = low[k]
        zz[8 + k : 9 + k, :] = high[k]
    for out, still, e, i in ((xhi, shi, NX - 1, NX - 2), (xlo, slo, 0, 1)):
        for k in range(9):
            out[k] = still[k]
        for k in range(5):
            out[9 + k] = part[k, x_row(e), :] + still[9 + k]
        for k in range(2):
            out[14 + k] = part[k, x_row(i), :] + still[14 + k]
        out[16] = zz[...]
        for k in range(8):
            out[17, k : k + 1, :] = zr[k, e : e + 1, :]
        out[17, 8:9, :] = zr[1, i : i + 1, :] / (1.0 + zr[0, i : i + 1, :])
        out[17, 9:16, :] = jnp.zeros((7, NY), F32)


def shifted_x(own, low, high, at_x):
    up = jnp.where(at_x == NX - 1, pltpu.roll(high, NX - 1, 1), pltpu.roll(own, NY - 1, 1))
    down = jnp.where(at_x == 0, pltpu.roll(low, NY - NX + 1, 1), pltpu.roll(own, 1, 1))
    return up, down


def halo_step(
    mesh, u_ref, g_ref, s_ref, vel, pr, part, ylo, yhi, yl, yh, zr, xl, xh, zz,
    o_ref, xc, hxl, hxh, hyl, hyh, hz, vx, ax, bx, zc,
):
    (mxl, mxh), (myl, myh), (mzl, mzh), first = masks(mesh)
    for z in range(NZ):
        vx[pl.ds(24 * z + 8, 8), :] = vel[0, layer(z), :]
    low = [xl[k] * mxl for k in range(8)]
    high = [xh[k] * mxh for k in range(8)]
    prim = primitives(*low[:6])
    vx[pl.ds(7, NZ, stride=24), :] = prim[0]
    slope = 0.5 * (vx[pl.ds(8, NZ, stride=24), :] - low[7])
    f_low = flux(low[:5], 0, prim[0], total_pressure(prim[4], low[6], low[0], slope))
    prim = primitives(*high[:6])
    vx[pl.ds(16, NZ, stride=24), :] = prim[0]
    slope = 0.5 * (high[7] - vx[pl.ds(15, NZ, stride=24), :])
    f_high = flux(high[:5], 0, prim[0], total_pressure(prim[4], high[6], high[0], slope))
    for k in range(5):
        bx[k, pl.ds(7, NZ, stride=16), :] = lower_part(f_low[k], low[k])
        ax[k, pl.ds(8, NZ, stride=16), :] = upper_part(f_high[k], high[k])
    for z in range(NZ):
        st = [u_ref[k, layer(z), :] for k in range(5)]
        ux, press = vel[0, layer(z), :], pr[layer(z), :]
        slope = 0.5 * (vx[pl.ds(24 * z + 9, 8), :] - vx[pl.ds(24 * z + 7, 8), :])
        fx = flux(st, 0, ux, total_pressure(press, s_ref[0, layer(z), :].astype(F32), st[0], slope))
        for k in range(5):
            ax[k, pl.ds(16 * z, 8), :] = upper_part(fx[k], st[k])
            bx[k, pl.ds(16 * z + 8, 8), :] = lower_part(fx[k], st[k])
    for z in range(NZ):
        for k in range(5):
            o_ref[k, layer(z), :] = part[k, layer(z), :] - time_ratio * (
                ax[k, pl.ds(16 * z + 1, 8), :] - bx[k, pl.ds(16 * z + 7, 8), :]
            )
    for out, ref, mask in ((hxl, xl, mxl), (hxh, xh, mxh)):
        if ref is xl:
            near = [-ax[k, pl.ds(0, NZ, stride=16), :] for k in range(5)]
            next_ = [-upper_part(f_low[k], low[k]) for k in range(2)]
        else:
            near = [bx[k, pl.ds(15, NZ, stride=16), :] for k in range(5)]
            next_ = [lower_part(f_high[k], high[k]) for k in range(2)]
        st = [(ref[9 + k] + time_ratio * near[k]) * mask for k in range(5)]
        st2 = [(ref[14 + k] + time_ratio * next_[k]) * mask for k in range(2)]
        out[0] = st[0]
        out[1] = st[1]
        out[2] = primitives(*st, ref[5] * mask)[4]
        out[3] = ref[8] * mask
        out[4] = st2[1] / (1.0 + st2[0])
        base = 0 if ref is xl else 3
        inv, gamma = 1.0 / (1.0 + st[0]), ref[5] * mask
        xc[base] = (2.0 - gamma) * (st[1] * inv)
        xc[base + 1] = inv
        xc[base + 2] = gamma
    lane = lax.broadcasted_iota(jnp.int32, (1, NY), 1)
    at_x = lax.bitwise_and(lane, NX - 1)
    for side, ref, mask, own, out, sign in ((0, yl, myl, ylo, hyl, -1.0), (1, yh, myh, yhi, hyh, 1.0)):

        def items(values, m):
            return [values[k : k + 1] * m for k in range(8)]

        here = items(ref, mask)
        near_l, near_h = items(xl[16, 8 * side : 8 * side + 8, :], mxl), items(xh[16, 8 * side : 8 * side + 8, :], mxh)
        ux, ux_l, ux_h = [v[1] / (1.0 + v[0]) for v in (here, near_l, near_h)]
        up, down = shifted_x(ux, ux_l, ux_h, at_x)
        slope = 0.5 * (up - down)
        slope_h = 0.5 * (pltpu.roll(ux_h, NY - 1, 1) - pltpu.roll(ux, NY - NX + 1, 1))
        slope_l = 0.5 * (pltpu.roll(ux, NX - 1, 1) - pltpu.roll(ux_l, 1, 1))

        def fx_of(v, speed, slope):
            return [v[1], v[1] * speed + total_pressure(v[5], v[6], v[0], slope), v[2] * speed]

        f_here, f_l, f_h = fx_of(here, ux, slope), fx_of(near_l, ux_l, slope_l), fx_of(near_h, ux_h, slope_h)
        uz = here[3] / (1.0 + here[0])
        near_z = items(zz[8 * side : 8 * side + 8, :], 1.0)
        uz_z = near_z[3] / (1.0 + near_z[0])
        fz, fz_z = [[v[3], v[1] * w, v[2] * w] for v, w in ((here, uz), (near_z, uz_z))]
        self_ = items(own, 1.0)
        uy = self_[2] / (1.0 + self_[0])
        uy_here = here[2] / (1.0 + here[0])
        slope = 0.5 * (self_[7] - uy_here if side == 0 else uy_here - self_[7])
        fy = [self_[2], self_[1] * uy, self_[2] * uy + total_pressure(self_[5], self_[6], self_[0], slope)]
        new = []
        for k in range(3):
            a_x, _ = shifted_x(upper_part(f_here[k], here[k]), ux_l, upper_part(f_h[k], near_h[k]), at_x)
            _, b_x = shifted_x(lower_part(f_here[k], here[k]), lower_part(f_l[k], near_l[k]), ux_h, at_x)
            a_z = jnp.where(
                lane >= NY - NX,
                pltpu.roll(upper_part(fz_z[k], near_z[k]), NY - NX, 1) * mzh,
                pltpu.roll(upper_part(fz[k], here[k]), NY - NX, 1),
            )
            b_z = jnp.where(
                lane < NX,
                pltpu.roll(lower_part(fz_z[k], near_z[k]), NX, 1) * mzl,
                pltpu.roll(lower_part(fz[k], here[k]), NX, 1),
            )
            facing = sign * 0.5 * fy[k] + HALF_C * self_[k]
            new.append(mask * (ref[8 + k : 9 + k] + time_ratio * (facing - (a_x - b_x) - (a_z - b_z))))
        r, mx, my = new
        combine = lower_part if side == 0 else upper_part
        out[0:1, :] = combine(my, r)
        out[1:2, :] = combine(mx * (my / (1.0 + r)), mx)
        out[2:8, :] = jnp.zeros((6, NY), F32)
    rows = []
    for side in range(2):
        v = [zz[8 * side + k : 8 * side + k + 1, :] for k in range(8)]
        speed = v[2] / (1.0 + v[0])
        fy = [v[2], v[1] * speed, v[3] * speed]
        combine = upper_part if side else lower_part
        rows += [combine(f, v[k]) for f, k in zip(fy, (0, 1, 3))]
    zc[...] = jnp.concatenate(rows + [jnp.zeros((2, NY), F32)], axis=0).T
    cols = zc[dyn_layer(jnp.where(first, 0, NZ - 1)), :]
    full = lanes()
    deep = lax.broadcasted_iota(jnp.int32, (NX, NY), 0)
    here = [zr[k] for k in range(8)]
    near_l = [xl[17, k : k + 1, :] * mxl for k in range(9)]
    near_h = [xh[17, k : k + 1, :] * mxh for k in range(9)]
    ux, ux_l, ux_h = [v[1] / (1.0 + v[0]) for v in (here, near_l, near_h)]

    def next_x(value, row):
        return jnp.where(deep == NX - 1, row, pltpu.roll(value, NX - 1, 0))

    def prev_x(value, row):
        return jnp.where(deep == 0, row, pltpu.roll(value, 1, 0))

    slope = 0.5 * (next_x(ux, ux_h) - prev_x(ux, ux_l))
    slope_h = 0.5 * (near_h[8] - ux[NX - 1 : NX])
    slope_l = 0.5 * (ux[0:1] - near_l[8])

    def fx_layer(v, speed, slope):
        return [v[1], v[1] * speed + total_pressure(v[5], v[6], v[0], slope), v[3] * speed]

    f_here, f_l, f_h = fx_layer(here, ux, slope), fx_layer(near_l, ux_l, slope_l), fx_layer(near_h, ux_h, slope_h)
    uy = here[2] / (1.0 + here[0])
    fy = [here[2], here[1] * uy, here[3] * uy]
    za, zb = dyn_layer(face_layer(first, 0)), dyn_layer(face_layer(first, 1))
    sign = jnp.where(first, 1.0, -1.0)
    st = [u_ref[k, za, :] for k in range(5)]
    slope = (sign * 0.5) * (here[3] / (1.0 + here[0]) - vel[2, zb, :])
    fz = flux(st, 2, vel[2, za, :], total_pressure(pr[za, :], s_ref[0, za, :].astype(F32), st[0], slope))
    new = []
    for n, k in enumerate((0, 1, 3)):
        a_x = next_x(upper_part(f_here[n], here[k]), upper_part(f_h[n], near_h[k]))
        b_x = prev_x(lower_part(f_here[n], here[k]), lower_part(f_l[n], near_l[k]))
        a_y = y_next(upper_part(fy[n], here[k]), cols[:, 3 + n : 4 + n], full)
        b_y = y_prev(lower_part(fy[n], here[k]), cols[:, n : n + 1], full)
        facing = sign * 0.5 * fz[k] + HALF_C * st[k]
        new.append(zr[8 + n] + time_ratio * (facing - (a_x - b_x) - (a_y - b_y)))
    r, mx, mz = new
    hz[0] = 0.5 * mz - (sign * HALF_C) * r
    hz[1] = 0.5 * mx * (mz / (1.0 + r)) - (sign * HALF_C) * mx


def forward_kernel(
    mesh, u0_ref, g_ref, s_ref, vel, pr, part, ylo_in, yhi_in, yl, yh, zr, xl, xh, zz, n_ref, m_ref,
    u_ref, lam_ref, cf_ref, cfh_ref, mis_ref, xc, ylo, yhi, zs, yown,
    hxl, hxh, hyl, hyh, hz, vx, ax, bx, az, bz, ch, yc, yp, zc,
):
    halo_step(
        mesh, u0_ref, g_ref, s_ref, vel, pr, part, ylo_in, yhi_in, yl, yh, zr, xl, xh, zz,
        u_ref, xc, hxl, hxh, hyl, hyh, hz, vx, ax, bx, zc,
    )
    speed_kernel(
        mesh, u_ref, g_ref, s_ref, hxl, hxh, hyl, hyh, hz, n_ref, m_ref,
        lam_ref, cf_ref, cfh_ref, mis_ref, ylo, yhi, zs, yown,
        vx, ax, bx, az, bz, ch, yc, yp,
    )


def columns_of(low, high, count, low_mask, high_mask):
    rows = [low[k : k + 1] * low_mask for k in range(count)]
    rows += [high[k : k + 1] * high_mask for k in range(count)]
    rows.append(jnp.zeros((8 - 2 * count, NY), F32))
    return jnp.concatenate(rows, axis=0).T


def speed_kernel(
    mesh, u_ref, g_ref, s_ref, xl, xh, yl, yh, zr, n_ref, m_ref,
    lam_ref, cf_ref, cfh_ref, mis_ref, ylo, yhi, zs, yown,
    vx, ax, bx, az, bz, ch, yc, yp,
):
    (mxl, mxh), (myl, myh), (mzl, mzh), first = masks(mesh)
    lane = lanes()
    for z in range(NZ):
        vx[pl.ds(24 * z + 8, 8), :] = u_ref[1, layer(z), :] / (1.0 + u_ref[0, layer(z), :])
    for side, ref, mask in ((0, xl, mxl), (1, xh, mxh)):
        r, mx, press, sw, second = [ref[k] * mask for k in range(5)]
        speed = mx / (1.0 + r)
        vx[pl.ds(16 if side else 7, NZ, stride=24), :] = speed
        own = vx[pl.ds(15 if side else 8, NZ, stride=24), :]
        slope = 0.5 * (second - own if side else own - second)
        squeeze = jnp.minimum(slope, 0.0)
        visc = sw * quad_viscosity * (1.0 + r) * squeeze
        cfh_ref[side] = 2.0 * visc
        f1 = mx * speed + press + visc * squeeze
        if side:
            ax[0, pl.ds(8, NZ, stride=16), :] = upper_part(mx, r)
            ax[1, pl.ds(8, NZ, stride=16), :] = upper_part(f1, mx)
        else:
            bx[0, pl.ds(7, NZ, stride=16), :] = lower_part(mx, r)
            bx[1, pl.ds(7, NZ, stride=16), :] = lower_part(f1, mx)
    for k in range(2):
        bz[k, layer(0), :] = zr[k] * mzl
        az[k, layer(NZ), :] = zr[k] * mzh
    yc[...] = columns_of(yl, yh, 2, myl, myh)
    for z in range(NZ):
        r, mx, my, mz, en = [u_ref[k, layer(z), :] for k in range(5)]
        ux, uy, uz, _, press = primitives(r, mx, my, mz, en, g_ref[layer(z), :])
        squeeze = jnp.minimum(0.5 * (vx[pl.ds(24 * z + 9, 8), :] - vx[pl.ds(24 * z + 7, 8), :]), 0.0)
        visc = s_ref[1, layer(z), :].astype(F32) * quad_viscosity * (1.0 + r) * squeeze
        cf_ref[layer(z), :] = 2.0 * visc
        f1 = mx * ux + press + visc * squeeze
        for k, st, fx, fy, fz in ((0, r, mx, my, mz), (1, mx, f1, mx * uy, mx * uz)):
            ax[k, pl.ds(16 * z, 8), :] = upper_part(fx, st)
            bx[k, pl.ds(16 * z + 8, 8), :] = lower_part(fx, st)
            az[k, layer(z), :] = upper_part(fz, st)
            bz[k, layer(z + 1), :] = lower_part(fz, st)
            ch[k, layer(z), :] = (
                3.0 * signal_speed * st
                + y_next(upper_part(fy, st), yc[layer(z), 2 + k : 3 + k], lane)
                - y_prev(lower_part(fy, st), yc[layer(z), k : k + 1], lane)
            )
    mis = jnp.zeros((NX, NY), F32)
    for z in range(NZ):
        new = []
        for k in range(2):
            change = (
                ch[k, layer(z), :]
                + (ax[k, pl.ds(16 * z + 1, 8), :] - bx[k, pl.ds(16 * z + 7, 8), :])
                + (az[k, layer(z + 1), :] - bz[k, layer(z), :])
            )
            new.append(u_ref[k, layer(z), :] - time_ratio * change)
        inv = 1.0 / (1.0 + new[0])
        speed = new[1] * inv
        off = speed - m_ref[layer(z), :]
        weight = n_ref[layer(z), :] * off
        mis = mis + weight * off
        lam_m = 2.0 * weight * inv
        lam_r = -lam_m * speed
        lam_ref[0, layer(z), :] = lam_r
        lam_ref[1, layer(z), :] = lam_m
        inv = 1.0 / (1.0 + u_ref[0, layer(z), :])
        extra = [u_ref[1, layer(z), :] * inv, u_ref[2, layer(z), :] * inv, g_ref[layer(z), :]]
        yp[layer(z), :] = pack_edges([lam_r, lam_m] + extra, lane)
    mis_ref[...] = mis
    za, zb = dyn_layer(face_layer(first, 0)), dyn_layer(face_layer(first, 1))
    inv = 1.0 / (1.0 + u_ref[0, za, :])
    ux = u_ref[1, za, :] * inv
    zs[0] = lam_ref[0, za, :]
    zs[1] = lam_ref[1, za, :]
    zs[2] = jnp.where(first, -HALF_T, HALF_T) * (lam_ref[0, zb, :] + lam_ref[1, zb, :] * ux)
    zs[3] = ux
    zs[4] = u_ref[3, za, :] * inv
    zs[5] = g_ref[za, :]
    rows = yp[...].T
    for out, edge, second, own, sign in ((yhi, 1, 0, 2, -HALF_T), (ylo, 2, 3, 0, HALF_T)):
        lam_r, lam_m, ux, uy, gamma = [rows[4 * i + edge : 4 * i + edge + 1] for i in range(5)]
        out[0:1] = lam_r
        out[1:2] = lam_m
        out[2:3] = sign * (rows[second : second + 1] + rows[4 + second : 5 + second] * ux)
        out[3:4] = ux
        out[4:5] = uy
        out[5:6] = gamma
        out[6:8] = jnp.zeros((2, NY), F32)
        yown[own : own + 1] = lam_r
        yown[own + 1 : own + 2] = lam_m
    yown[4:8] = jnp.zeros((4, NY), F32)


def edge_kernel(mesh, u_ref, lam_ref, cf_ref, yl, yh, zr, xlo, xhi, yc):
    _, (myl, myh), (mzl, mzh), _ = masks(mesh)
    low_y, high_y = yl[1:2] * myl, yh[1:2] * myh
    yc[:, 0:8] = jnp.concatenate([low_y, high_y, jnp.zeros((6, NY), F32)], axis=0).T
    lane = lax.broadcasted_iota(jnp.int32, (NZ, NY), 1)
    deep = lax.broadcasted_iota(jnp.int32, (NZ, NY), 0)
    for out, e, i, i2, sign in ((xhi, NX - 1, NX - 2, NX - 3, 1.0), (xlo, 0, 1, 2, -1.0)):
        r, my, mz = [u_ref[k, x_row(e), :] for k in (0, 2, 3)]
        inv = 1.0 / (1.0 + r)
        lm, lm_i = lam_ref[1, x_row(e), :], lam_ref[1, x_row(i), :]
        col = yc[x_row(e), :]
        side = zr[1, e : e + 1, :]
        up_y = jnp.where(lane == NY - 1, col[:, 1:2], pltpu.roll(lm, NY - 1, 1))
        down_y = jnp.where(lane == 0, col[:, 0:1], pltpu.roll(lm, 1, 1))
        up_z = jnp.where(deep == NZ - 1, side * mzh, pltpu.roll(lm, NZ - 1, 0))
        down_z = jnp.where(deep == 0, side * mzl, pltpu.roll(lm, 1, 0))
        slope = (sign * HALF_T) * (lm - lam_ref[1, x_row(i2), :]) * cf_ref[x_row(i), :]
        out[0] = lam_ref[0, x_row(e), :]
        out[1] = lm
        out[2] = lm_i
        out[3] = (
            STAY * lm
            + NEAR * (lm_i + (up_y + down_y) + (up_z + down_z))
            - (sign * HALF_T) * lam_ref[0, x_row(i), :]
            + HALF_T * ((up_y - down_y) * (my * inv) + (up_z - down_z) * (mz * inv))
            + (sign * 0.5) * slope * inv
        )
        out[4] = jnp.where(deep == 0, low_y, jnp.where(deep == 1, high_y, jnp.where(deep == 2, side, 0.0)))


def lean_kernel(mesh, u_ref, lam_ref, yl, yh, zr, base, vel, inv_ref, heat, lz, yc):
    _, (myl, myh), (mzl, mzh), _ = masks(mesh)
    lane = lanes()
    for k in range(2):
        for z in range(NZ):
            lz[k, layer(z + 1), :] = lam_ref[k, layer(z), :]
        lz[k, layer(0), :] = zr[k] * mzl
        lz[k, layer(NZ + 1), :] = zr[k] * mzh
    yc[...] = columns_of(yl, yh, 2, myl, myh)
    for z in range(NZ):
        r, mx, my, mz, en = [u_ref[k, layer(z), :] for k in range(5)]
        inv = 1.0 / (1.0 + r)
        ux, uy, uz = mx * inv, my * inv, mz * inv
        heat[layer(z), :] = en - 0.5 * (mx * ux + my * uy + mz * uz)
        inv_ref[layer(z), :] = inv
        for k, value in enumerate((ux, uy, uz)):
            vel[k, layer(z), :] = value
        lr, lm = lam_ref[0, layer(z), :], lam_ref[1, layer(z), :]
        lr_z = [lz[0, layer(z + s), :] for s in (0, 2)]
        lm_z = [lz[1, layer(z + s), :] for s in (0, 2)]
        lr_y = [y_prev(lr, yc[layer(z), 0:1], lane), y_next(lr, yc[layer(z), 2:3], lane)]
        lm_y = [y_prev(lm, yc[layer(z), 1:2], lane), y_next(lm, yc[layer(z), 3:4], lane)]
        phi_y1 = HALF_T * (lm_y[1] - lm_y[0])
        phi_z1 = HALF_T * (lm_z[1] - lm_z[0])
        near = (lm_y[0] + lm_y[1]) + (lm_z[0] + lm_z[1])
        base[0, layer(z), :] = STAY * lm + NEAR * near + phi_y1 * uy + phi_z1 * uz
        base[1, layer(z), :] = HALF_T * (lr_y[1] - lr_y[0]) + phi_y1 * ux
        base[2, layer(z), :] = HALF_T * (lr_z[1] - lr_z[0]) + phi_z1 * ux


def gradient_kernel(
    mesh, vel, heat_ref, u_ref, g_ref, base, vel_1, inv_1, heat_1, lam_ref, cf_ref, cfh_ref, xc, yown, yl, yh, zr, xl, xh, mis_ref, v_ref,
    grad_ref, row_ref,
    lx, px, dx, dg, yc, gx, gy, gz,
):
    (mxl, mxh), (myl, myh), (mzl, mzh), first = masks(mesh)
    lane = lanes()
    for k in range(2):
        for z in range(NZ):
            lx[k, pl.ds(24 * z + 8, 8), :] = lam_ref[k, layer(z), :]
        lx[k, pl.ds(7, NZ, stride=24), :] = xl[k] * mxl
        lx[k, pl.ds(16, NZ, stride=24), :] = xh[k] * mxh
    phi_low = HALF_T * (lam_ref[1, x_row(0), :] - xl[2] * mxl)
    phi_high = HALF_T * (xh[2] * mxh - lam_ref[1, x_row(NX - 1), :])
    dx[pl.ds(7, NZ, stride=24), :] = phi_low * cfh_ref[0]
    dx[pl.ds(16, NZ, stride=24), :] = phi_high * cfh_ref[1]
    for z in range(NZ):
        phi = HALF_T * (lx[1, pl.ds(24 * z + 9, 8), :] - lx[1, pl.ds(24 * z + 7, 8), :])
        px[layer(z), :] = phi
        dx[pl.ds(24 * z + 8, 8), :] = phi * cf_ref[layer(z), :]
    gx[1, pl.ds(7, NZ, stride=24), :] = mxl * phi_low * xc[2]
    gx[1, pl.ds(16, NZ, stride=24), :] = mxh * phi_high * xc[5]
    gx[0, pl.ds(7, NZ, stride=24), :] = mxl * (
        xl[3]
        + HALF_T * lam_ref[0, x_row(0), :]
        + NEAR * lam_ref[1, x_row(0), :]
        + phi_low * xc[0]
        - 0.5 * dx[pl.ds(8, NZ, stride=24), :] * xc[1]
    )
    gx[0, pl.ds(16, NZ, stride=24), :] = mxh * (
        xh[3]
        - HALF_T * lam_ref[0, x_row(NX - 1), :]
        + NEAR * lam_ref[1, x_row(NX - 1), :]
        + phi_high * xc[3]
        + 0.5 * dx[pl.ds(15, NZ, stride=24), :] * xc[4]
    )
    at_x = lax.bitwise_and(lax.broadcasted_iota(jnp.int32, (1, NY), 1), NX - 1)
    from_high, from_low = pltpu.roll(xh[4], NX - 1, 1) * mxh, pltpu.roll(xl[4], NY - NX + 1, 1) * mxl
    halo = []
    for side, ref, mask, sign in ((0, yl, myl, HALF_T), (1, yh, myh, -HALF_T)):
        items = ref[...]
        up = jnp.where(at_x == NX - 1, from_high[side : side + 1], pltpu.roll(items, NY - 1, 1)[1:2])
        down = jnp.where(at_x == 0, from_low[side : side + 1], pltpu.roll(items, 1, 1)[1:2])
        d_en = HALF_T * (up - down) * items[5:6]
        own_r, own_m = yown[2 * side : 2 * side + 1], yown[2 * side + 1 : 2 * side + 2]
        d_my = items[2:3] + sign * (own_r + own_m * items[3:4]) - d_en * items[4:5]
        halo += [d_my * mask, d_en * mask]
    yc[...] = jnp.concatenate(halo + [jnp.zeros((4, NY), F32)], axis=0).T
    deep = lax.broadcasted_iota(jnp.int32, (NX, NY), 0)
    up = jnp.where(deep == NX - 1, xh[4, 2:3, :] * mxh, pltpu.roll(zr[1], NX - 1, 0))
    down = jnp.where(deep == 0, xl[4, 2:3, :] * mxl, pltpu.roll(zr[1], 1, 0))
    d_en = HALF_T * (up - down) * zr[5]
    za = dyn_layer(face_layer(first, 0))
    d_mz = (
        zr[2]
        + jnp.where(first, -HALF_T, HALF_T) * (lam_ref[0, za, :] + lam_ref[1, za, :] * zr[3])
        - d_en * zr[4]
    )
    for k, value in ((0, d_mz), (1, d_en)):
        gz[k, layer(0), :] = value * mzl
        gz[k, layer(NZ + 1), :] = value * mzh
    for z in range(NZ):
        ux, uy, uz = [vel_1[k, layer(z), :] for k in range(3)]
        lr_x = [lx[0, pl.ds(24 * z + s, 8), :] for s in (7, 9)]
        lm_x = [lx[1, pl.ds(24 * z + s, 8), :] for s in (7, 9)]
        phi_x1 = px[layer(z), :]
        d_speed = phi_x1 * u_ref[1, layer(z), :] + 0.5 * (dx[pl.ds(24 * z + 7, 8), :] - dx[pl.ds(24 * z + 9, 8), :])
        d_en = phi_x1 * g_ref[layer(z), :]
        gx[0, pl.ds(24 * z + 8, 8), :] = (
            base[0, layer(z), :]
            + NEAR * (lm_x[0] + lm_x[1])
            + HALF_T * (lr_x[1] - lr_x[0])
            + (phi_x1 - d_en) * ux
            + d_speed * inv_1[layer(z), :]
        )
        gx[1, pl.ds(24 * z + 8, 8), :] = d_en
        gy[layer(z), :] = base[1, layer(z), :] - d_en * uy
        gz[0, layer(z + 1), :] = base[2, layer(z), :] - d_en * uz
        gz[1, layer(z + 1), :] = d_en
        dg[layer(z), :] = phi_x1 * heat_1[layer(z), :]
    acc = jnp.zeros((NX, NY), F32)
    for z in range(NZ):
        ux, uy, uz = [vel[k, layer(z), :] for k in range(3)]
        heat = heat_ref[layer(z), :]
        dif_x = [gx[k, pl.ds(24 * z + 9, 8), :] - gx[k, pl.ds(24 * z + 7, 8), :] for k in range(2)]
        dif_z = [gz[k, layer(z + 2), :] - gz[k, layer(z), :] for k in range(2)]
        dif_y = []
        for k, own in ((0, gy[layer(z), :]), (1, gz[1, layer(z + 1), :])):
            dif_y.append(
                y_next(own, yc[layer(z), 2 + k : 3 + k], lane) - y_prev(own, yc[layer(z), k : k + 1], lane)
            )
        d_press = HALF_T * (
            (dif_x[0] + ux * dif_x[1]) + (dif_y[0] + uy * dif_y[1]) + (dif_z[0] + uz * dif_z[1])
        )
        grad = dg[layer(z), :] + d_press * heat
        grad_ref[layer(z), :] = grad
        acc = acc + grad * grad
    total = jnp.sum(jnp.sum(acc, axis=0, keepdims=True), axis=1, keepdims=True)
    miss = jnp.sum(jnp.sum(mis_ref[...], axis=0, keepdims=True), axis=1, keepdims=True)
    miss = miss + jnp.sum(v_ref[...], axis=1, keepdims=True)
    row = jnp.where(lane == 0, total, jnp.where(lane == 1, miss, 0.0))
    for i in range(row_ref.shape[0] // NX):
        row_ref[layer(i), :] = row[:, :NARROW]


def scale_kernel(devices, count, grad_ref, rows_ref, out_ref, misfit_ref):
    acc = rows_ref[layer(0), :]
    for i in range(1, devices // NX):
        acc = acc + rows_ref[layer(i), :]
    row = jnp.sum(acc, axis=0, keepdims=True)
    misfit_ref[0, 0] = row[0, 1] / (devices * count)
    scale = 1.0 / jnp.sqrt(row[0:1, 0:1] / (devices * CELLS * NY) + small_eps)
    out_ref[...] = grad_ref[...] * scale


def split3(value):
    hi = value.astype(jnp.bfloat16)
    rest = value - hi.astype(F32)
    mid = rest.astype(jnp.bfloat16)
    low = (rest - mid.astype(F32)).astype(jnp.bfloat16)
    return hi, mid, low


def probe_kernel(p_ref, o_ref, n_ref, m_ref, v_ref):
    count = p_ref.shape[1]
    probes, obs = p_ref[...], o_ref[...]
    row = lax.broadcasted_iota(jnp.int32, (CELLS, count), 0)
    on_a = row == lax.shift_right_logical(probes, 7)
    on_b = row == lax.bitwise_and(probes, NY - 1)
    one_a = jnp.where(on_a, 1.0, 0.0).astype(jnp.bfloat16)
    one_b = jnp.where(on_b, 1.0, 0.0).astype(jnp.bfloat16)

    def nt(a, b):
        return lax.dot_general(a, b, (((1,), (1,)), ((), ())), preferred_element_type=F32)

    parts = [jnp.where(on_a, part.astype(F32), 0.0).astype(jnp.bfloat16) for part in split3(obs)]
    hits = nt(one_a, one_b)
    sums = nt(parts[0], one_b) + (nt(parts[1], one_b) + nt(parts[2], one_b))
    n_ref[...] = hits
    mean = sums / jnp.maximum(hits, 1.0)
    m_ref[...] = mean
    mean_t = split3(mean.T)
    picked = sum(jnp.dot(part, one_a, preferred_element_type=F32) for part in reversed(mean_t))
    at_probe = jnp.sum(jnp.where(on_b, picked, 0.0), axis=0, keepdims=True)
    off = obs - at_probe
    v_ref[...] = off * off


SMALL = pltpu.CompilerParams(vmem_limit_bytes=12 * 1024 * 1024)

LARGE = pltpu.CompilerParams(vmem_limit_bytes=55168 * 1024)


def rows_of(*shape):
    return jax.ShapeDtypeStruct(shape, F32)


def vmem(*shape):
    return pltpu.VMEM(shape, F32)


def call(kernel, outs, scratch, params=SMALL):
    return pl.pallas_call(
        kernel,
        out_shape=outs,
        scratch_shapes=scratch,
        cost_estimate=pl.CostEstimate(flops=100000, bytes_accessed=100000, transcendentals=0),
        compiler_params=params,
    )


def ring(sizes, axis, step):
    n = sizes[axis]
    return [(i, (i + step) % n) for i in range(n)]


def exchange_x(sizes, xlo, xhi):
    return (
        lax.ppermute(xhi, "gx", ring(sizes, "gx", 1)),
        lax.ppermute(xlo, "gx", ring(sizes, "gx", -1)),
    )


def exchange_z(sizes, zs):
    return lax.ppermute(zs, "gz", ring(sizes, "gz", 1))


def exchange_yz(sizes, ylo, yhi, zs):
    zr = exchange_z(sizes, zs)
    yl = lax.ppermute(yhi, "gy", ring(sizes, "gy", 1))
    yh = lax.ppermute(ylo, "gy", ring(sizes, "gy", -1))
    return yl, yh, zr


def local(sizes, checkpoint, gruneisen, switch, probes, observed):
    bind = functools.partial
    state = checkpoint.reshape(5, CELLS, NY)
    gamma = gruneisen.reshape(CELLS, NY)
    sw = switch.reshape(2, CELLS, NY)
    plane = rows_of(8, NY)

    def x_slabs(items):
        return [rows_of(items, NZ, NY)] * 2

    pair = rows_of(16, NY)
    tall = (NZ + 2) * NX
    *sent_y, sent_z = pl.pallas_call(
        bind(prep_kernel, sizes),
        out_shape=[pair, pair, rows_of(11, NX, NY)],
        grid=(1,),
        in_specs=[
            pl.BlockSpec((5, CELLS, NY), lambda i: (0, 0, 0)),
            pl.BlockSpec((CELLS, NY), lambda i: (0, 0)),
            pl.BlockSpec((1, CELLS, NY), lambda i: (0, 0, 0)),
        ],
        scratch_shapes=[vmem(CELLS, NY)],
        compiler_params=LARGE,
    )(state, gamma, sw)
    got_yz = exchange_yz(sizes, *sent_y, sent_z)
    hits, mean, spread = call(
        probe_kernel,
        [rows_of(CELLS, NY), rows_of(CELLS, NY), rows_of(1, probes.shape[0])],
        [],
    )(probes.reshape(1, -1), observed.reshape(1, -1))
    grid = rows_of(CELLS, NY)
    vel, heat, press, inner, slo, shi = call(still_kernel, [rows_of(3, CELLS, NY), grid, grid, rows_of(5, CELLS, NY)] + x_slabs(16), [])(
        state, gamma, sw
    )
    part, xlo, xhi, zz = call(
        bind(side_kernel, sizes),
        [rows_of(5, CELLS, NY)] + x_slabs(18) + [pair],
        [
            vmem(tall, NY), vmem(5, tall, NY), vmem(5, tall, NY), vmem(32, NY),
        ],
    )(state, sw, vel, press, inner, slo, shi, *sent_y, *got_yz)
    got_x = exchange_x(sizes, xlo, xhi)
    zz = exchange_z(sizes, zz)
    state_1, lam_2, coef, coef_halo, mis, beside, *sent, yown = call(
        bind(forward_kernel, sizes),
        [rows_of(5, CELLS, NY), rows_of(2, CELLS, NY), rows_of(CELLS, NY), rows_of(2, NZ, NY), plane]
        + [rows_of(6, NZ, NY), plane, plane, rows_of(6, NX, NY), plane],
        [
            vmem(5, NZ, NY), vmem(5, NZ, NY), vmem(8, NY), vmem(8, NY), vmem(2, NX, NY),
            vmem(NZ * 24, NY), vmem(5, NZ * 16, NY), vmem(5, NZ * 16, NY), vmem(2, tall, NY), vmem(2, tall, NY),
            vmem(2, CELLS, NY), vmem(CELLS, 8), vmem(CELLS, NY), vmem(CELLS, 8),
        ],
    )(state, gamma, sw, vel, press, part, *sent_y, *got_yz, *got_x, zz, hits, mean)
    got_yz = exchange_yz(sizes, *sent)
    sent = call(bind(edge_kernel, sizes), x_slabs(5), [vmem(CELLS, NY)])(state_1, lam_2, coef, *got_yz)
    got_x = exchange_x(sizes, *sent)
    lean = call(
        bind(lean_kernel, sizes),
        [rows_of(3, CELLS, NY), rows_of(3, CELLS, NY), grid, grid],
        [vmem(2, tall, NY), vmem(CELLS, 8)],
    )(state_1, lam_2, *got_yz)
    devices = sizes["gx"] * sizes["gy"] * sizes["gz"]
    gradient, rows = call(
        bind(gradient_kernel, sizes),
        [rows_of(CELLS, NY), rows_of(devices, NARROW)],
        [
            vmem(2, NZ * 24, NY), vmem(CELLS, NY), vmem(NZ * 24, NY), vmem(CELLS, NY),
            vmem(CELLS, 8), vmem(2, NZ * 24, NY), vmem(CELLS, NY), vmem(2, tall, NY),
        ],
    )(vel, heat, state_1, gamma, *lean, lam_2, coef, coef_halo, beside, yown, *got_yz, *got_x, mis, spread)
    rows = lax.all_to_all(rows, ("gx", "gy", "gz"), 0, 0, tiled=True)
    direction, misfit = pl.pallas_call(
        bind(scale_kernel, devices, probes.shape[0]),
        out_shape=[rows_of(CELLS, NY), rows_of(1, 1)],
        out_specs=[pl.BlockSpec(memory_space=pltpu.VMEM), pl.BlockSpec(memory_space=pltpu.SMEM)],
        compiler_params=SMALL,
    )(gradient, rows)
    return direction.reshape(NZ, NX, NY), misfit.reshape(())


def solution(mesh):
    block = P("gz", "gx", "gy")
    parted = P(None, "gz", "gx", "gy")
    listed = P(("gx", "gy", "gz"))
    return jax.shard_map(
        functools.partial(local, dict(mesh.shape)),
        mesh=mesh,
        in_specs=(parted, block, parted, listed, listed),
        out_specs=(block, P()),
        check_vma=False,
    )
```
